128 devices in a mesh: seq: 8 (over z_hi, y), fsdp: 16 (over x, z_lo, core).
Axes of the slice: x: 4, y: 4, z: 4 (z_hi: 2, z_lo: 2; z = z_hi * 2 + z_lo), core: 2. Of those that a mesh axis runs over, the one named last changes fastest.
Arguments:
- hidden_in: bfloat16 [16, 1024, 2048], P('fsdp', 'seq'), may hold values from -6 to 6
- cotangent: bfloat16 [16, 1024, 2048], P('fsdp', 'seq'), may hold values from -6 to 6
- seq_lengths: int32 [16, 2], P('fsdp'), may hold values from 65 to 896, as said below
- slot_block: int32 [16, 8], P('fsdp'), may hold values from 0 to 7, as said below
- ln1_gain: bfloat16 [2048], P(('seq', 'fsdp')), may hold values from 0.25 to 1.75
- ln1_bias: bfloat16 [2048], P(('seq', 'fsdp')), may hold values from -1.1953125 to 1.1953125
- w_qkv: bfloat16 [2048, 6144], P(('seq', 'fsdp')), may hold values from -0.125 to 0.125
- qkv_bias: bfloat16 [6144], P(('seq', 'fsdp')), may hold values from -1.1953125 to 1.1953125
- w_out: bfloat16 [2048, 2048], P(('seq', 'fsdp')), may hold values from -0.5 to 0.5
- ln2_gain: bfloat16 [2048], P(('seq', 'fsdp')), may hold values from 0.25 to 1.75
- ln2_bias: bfloat16 [2048], P(('seq', 'fsdp')), may hold values from -1.1953125 to 1.1953125
- w_gate: bfloat16 [2048, 5632], P(('seq', 'fsdp')), may hold values from -0.125 to 0.125
- w_up: bfloat16 [2048, 5632], P(('seq', 'fsdp')), may hold values from -0.125 to 0.125
- w_down: bfloat16 [2048, 5632], P(('seq', 'fsdp')), may hold values from -0.078125 to 0.078125
Outputs:
- hidden_out: bfloat16 [16, 1024, 2048], P('fsdp', 'seq')
- input_grad: float32 [16, 1024, 2048], P('fsdp', 'seq')
- ln1_gain_grad: float32 [2048], P(('seq', 'fsdp'))
- ln1_bias_grad: float32 [2048], P(('seq', 'fsdp'))
- w_qkv_grad: float32 [2048, 6144], P(('seq', 'fsdp'))
- qkv_bias_grad: float32 [6144], P(('seq', 'fsdp'))
- w_out_grad: float32 [2048, 2048], P(('seq', 'fsdp'))
- ln2_gain_grad: float32 [2048], P(('seq', 'fsdp'))
- ln2_bias_grad: float32 [2048], P(('seq', 'fsdp'))
- w_gate_grad: float32 [2048, 5632], P(('seq', 'fsdp'))
- w_up_grad: float32 [2048, 5632], P(('seq', 'fsdp'))
- w_down_grad: float32 [2048, 5632], P(('seq', 'fsdp'))
The draws below stay inside these ranges and needn't reach their ends.
Inputs may be any that keep to these rules, and one draw needn't show every extreme that they name: `seq_lengths`: each group holds two sequences, in this order, each padded to whole 128-token blocks; together their blocks fill the group's 8 blocks, and each has less than half a block of padding. `slot_block`: each row is an order of the group's block numbers; slot s lies on seq device s.
All inputs are finite; a program needn't handle non-finite values.
Results may differ from the reference program's by a relative error of at most 0.018.
Values may be sent and summed in bfloat16 or wider, within the bound.
A program may use at most 704 MiB of HBM per device.

```python
import jax
import jax.numpy as jnp
from jax import lax

D = 2048
HEADS = 32
HEAD_DIM = 64
ROT = 16
FF = 5632
BLOCK = 128
BLK_DEV = 1
GROUP_TOK = 1024
N_SEQ = 8
N_FSDP = 16


def group_plan(group_key, forced):
    key_short, key_order, key_trim, key_perm = jax.random.split(group_key, 4)
    total_blocks = BLK_DEV * N_SEQ
    shorter = jax.random.randint(key_short, (), 1, min(total_blocks // 2, total_blocks - 3) + 1)
    shorter = jnp.where(forced, 1, shorter)
    longer = total_blocks - shorter
    long_first = jax.random.randint(key_order, (), 0, 2) == 1
    trim_tokens = jax.random.randint(key_trim, (2,), 0, BLOCK // 2)
    forced_trims = jnp.where(long_first, jnp.array([0, BLOCK // 2 - 1]), jnp.array([BLOCK // 2 - 1, 0]))
    trim_tokens = jnp.where(forced, forced_trims, trim_tokens)
    first_blocks = jnp.where(long_first, longer, shorter)
    lengths = jnp.stack([first_blocks, total_blocks - first_blocks]) * BLOCK - trim_tokens
    long_start = jnp.where(long_first, 0, shorter)
    placing = jax.random.permutation(key_perm, total_blocks)
    targets = ((0, long_start), (N_SEQ // 2 * BLK_DEV, long_start + 1), (total_blocks - 1, long_start + longer - 1))
    for target_slot, target_block in targets:
        current = jnp.argmax(placing == target_block)
        displaced = placing[target_slot]
        placing = placing.at[current].set(displaced).at[target_slot].set(target_block)
    return (lengths.astype(jnp.int32), placing.astype(jnp.int32))


def block_plans(key):
    chooser, plan_key = jax.random.split(key)
    chosen = jax.random.randint(chooser, (), 0, N_FSDP)
    forced_flags = jnp.arange(N_FSDP) == chosen
    return jax.vmap(group_plan)(jax.random.split(plan_key, N_FSDP), forced_flags)


def draw_seq_lengths(key, part):
    return block_plans(key)[0]


def draw_slot_block(key, part):
    return block_plans(key)[1]


def levels(stream_key, shape, cuts, smallest, high):
    level, own = 1.0, jax.random.fold_in(stream_key, 6)
    for dim, shards_of in cuts:
        draws = jnp.exp(jax.random.uniform(jax.random.fold_in(own, dim), (shards_of,), jnp.float32, smallest / len(cuts), high / len(cuts)))
        level = level * jnp.repeat(draws, shape[dim] // shards_of).reshape([-1 if axis == dim else 1 for axis in range(len(shape))])
    return level


def scatter_about(rng, extent, width, most, pieces=(), kind=jnp.bfloat16):
    values = jax.random.normal(rng, extent, jnp.float32) * width
    if len(pieces) > 0:
        values = levels(rng, extent, pieces, -0.22, 0.18) * values
    return jnp.clip(values, min=-most, max=most).astype(kind)


def setup_inputs(seed: int = 0) -> dict:
    splits = jax.random.split(jax.random.key(seed), 15)
    return {
        "hidden_in": scatter_about(splits[0], (N_FSDP, GROUP_TOK, D), 1.0, 6.0, ((0, 16), (1, 8))),
        "cotangent": scatter_about(splits[1], (N_FSDP, GROUP_TOK, D), 1.0, 6.0, ((0, 16), (1, 8))),
        "seq_lengths": draw_seq_lengths(jax.random.fold_in(splits[14], 71), 0),
        "slot_block": draw_slot_block(jax.random.fold_in(splits[14], 71), 0),
        "ln1_gain": jnp.clip(1.0 + 0.15 * jax.random.normal(splits[4], (D,), jnp.float32), 0.25, 1.75).astype(jnp.bfloat16),
        "ln1_bias": scatter_about(splits[5], (D,), 0.3, 1.1953125, ((0, 128),)),
        "w_qkv": scatter_about(splits[6], (D, 3 * D), D ** -0.5, 0.125, ((0, 128),)),
        "qkv_bias": scatter_about(splits[7], (3 * D,), 0.3, 1.1953125, ((0, 128),)),
        "w_out": scatter_about(splits[8], (D, D), (D // 16) ** -0.5, 0.5, ((0, 128),)),
        "ln2_gain": jnp.clip(1.0 + 0.15 * jax.random.normal(splits[9], (D,), jnp.float32), 0.25, 1.75).astype(jnp.bfloat16),
        "ln2_bias": scatter_about(splits[10], (D,), 0.3, 1.1953125, ((0, 128),)),
        "w_gate": scatter_about(splits[11], (D, FF), D ** -0.5, 0.125, ((0, 128),)),
        "w_up": scatter_about(splits[12], (D, FF), D ** -0.5, 0.125, ((0, 128),)),
        "w_down": scatter_about(splits[13], (D, FF), FF ** -0.5, 0.078125, ((0, 128),)),
    }


@jax.custom_vjp
def low(v):
    return lax.optimization_barrier(v.astype(jnp.bfloat16)).astype(jnp.float32)

@jax.custom_vjp
def low_back(v):
    return v

def low_keep(v):
    return (low(v), None)

def low_pass(kept, grad):
    return (grad,)

def back_keep(v):
    return (v, None)

def back_low(kept, grad):
    return (low(grad),)
low.defvjp(low_keep, low_pass)
low_back.defvjp(back_keep, back_low)
EPS = 1e-05
NEG = -1e+30

def token_places(lengths, slot_table):
    first_pad = (lengths[0] + BLOCK - 1) // BLOCK * BLOCK
    offsets = jnp.arange(BLOCK, dtype=jnp.int32)
    placed = (slot_table[:, None] * BLOCK + offsets[None, :]).reshape(-1)
    second = (placed >= first_pad).astype(jnp.int32)
    position = placed - second * first_pad
    length_limit = jnp.where(second == 1, lengths[1], lengths[0])
    return (second, position, position < length_limit)

def rotary_tables(position):
    freq_steps = jnp.arange(ROT // 2, dtype=jnp.float32)
    inverse = 10000.0 ** (-2.0 * freq_steps / ROT)
    phases = position.astype(jnp.float32)[:, None] * inverse[None, :]
    return (jnp.cos(phases), jnp.sin(phases))

def rotate(shaped, cosine, sines):
    half_rot = ROT // 2
    front = shaped[..., :half_rot]
    behind = shaped[..., half_rot:ROT]
    cos_part = cosine[:, None, :]
    sin_part = sines[:, None, :]
    return jnp.concatenate([front * cos_part - behind * sin_part, behind * cos_part + front * sin_part, shaped[..., ROT:]], axis=-1)

def layer_norm(values, gain, bias):
    average = lax.optimization_barrier(jnp.mean(values, axis=-1, keepdims=True))
    centred = values - average
    inv_scale = lax.rsqrt(lax.optimization_barrier(jnp.mean(centred * centred, axis=-1, keepdims=True)) + EPS)
    return centred * inv_scale * gain + bias

def layer_forward(hidden, gain_one, bias_one, qkv_weight, qkv_shift, out_weight, gain_two, bias_two, gate_weight, up_weight, down_weight, second, position, valid):
    highest = lax.Precision.HIGHEST
    score_scale = HEAD_DIM ** (-0.5)
    token_count = hidden.shape[0]
    normed_one = low(layer_norm(hidden, gain_one, bias_one))
    joined = low_back(jnp.dot(normed_one, qkv_weight, precision=highest) + qkv_shift)
    cosine, sines = rotary_tables(position)
    queries = low(rotate(joined[:, :D].reshape(token_count, HEADS, HEAD_DIM), cosine, sines))
    key_rows = low(rotate(joined[:, D:2 * D].reshape(token_count, HEADS, HEAD_DIM), cosine, sines))
    value_rows = low(joined[:, 2 * D:].reshape(token_count, HEADS, HEAD_DIM))
    allowed = (second[:, None] == second[None, :]) & (position[None, :] <= position[:, None]) & valid[None, :]

    def one_head(operands):
        head_query, head_key, head_value = operands
        raw = jnp.dot(head_query, head_key.T, precision=highest) * score_scale
        scores = low_back(jnp.where(allowed, raw, NEG))
        weights = low(jnp.exp(scores - jax.nn.logsumexp(scores, axis=-1, keepdims=True)))
        return jnp.dot(weights, head_value, precision=highest)
    mixed = lax.map(jax.checkpoint(one_head), (queries.transpose(1, 0, 2), key_rows.transpose(1, 0, 2), value_rows.transpose(1, 0, 2)))
    attended = low_back(low(mixed.transpose(1, 0, 2).reshape(token_count, D)))
    branch = low_back(jnp.dot(attended, out_weight, precision=highest))
    middle = hidden + branch
    normed_two = low(layer_norm(middle, gain_two, bias_two))
    gate = low_back(jnp.dot(normed_two, gate_weight, precision=highest))
    up_proj = low_back(jnp.dot(normed_two, up_weight, precision=highest))
    inner = low(jax.nn.silu(gate) * up_proj)
    return middle + jnp.dot(inner, down_weight.T, precision=highest)

def reference(hidden_in, cotangent, seq_lengths, slot_block, ln1_gain, ln1_bias, w_qkv, qkv_bias, w_out, ln2_gain, ln2_bias, w_gate, w_up, w_down):
    params = tuple((weight.astype(jnp.float32) for weight in (ln1_gain, ln1_bias, w_qkv, qkv_bias, w_out, ln2_gain, ln2_bias, w_gate, w_up, w_down)))
    zeroes = tuple((jnp.zeros(weight.shape, jnp.float32) for weight in params))

    def one_group(totals, operands):
        group_hidden, group_cot, lengths, slot_table = operands
        second, position, valid = token_places(lengths, slot_table)

        def run_layer(hidden, *weights):
            return layer_forward(hidden, *weights, second, position, valid)
        output, pullback = jax.vjp(run_layer, group_hidden.astype(jnp.float32), *params)
        grads = pullback(group_cot.astype(jnp.float32) * valid[:, None].astype(jnp.float32))
        totals = tuple((total + grad for total, grad in zip(totals, grads[1:])))
        return (totals, (output.astype(jnp.bfloat16), grads[0]))
    totals, (outputs, input_grad) = lax.scan(one_group, zeroes, (hidden_in, cotangent, seq_lengths, slot_block))
    return (outputs, input_grad, totals[0], totals[1], totals[2], totals[3], totals[4], totals[5], totals[6], totals[7], totals[8], totals[9])
```

```python
import jax
import jax.numpy as jnp
from jax import lax
from jax.sharding import Mesh
from jax.sharding import PartitionSpec as P

D = 2048
HEADS = 32
HEAD_DIM = 64
ROT = 16
FF = 5632
BLOCK = 128
TP = 8
HD = D // TP
FC = FF // TP

EPS = 1e-05
NEG = -1e30
SCALE = HEAD_DIM ** (-0.5)
TPA = ("y", "core")
TOK = ("core", "y")
XZ = ("x", "zh", "zl")
ROWS = ("zh", "y", "x", "zl", "core")
GRP = ("x", "zl", "core")
SLOT = ("zh", "y")


def permute_features(v):
    lead = v.shape[:-1]
    n = len(lead)
    v = v.reshape(lead + (2, 4, 4, 2, 32))
    v = v.transpose(tuple(range(n)) + (n + 2, n, n + 3, n + 1, n + 4))
    return v.reshape(lead + (D,))


def restore_features(v):
    lead = v.shape[:-1]
    n = len(lead)
    v = v.reshape(lead + (4, 2, 2, 4, 32))
    v = v.transpose(tuple(range(n)) + (n + 1, n + 3, n, n + 2, n + 4))
    return v.reshape(lead + (D,))


def block_places(lengths, blocks):
    first_pad = (lengths[0] + BLOCK - 1) // BLOCK * BLOCK
    offsets = jnp.arange(BLOCK, dtype=jnp.int32)
    placed = (blocks[:, None] * BLOCK + offsets[None, :]).reshape(-1)
    second = (placed >= first_pad).astype(jnp.int32)
    position = placed - second * first_pad
    limit = jnp.where(second == 1, lengths[1], lengths[0])
    return second, position, position < limit


def rotary_tables(position):
    freq_steps = jnp.arange(ROT // 2, dtype=jnp.float32)
    inverse = 10000.0 ** (-2.0 * freq_steps / ROT)
    phases = position.astype(jnp.float32)[..., None] * inverse
    return jnp.cos(phases), jnp.sin(phases)


def rotate(shaped, cosine, sines, direction):
    half = ROT // 2
    front = shaped[..., :half]
    behind = shaped[..., half:ROT]
    c = cosine[:, :, None, :]
    s = sines[:, :, None, :] * direction
    return jnp.concatenate(
        [front * c - behind * s, behind * c + front * s, shaped[..., ROT:]], axis=-1
    )


def layer_norm(values):
    average = jnp.mean(values, axis=-1, keepdims=True)
    centred = values - average
    inv_scale = lax.rsqrt(jnp.mean(centred * centred, axis=-1, keepdims=True) + EPS)
    return centred * inv_scale, inv_scale


def norm_back(grad_in, normed, inv_scale, gain):
    scaled = grad_in * gain
    return inv_scale * (
        scaled
        - jnp.mean(scaled, axis=-1, keepdims=True)
        - normed * jnp.mean(scaled * normed, axis=-1, keepdims=True)
    )


def mm(a, b):
    return jnp.dot(a, b, preferred_element_type=jnp.float32)


def mm_nt(a, b):
    return lax.dot_general(a, b, (((1,), (1,)), ((), ())), preferred_element_type=jnp.float32)


def mm_tn(a, b):
    return lax.dot_general(a, b, (((0,), (0,)), ((), ())), preferred_element_type=jnp.float32)


def gather_weight(w):
    w = lax.all_to_all(w, TPA, 0, 0, tiled=True).reshape(BLOCK, -1)
    return lax.all_gather(w, XZ, axis=0, tiled=True)


def scatter_grad(g):
    g = lax.psum_scatter(g.astype(jnp.bfloat16), XZ, scatter_dimension=0, tiled=True)
    return lax.all_to_all(g.reshape(TP, 16, -1), TPA, 0, 0, tiled=True)


def gather_tokens(v):
    return lax.all_gather(v, TOK, axis=0, tiled=True)


def scatter_tokens(v):
    return lax.psum_scatter(v, TOK, scatter_dimension=0, tiled=True)


def body(
    hidden_in,
    cotangent,
    seq_lengths,
    slot_block,
    ln1_gain,
    ln1_bias,
    w_qkv,
    qkv_bias,
    w_out,
    ln2_gain,
    ln2_bias,
    w_gate,
    w_up,
    w_down,
):
    bf = jnp.bfloat16
    f32 = jnp.float32
    zh = lax.axis_index("zh")
    y = lax.axis_index("y")
    core = lax.axis_index("core")

    part_qkv = w_qkv.reshape(16, 3, 2, 4, HD).transpose(3, 2, 0, 1, 4).reshape(TP, 16, 3 * HD)
    part_gate, part_up, part_down = (
        w.reshape(16, TP, FC).transpose(1, 0, 2) for w in (w_gate, w_up, w_down)
    )
    qkv_full = gather_weight(part_qkv)
    out_rows = lax.all_gather(permute_features(w_out), XZ + ("core",), axis=0, tiled=True)
    out_full = lax.dynamic_index_in_dim(
        out_rows.reshape(4, 2, HEAD_DIM, D), core, axis=1, keepdims=False
    ).reshape(HD, D)
    gate_full = gather_weight(part_gate)
    up_full = gather_weight(part_up)
    down_full = gather_weight(part_down)

    small = jnp.concatenate([ln1_gain, ln1_bias, ln2_gain, ln2_bias, qkv_bias])
    small = lax.all_gather(small, ROWS, axis=0, tiled=False)
    gain_one, bias_one, gain_two, bias_two = (
        permute_features(small[:, 16 * i : 16 * i + 16].reshape(D).astype(f32)) for i in range(4)
    )
    shift = small[:, 64:].reshape(3, 2, 4, HD)
    shift = lax.dynamic_index_in_dim(shift, core, axis=1, keepdims=False)
    shift = lax.dynamic_index_in_dim(shift, y, axis=1, keepdims=False).reshape(3 * HD).astype(f32)

    plan = jnp.concatenate([seq_lengths[0], slot_block[0]])
    plan = lax.all_gather(plan, "core", axis=0, tiled=False)
    blocks = plan[:, 2:].reshape(2, 2, 4)
    own_blocks = lax.dynamic_index_in_dim(blocks, zh, axis=1, keepdims=False)
    other_blocks = lax.dynamic_index_in_dim(blocks, 1 - zh, axis=1, keepdims=False)
    second, position, valid = jax.vmap(block_places)(
        plan[:, :2], jnp.concatenate([own_blocks, other_blocks], axis=1)
    )
    half = 4 * BLOCK
    q_second, q_position = second[:, :half], position[:, :half]
    allowed = (
        (q_second[:, :, None] == second[:, None, :])
        & (position[:, None, :] <= q_position[:, :, None])
        & valid[:, None, :]
    )
    cosine, sines = rotary_tables(q_position)
    own_valid = lax.dynamic_index_in_dim(
        lax.dynamic_index_in_dim(valid[:, :half].reshape(2, 4, BLOCK), core, 0, False), y, 0, False
    )

    hidden = permute_features(hidden_in[0]).astype(f32)
    grad_out = permute_features(cotangent[0]) * own_valid[:, None].astype(bf)
    grad_out_all = gather_tokens(grad_out)

    normed_one, inv_one = layer_norm(hidden)
    lowered_one = (normed_one * gain_one + bias_one).astype(bf)
    one_all = gather_tokens(lowered_one)
    joined = mm(one_all, qkv_full) + shift
    joined = joined.reshape(2, half, 3, 4, HEAD_DIM)
    queries = rotate(joined[:, :, 0], cosine, sines, 1.0).astype(bf)
    own_keys = rotate(joined[:, :, 1], cosine, sines, 1.0).astype(bf)
    own_values = joined[:, :, 2].astype(bf)
    swap = [(0, 1), (1, 0)]
    own_kv = jnp.stack([own_keys, own_values])
    other_kv = lax.ppermute(own_kv, "zh", swap)
    keys, values = jnp.concatenate([own_kv, other_kv], axis=2)

    raw = jnp.einsum("gthd,gshd->ghts", queries, keys, preferred_element_type=f32) * SCALE
    scores = jnp.where(allowed[:, None], raw, NEG)
    highest = jnp.max(scores, axis=-1, keepdims=True)
    log_total = highest + jnp.log(jnp.sum(jnp.exp(scores - highest), axis=-1, keepdims=True))
    probs = jnp.exp(scores - log_total)
    weights = probs.astype(bf)
    mixed = jnp.einsum("ghts,gshd->gthd", weights, values, preferred_element_type=f32)
    attended = mixed.reshape(2 * half, HD).astype(bf)

    middle = hidden + scatter_tokens(mm(attended, out_full).astype(bf)).astype(f32)
    normed_two, inv_two = layer_norm(middle)
    lowered_two = (normed_two * gain_two + bias_two).astype(bf)
    two_all = gather_tokens(lowered_two)
    gate = mm(two_all, gate_full)
    up_proj = mm(two_all, up_full)
    sig = jax.nn.sigmoid(gate)
    activated = gate * sig
    inner = (activated * up_proj).astype(bf)
    hidden_out = (middle + scatter_tokens(mm_nt(inner, down_full).astype(bf)).astype(f32)).astype(bf)

    inner_grad = mm(grad_out_all, down_full)
    gate_grad = (inner_grad * up_proj * sig * (1.0 + gate * (1.0 - sig))).astype(bf)
    up_grad = (inner_grad * activated).astype(bf)
    two_grad = scatter_tokens(
        (mm_nt(gate_grad, gate_full) + mm_nt(up_grad, up_full)).astype(bf)
    ).astype(f32)
    middle_grad = grad_out.astype(f32) + norm_back(two_grad, normed_two, inv_two, gain_two)
    branch_grad = middle_grad.astype(bf)
    branch_all = gather_tokens(branch_grad)
    attended_grad = mm_nt(branch_all, out_full).astype(bf)

    gate_sum = scatter_grad(mm_tn(two_all, gate_grad))
    up_sum = scatter_grad(mm_tn(two_all, up_grad))
    down_sum = scatter_grad(mm_tn(grad_out_all, inner))
    out_part = mm_tn(attended, branch_all).astype(bf).reshape(4, 1, HEAD_DIM, D)
    own_plane = (jnp.arange(2) == core)[None, :, None, None]
    out_part = jnp.where(own_plane, out_part, jnp.zeros((), bf)).reshape(4 * 2 * HEAD_DIM, D)
    out_sum = lax.psum_scatter(out_part, XZ + ("core",), scatter_dimension=0, tiled=True)

    grad_heads = attended_grad.reshape(2, half, 4, HEAD_DIM)
    prob_grad = jnp.einsum("gthd,gshd->ghts", grad_heads, values, preferred_element_type=f32)
    score_grad = (
        probs * (prob_grad - jnp.sum(probs * prob_grad, axis=-1, keepdims=True))
    ).astype(bf)
    query_grad = jnp.einsum("ghts,gshd->gthd", score_grad, keys, preferred_element_type=f32) * SCALE
    key_part = (
        jnp.einsum("ghts,gthd->gshd", score_grad, queries, preferred_element_type=f32) * SCALE
    )
    value_part = jnp.einsum("ghts,gthd->gshd", weights, grad_heads, preferred_element_type=f32)
    kv_part = jnp.stack([key_part, value_part])
    kv_back = lax.ppermute(kv_part[:, :, half:].astype(bf), "zh", swap).astype(f32)
    key_grad, value_grad = kv_part[:, :, :half] + kv_back
    joined_grad = jnp.stack(
        [
            rotate(query_grad, cosine, sines, -1.0),
            rotate(key_grad, cosine, sines, -1.0),
            value_grad,
        ],
        axis=2,
    ).astype(bf).reshape(2 * half, 3 * HD)
    qkv_sum = scatter_grad(mm_tn(one_all, joined_grad))
    one_grad = scatter_tokens(mm_nt(joined_grad, qkv_full).astype(bf)).astype(f32)
    input_grad = middle_grad + norm_back(one_grad, normed_one, inv_one, gain_one)

    shift_part = jnp.sum(joined_grad.astype(f32), axis=0).reshape(3, 1, 1, HD)
    mine = ((jnp.arange(2) == core)[:, None] & (jnp.arange(4) == y)[None, :])[None, :, :, None]
    shift_part = jnp.where(mine, shift_part, 0.0).reshape(3 * D)
    terms = jnp.stack(
        [
            jnp.sum(one_grad * normed_one, axis=0),
            jnp.sum(one_grad, axis=0),
            jnp.sum(two_grad * normed_two, axis=0),
            jnp.sum(two_grad, axis=0),
        ]
    )
    terms = restore_features(terms).reshape(4, 128, 16).transpose(1, 0, 2).reshape(128, 64)
    small_sum = lax.psum_scatter(
        jnp.concatenate([terms, shift_part.reshape(128, 48)], axis=1).reshape(-1),
        ROWS,
        scatter_dimension=0,
        tiled=True,
    )

    def whole(g):
        return g.transpose(1, 0, 2).reshape(16, FF).astype(f32)

    qkv_grad = (
        qkv_sum.reshape(4, 2, 16, 3, HD).transpose(2, 3, 1, 0, 4).reshape(16, 3 * D).astype(f32)
    )
    return (
        restore_features(hidden_out)[None],
        restore_features(input_grad)[None],
        small_sum[:16],
        small_sum[16:32],
        qkv_grad,
        small_sum[64:],
        restore_features(out_sum.astype(f32)),
        small_sum[32:48],
        small_sum[48:64],
        whole(gate_sum),
        whole(up_sum),
        whole(down_sum),
    )


def solution(mesh):
    inner = Mesh(mesh.devices.reshape(2, 4, 4, 2, 2), ROWS)
    rows = P(ROWS)
    tokens = P(GRP, SLOT, None)
    placed = (
        tokens,
        tokens,
        P(GRP, None),
        P(GRP, None),
        rows,
        rows,
        P(ROWS, None),
        rows,
        P(ROWS, None),
        rows,
        rows,
        P(ROWS, None),
        P(ROWS, None),
        P(ROWS, None),
    )
    return jax.shard_map(
        body,
        mesh=inner,
        in_specs=placed,
        out_specs=(
            tokens,
            tokens,
            rows,
            rows,
            P(ROWS, None),
            rows,
            P(ROWS, None),
            rows,
            rows,
            P(ROWS, None),
            P(ROWS, None),
            P(ROWS, None),
        ),
        check_vma=False,
    )
```

```python
import functools

import jax
import jax.numpy as jnp
from jax import lax
from jax.experimental import pallas as pl
from jax.experimental.pallas import tpu as pltpu
from jax.sharding import Mesh
from jax.sharding import PartitionSpec as P

D = 2048
HEADS = 32
HEAD_DIM = 64
ROT = 16
FF = 5632
BLOCK = 128
TP = 8
HD = D // TP
FC = FF // TP

EPS = 1e-05
NEG = -1e30
SCALE = HEAD_DIM ** (-0.5)
TPA = ("y", "core")
XZ = ("x", "zh", "zl")
ROWS = ("zh", "y", "x", "zl", "core")
GRP = ("x", "zl", "core")
SLOT = ("zh", "y")


def permute_features(v):
    lead = v.shape[:-1]
    n = len(lead)
    v = v.reshape(lead + (2, 4, 4, 2, 32))
    v = v.transpose(tuple(range(n)) + (n + 2, n, n + 3, n + 1, n + 4))
    return v.reshape(lead + (D,))


def restore_features(v):
    lead = v.shape[:-1]
    n = len(lead)
    v = v.reshape(lead + (4, 2, 2, 4, 32))
    v = v.transpose(tuple(range(n)) + (n + 1, n + 3, n, n + 2, n + 4))
    return v.reshape(lead + (D,))


def block_places(lengths, blocks):
    first_pad = (lengths[0] + BLOCK - 1) // BLOCK * BLOCK
    offsets = jnp.arange(BLOCK, dtype=jnp.int32)
    placed = (blocks[:, None] * BLOCK + offsets[None, :]).reshape(-1)
    second = (placed >= first_pad).astype(jnp.int32)
    position = placed - second * first_pad
    limit = jnp.where(second == 1, lengths[1], lengths[0])
    return second, position, position < limit


def rotary_tables(position):
    freq_steps = jnp.arange(ROT // 2, dtype=jnp.float32)
    inverse = 10000.0 ** (-2.0 * freq_steps / ROT)
    phases = position.astype(jnp.float32)[..., None] * inverse
    return jnp.cos(phases), jnp.sin(phases)


def rotate(shaped, cosine, sines, direction):
    half = ROT // 2
    front = shaped[..., :half]
    behind = shaped[..., half:ROT]
    c = cosine[:, :, None, :]
    s = sines[:, :, None, :] * direction
    return jnp.concatenate(
        [front * c - behind * s, behind * c + front * s, shaped[..., ROT:]], axis=-1
    )


def layer_norm(values):
    average = jnp.mean(values, axis=-1, keepdims=True)
    centred = values - average
    inv_scale = lax.rsqrt(jnp.mean(centred * centred, axis=-1, keepdims=True) + EPS)
    return centred * inv_scale, inv_scale


def norm_back(grad_in, normed, inv_scale, gain):
    scaled = grad_in * gain
    return inv_scale * (
        scaled
        - jnp.mean(scaled, axis=-1, keepdims=True)
        - normed * jnp.mean(scaled * normed, axis=-1, keepdims=True)
    )


def mm(a, b):
    return jnp.dot(a, b, preferred_element_type=jnp.float32)


def mm_nt(a, b):
    return lax.dot_general(a, b, (((1,), (1,)), ((), ())), preferred_element_type=jnp.float32)


def mm_tn(a, b):
    return lax.dot_general(a, b, (((0,), (0,)), ((), ())), preferred_element_type=jnp.float32)


FP = 768
HALF = BLOCK // 2
ANY = pl.BlockSpec(memory_space=pl.ANY)
VM = pl.BlockSpec(memory_space=pltpu.VMEM)
BF = jnp.bfloat16
F32 = jnp.float32


def params(cid):
    return pltpu.CompilerParams(
        collective_id=cid, has_side_effects=True, vmem_limit_bytes=56 * 1024 * 1024
    )


def meet(peers):
    barrier = pltpu.get_barrier_semaphore()
    for peer in peers:
        pl.semaphore_signal(
            barrier, inc=1, device_id=peer, device_id_type=pl.DeviceIdType.MESH
        )
    pl.semaphore_wait(barrier, len(peers))


def remote(sems, i, src, dst, peer):
    return pltpu.make_async_remote_copy(
        src_ref=src,
        dst_ref=dst,
        send_sem=sems[0].at[i],
        recv_sem=sems[1].at[i],
        device_id=peer,
        device_id_type=pl.DeviceIdType.MESH,
    )


def ring():
    y = lax.axis_index("y")
    c = lax.axis_index("core")
    up = lax.rem(y + 1, 4)
    opp = lax.rem(y + 2, 4)
    dn = lax.rem(y + 3, 4)
    return y, c, up, opp, dn


def ring_peers(up, dn, c):
    return {"y": up}, {"y": dn}, {"core": 1 - c}


N_AG = 11
N_RS = 10


def ring_gather(own, full, local_sem, sems):
    y, c, up, opp, dn = ring()
    to_up, to_dn, to_sib = ring_peers(up, dn, c)
    first, last = pl.ds(0, HALF), pl.ds(HALF, HALF)
    cp = functools.partial(remote, sems)
    up1 = cp(0, own.at[first], full.at[y, c, first], to_up)
    dn1 = cp(1, own.at[last], full.at[y, c, last], to_dn)
    up2 = cp(2, own.at[last], full.at[y, c, last], to_up)
    dn2 = cp(3, own.at[first], full.at[y, c, first], to_dn)
    sib0 = cp(4, own, full.at[y, c], to_sib)
    here = pltpu.make_async_copy(own, full.at[y, c], local_sem)
    for one in (up1, dn1, up2, dn2, sib0, here):
        one.start()
    up1.wait_recv()
    far1 = cp(5, full.at[dn, c, first], full.at[dn, c, first], to_up)
    far1.start()
    dn1.wait_recv()
    far2 = cp(6, full.at[up, c, last], full.at[up, c, last], to_dn)
    far2.start()
    up2.wait_recv()
    sib1 = cp(7, full.at[dn, c], full.at[dn, c], to_sib)
    sib1.start()
    dn2.wait_recv()
    sib2 = cp(8, full.at[up, c], full.at[up, c], to_sib)
    sib2.start()
    far1.wait_recv()
    sib3 = cp(9, full.at[opp, c, first], full.at[opp, c, first], to_sib)
    sib3.start()
    far2.wait_recv()
    sib4 = cp(10, full.at[opp, c, last], full.at[opp, c, last], to_sib)
    sib4.start()
    for one in (sib0, sib1, sib2, sib3, sib4):
        one.wait_recv()
    here.wait()
    for one in (up1, dn1, up2, dn2, sib0, far1, far2, sib1, sib2, sib3, sib4):
        one.wait_send()


def rows_loop(count, step, body):
    @pl.loop(0, count // step)
    def _(i):
        body(pl.ds(pl.multiple_of(i * step, step), step))


RS_SCRATCH = [
    pltpu.VMEM((4, 2, BLOCK, D), F32),
    pltpu.VMEM((4, BLOCK, D), BF),
    pltpu.VMEM((4, BLOCK, D), BF),
    pltpu.VMEM((2, HALF, D), BF),
    pltpu.VMEM((2, HALF, D), BF),
    pltpu.VMEM((2, BLOCK, D), BF),
    pltpu.VMEM((2, BLOCK, D), BF),
    pltpu.SemaphoreType.DMA((N_RS,)),
    pltpu.SemaphoreType.DMA((N_RS,)),
]


def ring_scatter(partial, scratch):
    part, sib_out, sib_in, far_out, far_in, near_out, near_in, *sems = scratch
    y, c, up, opp, dn = ring()
    to_up, to_dn, to_sib = ring_peers(up, dn, c)
    first, last = pl.ds(0, HALF), pl.ds(HALF, HALF)
    cp = functools.partial(remote, sems)
    order = (opp, up, dn, y)
    sib = [cp(j, sib_out.at[j], sib_in.at[j], to_sib) for j in range(4)]

    def produce(j):
        partial(order[j], part.at[j])

        def lower(r):
            sib_out[j, r, :] = part[j, 1 - c, r, :].astype(BF)

        rows_loop(BLOCK, 32, lower)
        sib[j].start()

    far = [
        cp(4, far_out.at[0], far_in.at[0], to_up),
        cp(5, far_out.at[1], far_in.at[1], to_dn),
    ]
    near_early = [
        cp(6, near_out.at[0, last], near_in.at[0, last], to_up),
        cp(7, near_out.at[1, first], near_in.at[1, first], to_dn),
    ]
    near_late = [
        cp(8, near_out.at[0, first], near_in.at[0, first], to_up),
        cp(9, near_out.at[1, last], near_in.at[1, last], to_dn),
    ]
    produce(0)
    produce(1)
    sib[0].wait_recv()
    for k in range(2):

        def add_far(r, k=k):
            q = pl.ds(k * HALF + r.start, r.size)
            far_out[k, r, :] = (part[0, c, q, :] + sib_in[0, q, :].astype(F32)).astype(BF)

        rows_loop(HALF, 32, add_far)
        far[k].start()
    produce(2)
    for k in range(2):
        sib[1 + k].wait_recv()

        def add_near(r, k=k):
            q = pl.ds((1 - k) * HALF + r.start, r.size)
            near_out[k, q, :] = (part[1 + k, c, q, :] + sib_in[1 + k, q, :].astype(F32)).astype(BF)

        rows_loop(HALF, 32, add_near)
        near_early[k].start()
    produce(3)
    for k in range(2):
        far[k].wait_recv()

        def add_late(r, k=k):
            q = pl.ds(k * HALF + r.start, r.size)
            near_out[k, q, :] = (
                part[1 + k, c, q, :] + sib_in[1 + k, q, :].astype(F32) + far_in[k, r, :].astype(F32)
            ).astype(BF)

        rows_loop(HALF, 32, add_late)
        near_late[k].start()
    sib[3].wait_recv()
    for one in near_early + near_late:
        one.wait_recv()

    def finish(r):
        part[3, c, r, :] = (
            part[3, c, r, :]
            + sib_in[3, r, :].astype(F32)
            + near_in[0, r, :].astype(F32)
            + near_in[1, r, :].astype(F32)
        )

    rows_loop(BLOCK, 32, finish)
    for one in sib + far + near_early + near_late:
        one.wait_send()
    return part.at[3, c]


AG_SCRATCH = [
    pltpu.VMEM((BLOCK, D), BF),
    pltpu.SemaphoreType.DMA,
    pltpu.SemaphoreType.DMA((N_AG,)),
    pltpu.SemaphoreType.DMA((N_AG,)),
]
FULL = jax.ShapeDtypeStruct((4, 2, BLOCK, D), BF)


def kernel_norm_gather(hidden, gains, full, own, local_sem, *sems):
    y, c, up, opp, dn = ring()
    meet(ring_peers(up, dn, c))

    def norm(r):
        normed, _ = layer_norm(hidden[r, :].astype(F32))
        own[r, :] = (normed * gains[0:1, :] + gains[1:2, :]).astype(BF)

    rows_loop(BLOCK, 16, norm)
    ring_gather(own, full, local_sem, sems)


def norm_gather(hidden, gains, cid):
    return pl.pallas_call(
        kernel_norm_gather,
        out_shape=FULL,
        in_specs=[VM, VM],
        out_specs=ANY,
        scratch_shapes=AG_SCRATCH,
        compiler_params=params(cid),
        name="norm_gather",
    )(hidden, gains)


NT = (((1,), (1,)), ((), ()))


def kernel_out_proj(attended, weight, hidden, gains, middle, full, *scratch):
    own, local_sem, *sems = scratch[:4]
    y, c, up, opp, dn = ring()
    meet(ring_peers(up, dn, c))

    def partial(block, out):
        a = attended[block].reshape(2 * BLOCK, HD)

        @pl.loop(0, 4)
        def _(i):
            q = pl.ds(pl.multiple_of(i * 512, 512), 512)
            out[:, :, q] = jnp.dot(a, weight[:, q], preferred_element_type=F32).reshape(
                2, BLOCK, 512
            )

    total = ring_scatter(partial, scratch[4:])

    def norm(r):
        row = hidden[r, :].astype(F32) + total[r, :]
        middle[r, :] = row
        normed, _ = layer_norm(row)
        own[r, :] = (normed * gains[2:3, :] + gains[3:4, :]).astype(BF)

    rows_loop(BLOCK, 16, norm)
    ring_gather(own, full, local_sem, sems)


def out_proj(attended, weight, hidden, gains, cid):
    return pl.pallas_call(
        kernel_out_proj,
        out_shape=(jax.ShapeDtypeStruct((BLOCK, D), F32), FULL),
        in_specs=[VM] * 4,
        out_specs=(VM, ANY),
        scratch_shapes=AG_SCRATCH + RS_SCRATCH,
        compiler_params=params(cid),
        name="out_proj",
    )(attended, weight, hidden, gains)


def kernel_mlp_back(
    gate_grad, up_grad, w_gate, w_up, middle, grad_out, gains, middle_grad, sums, full, *scratch
):
    own, local_sem, *sems = scratch[:4]
    y, c, up, opp, dn = ring()
    meet(ring_peers(up, dn, c))

    def partial(block, out):
        a = gate_grad[block].reshape(2 * BLOCK, FP)
        b = up_grad[block].reshape(2 * BLOCK, FP)

        @pl.loop(0, 4)
        def _(i):
            q = pl.ds(pl.multiple_of(i * 512, 512), 512)
            out[:, :, q] = (
                lax.dot_general(a, w_gate[q, :], NT, preferred_element_type=F32)
                + lax.dot_general(b, w_up[q, :], NT, preferred_element_type=F32)
            ).reshape(2, BLOCK, 512)

    total = ring_scatter(partial, scratch[4:])
    sums[...] = jnp.zeros_like(sums)

    def back(r):
        row = total[r, :]
        normed, inv = layer_norm(middle[r, :])
        grad = grad_out[r, :].astype(F32) + norm_back(row, normed, inv, gains[2:3, :])
        middle_grad[r, :] = grad
        own[r, :] = grad.astype(BF)
        sums[0:1, :] += jnp.sum(row * normed, axis=0, keepdims=True)
        sums[1:2, :] += jnp.sum(row, axis=0, keepdims=True)

    rows_loop(BLOCK, 16, back)
    ring_gather(own, full, local_sem, sems)


def mlp_back(gate_grad, up_grad, w_gate, w_up, middle, grad_out, gains, cid):
    return pl.pallas_call(
        kernel_mlp_back,
        out_shape=(
            jax.ShapeDtypeStruct((BLOCK, D), F32),
            jax.ShapeDtypeStruct((8, D), F32),
            FULL,
        ),
        in_specs=[VM] * 7,
        out_specs=(VM, VM, ANY),
        scratch_shapes=AG_SCRATCH + RS_SCRATCH,
        compiler_params=params(cid),
        name="mlp_back",
    )(gate_grad, up_grad, w_gate, w_up, middle, grad_out, gains)


def kernel_qkv_back(joined_grad, weight, hidden, middle_grad, gains, input_grad, sums, *scratch):
    y, c, up, opp, dn = ring()
    meet(ring_peers(up, dn, c))

    def partial(block, out):
        a = joined_grad[block].reshape(2 * BLOCK, 3 * HD)

        @pl.loop(0, 4)
        def _(i):
            q = pl.ds(pl.multiple_of(i * 512, 512), 512)
            out[:, :, q] = lax.dot_general(
                a, weight[q, :], NT, preferred_element_type=F32
            ).reshape(2, BLOCK, 512)

    total = ring_scatter(partial, scratch)
    sums[...] = jnp.zeros_like(sums)

    def back(r):
        row = total[r, :]
        normed, inv = layer_norm(hidden[r, :].astype(F32))
        input_grad[r, :] = middle_grad[r, :] + norm_back(row, normed, inv, gains[0:1, :])
        sums[0:1, :] += jnp.sum(row * normed, axis=0, keepdims=True)
        sums[1:2, :] += jnp.sum(row, axis=0, keepdims=True)

    rows_loop(BLOCK, 16, back)


def qkv_back(joined_grad, weight, hidden, middle_grad, gains, cid):
    return pl.pallas_call(
        kernel_qkv_back,
        out_shape=(jax.ShapeDtypeStruct((BLOCK, D), F32), jax.ShapeDtypeStruct((8, D), F32)),
        in_specs=[VM] * 5,
        out_specs=(VM, VM),
        scratch_shapes=RS_SCRATCH,
        compiler_params=params(cid),
        name="qkv_back",
    )(joined_grad, weight, hidden, middle_grad, gains)


TP_STEPS = [(dy, dc) for dy in range(4) for dc in range(2) if (dy, dc) != (0, 0)]
XZ_STEPS = [(dx, dz) for dx in range(4) for dz in range(4) if (dx, dz) != (0, 0)]


def tp_peer(step):
    y = lax.rem(lax.axis_index("y") + step[0], 4)
    c = lax.rem(lax.axis_index("core") + step[1], 2)
    return {"y": y, "core": c}, y * 2 + c


def xz_peer(step):
    x = lax.rem(lax.axis_index("x") + step[0], 4)
    z = lax.rem(lax.axis_index("zh") * 2 + lax.axis_index("zl") + step[1], 4)
    return {"x": x, "zh": z // 2, "zl": lax.rem(z, 2)}, x * 4 + z


def meet_all(split):
    peers = [tp_peer(s)[0] for s in TP_STEPS] + [xz_peer(s)[0] for s in XZ_STEPS]
    barrier = pltpu.get_barrier_semaphore()
    for peer in peers:
        pl.semaphore_signal(
            barrier, inc=1, device_id=peer, device_id_type=pl.DeviceIdType.MESH
        )

    @pl.when(split)
    def _():
        pl.semaphore_signal(
            barrier, inc=1, device_id=swap_peer(), device_id_type=pl.DeviceIdType.MESH
        )

    pl.semaphore_wait(barrier, len(peers) + split.astype(jnp.int32))


def swap_peer():
    return {"zh": lax.axis_index("core"), "core": lax.axis_index("zh")}


def swap_start(split, src, dst, local_sem, sems, i):
    @pl.when(split)
    def _():
        remote(sems, i, src, dst, swap_peer()).start()

    @pl.when(jnp.logical_not(split))
    def _():
        pltpu.make_async_copy(src, dst, local_sem).start()


def swap_wait(split, src, dst, local_sem, sems, i):
    @pl.when(split)
    def _():
        remote(sems, i, src, dst, swap_peer()).wait()

    @pl.when(jnp.logical_not(split))
    def _():
        pltpu.make_async_copy(src, dst, local_sem).wait()


N_TP = len(TP_STEPS)
N_XZ = len(XZ_STEPS)


def kernel_spread(small, qkv, mlp, out, small_all, qkv_all, mlp_all, out_all, local, *sems):
    me = lax.axis_index("y") * 2 + lax.axis_index("core")
    xz = lax.axis_index("x") * 4 + lax.axis_index("zh") * 2 + lax.axis_index("zl")
    split = lax.axis_index("zh") != lax.axis_index("core")
    meet_all(split)
    cp = functools.partial(remote, sems)
    tiny, big = [], []
    for k, step in enumerate(TP_STEPS):
        peer, there = tp_peer(step)
        tiny.append(cp(k, small, small_all.at[xz, me], peer))
        big.append(cp(N_TP + k, qkv.at[there], qkv_all.at[me], peer))
        big.append(cp(2 * N_TP + k, mlp.at[there], mlp_all.at[:, me], peer))
    keep = [
        pltpu.make_async_copy(small, small_all.at[xz, me], local.at[0]),
        pltpu.make_async_copy(qkv.at[me], qkv_all.at[me], local.at[1]),
        pltpu.make_async_copy(mlp.at[me], mlp_all.at[:, me], local.at[2]),
    ]
    for one in tiny + keep:
        one.start()
    for one in big:
        one.start()
    swap_start(split, out, out_all, local.at[3], sems, 3 * N_TP + N_XZ)
    for one in tiny:
        one.wait()
    keep[0].wait()
    wide = []
    for k, step in enumerate(XZ_STEPS):
        peer, _ = xz_peer(step)
        wide.append(cp(3 * N_TP + k, small_all.at[xz], small_all.at[xz], peer))
    for one in wide:
        one.start()
    for one in wide + big + keep[1:]:
        one.wait()
    swap_wait(split, out, out_all, local.at[3], sems, 3 * N_TP + N_XZ)


def spread(small, qkv, mlp, out, cid):
    n = 3 * N_TP + N_XZ + 1
    return pl.pallas_call(
        kernel_spread,
        out_shape=(
            jax.ShapeDtypeStruct((16, TP, 1, 128), F32),
            jax.ShapeDtypeStruct((TP, 16, FP), BF),
            jax.ShapeDtypeStruct((3, TP, 16, FP), BF),
            jax.ShapeDtypeStruct((16, D), BF),
        ),
        in_specs=[ANY] * 4,
        out_specs=(ANY,) * 4,
        scratch_shapes=[
            pltpu.SemaphoreType.DMA((4,)),
            pltpu.SemaphoreType.DMA((n,)),
            pltpu.SemaphoreType.DMA((n,)),
        ],
        compiler_params=params(cid),
        name="spread",
    )(small, qkv, mlp, out)


def kernel_collect(
    terms, shift, qkv, mlp, out, small_all, qkv_all, mlp_all, out_all, terms_in, shift_in, own, local, *sems
):
    me = lax.axis_index("y") * 2 + lax.axis_index("core")
    xz = lax.axis_index("x") * 4 + lax.axis_index("zh") * 2 + lax.axis_index("zl")
    split = lax.axis_index("zh") != lax.axis_index("core")
    meet_all(split)
    cp = functools.partial(remote, sems)
    wide, big = [], []
    for k, step in enumerate(XZ_STEPS):
        peer, there = xz_peer(step)
        wide.append(cp(k, terms.at[there], terms_in.at[xz], peer))
        wide.append(cp(N_XZ + k, shift, shift_in.at[xz], peer))
    for k, step in enumerate(TP_STEPS):
        peer, there = tp_peer(step)
        big.append(cp(2 * N_XZ + k, qkv.at[there], qkv_all.at[me], peer))
        big.append(cp(2 * N_XZ + N_TP + k, mlp.at[:, there], mlp_all.at[me], peer))
    keep = [
        pltpu.make_async_copy(terms.at[xz], terms_in.at[xz], local.at[0]),
        pltpu.make_async_copy(shift, shift_in.at[xz], local.at[1]),
        pltpu.make_async_copy(qkv.at[me], qkv_all.at[me], local.at[2]),
        pltpu.make_async_copy(mlp.at[:, me], mlp_all.at[me], local.at[3]),
    ]
    for one in wide + keep:
        one.start()
    for one in big:
        one.start()
    last = 2 * N_XZ + 3 * N_TP
    swap_start(split, out, out_all, local.at[4], sems, last)
    for one in wide + keep[:2]:
        one.wait()
    own[0:8, :] = jnp.sum(terms_in[...], axis=0)
    own[8:16, :] = jnp.sum(shift_in[...], axis=0)
    tiny = []
    for k, step in enumerate(TP_STEPS):
        peer, _ = tp_peer(step)
        tiny.append(cp(2 * N_XZ + 2 * N_TP + k, own, small_all.at[me], peer))
    tiny.append(pltpu.make_async_copy(own, small_all.at[me], local.at[0]))
    for one in tiny:
        one.start()
    for one in tiny + big + keep[2:]:
        one.wait()
    swap_wait(split, out, out_all, local.at[4], sems, last)


def collect(terms, shift, qkv, mlp, out, cid):
    n = 2 * N_XZ + 3 * N_TP + 1
    return pl.pallas_call(
        kernel_collect,
        out_shape=(
            jax.ShapeDtypeStruct((TP, 16, 128), F32),
            jax.ShapeDtypeStruct((TP, 16, FP), BF),
            jax.ShapeDtypeStruct((TP, 3, 16, FP), BF),
            jax.ShapeDtypeStruct((16, D), BF),
        ),
        in_specs=[ANY] * 5,
        out_specs=(ANY,) * 4,
        scratch_shapes=[
            pltpu.VMEM((16, 8, 128), F32),
            pltpu.VMEM((16, 8, 128), F32),
            pltpu.VMEM((16, 128), F32),
            pltpu.SemaphoreType.DMA((5,)),
            pltpu.SemaphoreType.DMA((n,)),
            pltpu.SemaphoreType.DMA((n,)),
        ],
        compiler_params=params(cid),
        name="collect",
    )(terms, shift, qkv, mlp, out)


def body(
    hidden_in,
    cotangent,
    seq_lengths,
    slot_block,
    ln1_gain,
    ln1_bias,
    w_qkv,
    qkv_bias,
    w_out,
    ln2_gain,
    ln2_bias,
    w_gate,
    w_up,
    w_down,
):
    bf, f32 = BF, F32
    zh = lax.axis_index("zh")
    y = lax.axis_index("y")
    core = lax.axis_index("core")
    xz = lax.axis_index("x") * 4 + zh * 2 + lax.axis_index("zl")

    def by_part(w):
        w = w.reshape(-1, 3, 2, 4, 4, 2, 2, 16)
        w = jnp.concatenate([w[:, :2], w[:, 2:].swapaxes(5, 6)], axis=1)
        return w.transpose(3, 2, 0, 1, 4, 5, 6, 7).reshape(TP, -1, 3 * HD)

    part_qkv = by_part(w_qkv)
    part_mlp = jnp.stack(
        [
            jnp.pad(w.reshape(16, TP, FC).transpose(1, 0, 2), ((0, 0), (0, 0), (0, FP - FC)))
            for w in (w_gate, w_up, w_down)
        ],
        axis=1,
    )
    lengths = seq_lengths[0]
    small = jnp.concatenate(
        [
            ln1_gain.astype(f32),
            ln1_bias.astype(f32),
            ln2_gain.astype(f32),
            ln2_bias.astype(f32),
            qkv_bias.astype(f32),
            lengths.astype(f32),
            slot_block[0].astype(f32),
            jnp.zeros(6, f32),
        ]
    ).reshape(1, 128)
    small_all, qkv_rows, mlp_rows, out_rows = spread(
        small, part_qkv, part_mlp, permute_features(w_out), 0
    )
    out_rows = out_rows.reshape(16, 8, HD).swapaxes(0, 1).reshape(BLOCK, HD)
    attn_full = lax.all_gather(
        jnp.concatenate([qkv_rows.reshape(BLOCK, FP), out_rows], axis=1), XZ, axis=0, tiled=True
    )
    mlp_full = lax.all_gather(mlp_rows.reshape(3, BLOCK, FP), XZ, axis=0, tiled=False)
    qkv_full = attn_full[:, :FP]
    out_full = (
        attn_full[:, FP:].reshape(16, 8, 16, HD).transpose(0, 2, 1, 3).reshape(HD, D)
    )
    gate_full, up_full, down_full = (mlp_full[:, i].reshape(D, FP) for i in range(3))

    small_all = small_all.reshape(BLOCK, 128)
    gains = (
        jnp.concatenate([small_all[:, 16 * i : 16 * i + 16].reshape(1, D) for i in range(4)])
    )
    gains = jnp.pad(gains, ((0, 4), (0, 0)))
    natural = small_all[:, 64:112].reshape(4, 2, 2, 4, 2, 48).transpose(1, 3, 0, 2, 4, 5)
    shift = by_part(natural.reshape(1, 3 * D))
    shift = lax.dynamic_index_in_dim(shift, y * 2 + core, 0, False)

    plan = lax.dynamic_slice_in_dim(small_all, xz * TP + y * 2, 2, 0)[:, 112:122].astype(jnp.int32)
    blocks = plan[:, 2:].reshape(2, 2, 4)
    own_blocks = lax.dynamic_index_in_dim(blocks, zh, axis=1, keepdims=False)
    other_blocks = lax.dynamic_index_in_dim(blocks, 1 - zh, axis=1, keepdims=False)
    second, position, valid = jax.vmap(block_places)(
        plan[:, :2], jnp.concatenate([own_blocks, other_blocks], axis=1)
    )
    half = 4 * BLOCK
    q_second, q_position = second[:, :half], position[:, :half]
    allowed = (
        (q_second[:, :, None] == second[:, None, :])
        & (position[:, None, :] <= q_position[:, :, None])
        & valid[:, None, :]
    )
    cosine, sines = rotary_tables(q_position)
    place = (zh * 4 + y) * BLOCK
    _, _, slot_valid = block_places(lengths, slot_block[0])
    own_valid = lax.dynamic_slice_in_dim(slot_valid, place, BLOCK, 0)

    def by_group(v):
        return v.reshape(4, 2, BLOCK, -1).swapaxes(0, 1).reshape(2, half, -1)

    def by_token(v):
        return v.reshape(2, 4, BLOCK, -1).swapaxes(0, 1)

    hidden = permute_features(hidden_in[0])
    grad_out = permute_features(cotangent[0]) * own_valid[:, None].astype(bf)
    grad_out_all = lax.all_gather(grad_out, TPA, axis=0, tiled=True)

    one_all = norm_gather(hidden, gains, 1).reshape(TP * BLOCK, D)
    joined = by_group(mm(one_all, qkv_full) + shift).reshape(2, half, 3, 4, HEAD_DIM)
    queries = rotate(joined[:, :, 0], cosine, sines, 1.0).astype(bf)
    own_keys = rotate(joined[:, :, 1], cosine, sines, 1.0).astype(bf)
    own_values = joined[:, :, 2].astype(bf)
    swap = [(0, 1), (1, 0)]
    own_kv = jnp.stack([own_keys, own_values])
    other_kv = lax.ppermute(own_kv, "zh", swap)
    keys, values = jnp.concatenate([own_kv, other_kv], axis=2)

    raw = jnp.einsum("gthd,gshd->ghts", queries, keys, preferred_element_type=f32) * SCALE
    scores = jnp.where(allowed[:, None], raw, NEG)
    highest = jnp.max(scores, axis=-1, keepdims=True)
    log_total = highest + jnp.log(jnp.sum(jnp.exp(scores - highest), axis=-1, keepdims=True))
    probs = jnp.exp(scores - log_total)
    weights = probs.astype(bf)
    mixed = jnp.einsum("ghts,gshd->gthd", weights, values, preferred_element_type=f32)
    attended = by_token(mixed.reshape(2, half, HD).astype(bf))

    middle, two_all = out_proj(attended, out_full, hidden, gains, 2)
    two_all = two_all.reshape(TP * BLOCK, D)
    gate = mm(two_all, gate_full)
    up_proj = mm(two_all, up_full)
    sig = jax.nn.sigmoid(gate)
    activated = gate * sig
    inner = (activated * up_proj).astype(bf)
    hidden_out = lax.psum_scatter(
        mm_nt(inner, down_full).astype(bf), TPA, scatter_dimension=0, tiled=True
    )
    hidden_out = (middle + hidden_out.astype(f32)).astype(bf)

    inner_grad = mm(grad_out_all, down_full)
    gate_grad = (inner_grad * up_proj * sig * (1.0 + gate * (1.0 - sig))).astype(bf)
    up_grad = (inner_grad * activated).astype(bf)
    middle_grad, two_sums, branch_all = mlp_back(
        gate_grad.reshape(4, 2, BLOCK, FP),
        up_grad.reshape(4, 2, BLOCK, FP),
        gate_full,
        up_full,
        middle,
        grad_out,
        gains,
        3,
    )
    branch_all = branch_all.reshape(TP * BLOCK, D)
    attended_grad = mm_nt(branch_all, out_full).astype(bf)

    mlp_part = jnp.stack(
        [mm_tn(two_all, gate_grad), mm_tn(two_all, up_grad), mm_tn(grad_out_all, inner)], axis=0
    ).astype(bf)
    mlp_part = mlp_part.reshape(3, 16, BLOCK, FP).swapaxes(0, 1).reshape(-1, FP)
    mlp_sum = lax.psum_scatter(mlp_part, XZ, scatter_dimension=0, tiled=True)
    out_part = mm_tn(attended.reshape(TP * BLOCK, HD), branch_all).astype(bf)
    out_sum = lax.psum_scatter(out_part, XZ, scatter_dimension=0, tiled=True)

    grad_heads = by_group(attended_grad).reshape(2, half, 4, HEAD_DIM)
    prob_grad = jnp.einsum("gthd,gshd->ghts", grad_heads, values, preferred_element_type=f32)
    score_grad = (
        probs * (prob_grad - jnp.sum(probs * prob_grad, axis=-1, keepdims=True))
    ).astype(bf)
    query_grad = jnp.einsum("ghts,gshd->gthd", score_grad, keys, preferred_element_type=f32) * SCALE
    key_part = (
        jnp.einsum("ghts,gthd->gshd", score_grad, queries, preferred_element_type=f32) * SCALE
    )
    value_part = jnp.einsum("ghts,gthd->gshd", weights, grad_heads, preferred_element_type=f32)
    kv_part = jnp.stack([key_part, value_part])
    kv_back = lax.ppermute(kv_part[:, :, half:].astype(bf), "zh", swap).astype(f32)
    key_grad, value_grad = kv_part[:, :, :half] + kv_back
    joined_grad = jnp.stack(
        [
            rotate(query_grad, cosine, sines, -1.0),
            rotate(key_grad, cosine, sines, -1.0),
            value_grad,
        ],
        axis=2,
    ).astype(bf)
    joined_grad = by_token(joined_grad.reshape(2, half, 3 * HD))
    flat_grad = joined_grad.reshape(TP * BLOCK, 3 * HD)
    qkv_sum = lax.psum_scatter(
        mm_tn(one_all, flat_grad).astype(bf), XZ, scatter_dimension=0, tiled=True
    )
    input_grad, one_sums = qkv_back(joined_grad, qkv_full, hidden, middle_grad, gains, 4)

    terms = jnp.concatenate([one_sums[:2], two_sums[:2]]).reshape(4, 16, 128).swapaxes(0, 1)
    terms = jnp.pad(terms, ((0, 0), (0, 4), (0, 0)))
    shift_part = jnp.sum(flat_grad.astype(f32), axis=0).reshape(6, 128)
    shift_part = jnp.pad(shift_part, ((0, 2), (0, 0)))
    small_sum, qkv_all, mlp_all, out_all = collect(
        terms, shift_part, qkv_sum.reshape(TP, 16, FP), mlp_sum.reshape(3, TP, 16, FP), out_sum, 5
    )

    def restore_parts(g):
        g = g.reshape(4, 2, -1, 3, 4, 2, 2, 16).transpose(2, 3, 1, 0, 4, 5, 6, 7)
        g = jnp.concatenate([g[:, :2], g[:, 2:].swapaxes(5, 6)], axis=1)
        return g.reshape(-1, 3 * D)

    vectors = jnp.sum(small_sum[:, :4], axis=0)
    vectors = lax.dynamic_slice_in_dim(vectors, (y * 2 + core) * 16, 16, 1)
    shift_grad = restore_parts(small_sum[:, 8:14].reshape(TP, 1, FP)).reshape(128, 48)
    row = (zh * 4 + y) * 16 + lax.axis_index("x") * 4 + lax.axis_index("zl") * 2 + core
    shift_grad = lax.dynamic_index_in_dim(shift_grad, row, 0, False)

    def whole(i):
        return mlp_all[:, i, :, :FC].swapaxes(0, 1).reshape(16, FF).astype(f32)

    return (
        restore_features(hidden_out)[None],
        restore_features(input_grad)[None],
        vectors[0],
        vectors[1],
        restore_parts(qkv_all.astype(f32)),
        shift_grad,
        restore_features(out_all.astype(f32)),
        vectors[2],
        vectors[3],
        whole(0),
        whole(1),
        whole(2),
    )


def solution(mesh):
    inner = Mesh(mesh.devices.reshape(2, 4, 4, 2, 2), ROWS)
    rows = P(ROWS)
    tokens = P(GRP, SLOT, None)
    placed = (
        tokens,
        tokens,
        P(GRP, None),
        P(GRP, None),
        rows,
        rows,
        P(ROWS, None),
        rows,
        P(ROWS, None),
        rows,
        rows,
        P(ROWS, None),
        P(ROWS, None),
        P(ROWS, None),
    )
    return jax.shard_map(
        body,
        mesh=inner,
        in_specs=placed,
        out_specs=(
            tokens,
            tokens,
            rows,
            rows,
            P(ROWS, None),
            rows,
            P(ROWS, None),
            rows,
            rows,
            P(ROWS, None),
            P(ROWS, None),
            P(ROWS, None),
        ),
        check_vma=False,
    )
```

```python
import functools

import jax
import jax.numpy as jnp
from jax import lax
from jax.experimental import pallas as pl
from jax.experimental.pallas import tpu as pltpu
from jax.sharding import Mesh
from jax.sharding import PartitionSpec as P

D = 2048
HEADS = 32
HEAD_DIM = 64
ROT = 16
FF = 5632
BLOCK = 128
TP = 8
HD = D // TP
FC = FF // TP

EPS = 1e-05
NEG = -1e30
SCALE = HEAD_DIM ** (-0.5)
TPA = ("y", "core")
XZ = ("x", "zh", "zl")
ROWS = ("zh", "y", "x", "zl", "core")
GRP = ("x", "zl", "core")
SLOT = ("zh", "y")


def permute_features(v):
    lead = v.shape[:-1]
    n = len(lead)
    v = v.reshape(lead + (2, 4, 4, 2, 32))
    v = v.transpose(tuple(range(n)) + (n + 2, n, n + 3, n + 1, n + 4))
    return v.reshape(lead + (D,))


def restore_features(v):
    lead = v.shape[:-1]
    n = len(lead)
    v = v.reshape(lead + (4, 2, 2, 4, 32))
    v = v.transpose(tuple(range(n)) + (n + 1, n + 3, n, n + 2, n + 4))
    return v.reshape(lead + (D,))


def block_places(lengths, blocks):
    first_pad = (lengths[0] + BLOCK - 1) // BLOCK * BLOCK
    offsets = jnp.arange(BLOCK, dtype=jnp.int32)
    placed = (blocks[:, None] * BLOCK + offsets[None, :]).reshape(-1)
    second = (placed >= first_pad).astype(jnp.int32)
    position = placed - second * first_pad
    limit = jnp.where(second == 1, lengths[1], lengths[0])
    return second, position, position < limit


def rotary_tables(position):
    freq_steps = jnp.arange(ROT // 2, dtype=jnp.float32)
    inverse = 10000.0 ** (-2.0 * freq_steps / ROT)
    phases = position.astype(jnp.float32)[..., None] * inverse
    return jnp.cos(phases), jnp.sin(phases)


def rotate(shaped, cosine, sines, direction):
    half = ROT // 2
    front = shaped[..., :half]
    behind = shaped[..., half:ROT]
    c = cosine[:, :, None, :]
    s = sines[:, :, None, :] * direction
    return jnp.concatenate(
        [front * c - behind * s, behind * c + front * s, shaped[..., ROT:]], axis=-1
    )


def layer_norm(values):
    average = jnp.mean(values, axis=-1, keepdims=True)
    centred = values - average
    inv_scale = lax.rsqrt(jnp.mean(centred * centred, axis=-1, keepdims=True) + EPS)
    return centred * inv_scale, inv_scale


def norm_back(grad_in, normed, inv_scale, gain):
    scaled = grad_in * gain
    return inv_scale * (
        scaled
        - jnp.mean(scaled, axis=-1, keepdims=True)
        - normed * jnp.mean(scaled * normed, axis=-1, keepdims=True)
    )


def mm(a, b):
    return jnp.dot(a, b, preferred_element_type=jnp.float32)


def mm_nt(a, b):
    return lax.dot_general(a, b, (((1,), (1,)), ((), ())), preferred_element_type=jnp.float32)


def mm_tn(a, b):
    return lax.dot_general(a, b, (((0,), (0,)), ((), ())), preferred_element_type=jnp.float32)


FP = 768
HALF = BLOCK // 2
ANY = pl.BlockSpec(memory_space=pl.ANY)
VM = pl.BlockSpec(memory_space=pltpu.VMEM)
BF = jnp.bfloat16
F32 = jnp.float32


def params(cid):
    return pltpu.CompilerParams(
        collective_id=cid, has_side_effects=True, vmem_limit_bytes=56 * 1024 * 1024
    )


def meet(peers):
    barrier = pltpu.get_barrier_semaphore()
    for peer in peers:
        pl.semaphore_signal(
            barrier, inc=1, device_id=peer, device_id_type=pl.DeviceIdType.MESH
        )
    pl.semaphore_wait(barrier, len(peers))


def remote(sems, i, src, dst, peer):
    return pltpu.make_async_remote_copy(
        src_ref=src,
        dst_ref=dst,
        send_sem=sems[0].at[i],
        recv_sem=sems[1].at[i],
        device_id=peer,
        device_id_type=pl.DeviceIdType.MESH,
    )


def ring():
    y = lax.axis_index("y")
    c = lax.axis_index("core")
    up = lax.rem(y + 1, 4)
    opp = lax.rem(y + 2, 4)
    dn = lax.rem(y + 3, 4)
    return y, c, up, opp, dn


def ring_peers(up, dn, c):
    return {"y": up}, {"y": dn}, {"core": 1 - c}


N_AG = 11
N_RS = 10


def ring_gather(own, full, local_sem, sems):
    y, c, up, opp, dn = ring()
    to_up, to_dn, to_sib = ring_peers(up, dn, c)
    first, last = pl.ds(0, HALF), pl.ds(HALF, HALF)
    cp = functools.partial(remote, sems)
    up1 = cp(0, own.at[first], full.at[y, c, first], to_up)
    dn1 = cp(1, own.at[last], full.at[y, c, last], to_dn)
    up2 = cp(2, own.at[last], full.at[y, c, last], to_up)
    dn2 = cp(3, own.at[first], full.at[y, c, first], to_dn)
    sib0 = cp(4, own, full.at[y, c], to_sib)
    here = pltpu.make_async_copy(own, full.at[y, c], local_sem)
    for one in (up1, dn1, up2, dn2, sib0, here):
        one.start()
    up1.wait_recv()
    far1 = cp(5, full.at[dn, c, first], full.at[dn, c, first], to_up)
    far1.start()
    dn1.wait_recv()
    far2 = cp(6, full.at[up, c, last], full.at[up, c, last], to_dn)
    far2.start()
    up2.wait_recv()
    sib1 = cp(7, full.at[dn, c], full.at[dn, c], to_sib)
    sib1.start()
    dn2.wait_recv()
    sib2 = cp(8, full.at[up, c], full.at[up, c], to_sib)
    sib2.start()
    far1.wait_recv()
    sib3 = cp(9, full.at[opp, c, first], full.at[opp, c, first], to_sib)
    sib3.start()
    far2.wait_recv()
    sib4 = cp(10, full.at[opp, c, last], full.at[opp, c, last], to_sib)
    sib4.start()
    for one in (sib0, sib1, sib2, sib3, sib4):
        one.wait_recv()
    here.wait()
    for one in (up1, dn1, up2, dn2, sib0, far1, far2, sib1, sib2, sib3, sib4):
        one.wait_send()


def rows_loop(count, step, body):
    @pl.loop(0, count // step)
    def _(i):
        body(pl.ds(pl.multiple_of(i * step, step), step))


RS_SCRATCH = [
    pltpu.VMEM((4, 2, BLOCK, D), F32),
    pltpu.VMEM((4, BLOCK, D), BF),
    pltpu.VMEM((4, BLOCK, D), BF),
    pltpu.VMEM((2, HALF, D), BF),
    pltpu.VMEM((2, HALF, D), BF),
    pltpu.VMEM((2, BLOCK, D), BF),
    pltpu.VMEM((2, BLOCK, D), BF),
    pltpu.SemaphoreType.DMA((N_RS,)),
    pltpu.SemaphoreType.DMA((N_RS,)),
]


def ring_scatter(partial, scratch, between=None):
    part, sib_out, sib_in, far_out, far_in, near_out, near_in, *sems = scratch
    y, c, up, opp, dn = ring()
    to_up, to_dn, to_sib = ring_peers(up, dn, c)
    first, last = pl.ds(0, HALF), pl.ds(HALF, HALF)
    cp = functools.partial(remote, sems)
    order = (opp, up, dn, y)
    sib = [cp(j, sib_out.at[j], sib_in.at[j], to_sib) for j in range(4)]

    def produce(j):
        partial(order[j], part.at[j])

        def lower(r):
            sib_out[j, r, :] = part[j, 1 - c, r, :].astype(BF)

        rows_loop(BLOCK, 32, lower)
        sib[j].start()

    far = [
        cp(4, far_out.at[0], far_in.at[0], to_up),
        cp(5, far_out.at[1], far_in.at[1], to_dn),
    ]
    near_early = [
        cp(6, near_out.at[0, last], near_in.at[0, last], to_up),
        cp(7, near_out.at[1, first], near_in.at[1, first], to_dn),
    ]
    near_late = [
        cp(8, near_out.at[0, first], near_in.at[0, first], to_up),
        cp(9, near_out.at[1, last], near_in.at[1, last], to_dn),
    ]
    produce(0)
    produce(1)
    sib[0].wait_recv()
    for k in range(2):

        def add_far(r, k=k):
            q = pl.ds(k * HALF + r.start, r.size)
            far_out[k, r, :] = (part[0, c, q, :] + sib_in[0, q, :].astype(F32)).astype(BF)

        rows_loop(HALF, 32, add_far)
        far[k].start()
    produce(2)
    for k in range(2):
        sib[1 + k].wait_recv()

        def add_near(r, k=k):
            q = pl.ds((1 - k) * HALF + r.start, r.size)
            near_out[k, q, :] = (part[1 + k, c, q, :] + sib_in[1 + k, q, :].astype(F32)).astype(BF)

        rows_loop(HALF, 32, add_near)
        near_early[k].start()
    produce(3)
    for k in range(2):
        far[k].wait_recv()

        def add_late(r, k=k):
            q = pl.ds(k * HALF + r.start, r.size)
            near_out[k, q, :] = (
                part[1 + k, c, q, :] + sib_in[1 + k, q, :].astype(F32) + far_in[k, r, :].astype(F32)
            ).astype(BF)

        rows_loop(HALF, 32, add_late)
        near_late[k].start()
    if between is not None:
        between()
    sib[3].wait_recv()
    for one in near_early + near_late:
        one.wait_recv()

    def finish(r):
        part[3, c, r, :] = (
            part[3, c, r, :]
            + sib_in[3, r, :].astype(F32)
            + near_in[0, r, :].astype(F32)
            + near_in[1, r, :].astype(F32)
        )

    rows_loop(BLOCK, 32, finish)
    for one in sib + far + near_early + near_late:
        one.wait_send()
    return part.at[3, c]


AG_SCRATCH = [
    pltpu.VMEM((BLOCK, D), BF),
    pltpu.SemaphoreType.DMA,
    pltpu.SemaphoreType.DMA((N_AG,)),
    pltpu.SemaphoreType.DMA((N_AG,)),
]
FULL = jax.ShapeDtypeStruct((4, 2, BLOCK, D), BF)


def kernel_norm_gather(hidden, gains, full, own, local_sem, *sems):
    y, c, up, opp, dn = ring()
    meet(ring_peers(up, dn, c))

    def norm(r):
        normed, _ = layer_norm(hidden[r, :].astype(F32))
        own[r, :] = (normed * gains[0:1, :] + gains[1:2, :]).astype(BF)

    rows_loop(BLOCK, 16, norm)
    ring_gather(own, full, local_sem, sems)


def norm_gather(hidden, gains, cid):
    return pl.pallas_call(
        kernel_norm_gather,
        out_shape=FULL,
        in_specs=[VM, VM],
        out_specs=ANY,
        scratch_shapes=AG_SCRATCH,
        compiler_params=params(cid),
        name="norm_gather",
    )(hidden, gains)


NT = (((1,), (1,)), ((), ()))


def kernel_out_proj(attended, weight, hidden, gains, middle, full, *scratch):
    own, local_sem, *sems = scratch[:4]
    y, c, up, opp, dn = ring()
    meet(ring_peers(up, dn, c))

    def partial(block, out):
        a = attended[block].reshape(2 * BLOCK, HD)

        @pl.loop(0, 4)
        def _(i):
            q = pl.ds(pl.multiple_of(i * 512, 512), 512)
            out[:, :, q] = jnp.dot(a, weight[:, q], preferred_element_type=F32).reshape(
                2, BLOCK, 512
            )

    total = ring_scatter(partial, scratch[4:])

    def norm(r):
        row = hidden[r, :].astype(F32) + total[r, :]
        middle[r, :] = row
        normed, _ = layer_norm(row)
        own[r, :] = (normed * gains[2:3, :] + gains[3:4, :]).astype(BF)

    rows_loop(BLOCK, 16, norm)
    ring_gather(own, full, local_sem, sems)


def out_proj(attended, weight, hidden, gains, cid):
    return pl.pallas_call(
        kernel_out_proj,
        out_shape=(jax.ShapeDtypeStruct((BLOCK, D), F32), FULL),
        in_specs=[VM] * 4,
        out_specs=(VM, ANY),
        scratch_shapes=AG_SCRATCH + RS_SCRATCH,
        compiler_params=params(cid),
        name="out_proj",
    )(attended, weight, hidden, gains)


def kernel_mlp_back(
    gate_grad, up_grad, w_gate, w_up, middle, grad_out, gains, middle_grad, sums, full, *scratch
):
    own, local_sem, *sems = scratch[:4]
    y, c, up, opp, dn = ring()
    meet(ring_peers(up, dn, c))

    def partial(block, out):
        a = gate_grad[block].reshape(2 * BLOCK, FP)
        b = up_grad[block].reshape(2 * BLOCK, FP)

        @pl.loop(0, 4)
        def _(i):
            q = pl.ds(pl.multiple_of(i * 512, 512), 512)
            out[:, :, q] = (
                lax.dot_general(a, w_gate[q, :], NT, preferred_element_type=F32)
                + lax.dot_general(b, w_up[q, :], NT, preferred_element_type=F32)
            ).reshape(2, BLOCK, 512)

    total = ring_scatter(partial, scratch[4:])
    sums[...] = jnp.zeros_like(sums)

    def back(r):
        row = total[r, :]
        normed, inv = layer_norm(middle[r, :])
        grad = grad_out[r, :].astype(F32) + norm_back(row, normed, inv, gains[2:3, :])
        middle_grad[r, :] = grad
        own[r, :] = grad.astype(BF)
        sums[0:1, :] += jnp.sum(row * normed, axis=0, keepdims=True)
        sums[1:2, :] += jnp.sum(row, axis=0, keepdims=True)

    rows_loop(BLOCK, 16, back)
    ring_gather(own, full, local_sem, sems)


def mlp_back(gate_grad, up_grad, w_gate, w_up, middle, grad_out, gains, cid):
    return pl.pallas_call(
        kernel_mlp_back,
        out_shape=(
            jax.ShapeDtypeStruct((BLOCK, D), F32),
            jax.ShapeDtypeStruct((8, D), F32),
            FULL,
        ),
        in_specs=[VM] * 7,
        out_specs=(VM, VM, ANY),
        scratch_shapes=AG_SCRATCH + RS_SCRATCH,
        compiler_params=params(cid),
        name="mlp_back",
    )(gate_grad, up_grad, w_gate, w_up, middle, grad_out, gains)


NN = (((1,), (0,)), ((), ()))
TN = (((0,), (0,)), ((), ()))
TOKENS = 4 * BLOCK
KEYS = 2 * TOKENS
TILE = 2 * BLOCK


def dot(a, b, dims):
    return lax.dot_general(a, b, dims, preferred_element_type=F32)


def lane(n):
    return lax.broadcasted_iota(jnp.int32, (1, n), 1)


def turn_tables(base):
    entry = lax.rem(lane(BLOCK), HEAD_DIM)
    freq = jnp.exp(
        lax.rem(entry, ROT // 2).astype(F32) * (-2.0 / ROT * 9.210340371976184)
    )
    freq = jnp.where(entry < ROT, freq, 0.0)
    place = (base + lax.broadcasted_iota(jnp.int32, (BLOCK, 1), 0)).astype(F32)
    phase = place * freq
    return jnp.cos(phase), jnp.sin(phase)


def turn(v, cosine, sines, direction):
    entry = lax.rem(lane(BLOCK), HEAD_DIM)
    s = sines * direction
    ahead = pltpu.roll(v, BLOCK - ROT // 2, 1)
    behind = pltpu.roll(v, ROT // 2, 1)
    return v * cosine + jnp.where(entry < ROT // 2, -ahead, behind) * s


def key_bias(table, g, tile):
    token = lane(BLOCK)
    q_code, q_low = [], []
    for j in range(2):
        low = table[g, 1, 2 * tile + j] * 4096
        q_code.append(low + table[g, 0, 2 * tile + j] + token)
        q_low.append(low + jnp.zeros_like(token))
    q_code = jnp.concatenate(q_code, axis=1)
    q_low = jnp.concatenate(q_low, axis=1)
    column = lax.broadcasted_iota(jnp.int32, (BLOCK, 1), 0)
    rows = []
    for k in range(8):
        place = table[g, 0, k] + column
        code = jnp.where(place < table[g, 2, k], table[g, 1, k] * 4096 + place, 1 << 20)
        kept = jnp.logical_and(code <= q_code, code >= q_low)
        rows.append(jnp.where(kept, 0.0, NEG))
    return jnp.concatenate(rows, axis=0)


def head_mask(h):
    first = lane(BLOCK) < HEAD_DIM
    return jnp.where(first if h == 0 else jnp.logical_not(first), 1.0, 0.0).astype(BF)


def kernel_attend(
    table, tokens, weight, shift, queries, kv, lse, attended, cosines, sines, send, recv
):
    zh = lax.axis_index("zh")
    partner = {"zh": 1 - zh}
    meet([partner])
    sems = (send, recv)

    @pl.loop(0, 4)
    def _(y):
        at = pl.ds(pl.multiple_of(y * BLOCK, BLOCK), BLOCK)
        for g in range(2):
            cosine, sine = turn_tables(table[g, 0, y])
            cosines[g, at, :] = cosine
            sines[g, at, :] = sine
        a = tokens[y].reshape(TILE, D)
        new = dot(a, weight[:, HD:], NN) + shift[:, HD:]
        for g in range(2):
            rows = slice(g * BLOCK, (g + 1) * BLOCK)
            for pair in range(2):
                q = slice(pair * BLOCK, (pair + 1) * BLOCK)
                turned = turn(new[rows, q], cosines[g, at, :], sines[g, at, :], 1.0)
                kv[0, g, at, q] = turned.astype(BF)
            kv[1, g, at, :] = new[rows, HD:].astype(BF)

    own, other = pl.ds(0, TOKENS), pl.ds(TOKENS, TOKENS)
    trade = [
        remote(sems, g, kv.at[:, g, own, :], kv.at[:, g, other, :], partner) for g in range(2)
    ]
    for one in trade:
        one.start()

    @pl.loop(0, 4)
    def _(y):
        at = pl.ds(pl.multiple_of(y * BLOCK, BLOCK), BLOCK)
        new = dot(tokens[y].reshape(TILE, D), weight[:, :HD], NN) + shift[:, :HD]
        for g in range(2):
            rows = slice(g * BLOCK, (g + 1) * BLOCK)
            for pair in range(2):
                q = slice(pair * BLOCK, (pair + 1) * BLOCK)
                turned = turn(new[rows, q], cosines[g, at, :], sines[g, at, :], 1.0)
                queries[g, at, q] = turned.astype(BF) * jnp.asarray(SCALE, BF)

    for g in range(2):
        trade[g].wait_recv()

        @pl.loop(0, 2)
        def _(tile, g=g):
            at = pl.ds(pl.multiple_of(tile * TILE, TILE), TILE)
            bias = key_bias(table, g, tile)
            for pair in range(2):
                q = slice(pair * BLOCK, (pair + 1) * BLOCK)
                k_all = kv[0, g, :, q]
                v_all = kv[1, g, :, q]
                out = jnp.zeros((TILE, BLOCK), F32)
                for h in range(2):
                    s = dot(k_all, queries[g, at, q] * head_mask(h), NT) + bias
                    top = jnp.max(s, axis=0, keepdims=True)
                    p = jnp.exp(s - top)
                    total = jnp.sum(p, axis=0, keepdims=True)
                    w = (p * (1.0 / total)).astype(BF)
                    lse[g, 2 * pair + h : 2 * pair + h + 1, at] = top + jnp.log(total)
                    out = out + dot(w, v_all * head_mask(h), TN)
                for j in range(2):
                    attended[2 * tile + j, g, :, q] = out[j * BLOCK : (j + 1) * BLOCK].astype(BF)

    for one in trade:
        one.wait_send()


SM = pl.BlockSpec(memory_space=pltpu.SMEM)


def attend(table, tokens, weight, shift, cid):
    return pl.pallas_call(
        kernel_attend,
        out_shape=(
            jax.ShapeDtypeStruct((2, TOKENS, HD), BF),
            jax.ShapeDtypeStruct((2, 2, KEYS, HD), BF),
            jax.ShapeDtypeStruct((2, 8, TOKENS), F32),
            jax.ShapeDtypeStruct((4, 2, BLOCK, HD), BF),
        ),
        in_specs=[SM, VM, VM, VM],
        out_specs=(VM,) * 4,
        scratch_shapes=[
            pltpu.VMEM((2, TOKENS, BLOCK), F32),
            pltpu.VMEM((2, TOKENS, BLOCK), F32),
            pltpu.SemaphoreType.DMA((2,)),
            pltpu.SemaphoreType.DMA((2,)),
        ],
        compiler_params=params(cid),
        name="attend",
    )(table, tokens, weight, shift)


def kernel_attend_back(
    table,
    branch,
    weight,
    attended,
    queries,
    kv,
    lse,
    joined_grad,
    out_part,
    grads,
    dq,
    dkv,
    kv_out,
    kv_in,
    send,
    recv,
):
    zh = lax.axis_index("zh")
    partner = {"zh": 1 - zh}
    meet([partner])
    sems = (send, recv)

    @pl.loop(0, 4)
    def _(y):
        at = pl.ds(pl.multiple_of(y * BLOCK, BLOCK), BLOCK)
        new = dot(branch[y].reshape(TILE, D), weight[...], NT)
        for g in range(2):
            grads[g, at, :] = new[g * BLOCK : (g + 1) * BLOCK].astype(BF)

    trade = [remote(sems, g, kv_out.at[g], kv_in.at[g], partner) for g in range(2)]
    own, other = pl.ds(0, TOKENS), pl.ds(TOKENS, TOKENS)
    for g in range(2):

        @pl.loop(0, 2)
        def _(tile, g=g):
            at = pl.ds(pl.multiple_of(tile * TILE, TILE), TILE)
            bias = key_bias(table, g, tile)
            for pair in range(2):
                q = slice(pair * BLOCK, (pair + 1) * BLOCK)
                k_all = kv[0, g, :, q]
                v_all = kv[1, g, :, q]
                new_q = jnp.zeros((TILE, BLOCK), F32)
                new_k = jnp.zeros((KEYS, BLOCK), F32)
                new_v = jnp.zeros((KEYS, BLOCK), F32)
                for h in range(2):
                    q_head = queries[g, at, q] * head_mask(h)
                    g_head = grads[g, at, q] * head_mask(h)
                    s = dot(k_all, q_head, NT) + bias
                    p = jnp.exp(s - lse[g, 2 * pair + h : 2 * pair + h + 1, at])
                    p_grad = dot(v_all, g_head, NT)
                    mean = jnp.sum(p * p_grad, axis=0, keepdims=True)
                    s_grad = (p * (p_grad - mean)).astype(BF)
                    new_v = new_v + dot(p.astype(BF), g_head, NN)
                    new_k = new_k + dot(s_grad, q_head, NN)
                    new_q = new_q + dot(s_grad, k_all * head_mask(h), TN)
                dq[g, at, q] = new_q * SCALE

                @pl.when(tile == 0)
                def _():
                    dkv[0, g, :, q] = new_k
                    dkv[1, g, :, q] = new_v

                @pl.when(tile != 0)
                def _():
                    dkv[0, g, :, q] += new_k
                    dkv[1, g, :, q] += new_v

        for i in range(2):
            kv_out[g, i] = dkv[i, g, other, :].astype(BF)
        trade[g].start()

    @pl.loop(0, 8)
    def _(i):
        q = pl.ds(pl.multiple_of(i * TILE, TILE), TILE)
        new = dot(attended[...].reshape(8 * BLOCK, HD), branch[:, :, :, q].reshape(8 * BLOCK, TILE), TN)
        for x in range(4):
            for zl in range(2):
                for a in range(2):
                    row = x * 64 + zl * 32 + a * 16
                    out_part[x * 4 + a * 2 + zl, :, q] = new[row : row + 16].astype(BF)

    for g in range(2):
        trade[g].wait_recv()

        @pl.loop(0, 4)
        def _(y, g=g):
            at = pl.ds(pl.multiple_of(y * BLOCK, BLOCK), BLOCK)
            cosine, sine = turn_tables(table[g, 0, y])
            for pair in range(2):
                q = slice(pair * BLOCK, (pair + 1) * BLOCK)
                joined_grad[y, g, :, q] = turn(dq[g, at, q], cosine, sine, -1.0).astype(BF)
                new = dkv[0, g, at, q] + kv_in[g, 0, at, q].astype(F32)
                joined_grad[y, g, :, HD + pair * BLOCK : HD + (pair + 1) * BLOCK] = turn(
                    new, cosine, sine, -1.0
                ).astype(BF)
            joined_grad[y, g, :, 2 * HD :] = (
                dkv[1, g, at, :] + kv_in[g, 1, at, :].astype(F32)
            ).astype(BF)

    for one in trade:
        one.wait_send()


def attend_back(table, branch, weight, attended, queries, kv, lse, cid):
    return pl.pallas_call(
        kernel_attend_back,
        out_shape=(
            jax.ShapeDtypeStruct((4, 2, BLOCK, 3 * HD), BF),
            jax.ShapeDtypeStruct((16, 16, D), BF),
        ),
        in_specs=[SM] + [VM] * 6,
        out_specs=(VM, VM),
        scratch_shapes=[
            pltpu.VMEM((2, TOKENS, HD), BF),
            pltpu.VMEM((2, TOKENS, HD), F32),
            pltpu.VMEM((2, 2, KEYS, HD), F32),
            pltpu.VMEM((2, 2, TOKENS, HD), BF),
            pltpu.VMEM((2, 2, TOKENS, HD), BF),
            pltpu.SemaphoreType.DMA((2,)),
            pltpu.SemaphoreType.DMA((2,)),
        ],
        compiler_params=params(cid),
        name="attend_back",
    )(table, branch, weight, attended, queries, kv, lse)


def kernel_mlp(two, grad_out, w, inner, gate_grad, up_grad, out):
    w_gate, w_up, w_down = (w[:, i].reshape(D, FP) for i in range(3))
    gate = dot(two[...], w_gate, NN)
    up = dot(two[...], w_up, NN)
    grad = dot(grad_out[...], w_down, NN)
    sig = 1.0 / (1.0 + jnp.exp(-gate))
    active = gate * sig
    low = (active * up).astype(BF)
    inner[...] = low
    gate_grad[...] = (grad * up * sig * (1.0 + gate * (1.0 - sig))).astype(BF)
    up_grad[...] = (grad * active).astype(BF)
    for i in range(4):
        q = slice(i * 512, (i + 1) * 512)
        out[:, q] = dot(low, w[4 * i : 4 * i + 4, 2].reshape(512, FP), NT).astype(BF)


def mlp(two, grad_out, w):
    rows = pl.BlockSpec((TILE, D), lambda i: (i, 0))
    cols = pl.BlockSpec((TILE, FP), lambda i: (i, 0))
    hidden = jax.ShapeDtypeStruct((TP * BLOCK, FP), BF)
    return pl.pallas_call(
        kernel_mlp,
        grid=(4,),
        out_shape=(hidden, hidden, hidden, jax.ShapeDtypeStruct((TP * BLOCK, D), BF)),
        in_specs=[rows, rows, pl.BlockSpec((16, 3, BLOCK, FP), lambda i: (0, 0, 0, 0))],
        out_specs=(cols, cols, cols, rows),
        compiler_params=pltpu.CompilerParams(vmem_limit_bytes=56 * 1024 * 1024),
        cost_estimate=pl.CostEstimate(
            flops=4 * 2 * 1024 * D * FP, bytes_accessed=28 * 2**20, transcendentals=1024 * FP
        ),
        name="mlp",
    )(two, grad_out, w)


def kernel_mlp_weights(two, grad_out, gate_grad, up_grad, inner, out):
    for k, (a, b) in enumerate(((two, gate_grad), (two, up_grad), (grad_out, inner))):
        out[:, k] = dot(a[...], b[...], TN).astype(BF).reshape(2, BLOCK, FP)


def mlp_weights(two, grad_out, gate_grad, up_grad, inner):
    cols = pl.BlockSpec((TP * BLOCK, TILE), lambda i: (0, i))
    whole = pl.BlockSpec((TP * BLOCK, FP), lambda i: (0, 0))
    return pl.pallas_call(
        kernel_mlp_weights,
        grid=(8,),
        out_shape=jax.ShapeDtypeStruct((16, 3, BLOCK, FP), BF),
        in_specs=[cols, cols, whole, whole, whole],
        out_specs=pl.BlockSpec((2, 3, BLOCK, FP), lambda i: (i, 0, 0, 0)),
        compiler_params=pltpu.CompilerParams(vmem_limit_bytes=56 * 1024 * 1024),
        cost_estimate=pl.CostEstimate(
            flops=3 * 2 * 1024 * D * FP, bytes_accessed=22 * 2**20, transcendentals=0
        ),
        name="mlp_weights",
    )(two, grad_out, gate_grad, up_grad, inner)


class PlaneScatter:
    COPIES = 12

    def __init__(self, part, a_in, b_in, a_mid, b_mid, a_last, b_last, send, recv):
        self.refs = part, a_in, b_in, a_mid, b_mid, a_last, b_last
        sems = send, recv
        half = part.shape[-1] // 2
        self.lanes = pl.ds(0, half), pl.ds(half, half)
        self.x = lax.axis_index("x")
        self.z = lax.axis_index("zh") * 2 + lax.axis_index("zl")
        self.one, self.two = [], []
        for d in range(1, 4):
            x = lax.rem(self.x + d, 4)
            z = lax.rem(self.z + d, 4)
            to_x = {"x": x}
            to_z = {"zh": z // 2, "zl": lax.rem(z, 2)}
            a, b = self.lanes
            k = d - 1
            self.one.append(remote(sems, k, part.at[:, z, :, a], a_in.at[k], to_z))
            self.one.append(remote(sems, 3 + k, part.at[x, :, :, b], b_in.at[k], to_x))
            self.two.append(remote(sems, 6 + k, a_mid.at[x], a_last.at[k], to_x))
            self.two.append(remote(sems, 9 + k, b_mid.at[z], b_last.at[k], to_z))

    def start(self):
        for copy in self.one:
            copy.start()

    def middle(self):
        part, a_in, b_in, a_mid, b_mid, _, _ = self.refs
        for copy in self.one:
            copy.wait_recv()
        a, b = self.lanes

        @pl.loop(0, 4)
        def _(i):
            a_mid[i] = (
                part[i, self.z, :, a].astype(F32) + jnp.sum(a_in[:, i].astype(F32), axis=0)
            ).astype(BF)
            b_mid[i] = (
                part[self.x, i, :, b].astype(F32) + jnp.sum(b_in[:, i].astype(F32), axis=0)
            ).astype(BF)

        for copy in self.two:
            copy.start()

    def finish(self, out):
        _, _, _, a_mid, b_mid, a_last, b_last = self.refs
        for copy in self.two:
            copy.wait_recv()
        a, b = self.lanes
        out[:, a] = (
            a_mid[self.x].astype(F32) + jnp.sum(a_last[...].astype(F32), axis=0)
        ).astype(BF)
        out[:, b] = (
            b_mid[self.z].astype(F32) + jnp.sum(b_last[...].astype(F32), axis=0)
        ).astype(BF)
        for copy in self.one + self.two:
            copy.wait_send()


def plane_scratch(rows, lanes):
    half = lanes // 2
    return [
        pltpu.VMEM((3, 4, rows, half), BF),
        pltpu.VMEM((3, 4, rows, half), BF),
        pltpu.VMEM((4, rows, half), BF),
        pltpu.VMEM((4, rows, half), BF),
        pltpu.VMEM((3, rows, half), BF),
        pltpu.VMEM((3, rows, half), BF),
        pltpu.SemaphoreType.DMA((PlaneScatter.COPIES,)),
        pltpu.SemaphoreType.DMA((PlaneScatter.COPIES,)),
    ]


def plane_peers():
    peers = []
    for d in range(1, 4):
        z = lax.rem(lax.axis_index("zh") * 2 + lax.axis_index("zl") + d, 4)
        peers.append({"x": lax.rem(lax.axis_index("x") + d, 4)})
        peers.append({"zh": z // 2, "zl": lax.rem(z, 2)})
    return peers


def kernel_qkv_back(
    joined_grad,
    weight,
    hidden,
    middle_grad,
    gains,
    tokens,
    out_part,
    input_grad,
    sums,
    shift_sum,
    qkv_sum,
    out_sum,
    part,
    *scratch,
):
    y, c, up, opp, dn = ring()
    meet(list(ring_peers(up, dn, c)) + plane_peers())
    out_scatter = PlaneScatter(out_part, *scratch[:8])
    qkv_scatter = PlaneScatter(part, *scratch[8:16])
    out_scatter.start()
    flat = joined_grad[...].reshape(TP * BLOCK, 3 * HD)

    @pl.loop(0, 8)
    def _(i):
        q = pl.ds(pl.multiple_of(i * TILE, TILE), TILE)
        new = dot(tokens[:, :, :, q].reshape(TP * BLOCK, TILE), flat, TN).astype(BF)
        part[i // 2, 2 * lax.rem(i, 2)] = new[:BLOCK]
        part[i // 2, 2 * lax.rem(i, 2) + 1] = new[BLOCK:]

    qkv_scatter.start()

    def partial(block, out):
        a = joined_grad[block].reshape(2 * BLOCK, 3 * HD)

        @pl.loop(0, 4)
        def _(i):
            q = pl.ds(pl.multiple_of(i * 512, 512), 512)
            out[:, :, q] = dot(a, weight[q, :], NT).reshape(2, BLOCK, 512)

    def between():
        out_scatter.middle()
        shift_sum[...] = jnp.broadcast_to(
            jnp.sum(flat.astype(F32), axis=0, keepdims=True), shift_sum.shape
        )
        qkv_scatter.middle()

    total = ring_scatter(partial, scratch[16:], between)
    sums[...] = jnp.zeros_like(sums)

    def back(r):
        row = total[r, :]
        normed, inv = layer_norm(hidden[r, :].astype(F32))
        input_grad[r, :] = middle_grad[r, :] + norm_back(row, normed, inv, gains[0:1, :])
        sums[0:1, :] += jnp.sum(row * normed, axis=0, keepdims=True)
        sums[1:2, :] += jnp.sum(row, axis=0, keepdims=True)

    rows_loop(BLOCK, 16, back)
    out_scatter.finish(out_sum)
    qkv_scatter.finish(qkv_sum)


def qkv_back(joined_grad, weight, hidden, middle_grad, gains, tokens, out_part, cid):
    return pl.pallas_call(
        kernel_qkv_back,
        out_shape=(
            jax.ShapeDtypeStruct((BLOCK, D), F32),
            jax.ShapeDtypeStruct((8, D), F32),
            jax.ShapeDtypeStruct((8, 3 * HD), F32),
            jax.ShapeDtypeStruct((BLOCK, 3 * HD), BF),
            jax.ShapeDtypeStruct((16, D), BF),
        ),
        in_specs=[VM] * 7,
        out_specs=(VM,) * 5,
        scratch_shapes=[pltpu.VMEM((4, 4, BLOCK, 3 * HD), BF)]
        + plane_scratch(16, D)
        + plane_scratch(BLOCK, 3 * HD)
        + RS_SCRATCH,
        compiler_params=params(cid),
        name="qkv_back",
    )(joined_grad, weight, hidden, middle_grad, gains, tokens, out_part.reshape(4, 4, 16, D))


TP_STEPS = [(dy, dc) for dy in range(4) for dc in range(2) if (dy, dc) != (0, 0)]
XZ_STEPS = [(dx, dz) for dx in range(4) for dz in range(4) if (dx, dz) != (0, 0)]


def tp_peer(step):
    y = lax.rem(lax.axis_index("y") + step[0], 4)
    c = lax.rem(lax.axis_index("core") + step[1], 2)
    return {"y": y, "core": c}, y * 2 + c


def xz_peer(step):
    x = lax.rem(lax.axis_index("x") + step[0], 4)
    z = lax.rem(lax.axis_index("zh") * 2 + lax.axis_index("zl") + step[1], 4)
    return {"x": x, "zh": z // 2, "zl": lax.rem(z, 2)}, x * 4 + z


def meet_all(split):
    peers = [tp_peer(s)[0] for s in TP_STEPS] + [xz_peer(s)[0] for s in XZ_STEPS]
    barrier = pltpu.get_barrier_semaphore()
    for peer in peers:
        pl.semaphore_signal(
            barrier, inc=1, device_id=peer, device_id_type=pl.DeviceIdType.MESH
        )

    @pl.when(split)
    def _():
        pl.semaphore_signal(
            barrier, inc=1, device_id=swap_peer(), device_id_type=pl.DeviceIdType.MESH
        )

    pl.semaphore_wait(barrier, len(peers) + split.astype(jnp.int32))


def swap_peer():
    return {"zh": lax.axis_index("core"), "core": lax.axis_index("zh")}


def swap_start(split, src, dst, local_sem, sems, i):
    @pl.when(split)
    def _():
        remote(sems, i, src, dst, swap_peer()).start()

    @pl.when(jnp.logical_not(split))
    def _():
        pltpu.make_async_copy(src, dst, local_sem).start()


def swap_wait(split, src, dst, local_sem, sems, i):
    @pl.when(split)
    def _():
        remote(sems, i, src, dst, swap_peer()).wait()

    @pl.when(jnp.logical_not(split))
    def _():
        pltpu.make_async_copy(src, dst, local_sem).wait()


N_TP = len(TP_STEPS)
N_XZ = len(XZ_STEPS)


def kernel_spread(small, qkv, mlp, out, small_all, qkv_all, mlp_all, out_all, local, *sems):
    me = lax.axis_index("y") * 2 + lax.axis_index("core")
    xz = lax.axis_index("x") * 4 + lax.axis_index("zh") * 2 + lax.axis_index("zl")
    split = lax.axis_index("zh") != lax.axis_index("core")
    meet_all(split)
    cp = functools.partial(remote, sems)
    tiny, big = [], []
    for k, step in enumerate(TP_STEPS):
        peer, there = tp_peer(step)
        tiny.append(cp(k, small, small_all.at[xz, me], peer))
        big.append(cp(N_TP + k, qkv.at[there], qkv_all.at[me], peer))
        big.append(cp(2 * N_TP + k, mlp.at[there], mlp_all.at[:, me], peer))
    keep = [
        pltpu.make_async_copy(small, small_all.at[xz, me], local.at[0]),
        pltpu.make_async_copy(qkv.at[me], qkv_all.at[me], local.at[1]),
        pltpu.make_async_copy(mlp.at[me], mlp_all.at[:, me], local.at[2]),
    ]
    for one in tiny + keep:
        one.start()
    for one in big:
        one.start()
    swap_start(split, out, out_all, local.at[3], sems, 3 * N_TP + N_XZ)
    for one in tiny:
        one.wait()
    keep[0].wait()
    wide = []
    for k, step in enumerate(XZ_STEPS):
        peer, _ = xz_peer(step)
        wide.append(cp(3 * N_TP + k, small_all.at[xz], small_all.at[xz], peer))
    for one in wide:
        one.start()
    for one in wide + big + keep[1:]:
        one.wait()
    swap_wait(split, out, out_all, local.at[3], sems, 3 * N_TP + N_XZ)


def spread(small, qkv, mlp, out, cid):
    n = 3 * N_TP + N_XZ + 1
    return pl.pallas_call(
        kernel_spread,
        out_shape=(
            jax.ShapeDtypeStruct((16, TP, 1, 128), F32),
            jax.ShapeDtypeStruct((TP, 16, FP), BF),
            jax.ShapeDtypeStruct((3, TP, 16, FP), BF),
            jax.ShapeDtypeStruct((16, D), BF),
        ),
        in_specs=[ANY] * 4,
        out_specs=(ANY,) * 4,
        scratch_shapes=[
            pltpu.SemaphoreType.DMA((4,)),
            pltpu.SemaphoreType.DMA((n,)),
            pltpu.SemaphoreType.DMA((n,)),
        ],
        compiler_params=params(cid),
        name="spread",
    )(small, qkv, mlp, out)


def kernel_collect(
    terms, shift, qkv, mlp, out, small_all, qkv_all, mlp_all, out_all, terms_in, shift_in, own, local, *sems
):
    me = lax.axis_index("y") * 2 + lax.axis_index("core")
    xz = lax.axis_index("x") * 4 + lax.axis_index("zh") * 2 + lax.axis_index("zl")
    split = lax.axis_index("zh") != lax.axis_index("core")
    meet_all(split)
    cp = functools.partial(remote, sems)
    wide, big = [], []
    for k, step in enumerate(XZ_STEPS):
        peer, there = xz_peer(step)
        wide.append(cp(k, terms.at[there], terms_in.at[xz], peer))
        wide.append(cp(N_XZ + k, shift, shift_in.at[xz], peer))
    for k, step in enumerate(TP_STEPS):
        peer, there = tp_peer(step)
        big.append(cp(2 * N_XZ + k, qkv.at[there], qkv_all.at[me], peer))
        big.append(cp(2 * N_XZ + N_TP + k, mlp.at[:, there], mlp_all.at[me], peer))
    keep = [
        pltpu.make_async_copy(terms.at[xz], terms_in.at[xz], local.at[0]),
        pltpu.make_async_copy(shift, shift_in.at[xz], local.at[1]),
        pltpu.make_async_copy(qkv.at[me], qkv_all.at[me], local.at[2]),
        pltpu.make_async_copy(mlp.at[:, me], mlp_all.at[me], local.at[3]),
    ]
    for one in wide + keep:
        one.start()
    for one in big:
        one.start()
    last = 2 * N_XZ + 3 * N_TP
    swap_start(split, out, out_all, local.at[4], sems, last)
    for one in wide + keep[:2]:
        one.wait()
    own[0:8, :] = jnp.sum(terms_in[...], axis=0)
    own[8:16, :] = jnp.sum(shift_in[...], axis=0)
    tiny = []
    for k, step in enumerate(TP_STEPS):
        peer, _ = tp_peer(step)
        tiny.append(cp(2 * N_XZ + 2 * N_TP + k, own, small_all.at[me], peer))
    tiny.append(pltpu.make_async_copy(own, small_all.at[me], local.at[0]))
    for one in tiny:
        one.start()
    for one in tiny + big + keep[2:]:
        one.wait()
    swap_wait(split, out, out_all, local.at[4], sems, last)


def collect(terms, shift, qkv, mlp, out, cid):
    n = 2 * N_XZ + 3 * N_TP + 1
    return pl.pallas_call(
        kernel_collect,
        out_shape=(
            jax.ShapeDtypeStruct((TP, 16, 128), F32),
            jax.ShapeDtypeStruct((TP, 16, FP), BF),
            jax.ShapeDtypeStruct((TP, 3, 16, FP), BF),
            jax.ShapeDtypeStruct((16, D), BF),
        ),
        in_specs=[ANY] * 5,
        out_specs=(ANY,) * 4,
        scratch_shapes=[
            pltpu.VMEM((16, 8, 128), F32),
            pltpu.VMEM((16, 8, 128), F32),
            pltpu.VMEM((16, 128), F32),
            pltpu.SemaphoreType.DMA((5,)),
            pltpu.SemaphoreType.DMA((n,)),
            pltpu.SemaphoreType.DMA((n,)),
        ],
        compiler_params=params(cid),
        name="collect",
    )(terms, shift, qkv, mlp, out)


def body(
    hidden_in,
    cotangent,
    seq_lengths,
    slot_block,
    ln1_gain,
    ln1_bias,
    w_qkv,
    qkv_bias,
    w_out,
    ln2_gain,
    ln2_bias,
    w_gate,
    w_up,
    w_down,
):
    bf, f32 = BF, F32
    zh = lax.axis_index("zh")
    y = lax.axis_index("y")
    core = lax.axis_index("core")
    xz = lax.axis_index("x") * 4 + zh * 2 + lax.axis_index("zl")

    def by_part(w):
        return w.reshape(-1, 3, 2, 4, HD).transpose(3, 2, 0, 1, 4).reshape(TP, -1, 3 * HD)

    part_qkv = by_part(w_qkv)
    part_mlp = jnp.stack(
        [
            jnp.pad(w.reshape(16, TP, FC).transpose(1, 0, 2), ((0, 0), (0, 0), (0, FP - FC)))
            for w in (w_gate, w_up, w_down)
        ],
        axis=1,
    )
    lengths = seq_lengths[0]
    small = jnp.concatenate(
        [
            ln1_gain.astype(f32),
            ln1_bias.astype(f32),
            ln2_gain.astype(f32),
            ln2_bias.astype(f32),
            qkv_bias.astype(f32),
            lengths.astype(f32),
            slot_block[0].astype(f32),
            jnp.zeros(6, f32),
        ]
    ).reshape(1, 128)
    small_all, qkv_rows, mlp_rows, out_rows = spread(
        small, part_qkv, part_mlp, permute_features(w_out), 0
    )
    out_rows = out_rows.reshape(16, 8, HD).swapaxes(0, 1).reshape(BLOCK, HD)
    attn_full = lax.all_gather(
        jnp.concatenate([qkv_rows.reshape(BLOCK, FP), out_rows], axis=1), XZ, axis=0, tiled=True
    )
    mlp_full = lax.all_gather(mlp_rows.reshape(3, BLOCK, FP), XZ, axis=0, tiled=False)
    qkv_full = attn_full[:, :FP]
    out_full = (
        attn_full[:, FP:].reshape(4, 2, 2, 8, 16, HD).transpose(0, 2, 1, 4, 3, 5).reshape(HD, D)
    )
    gate_full, up_full = (mlp_full[:, i].reshape(D, FP) for i in range(2))

    small_all = small_all.reshape(BLOCK, 128)
    gains = (
        jnp.concatenate([small_all[:, 16 * i : 16 * i + 16].reshape(1, D) for i in range(4)])
    )
    gains = jnp.pad(gains, ((0, 4), (0, 0)))
    natural = small_all[:, 64:112].reshape(4, 2, 2, 4, 2, 48).transpose(1, 3, 0, 2, 4, 5)
    shift = by_part(natural.reshape(1, 3 * D))
    shift = lax.dynamic_index_in_dim(shift, y * 2 + core, 0, False)

    plan = lax.dynamic_slice_in_dim(small_all, xz * TP + y * 2, 2, 0)[:, 112:122].astype(jnp.int32)
    blocks = plan[:, 2:].reshape(2, 2, 4)
    own_blocks = lax.dynamic_index_in_dim(blocks, zh, axis=1, keepdims=False)
    other_blocks = lax.dynamic_index_in_dim(blocks, 1 - zh, axis=1, keepdims=False)
    start = jnp.concatenate([own_blocks, other_blocks], axis=1) * BLOCK
    first_pad = (plan[:, 0:1] + BLOCK - 1) // BLOCK * BLOCK
    second = (start >= first_pad).astype(jnp.int32)
    limit = jnp.where(second == 1, plan[:, 1:2], plan[:, 0:1])
    table = jnp.stack([start - second * first_pad, second, limit], axis=1)
    place = (zh * 4 + y) * BLOCK
    _, _, slot_valid = block_places(lengths, slot_block[0])
    own_valid = lax.dynamic_slice_in_dim(slot_valid, place, BLOCK, 0)

    hidden = permute_features(hidden_in[0])
    grad_out = permute_features(cotangent[0]) * own_valid[:, None].astype(bf)
    grad_out_all = lax.all_gather(grad_out, TPA, axis=0, tiled=True)

    one_all = norm_gather(hidden, gains, 1)
    queries, kv, lse, attended = attend(table, one_all, qkv_full, shift, 6)
    middle, two_all = out_proj(attended, out_full, hidden, gains, 2)
    two_all = two_all.reshape(TP * BLOCK, D)
    inner, gate_grad, up_grad, out_part = mlp(two_all, grad_out_all, mlp_full)
    mlp_part = mlp_weights(two_all, grad_out_all, gate_grad, up_grad, inner)
    mlp_part, gate_grad, up_grad, out_part = lax.optimization_barrier(
        (mlp_part, gate_grad, up_grad, out_part)
    )
    mlp_sum = lax.psum_scatter(
        mlp_part.reshape(16 * 3 * BLOCK, FP), XZ, scatter_dimension=0, tiled=True
    )
    hidden_out = lax.psum_scatter(out_part, TPA, scatter_dimension=0, tiled=True)
    hidden_out = (middle + hidden_out.astype(f32)).astype(bf)

    middle_grad, two_sums, branch_all = mlp_back(
        gate_grad.reshape(4, 2, BLOCK, FP),
        up_grad.reshape(4, 2, BLOCK, FP),
        gate_full,
        up_full,
        middle,
        grad_out,
        gains,
        3,
    )
    joined_grad, out_part = attend_back(table, branch_all, out_full, attended, queries, kv, lse, 7)
    input_grad, one_sums, shift_sum, qkv_sum, out_sum = qkv_back(
        joined_grad, qkv_full, hidden, middle_grad, gains, one_all, out_part, 4
    )

    terms = jnp.concatenate([one_sums[:2], two_sums[:2]]).reshape(4, 16, 128).swapaxes(0, 1)
    terms = jnp.pad(terms, ((0, 0), (0, 4), (0, 0)))
    shift_part = jnp.pad(shift_sum[0].reshape(6, 128), ((0, 2), (0, 0)))
    small_sum, qkv_all, mlp_all, out_all = collect(
        terms, shift_part, qkv_sum.reshape(TP, 16, FP), mlp_sum.reshape(3, TP, 16, FP), out_sum, 5
    )

    def restore_parts(g):
        return g.reshape(4, 2, -1, 3, HD).transpose(2, 3, 1, 0, 4).reshape(-1, 3 * D)

    vectors = jnp.sum(small_sum[:, :4], axis=0)
    vectors = lax.dynamic_slice_in_dim(vectors, (y * 2 + core) * 16, 16, 1)
    shift_grad = restore_parts(small_sum[:, 8:14].reshape(TP, 1, FP)).reshape(128, 48)
    row = (zh * 4 + y) * 16 + lax.axis_index("x") * 4 + lax.axis_index("zl") * 2 + core
    shift_grad = lax.dynamic_index_in_dim(shift_grad, row, 0, False)

    def whole(i):
        return mlp_all[:, i, :, :FC].swapaxes(0, 1).reshape(16, FF).astype(f32)

    return (
        restore_features(hidden_out)[None],
        restore_features(input_grad)[None],
        vectors[0],
        vectors[1],
        restore_parts(qkv_all.astype(f32)),
        shift_grad,
        restore_features(out_all.astype(f32)),
        vectors[2],
        vectors[3],
        whole(0),
        whole(1),
        whole(2),
    )


def solution(mesh):
    inner = Mesh(mesh.devices.reshape(2, 4, 4, 2, 2), ROWS)
    rows = P(ROWS)
    tokens = P(GRP, SLOT, None)
    placed = (
        tokens,
        tokens,
        P(GRP, None),
        P(GRP, None),
        rows,
        rows,
        P(ROWS, None),
        rows,
        P(ROWS, None),
        rows,
        rows,
        P(ROWS, None),
        P(ROWS, None),
        P(ROWS, None),
    )
    return jax.shard_map(
        body,
        mesh=inner,
        in_specs=placed,
        out_specs=(
            tokens,
            tokens,
            rows,
            rows,
            P(ROWS, None),
            rows,
            P(ROWS, None),
            rows,
            rows,
            P(ROWS, None),
            P(ROWS, None),
            P(ROWS, None),
        ),
        check_vma=False,
    )
```

```python
import functools

import jax
import jax.numpy as jnp
from jax import lax
from jax.experimental import pallas as pl
from jax.experimental.pallas import tpu as pltpu
from jax.sharding import Mesh
from jax.sharding import PartitionSpec as P

D = 2048
HEADS = 32
HEAD_DIM = 64
ROT = 16
FF = 5632
BLOCK = 128
TP = 8
HD = D // TP
FC = FF // TP

EPS = 1e-05
NEG = -1e30
SCALE = HEAD_DIM ** (-0.5)
TPA = ("y", "core")
XZ = ("x", "zh", "zl")
ROWS = ("zh", "y", "x", "zl", "core")
GRP = ("x", "zl", "core")
SLOT = ("zh", "y")


def permute_features(v):
    lead = v.shape[:-1]
    n = len(lead)
    v = v.reshape(lead + (2, 4, 4, 2, 32))
    v = v.transpose(tuple(range(n)) + (n + 2, n, n + 3, n + 1, n + 4))
    return v.reshape(lead + (D,))


def restore_features(v):
    lead = v.shape[:-1]
    n = len(lead)
    v = v.reshape(lead + (4, 2, 2, 4, 32))
    v = v.transpose(tuple(range(n)) + (n + 1, n + 3, n, n + 2, n + 4))
    return v.reshape(lead + (D,))


def block_places(lengths, blocks):
    first_pad = (lengths[0] + BLOCK - 1) // BLOCK * BLOCK
    offsets = jnp.arange(BLOCK, dtype=jnp.int32)
    placed = (blocks[:, None] * BLOCK + offsets[None, :]).reshape(-1)
    second = (placed >= first_pad).astype(jnp.int32)
    position = placed - second * first_pad
    limit = jnp.where(second == 1, lengths[1], lengths[0])
    return second, position, position < limit


def layer_norm(values):
    average = jnp.mean(values, axis=-1, keepdims=True)
    centred = values - average
    inv_scale = lax.rsqrt(jnp.mean(centred * centred, axis=-1, keepdims=True) + EPS)
    return centred * inv_scale, inv_scale


def norm_back(grad_in, normed, inv_scale, gain):
    scaled = grad_in * gain
    return inv_scale * (
        scaled
        - jnp.mean(scaled, axis=-1, keepdims=True)
        - normed * jnp.mean(scaled * normed, axis=-1, keepdims=True)
    )


FP = 768
HALF = BLOCK // 2
ANY = pl.BlockSpec(memory_space=pl.ANY)
VM = pl.BlockSpec(memory_space=pltpu.VMEM)
BF = jnp.bfloat16
F32 = jnp.float32


def params(cid):
    return pltpu.CompilerParams(
        collective_id=cid, has_side_effects=True, vmem_limit_bytes=56 * 1024 * 1024
    )


def meet(peers):
    barrier = pltpu.get_barrier_semaphore()
    for peer in peers:
        pl.semaphore_signal(
            barrier, inc=1, device_id=peer, device_id_type=pl.DeviceIdType.MESH
        )
    pl.semaphore_wait(barrier, len(peers))


def remote(sems, i, src, dst, peer):
    return pltpu.make_async_remote_copy(
        src_ref=src,
        dst_ref=dst,
        send_sem=sems[0].at[i],
        recv_sem=sems[1].at[i],
        device_id=peer,
        device_id_type=pl.DeviceIdType.MESH,
    )


def ring():
    y = lax.axis_index("y")
    c = lax.axis_index("core")
    up = lax.rem(y + 1, 4)
    opp = lax.rem(y + 2, 4)
    dn = lax.rem(y + 3, 4)
    return y, c, up, opp, dn


def ring_peers(up, dn, c):
    return {"y": up}, {"y": dn}, {"core": 1 - c}


N_AG = 11
N_RS = 10


class RingGather:
    def __init__(self, own, full, local_sem, sems):
        y, c, up, opp, dn = ring()
        to_up, to_dn, to_sib = ring_peers(up, dn, c)
        first, last = pl.ds(0, HALF), pl.ds(HALF, HALF)
        cp = functools.partial(remote, sems)

        def pass_on(i, block, peer, *rows):
            ref = full.at[(block, c) + rows]
            return cp(i, ref, ref, peer)

        self.up1 = cp(0, own.at[first], full.at[y, c, first], to_up)
        self.dn1 = cp(1, own.at[last], full.at[y, c, last], to_dn)
        self.up2 = cp(2, own.at[last], full.at[y, c, last], to_up)
        self.dn2 = cp(3, own.at[first], full.at[y, c, first], to_dn)
        self.here = pltpu.make_async_copy(own, full.at[y, c], local_sem)
        self.far1 = pass_on(5, dn, to_up, first)
        self.far2 = pass_on(6, up, to_dn, last)
        self.sib = [
            cp(4, own, full.at[y, c], to_sib),
            pass_on(7, dn, to_sib),
            pass_on(8, up, to_sib),
            pass_on(9, opp, to_sib, first),
            pass_on(10, opp, to_sib, last),
        ]

    def start(self):
        for one in (self.up1, self.dn1, self.up2, self.dn2, self.sib[0], self.here):
            one.start()

    def forward(self):
        self.up1.wait_recv()
        self.far1.start()
        self.dn1.wait_recv()
        self.far2.start()

    def share(self):
        self.up2.wait_recv()
        self.sib[1].start()
        self.dn2.wait_recv()
        self.sib[2].start()

    def share_far(self):
        self.far1.wait_recv()
        self.sib[3].start()
        self.far2.wait_recv()
        self.sib[4].start()

    def finish(self):
        for one in self.sib:
            one.wait_recv()
        self.here.wait()
        for one in [self.up1, self.dn1, self.up2, self.dn2, self.far1, self.far2] + self.sib:
            one.wait_send()

    def run(self, work=None):
        for step in (self.start, self.forward, self.share, self.share_far):
            step()
            if work is not None:
                work()
        self.finish()


def rows_loop(count, step, body):
    @pl.loop(0, count // step)
    def _(i):
        body(pl.ds(pl.multiple_of(i * step, step), step))


RS_SCRATCH = [
    pltpu.VMEM((4, BLOCK, D), F32),
    pltpu.VMEM((4, BLOCK, D), BF),
    pltpu.VMEM((4, BLOCK, D), BF),
    pltpu.VMEM((2, HALF, D), BF),
    pltpu.VMEM((2, HALF, D), BF),
    pltpu.VMEM((2, BLOCK, D), BF),
    pltpu.VMEM((2, BLOCK, D), BF),
    pltpu.SemaphoreType.DMA((N_RS,)),
    pltpu.SemaphoreType.DMA((N_RS,)),
]


class RingScatter:
    def __init__(self, mine, sib_out, sib_in, far_out, far_in, near_out, near_in, *sems):
        y, c, up, opp, dn = ring()
        to_up, to_dn, to_sib = ring_peers(up, dn, c)
        first, last = pl.ds(0, HALF), pl.ds(HALF, HALF)
        cp = functools.partial(remote, sems)
        self.order = (opp, up, dn, y)
        self.mine, self.sib_in = mine, sib_in
        self.far_out, self.far_in = far_out, far_in
        self.near_out, self.near_in = near_out, near_in
        self.sib = [cp(j, sib_out(j), sib_in.at[j], to_sib) for j in range(4)]
        self.far = [
            cp(4, far_out.at[0], far_in.at[0], to_up),
            cp(5, far_out.at[1], far_in.at[1], to_dn),
        ]
        self.early = [
            cp(6, near_out.at[0, last], near_in.at[0, last], to_up),
            cp(7, near_out.at[1, first], near_in.at[1, first], to_dn),
        ]
        self.late = [
            cp(8, near_out.at[0, first], near_in.at[0, first], to_up),
            cp(9, near_out.at[1, last], near_in.at[1, last], to_dn),
        ]

    def both(self, j, rows):
        return self.mine(j, rows) + self.sib_in[j, rows, :].astype(F32)

    def send_far(self):
        self.sib[0].wait_recv()
        for k in range(2):

            def add(r, k=k):
                q = pl.ds(k * HALF + r.start, r.size)
                self.far_out[k, r, :] = self.both(0, q).astype(BF)

            rows_loop(HALF, 32, add)
            self.far[k].start()

    def send_early(self, k):
        self.sib[1 + k].wait_recv()

        def add(r):
            q = pl.ds((1 - k) * HALF + r.start, r.size)
            self.near_out[k, q, :] = self.both(1 + k, q).astype(BF)

        rows_loop(HALF, 32, add)
        self.early[k].start()

    def send_late(self):
        for k in range(2):
            self.far[k].wait_recv()

            def add(r, k=k):
                q = pl.ds(k * HALF + r.start, r.size)
                self.near_out[k, q, :] = (
                    self.both(1 + k, q) + self.far_in[k, r, :].astype(F32)
                ).astype(BF)

            rows_loop(HALF, 32, add)
            self.late[k].start()

    def wait(self):
        self.sib[3].wait_recv()
        for one in self.early + self.late:
            one.wait_recv()

    def total(self, rows):
        return (
            self.both(3, rows)
            + self.near_in[0, rows, :].astype(F32)
            + self.near_in[1, rows, :].astype(F32)
        )

    def finish(self):
        for one in self.sib + self.far + self.early + self.late:
            one.wait_send()


def ring_scatter(partial, scratch, between=None):
    part, sib_out = scratch[:2]
    c = lax.axis_index("core")
    scatter = RingScatter(
        lambda j, rows: part[j, rows, :], lambda j: sib_out.at[j], *scratch[2:]
    )

    def produce(j):
        def put(columns, value):
            part[j, :, columns] = jnp.where(c == 0, value[0], value[1])
            sib_out[j, :, columns] = jnp.where(c == 0, value[1], value[0]).astype(BF)

        partial(scatter.order[j], put)
        scatter.sib[j].start()

    produce(0)
    produce(1)
    scatter.send_far()
    scatter.send_early(0)
    produce(2)
    scatter.send_early(1)
    scatter.send_late()
    produce(3)
    if between is not None:
        between()
    scatter.wait()
    return scatter


AG_SCRATCH = [
    pltpu.VMEM((BLOCK, D), BF),
    pltpu.SemaphoreType.DMA,
    pltpu.SemaphoreType.DMA((N_AG,)),
    pltpu.SemaphoreType.DMA((N_AG,)),
]
FULL = jax.ShapeDtypeStruct((4, 2, BLOCK, D), BF)


def order_out(gathered, weight):
    for x in range(4):
        for zl in range(2):
            for a in range(2):
                row = x * 64 + zl * 32 + a * 16
                weight[row : row + 16, :] = gathered[x, a * 2 + zl]


OUT_ROWS = pltpu.VMEM((HD, D), BF)


def kernel_out_proj(attended, gathered, hidden, gains, middle, full, weight, *scratch):
    own, local_sem, *sems = scratch[:4]
    y, c, up, opp, dn = ring()
    meet(ring_peers(up, dn, c))
    order_out(gathered, weight)

    def partial(block, put):
        a = attended[block].reshape(2 * BLOCK, HD)

        @pl.loop(0, 4)
        def _(i):
            q = pl.ds(pl.multiple_of(i * 512, 512), 512)
            put(q, jnp.dot(a, weight[:, q], preferred_element_type=F32).reshape(2, BLOCK, 512))

    scatter = ring_scatter(partial, scratch[4:])

    def norm(r):
        row = hidden[r, :].astype(F32) + scatter.total(r)
        middle[r, :] = row
        normed, _ = layer_norm(row)
        own[r, :] = (normed * gains[2:3, :] + gains[3:4, :]).astype(BF)

    rows_loop(BLOCK, 16, norm)
    RingGather(own, full, local_sem, sems).run()
    scatter.finish()


def out_proj(attended, weight, hidden, gains, cid):
    return pl.pallas_call(
        kernel_out_proj,
        out_shape=(jax.ShapeDtypeStruct((BLOCK, D), F32), FULL),
        in_specs=[VM] * 4,
        out_specs=(VM, ANY),
        scratch_shapes=[OUT_ROWS] + AG_SCRATCH + RS_SCRATCH,
        compiler_params=params(cid),
        name="out_proj",
    )(attended, weight, hidden, gains)


NN = (((1,), (0,)), ((), ()))
NT = (((1,), (1,)), ((), ()))
TN = (((0,), (0,)), ((), ()))
TOKENS = 4 * BLOCK
KEYS = 2 * TOKENS
TILE = 2 * BLOCK


def dot(a, b, dims):
    return lax.dot_general(a, b, dims, preferred_element_type=F32)


def lane(n):
    return lax.broadcasted_iota(jnp.int32, (1, n), 1)


def turn_tables(base):
    entry = lax.rem(lane(BLOCK), HEAD_DIM)
    freq = jnp.exp(
        lax.rem(entry, ROT // 2).astype(F32) * (-2.0 / ROT * 9.210340371976184)
    )
    freq = jnp.where(entry < ROT, freq, 0.0)
    place = (base + lax.broadcasted_iota(jnp.int32, (BLOCK, 1), 0)).astype(F32)
    phase = place * freq
    return jnp.cos(phase), jnp.sin(phase)


def turn(v, cosine, sines, direction):
    entry = lax.rem(lane(BLOCK), HEAD_DIM)
    s = sines * direction
    ahead = pltpu.roll(v, BLOCK - ROT // 2, 1)
    behind = pltpu.roll(v, ROT // 2, 1)
    return v * cosine + jnp.where(entry < ROT // 2, -ahead, behind) * s


def key_bias(table, g, tile):
    token = lane(BLOCK)
    q_code, q_low = [], []
    for j in range(2):
        low = table[g, 1, 2 * tile + j] * 4096
        q_code.append(low + table[g, 0, 2 * tile + j] + token)
        q_low.append(low + jnp.zeros_like(token))
    q_code = jnp.concatenate(q_code, axis=1)
    q_low = jnp.concatenate(q_low, axis=1)
    column = lax.broadcasted_iota(jnp.int32, (BLOCK, 1), 0)
    rows = []
    for k in range(8):
        place = table[g, 0, k] + column
        code = jnp.where(place < table[g, 2, k], table[g, 1, k] * 4096 + place, 1 << 20)
        kept = jnp.logical_and(code <= q_code, code >= q_low)
        rows.append(jnp.where(kept, 0.0, NEG))
    return jnp.concatenate(rows, axis=0)


def head_mask(h):
    first = lane(BLOCK) < HEAD_DIM
    return jnp.where(first if h == 0 else jnp.logical_not(first), 1.0, 0.0).astype(BF)


def kernel_attend(
    table,
    tokens,
    weight,
    shift,
    grad_out,
    out_rows,
    queries,
    kv,
    lse,
    attended,
    grad_all,
    out_full,
    cosines,
    sines,
    send,
    recv,
    *more_sems,
):
    partner = {"zh": 1 - lax.axis_index("zh")}
    y0, c, up, opp, dn = ring()
    meet(list(ring_peers(up, dn, c)) + plane_peers())
    sems = (send, recv)
    gather = RingGather(grad_out, grad_all, more_sems[0], more_sems[1:3])
    gather.start()
    plane = PlaneGather(out_rows, out_full, *more_sems[3:])
    plane.start()

    @pl.loop(0, 4)
    def _(y):
        at = pl.ds(pl.multiple_of(y * BLOCK, BLOCK), BLOCK)
        for g in range(2):
            cosine, sine = turn_tables(table[g, 0, y])
            cosines[g, at, :] = cosine
            sines[g, at, :] = sine
        a = tokens[y].reshape(TILE, D)
        new = dot(a, weight[:, HD:], NN) + shift[:, HD:]
        for g in range(2):
            rows = slice(g * BLOCK, (g + 1) * BLOCK)
            for pair in range(2):
                q = slice(pair * BLOCK, (pair + 1) * BLOCK)
                turned = turn(new[rows, q], cosines[g, at, :], sines[g, at, :], 1.0)
                kv[0, g, at, q] = turned.astype(BF)
            kv[1, g, at, :] = new[rows, HD:].astype(BF)

    own, other = pl.ds(0, TOKENS), pl.ds(TOKENS, TOKENS)
    trade = [
        remote(sems, g, kv.at[:, g, own, :], kv.at[:, g, other, :], partner) for g in range(2)
    ]
    for one in trade:
        one.start()
    gather.forward()
    plane.middle()

    @pl.loop(0, 4)
    def _(y):
        at = pl.ds(pl.multiple_of(y * BLOCK, BLOCK), BLOCK)
        new = dot(tokens[y].reshape(TILE, D), weight[:, :HD], NN) + shift[:, :HD]
        for g in range(2):
            rows = slice(g * BLOCK, (g + 1) * BLOCK)
            for pair in range(2):
                q = slice(pair * BLOCK, (pair + 1) * BLOCK)
                turned = turn(new[rows, q], cosines[g, at, :], sines[g, at, :], 1.0)
                queries[g, at, q] = turned.astype(BF) * jnp.asarray(SCALE, BF)

    gather.share()
    for g in range(2):
        trade[g].wait_recv()
        if g == 1:
            gather.share_far()

        @pl.loop(0, 2)
        def _(tile, g=g):
            at = pl.ds(pl.multiple_of(tile * TILE, TILE), TILE)
            bias = key_bias(table, g, tile)
            for pair in range(2):
                q = slice(pair * BLOCK, (pair + 1) * BLOCK)
                k_all = kv[0, g, :, q]
                v_all = kv[1, g, :, q]
                out = jnp.zeros((TILE, BLOCK), F32)
                for h in range(2):
                    s = dot(k_all, queries[g, at, q] * head_mask(h), NT) + bias
                    top = jnp.max(s, axis=0, keepdims=True)
                    p = jnp.exp(s - top)
                    total = jnp.sum(p, axis=0, keepdims=True)
                    w = (p * (1.0 / total)).astype(BF)
                    lse[g, 2 * pair + h : 2 * pair + h + 1, at] = top + jnp.log(total)
                    out = out + dot(w, v_all * head_mask(h), TN)
                for j in range(2):
                    attended[2 * tile + j, g, :, q] = out[j * BLOCK : (j + 1) * BLOCK].astype(BF)

    for one in trade:
        one.wait_send()
    gather.finish()
    plane.finish()


SM = pl.BlockSpec(memory_space=pltpu.SMEM)


def attend(table, tokens, weight, shift, grad_out, out_rows, cid):
    return pl.pallas_call(
        kernel_attend,
        out_shape=(
            jax.ShapeDtypeStruct((2, TOKENS, HD), BF),
            jax.ShapeDtypeStruct((2, 2, KEYS, HD), BF),
            jax.ShapeDtypeStruct((2, 8, TOKENS), F32),
            jax.ShapeDtypeStruct((4, 2, BLOCK, HD), BF),
            FULL,
            jax.ShapeDtypeStruct((4, 4, 16, D), BF),
        ),
        in_specs=[SM] + [VM] * 5,
        out_specs=(VM, VM, VM, VM, ANY, ANY),
        scratch_shapes=[
            pltpu.VMEM((2, TOKENS, BLOCK), F32),
            pltpu.VMEM((2, TOKENS, BLOCK), F32),
            pltpu.SemaphoreType.DMA((2,)),
            pltpu.SemaphoreType.DMA((2,)),
        ]
        + AG_SCRATCH[1:]
        + PG_SEMS,
        compiler_params=params(cid),
        name="attend",
    )(table, tokens, weight, shift, grad_out, out_rows)


def kernel_attend_back(
    table,
    branch,
    gathered,
    attended,
    queries,
    kv,
    lse,
    mlp_out,
    middle,
    joined_grad,
    out_part,
    hidden_out,
    weight,
    grads,
    dq,
    dkv,
    kv_out,
    kv_in,
    send,
    recv,
    *scratch,
):
    partner = {"zh": 1 - lax.axis_index("zh")}
    y0, c, up, opp, dn = ring()
    meet(list(ring_peers(up, dn, c)) + [partner])
    sems = (send, recv)
    order = (opp, up, dn, y0)
    scatter = RingScatter(
        lambda j, rows: mlp_out[order[j], c, rows, :].astype(F32),
        lambda j: mlp_out.at[order[j], 1 - c],
        *scratch,
    )
    for one in scatter.sib:
        one.start()
    order_out(gathered, weight)

    @pl.loop(0, 4)
    def _(y):
        at = pl.ds(pl.multiple_of(y * BLOCK, BLOCK), BLOCK)
        new = dot(branch[y].reshape(TILE, D), weight[...], NT)
        for g in range(2):
            grads[g, at, :] = new[g * BLOCK : (g + 1) * BLOCK].astype(BF)

    scatter.send_far()
    scatter.send_early(0)
    scatter.send_early(1)
    trade = [remote(sems, g, kv_out.at[g], kv_in.at[g], partner) for g in range(2)]
    own, other = pl.ds(0, TOKENS), pl.ds(TOKENS, TOKENS)
    for g in range(2):

        @pl.loop(0, 2)
        def _(tile, g=g):
            at = pl.ds(pl.multiple_of(tile * TILE, TILE), TILE)
            bias = key_bias(table, g, tile)
            for pair in range(2):
                q = slice(pair * BLOCK, (pair + 1) * BLOCK)
                k_all = kv[0, g, :, q]
                v_all = kv[1, g, :, q]
                new_q = jnp.zeros((TILE, BLOCK), F32)
                new_k = jnp.zeros((KEYS, BLOCK), F32)
                new_v = jnp.zeros((KEYS, BLOCK), F32)
                for h in range(2):
                    q_head = queries[g, at, q] * head_mask(h)
                    g_head = grads[g, at, q] * head_mask(h)
                    s = dot(k_all, q_head, NT) + bias
                    p = jnp.exp(s - lse[g, 2 * pair + h : 2 * pair + h + 1, at])
                    p_grad = dot(v_all, g_head, NT)
                    mean = jnp.sum(p * p_grad, axis=0, keepdims=True)
                    s_grad = (p * (p_grad - mean)).astype(BF)
                    new_v = new_v + dot(p.astype(BF), g_head, NN)
                    new_k = new_k + dot(s_grad, q_head, NN)
                    new_q = new_q + dot(s_grad, k_all * head_mask(h), TN)
                dq[g, at, q] = new_q * SCALE

                @pl.when(tile == 0)
                def _():
                    dkv[0, g, :, q] = new_k
                    dkv[1, g, :, q] = new_v

                @pl.when(tile != 0)
                def _():
                    dkv[0, g, :, q] += new_k
                    dkv[1, g, :, q] += new_v

        for i in range(2):
            kv_out[g, i] = dkv[i, g, other, :].astype(BF)
        trade[g].start()
        if g == 0:
            scatter.send_late()

    @pl.loop(0, 8)
    def _(i):
        q = pl.ds(pl.multiple_of(i * TILE, TILE), TILE)
        new = dot(attended[...].reshape(8 * BLOCK, HD), branch[:, :, :, q].reshape(8 * BLOCK, TILE), TN)
        for x in range(4):
            for zl in range(2):
                for a in range(2):
                    row = x * 64 + zl * 32 + a * 16
                    out_part[x * 4 + a * 2 + zl, :, q] = new[row : row + 16].astype(BF)

    scatter.wait()

    def add(r):
        hidden_out[r, :] = (middle[r, :] + scatter.total(r)).astype(BF)

    rows_loop(BLOCK, 32, add)
    for g in range(2):
        trade[g].wait_recv()

        @pl.loop(0, 4)
        def _(y, g=g):
            at = pl.ds(pl.multiple_of(y * BLOCK, BLOCK), BLOCK)
            cosine, sine = turn_tables(table[g, 0, y])
            for pair in range(2):
                q = slice(pair * BLOCK, (pair + 1) * BLOCK)
                joined_grad[y, g, :, q] = turn(dq[g, at, q], cosine, sine, -1.0).astype(BF)
                new = dkv[0, g, at, q] + kv_in[g, 0, at, q].astype(F32)
                joined_grad[y, g, :, HD + pair * BLOCK : HD + (pair + 1) * BLOCK] = turn(
                    new, cosine, sine, -1.0
                ).astype(BF)
            joined_grad[y, g, :, 2 * HD :] = (
                dkv[1, g, at, :] + kv_in[g, 1, at, :].astype(F32)
            ).astype(BF)

    for one in trade:
        one.wait_send()
    scatter.finish()


def attend_back(table, branch, weight, attended, queries, kv, lse, mlp_out, middle, cid):
    return pl.pallas_call(
        kernel_attend_back,
        out_shape=(
            jax.ShapeDtypeStruct((4, 2, BLOCK, 3 * HD), BF),
            jax.ShapeDtypeStruct((16, 16, D), BF),
            jax.ShapeDtypeStruct((BLOCK, D), BF),
        ),
        in_specs=[SM] + [VM] * 8,
        out_specs=(VM, VM, VM),
        scratch_shapes=[
            OUT_ROWS,
            pltpu.VMEM((2, TOKENS, HD), BF),
            pltpu.VMEM((2, TOKENS, HD), F32),
            pltpu.VMEM((2, 2, KEYS, HD), F32),
            pltpu.VMEM((2, 2, TOKENS, HD), BF),
            pltpu.VMEM((2, 2, TOKENS, HD), BF),
            pltpu.SemaphoreType.DMA((2,)),
            pltpu.SemaphoreType.DMA((2,)),
        ]
        + RS_SCRATCH[2:],
        compiler_params=params(cid),
        name="attend_back",
    )(table, branch, weight, attended, queries, kv, lse, mlp_out, middle)


def kernel_mlp(
    two,
    grad_all,
    w,
    middle,
    grad_out,
    gains,
    middle_grad,
    sums,
    out_part,
    mlp_part,
    full,
    inner,
    gate_grad,
    up_grad,
    *scratch,
):
    own, local_sem, *sems = scratch[:4]
    y, c, up, opp, dn = ring()
    meet(ring_peers(up, dn, c))

    held = jnp.logical_or(lane(FP) >= BLOCK, y < 2)

    def partial(block, put):
        a = two[block].reshape(TILE, D)
        gate = dot(a, w[:, 0].reshape(D, FP), NN)
        up_proj = dot(a, w[:, 1].reshape(D, FP), NN)
        grad = dot(grad_all[block].reshape(TILE, D), w[:, 2].reshape(D, FP), NN)
        sig = 1.0 / (1.0 + jnp.exp(-gate))
        active = gate * sig
        low = (active * up_proj).astype(BF)
        low_gate = (grad * up_proj * sig * (1.0 + gate * (1.0 - sig))).astype(BF)
        low_up = (grad * active).astype(BF)
        for ref, value in ((inner, low), (gate_grad, low_gate), (up_grad, low_up)):
            ref[block] = jnp.where(held, value, jnp.zeros((), BF)).reshape(2, BLOCK, FP)

        @pl.loop(0, 4)
        def _(i):
            q = pl.ds(pl.multiple_of(i * 512, 512), 512)
            wide = pl.ds(i * 4, 4)
            new = dot(gate_grad[block].reshape(TILE, FP), w[wide, 0].reshape(512, FP), NT)
            new = new + dot(up_grad[block].reshape(TILE, FP), w[wide, 1].reshape(512, FP), NT)
            put(q, new.reshape(2, BLOCK, 512))

        @pl.loop(0, 4)
        def _(i):
            q = pl.ds(pl.multiple_of(i * 512, 512), 512)
            wide = pl.ds(i * 4, 4)
            new = dot(inner[block].reshape(TILE, FP), w[wide, 2].reshape(512, FP), NT)
            out_part[block, :, :, q] = new.astype(BF).reshape(2, BLOCK, 512)

    scatter = ring_scatter(partial, scratch[4:])
    sums[...] = jnp.zeros_like(sums)

    def back(r):
        row = scatter.total(r)
        normed, inv = layer_norm(middle[r, :])
        grad = grad_out[r, :].astype(F32) + norm_back(row, normed, inv, gains[2:3, :])
        middle_grad[r, :] = grad
        own[r, :] = grad.astype(BF)
        sums[0:1, :] += jnp.sum(row * normed, axis=0, keepdims=True)
        sums[1:2, :] += jnp.sum(row, axis=0, keepdims=True)

    rows_loop(BLOCK, 16, back)
    done = []

    def weight_grads():
        begin = 2 * len(done)
        done.append(begin)

        @pl.loop(begin, begin + 2)
        def _(i):
            q = pl.ds(pl.multiple_of(i * TILE, TILE), TILE)
            a = two[:, :, :, q].reshape(TP * BLOCK, TILE)
            b = grad_all[:, :, :, q].reshape(TP * BLOCK, TILE)
            for k, (left, right) in enumerate(((a, gate_grad), (a, up_grad), (b, inner))):
                new = dot(left, right[...].reshape(TP * BLOCK, FP), TN).astype(BF)
                mlp_part[pl.ds(2 * i, 2), k] = new.reshape(2, BLOCK, FP)

    RingGather(own, full, local_sem, sems).run(weight_grads)
    scatter.finish()


def mlp(two, grad_all, w, middle, grad_out, gains, cid):
    return pl.pallas_call(
        kernel_mlp,
        out_shape=(
            jax.ShapeDtypeStruct((BLOCK, D), F32),
            jax.ShapeDtypeStruct((8, D), F32),
            FULL,
            jax.ShapeDtypeStruct((16, 3, BLOCK, FP), BF),
            FULL,
        ),
        in_specs=[VM] * 6,
        out_specs=(VM, VM, VM, VM, ANY),
        scratch_shapes=[pltpu.VMEM((4, 2, BLOCK, FP), BF)] * 3 + AG_SCRATCH + RS_SCRATCH,
        compiler_params=params(cid),
        name="mlp",
    )(two, grad_all, w, middle, grad_out, gains)


class PlaneScatter:
    COPIES = 12

    def __init__(self, part, a_in, b_in, a_mid, b_mid, a_last, b_last, send, recv):
        self.refs = part, a_in, b_in, a_mid, b_mid, a_last, b_last
        sems = send, recv
        half = part.shape[-1] // 2
        self.lanes = pl.ds(0, half), pl.ds(half, half)
        self.x = lax.axis_index("x")
        self.z = lax.axis_index("zh") * 2 + lax.axis_index("zl")
        self.one, self.two = [], []
        for d in range(1, 4):
            x = lax.rem(self.x + d, 4)
            z = lax.rem(self.z + d, 4)
            to_x = {"x": x}
            to_z = {"zh": z // 2, "zl": lax.rem(z, 2)}
            a, b = self.lanes
            k = d - 1
            self.one.append(remote(sems, k, part.at[:, z, :, a], a_in.at[k], to_z))
            self.one.append(remote(sems, 3 + k, part.at[x, :, :, b], b_in.at[k], to_x))
            self.two.append(remote(sems, 6 + k, a_mid.at[x], a_last.at[k], to_x))
            self.two.append(remote(sems, 9 + k, b_mid.at[z], b_last.at[k], to_z))

    def start(self):
        for copy in self.one:
            copy.start()

    def middle(self):
        part, a_in, b_in, a_mid, b_mid, _, _ = self.refs
        for copy in self.one:
            copy.wait_recv()
        a, b = self.lanes

        @pl.loop(0, 4)
        def _(i):
            a_mid[i] = (
                part[i, self.z, :, a].astype(F32) + jnp.sum(a_in[:, i].astype(F32), axis=0)
            ).astype(BF)
            b_mid[i] = (
                part[self.x, i, :, b].astype(F32) + jnp.sum(b_in[:, i].astype(F32), axis=0)
            ).astype(BF)

        for copy in self.two:
            copy.start()

    def finish(self, out):
        _, _, _, a_mid, b_mid, a_last, b_last = self.refs
        for copy in self.two:
            copy.wait_recv()
        a, b = self.lanes
        out[:, a] = (
            a_mid[self.x].astype(F32) + jnp.sum(a_last[...].astype(F32), axis=0)
        ).astype(BF)
        out[:, b] = (
            b_mid[self.z].astype(F32) + jnp.sum(b_last[...].astype(F32), axis=0)
        ).astype(BF)
        for copy in self.one + self.two:
            copy.wait_send()


def plane_scratch(rows, lanes):
    half = lanes // 2
    return [
        pltpu.VMEM((3, 4, rows, half), BF),
        pltpu.VMEM((3, 4, rows, half), BF),
        pltpu.VMEM((4, rows, half), BF),
        pltpu.VMEM((4, rows, half), BF),
        pltpu.VMEM((3, rows, half), BF),
        pltpu.VMEM((3, rows, half), BF),
        pltpu.SemaphoreType.DMA((PlaneScatter.COPIES,)),
        pltpu.SemaphoreType.DMA((PlaneScatter.COPIES,)),
    ]


def plane_peers():
    peers = []
    for d in range(1, 4):
        z = lax.rem(lax.axis_index("zh") * 2 + lax.axis_index("zl") + d, 4)
        peers.append({"x": lax.rem(lax.axis_index("x") + d, 4)})
        peers.append({"zh": z // 2, "zl": lax.rem(z, 2)})
    return peers


def kernel_qkv_back(
    joined_grad,
    weight,
    hidden,
    middle_grad,
    gains,
    tokens,
    out_part,
    input_grad,
    sums,
    shift_sum,
    qkv_sum,
    out_sum,
    part,
    *scratch,
):
    y, c, up, opp, dn = ring()
    meet(list(ring_peers(up, dn, c)) + plane_peers())
    out_scatter = PlaneScatter(out_part, *scratch[:8])
    qkv_scatter = PlaneScatter(part, *scratch[8:16])
    out_scatter.start()
    flat = joined_grad[...].reshape(TP * BLOCK, 3 * HD)

    @pl.loop(0, 8)
    def _(i):
        q = pl.ds(pl.multiple_of(i * TILE, TILE), TILE)
        new = dot(tokens[:, :, :, q].reshape(TP * BLOCK, TILE), flat, TN).astype(BF)
        part[i // 2, 2 * lax.rem(i, 2)] = new[:BLOCK]
        part[i // 2, 2 * lax.rem(i, 2) + 1] = new[BLOCK:]

    qkv_scatter.start()

    def partial(block, put):
        a = joined_grad[block].reshape(2 * BLOCK, 3 * HD)

        @pl.loop(0, 4)
        def _(i):
            q = pl.ds(pl.multiple_of(i * 512, 512), 512)
            put(q, dot(a, weight[q, :], NT).reshape(2, BLOCK, 512))

    def between():
        out_scatter.middle()
        shift_sum[...] = jnp.broadcast_to(
            jnp.sum(flat.astype(F32), axis=0, keepdims=True), shift_sum.shape
        )
        qkv_scatter.middle()

    scatter = ring_scatter(partial, scratch[16:], between)
    sums[...] = jnp.zeros_like(sums)

    def back(r):
        row = scatter.total(r)
        normed, inv = layer_norm(hidden[r, :].astype(F32))
        input_grad[r, :] = middle_grad[r, :] + norm_back(row, normed, inv, gains[0:1, :])
        sums[0:1, :] += jnp.sum(row * normed, axis=0, keepdims=True)
        sums[1:2, :] += jnp.sum(row, axis=0, keepdims=True)

    rows_loop(BLOCK, 16, back)
    scatter.finish()
    out_scatter.finish(out_sum)
    qkv_scatter.finish(qkv_sum)


def qkv_back(joined_grad, weight, hidden, middle_grad, gains, tokens, out_part, cid):
    return pl.pallas_call(
        kernel_qkv_back,
        out_shape=(
            jax.ShapeDtypeStruct((BLOCK, D), F32),
            jax.ShapeDtypeStruct((8, D), F32),
            jax.ShapeDtypeStruct((8, 3 * HD), F32),
            jax.ShapeDtypeStruct((BLOCK, 3 * HD), BF),
            jax.ShapeDtypeStruct((16, D), BF),
        ),
        in_specs=[VM] * 7,
        out_specs=(VM,) * 5,
        scratch_shapes=[pltpu.VMEM((4, 4, BLOCK, 3 * HD), BF)]
        + plane_scratch(16, D)
        + plane_scratch(BLOCK, 3 * HD)
        + RS_SCRATCH,
        compiler_params=params(cid),
        name="qkv_back",
    )(joined_grad, weight, hidden, middle_grad, gains, tokens, out_part.reshape(4, 4, 16, D))


TP_STEPS = [(dy, dc) for dy in range(4) for dc in range(2) if (dy, dc) != (0, 0)]
XZ_STEPS = [(dx, dz) for dx in range(4) for dz in range(4) if (dx, dz) != (0, 0)]


def tp_peer(step):
    y = lax.rem(lax.axis_index("y") + step[0], 4)
    c = lax.rem(lax.axis_index("core") + step[1], 2)
    return {"y": y, "core": c}, y * 2 + c


def xz_peer(step):
    x = lax.rem(lax.axis_index("x") + step[0], 4)
    z = lax.rem(lax.axis_index("zh") * 2 + lax.axis_index("zl") + step[1], 4)
    return {"x": x, "zh": z // 2, "zl": lax.rem(z, 2)}, x * 4 + z


def meet_all(split):
    peers = [tp_peer(s)[0] for s in TP_STEPS] + [xz_peer(s)[0] for s in XZ_STEPS]
    barrier = pltpu.get_barrier_semaphore()
    for peer in peers:
        pl.semaphore_signal(
            barrier, inc=1, device_id=peer, device_id_type=pl.DeviceIdType.MESH
        )

    @pl.when(split)
    def _():
        pl.semaphore_signal(
            barrier, inc=1, device_id=swap_peer(), device_id_type=pl.DeviceIdType.MESH
        )

    pl.semaphore_wait(barrier, len(peers) + split.astype(jnp.int32))


def swap_peer():
    return {"zh": lax.axis_index("core"), "core": lax.axis_index("zh")}


def swap_start(split, src, dst, local_sem, sems, i):
    @pl.when(split)
    def _():
        remote(sems, i, src, dst, swap_peer()).start()

    @pl.when(jnp.logical_not(split))
    def _():
        pltpu.make_async_copy(src, dst, local_sem).start()


def swap_wait(split, src, dst, local_sem, sems, i):
    @pl.when(split)
    def _():
        remote(sems, i, src, dst, swap_peer()).wait()

    @pl.when(jnp.logical_not(split))
    def _():
        pltpu.make_async_copy(src, dst, local_sem).wait()


N_TP = len(TP_STEPS)
N_XZ = len(XZ_STEPS)


class PlaneGather:
    COPIES = 12

    def __init__(self, src, full, local_sem, send, recv):
        sems = send, recv
        half = src.shape[-1] // 2
        a, b = pl.ds(0, half), pl.ds(half, half)
        rest = (slice(None),) * (len(src.shape) - 1)
        x = lax.axis_index("x")
        z = lax.axis_index("zh") * 2 + lax.axis_index("zl")
        self.one, self.two = [], []
        every = slice(None)
        for d in range(1, 4):
            k = d - 1
            z_to = lax.rem(z + d, 4)
            to_x = {"x": lax.rem(x + d, 4)}
            to_z = {"zh": z_to // 2, "zl": lax.rem(z_to, 2)}
            self.one.append(remote(sems, k, src.at[rest + (a,)], full.at[(x, z) + rest + (a,)], to_x))
            self.one.append(remote(sems, 3 + k, src.at[rest + (b,)], full.at[(x, z) + rest + (b,)], to_z))
            row = full.at[(every, z) + rest + (a,)]
            self.two.append(remote(sems, 6 + k, row, row, to_z))
            row = full.at[(x, every) + rest + (b,)]
            self.two.append(remote(sems, 9 + k, row, row, to_x))
        self.here = pltpu.make_async_copy(src, full.at[x, z], local_sem)

    def start(self):
        for copy in self.one:
            copy.start()
        self.here.start()

    def middle(self):
        self.here.wait()
        for copy in self.one:
            copy.wait_recv()
        for copy in self.two:
            copy.start()

    def finish(self):
        for copy in self.two:
            copy.wait_recv()
        for copy in self.one + self.two:
            copy.wait_send()


PG_SEMS = [
    pltpu.SemaphoreType.DMA,
    pltpu.SemaphoreType.DMA((PlaneGather.COPIES,)),
    pltpu.SemaphoreType.DMA((PlaneGather.COPIES,)),
]


def first_lane(rank):
    return jnp.where(rank < 4, 6 * rank, 5 * rank + 3) * BLOCK


def head_lane(part, rank):
    return part * D + (lax.rem(rank, 2) * 4 + rank // 2) * HD


def lanes_at(start, n):
    return pl.ds(pl.multiple_of(start, BLOCK), n)


def spread_gains(small_all, gains, shift, rank):
    rows = small_all[...].reshape(BLOCK, BLOCK)
    source = lax.broadcasted_iota(jnp.int32, (BLOCK, 1), 0)
    f = lane(D)
    mine = (f // 16) == source
    for i in range(4):
        pick = (source == 16 * i + lax.rem(f, 16)).astype(F32)
        value = jnp.dot(rows, pick, preferred_element_type=F32)
        gains[i : i + 1, :] = jnp.sum(jnp.where(mine, value, 0.0), axis=0, keepdims=True)
    core = lax.rem(source, 2)
    y = lax.rem(source // 2, 4)
    zl = lax.rem(source // 8, 2)
    zh = lax.rem(source // 16, 2)
    x = source // 32
    owner = (zh * 4 + y) * 16 + x * 4 + zl * 2 + core
    for i in range(3):
        j = head_lane(i, rank) + lane(HD)
        pick = (source == 64 + lax.rem(j, 48)).astype(F32)
        value = jnp.dot(rows, pick, preferred_element_type=F32)
        value = jnp.sum(jnp.where(j // 48 == owner, value, 0.0), axis=0, keepdims=True)
        shift[:, i * HD : (i + 1) * HD] = value


def kernel_front(
    small,
    hidden,
    w_qkv,
    w_gate,
    w_up,
    w_down,
    w_out,
    small_all,
    gains,
    shift,
    qkv_full,
    mlp_rows,
    out_rows,
    full,
    own,
    qkv_rows,
    local,
    send,
    recv,
    *sems,
):
    me = lax.axis_index("y") * 2 + lax.axis_index("core")
    xz = lax.axis_index("x") * 4 + lax.axis_index("zh") * 2 + lax.axis_index("zl")
    split = lax.axis_index("zh") != lax.axis_index("core")
    meet_all(split)
    cp = functools.partial(remote, (send, recv))
    tiny, qkv, mlp = [], [], []
    for k, step in enumerate(TP_STEPS):
        peer, there = tp_peer(step)
        tiny.append(cp(k, small, small_all.at[xz, me], peer))
        for i in range(3):
            src = w_qkv.at[:, lanes_at(head_lane(i, there), HD)]
            dst = qkv_rows.at[me, :, pl.ds(i * HD, HD)]
            qkv.append(cp((1 + i) * N_TP + k, src, dst, peer))
        for i, w in enumerate((w_gate, w_up, w_down)):
            src = w.at[:, lanes_at(first_lane(there), FP)]
            mlp.append(cp((4 + i) * N_TP + k, src, mlp_rows.at[i, me], peer))
    keep = [pltpu.make_async_copy(small, small_all.at[xz, me], local.at[0])]
    for i, w in enumerate((w_gate, w_up, w_down)):
        src = w_qkv.at[:, lanes_at(head_lane(i, me), HD)]
        dst = qkv_rows.at[me, :, pl.ds(i * HD, HD)]
        keep.append(pltpu.make_async_copy(src, dst, local.at[1 + i]))
        src = w.at[:, lanes_at(first_lane(me), FP)]
        keep.append(pltpu.make_async_copy(src, mlp_rows.at[i, me], local.at[4 + i]))
    for one in tiny + qkv + keep:
        one.start()
    last = 7 * N_TP + N_XZ
    for one in tiny:
        one.wait()
    keep[0].wait()
    wide = []
    for k, step in enumerate(XZ_STEPS):
        peer, _ = xz_peer(step)
        wide.append(cp(7 * N_TP + k, small_all.at[xz], small_all.at[xz], peer))
    for one in wide:
        one.start()
    for one in qkv + keep[1:]:
        one.wait()
    plane = PlaneGather(qkv_rows, qkv_full, *sems[:3])
    plane.start()
    for one in mlp:
        one.start()
    swap_start(split, w_out, out_rows, local.at[7], (send, recv), last)
    for one in wide:
        one.wait()
    gains[...] = jnp.zeros_like(gains)
    spread_gains(small_all, gains, shift, me)

    def norm(r):
        normed, _ = layer_norm(hidden[r, :].astype(F32))
        own[r, :] = (normed * gains[0:1, :] + gains[1:2, :]).astype(BF)

    rows_loop(BLOCK, 16, norm)
    gather = RingGather(own, full, sems[3], sems[4:])
    gather.start()
    plane.middle()
    gather.forward()
    gather.share()
    gather.share_far()
    for one in mlp:
        one.wait()
    swap_wait(split, w_out, out_rows, local.at[7], (send, recv), last)
    gather.finish()
    plane.finish()


def front(small, hidden, w_qkv, w_gate, w_up, w_down, w_out, cid):
    n = 7 * N_TP + N_XZ + 1
    return pl.pallas_call(
        kernel_front,
        out_shape=(
            jax.ShapeDtypeStruct((16, TP, 1, BLOCK), F32),
            jax.ShapeDtypeStruct((8, D), F32),
            jax.ShapeDtypeStruct((1, 3 * HD), F32),
            jax.ShapeDtypeStruct((4, 4, TP, 16, 3 * HD), BF),
            jax.ShapeDtypeStruct((3, TP, 16, FP), BF),
            jax.ShapeDtypeStruct((16, D), BF),
            FULL,
        ),
        in_specs=[ANY, VM] + [ANY] * 5,
        out_specs=(VM, VM, VM, ANY, ANY, ANY, ANY),
        scratch_shapes=[
            pltpu.VMEM((BLOCK, D), BF),
            pltpu.VMEM((TP, 16, 3 * HD), BF),
            pltpu.SemaphoreType.DMA((8,)),
            pltpu.SemaphoreType.DMA((n,)),
            pltpu.SemaphoreType.DMA((n,)),
        ]
        + PG_SEMS
        + AG_SCRATCH[1:],
        compiler_params=params(cid),
        name="front",
    )(small, hidden, w_qkv, w_gate, w_up, w_down, w_out)


def kernel_collect(
    one_sums,
    two_sums,
    shift,
    qkv,
    mlp,
    out,
    small,
    qkv_grad,
    gate_grad,
    up_grad,
    down_grad,
    out_grad,
    terms,
    terms_in,
    shift_own,
    shift_in,
    own,
    small_all,
    qkv_all,
    mlp_all,
    out_all,
    local,
    *sems,
):
    me = lax.axis_index("y") * 2 + lax.axis_index("core")
    xz = lax.axis_index("x") * 4 + lax.axis_index("zh") * 2 + lax.axis_index("zl")
    split = lax.axis_index("zh") != lax.axis_index("core")
    meet_all(split)
    cp = functools.partial(remote, sems)
    big, extra = [], []
    near, tile = pl.ds(BLOCK, FP - BLOCK), pl.ds(0, BLOCK)
    base = 2 * N_XZ + N_TP
    for k, step in enumerate(TP_STEPS):
        peer, there = tp_peer(step)
        dst = mlp_all.at[:, :, lanes_at(first_lane(me) + BLOCK, FP - BLOCK)]
        big.append(cp(base + k, mlp.at[:, there, :, near], dst, peer))
        dst = mlp_all.at[:, :, lanes_at(first_lane(me), BLOCK)]
        extra.append(cp(base + N_TP + k, mlp.at[:, there, :, tile], dst, peer))
        for i in range(3):
            dst = qkv_all.at[:, lanes_at(head_lane(i, me), HD)]
            big.append(cp(base + (2 + i) * N_TP + k, qkv.at[there, :, pl.ds(i * HD, HD)], dst, peer))
    keep = []
    dst = mlp_all.at[:, :, lanes_at(first_lane(me) + BLOCK, FP - BLOCK)]
    keep.append(pltpu.make_async_copy(mlp.at[:, me, :, near], dst, local.at[0]))
    for i in range(3):
        dst = qkv_all.at[:, lanes_at(head_lane(i, me), HD)]
        keep.append(pltpu.make_async_copy(qkv.at[me, :, pl.ds(i * HD, HD)], dst, local.at[1 + i]))
    dst = mlp_all.at[:, :, lanes_at(first_lane(me), BLOCK)]
    keep_tile = pltpu.make_async_copy(mlp.at[:, me, :, tile], dst, local.at[4])
    first_four = me < 4

    terms[...] = jnp.zeros_like(terms)
    shift_own[...] = jnp.zeros_like(shift_own)
    for p in range(16):
        q = slice(p * BLOCK, (p + 1) * BLOCK)
        terms[p, 0:2, :] = one_sums[0:2, q]
        terms[p, 2:4, :] = two_sums[0:2, q]
    for i in range(6):
        shift_own[i : i + 1, :] = shift[0:1, i * BLOCK : (i + 1) * BLOCK]
    wide = []
    for k, step in enumerate(XZ_STEPS):
        peer, there = xz_peer(step)
        wide.append(cp(k, terms.at[there], terms_in.at[xz], peer))
        wide.append(cp(N_XZ + k, shift_own, shift_in.at[xz], peer))
    for one in wide + big + keep:
        one.start()

    @pl.when(first_four)
    def _():
        keep_tile.start()
        for one in extra:
            one.start()

    last = base + 5 * N_TP
    swap_start(split, out, out_all, local.at[5], sems, last)
    for one in wide:
        one.wait()
    terms_in[xz] = terms[xz]
    shift_in[xz] = shift_own[...]
    own[0:8, :] = jnp.sum(terms_in[...], axis=0)
    own[8:16, :] = jnp.sum(shift_in[...], axis=0)
    tiny = []
    for k, step in enumerate(TP_STEPS):
        peer, _ = tp_peer(step)
        tiny.append(cp(2 * N_XZ + k, own, small_all.at[me], peer))
    for one in tiny:
        one.start()
    for one in big:
        one.wait()
    for one in keep:
        one.wait()
    for k, step in enumerate(TP_STEPS):
        source = lax.rem(lax.axis_index("y") + 4 - step[0], 4) * 2 + lax.rem(
            lax.axis_index("core") + 2 - step[1], 2
        )

        @pl.when(source < 4)
        def _(k=k):
            extra[k].wait_recv()

    @pl.when(first_four)
    def _():
        keep_tile.wait()
        for one in extra:
            one.wait_send()

    qkv_grad[...] = qkv_all[...].astype(F32)
    gate_grad[...] = mlp_all[0].astype(F32)
    up_grad[...] = mlp_all[1].astype(F32)
    down_grad[...] = mlp_all[2].astype(F32)
    swap_wait(split, out, out_all, local.at[5], sems, last)
    out_grad[...] = out_all[...].astype(F32)
    for one in tiny:
        one.wait()
    small_all[me] = own[...]
    small[...] = small_all[...]


def collect(one_sums, two_sums, shift, qkv, mlp, out, cid):
    n = 2 * N_XZ + 6 * N_TP + 1
    wide = jax.ShapeDtypeStruct((16, FF), F32)
    return pl.pallas_call(
        kernel_collect,
        out_shape=(
            jax.ShapeDtypeStruct((TP, 16, BLOCK), F32),
            jax.ShapeDtypeStruct((16, 3 * D), F32),
            wide,
            wide,
            wide,
            jax.ShapeDtypeStruct((16, D), F32),
        ),
        in_specs=[VM] * 3 + [ANY] * 3,
        out_specs=(VM,) * 6,
        scratch_shapes=[
            pltpu.VMEM((16, 8, BLOCK), F32),
            pltpu.VMEM((16, 8, BLOCK), F32),
            pltpu.VMEM((8, BLOCK), F32),
            pltpu.VMEM((16, 8, BLOCK), F32),
            pltpu.VMEM((16, BLOCK), F32),
            pltpu.VMEM((TP, 16, BLOCK), F32),
            pltpu.VMEM((16, 3 * D), BF),
            pltpu.VMEM((3, 16, FF), BF),
            pltpu.VMEM((16, D), BF),
            pltpu.SemaphoreType.DMA((6,)),
            pltpu.SemaphoreType.DMA((n,)),
            pltpu.SemaphoreType.DMA((n,)),
        ],
        compiler_params=params(cid),
        name="collect",
    )(one_sums, two_sums, shift, qkv, mlp, out)


def body(
    hidden_in,
    cotangent,
    seq_lengths,
    slot_block,
    ln1_gain,
    ln1_bias,
    w_qkv,
    qkv_bias,
    w_out,
    ln2_gain,
    ln2_bias,
    w_gate,
    w_up,
    w_down,
):
    bf, f32 = BF, F32
    zh = lax.axis_index("zh")
    y = lax.axis_index("y")
    core = lax.axis_index("core")
    xz = lax.axis_index("x") * 4 + zh * 2 + lax.axis_index("zl")

    lengths = seq_lengths[0]
    small = jnp.concatenate(
        [
            ln1_gain.astype(f32),
            ln1_bias.astype(f32),
            ln2_gain.astype(f32),
            ln2_bias.astype(f32),
            qkv_bias.astype(f32),
            lengths.astype(f32),
            slot_block[0].astype(f32),
            jnp.zeros(6, f32),
        ]
    ).reshape(1, BLOCK)
    hidden = permute_features(hidden_in[0])
    small_all, gains, shift, qkv_full, mlp_rows, out_rows, one_all = front(
        small, hidden, w_qkv, w_gate, w_up, w_down, w_out, 0
    )
    qkv_full = qkv_full.reshape(D, 3 * HD)
    mlp_full = lax.all_gather(mlp_rows.reshape(3, BLOCK, FP), XZ, axis=0, tiled=False)
    out_rows = permute_features(out_rows)
    small_all = small_all.reshape(BLOCK, BLOCK)

    plan = lax.dynamic_slice_in_dim(small_all, xz * TP + y * 2, 2, 0)[:, 112:122].astype(jnp.int32)
    blocks = plan[:, 2:].reshape(2, 2, 4)
    own_blocks = lax.dynamic_index_in_dim(blocks, zh, axis=1, keepdims=False)
    other_blocks = lax.dynamic_index_in_dim(blocks, 1 - zh, axis=1, keepdims=False)
    start = jnp.concatenate([own_blocks, other_blocks], axis=1) * BLOCK
    first_pad = (plan[:, 0:1] + BLOCK - 1) // BLOCK * BLOCK
    second = (start >= first_pad).astype(jnp.int32)
    limit = jnp.where(second == 1, plan[:, 1:2], plan[:, 0:1])
    table = jnp.stack([start - second * first_pad, second, limit], axis=1)
    place = (zh * 4 + y) * BLOCK
    _, _, slot_valid = block_places(lengths, slot_block[0])
    own_valid = lax.dynamic_slice_in_dim(slot_valid, place, BLOCK, 0)

    grad_out = permute_features(cotangent[0]) * own_valid[:, None].astype(bf)

    queries, kv, lse, attended, grad_all, out_full = attend(
        table, one_all, qkv_full, shift, grad_out, out_rows, 6
    )
    middle, two_all = out_proj(attended, out_full, hidden, gains, 2)
    middle_grad, two_sums, mlp_out, mlp_part, branch_all = mlp(
        two_all, grad_all, mlp_full, middle, grad_out, gains, 3
    )
    mlp_sum = lax.psum_scatter(
        mlp_part.reshape(16 * 3 * BLOCK, FP), XZ, scatter_dimension=0, tiled=True
    )
    joined_grad, out_part, hidden_out = attend_back(
        table, branch_all, out_full, attended, queries, kv, lse, mlp_out, middle, 7
    )
    input_grad, one_sums, shift_sum, qkv_sum, out_sum = qkv_back(
        joined_grad, qkv_full, hidden, middle_grad, gains, one_all, out_part, 4
    )

    small_sum, qkv_grad, gate_sum, up_sum, down_sum, out_grad = collect(
        one_sums,
        two_sums,
        shift_sum,
        qkv_sum.reshape(TP, 16, FP),
        mlp_sum.reshape(3, TP, 16, FP),
        out_sum,
        5,
    )
    vectors = jnp.sum(small_sum[:, :4], axis=0)
    vectors = lax.dynamic_slice_in_dim(vectors, (y * 2 + core) * 16, 16, 1)
    shift_grad = small_sum[:, 8:14].reshape(4, 2, 3, HD).transpose(2, 1, 0, 3).reshape(128, 48)
    row = (zh * 4 + y) * 16 + lax.axis_index("x") * 4 + lax.axis_index("zl") * 2 + core
    shift_grad = lax.dynamic_index_in_dim(shift_grad, row, 0, False)
    return (
        restore_features(hidden_out)[None],
        restore_features(input_grad)[None],
        vectors[0],
        vectors[1],
        qkv_grad,
        shift_grad,
        restore_features(out_grad),
        vectors[2],
        vectors[3],
        gate_sum,
        up_sum,
        down_sum,
    )


def solution(mesh):
    inner = Mesh(mesh.devices.reshape(2, 4, 4, 2, 2), ROWS)
    rows = P(ROWS)
    tokens = P(GRP, SLOT, None)
    placed = (
        tokens,
        tokens,
        P(GRP, None),
        P(GRP, None),
        rows,
        rows,
        P(ROWS, None),
        rows,
        P(ROWS, None),
        rows,
        rows,
        P(ROWS, None),
        P(ROWS, None),
        P(ROWS, None),
    )
    return jax.shard_map(
        body,
        mesh=inner,
        in_specs=placed,
        out_specs=(
            tokens,
            tokens,
            rows,
            rows,
            P(ROWS, None),
            rows,
            P(ROWS, None),
            rows,
            rows,
            P(ROWS, None),
            P(ROWS, None),
            P(ROWS, None),
        ),
        check_vma=False,
    )
```

```python
import functools

import jax
import jax.numpy as jnp
from jax import lax
from jax.experimental import pallas as pl
from jax.experimental.pallas import tpu as pltpu
from jax.sharding import Mesh
from jax.sharding import PartitionSpec as P

D = 2048
HEADS = 32
HEAD_DIM = 64
ROT = 16
FF = 5632
BLOCK = 128
TP = 8
HD = D // TP
FC = FF // TP

EPS = 1e-05
NEG = -1e30
SCALE = HEAD_DIM ** (-0.5)
TPA = ("y", "core")
XZ = ("x", "zh", "zl")
ROWS = ("zh", "y", "x", "zl", "core")
GRP = ("x", "zl", "core")
SLOT = ("zh", "y")


def permute_rows(row):
    group = lane(BLOCK) // 32
    tiles = []
    for x in range(4):
        for zh in range(2):
            for zl in range(2):
                out = None
                for y in range(4):
                    first = zh * 1024 + y * 256 + x * 64 + zl * 32
                    tile = first // BLOCK * BLOCK
                    shift = (32 * y - first % BLOCK) % BLOCK
                    value = row[:, tile : tile + BLOCK]
                    value = pltpu.roll(value, shift, 1) if shift else value
                    out = value if out is None else jnp.where(group == y, value, out)
                tiles.append(out)
    return jnp.concatenate(tiles, axis=1)


def restore_rows(row):
    group = lane(BLOCK) // 32
    tiles = []
    for t in range(D // BLOCK):
        out = None
        for j in range(4):
            first = t * BLOCK + 32 * j
            zh, y, x, zl = first // 1024, first // 256 % 4, first // 64 % 4, first // 32 % 2
            tile = (x * 4 + zh * 2 + zl) * BLOCK
            shift = (32 * j - 32 * y) % BLOCK
            value = row[:, tile : tile + BLOCK]
            value = pltpu.roll(value, shift, 1) if shift else value
            out = value if out is None else jnp.where(group == j, value, out)
        tiles.append(out)
    return jnp.concatenate(tiles, axis=1)


def layer_norm(values):
    average = jnp.mean(values, axis=-1, keepdims=True)
    centred = values - average
    inv_scale = lax.rsqrt(jnp.mean(centred * centred, axis=-1, keepdims=True) + EPS)
    return centred * inv_scale, inv_scale


def norm_back(grad_in, normed, inv_scale, gain):
    scaled = grad_in * gain
    return inv_scale * (
        scaled
        - jnp.mean(scaled, axis=-1, keepdims=True)
        - normed * jnp.mean(scaled * normed, axis=-1, keepdims=True)
    )


FP = 768
HALF = BLOCK // 2
ANY = pl.BlockSpec(memory_space=pl.ANY)
VM = pl.BlockSpec(memory_space=pltpu.VMEM)
BF = jnp.bfloat16
F32 = jnp.float32


def params(cid):
    return pltpu.CompilerParams(
        collective_id=cid, has_side_effects=True, vmem_limit_bytes=56 * 1024 * 1024
    )


def meet(peers):
    barrier = pltpu.get_barrier_semaphore()
    for peer in peers:
        pl.semaphore_signal(
            barrier, inc=1, device_id=peer, device_id_type=pl.DeviceIdType.MESH
        )
    pl.semaphore_wait(barrier, len(peers))


def remote(sems, i, src, dst, peer):
    return pltpu.make_async_remote_copy(
        src_ref=src,
        dst_ref=dst,
        send_sem=sems[0].at[i],
        recv_sem=sems[1].at[i],
        device_id=peer,
        device_id_type=pl.DeviceIdType.MESH,
    )


def ring():
    y = lax.axis_index("y")
    c = lax.axis_index("core")
    up = lax.rem(y + 1, 4)
    opp = lax.rem(y + 2, 4)
    dn = lax.rem(y + 3, 4)
    return y, c, up, opp, dn


def ring_peers(up, dn, c):
    return {"y": up}, {"y": dn}, {"core": 1 - c}


N_AG = 11
N_RS = 10


class RingGather:
    def __init__(self, own, full, local_sem, sems):
        y, c, up, opp, dn = ring()
        to_up, to_dn, to_sib = ring_peers(up, dn, c)
        first, last = pl.ds(0, HALF), pl.ds(HALF, HALF)
        cp = functools.partial(remote, sems)

        def pass_on(i, block, peer, *rows):
            ref = full.at[(block, c) + rows]
            return cp(i, ref, ref, peer)

        self.up1 = cp(0, own.at[first], full.at[y, c, first], to_up)
        self.dn1 = cp(1, own.at[last], full.at[y, c, last], to_dn)
        self.up2 = cp(2, own.at[last], full.at[y, c, last], to_up)
        self.dn2 = cp(3, own.at[first], full.at[y, c, first], to_dn)
        self.here = pltpu.make_async_copy(own, full.at[y, c], local_sem)
        self.far1 = pass_on(5, dn, to_up, first)
        self.far2 = pass_on(6, up, to_dn, last)
        self.sib = [
            cp(4, own, full.at[y, c], to_sib),
            pass_on(7, dn, to_sib),
            pass_on(8, up, to_sib),
            pass_on(9, opp, to_sib, first),
            pass_on(10, opp, to_sib, last),
        ]

    def start(self):
        for one in (self.up1, self.dn1, self.up2, self.dn2, self.sib[0], self.here):
            one.start()

    def forward(self):
        self.up1.wait_recv()
        self.far1.start()
        self.dn1.wait_recv()
        self.far2.start()

    def share(self):
        self.up2.wait_recv()
        self.sib[1].start()
        self.dn2.wait_recv()
        self.sib[2].start()

    def share_far(self):
        self.far1.wait_recv()
        self.sib[3].start()
        self.far2.wait_recv()
        self.sib[4].start()

    def finish(self):
        for one in self.sib:
            one.wait_recv()
        self.here.wait()
        for one in [self.up1, self.dn1, self.up2, self.dn2, self.far1, self.far2] + self.sib:
            one.wait_send()

    def run(self, work=None):
        for step in (self.start, self.forward, self.share, self.share_far):
            step()
            if work is not None:
                work()
        self.finish()


def rows_loop(count, step, body):
    @pl.loop(0, count // step)
    def _(i):
        body(pl.ds(pl.multiple_of(i * step, step), step))


RS_SCRATCH = [
    pltpu.VMEM((4, BLOCK, D), F32),
    pltpu.VMEM((4, BLOCK, D), BF),
    pltpu.VMEM((4, BLOCK, D), BF),
    pltpu.VMEM((2, HALF, D), BF),
    pltpu.VMEM((2, HALF, D), BF),
    pltpu.VMEM((2, BLOCK, D), BF),
    pltpu.VMEM((2, BLOCK, D), BF),
    pltpu.SemaphoreType.DMA((N_RS,)),
    pltpu.SemaphoreType.DMA((N_RS,)),
]


class RingScatter:
    def __init__(self, mine, sib_out, sib_in, far_out, far_in, near_out, near_in, *sems):
        y, c, up, opp, dn = ring()
        to_up, to_dn, to_sib = ring_peers(up, dn, c)
        first, last = pl.ds(0, HALF), pl.ds(HALF, HALF)
        cp = functools.partial(remote, sems)
        self.order = (opp, up, dn, y)
        self.mine, self.sib_in = mine, sib_in
        self.far_out, self.far_in = far_out, far_in
        self.near_out, self.near_in = near_out, near_in
        self.sib = [cp(j, sib_out(j), sib_in.at[j], to_sib) for j in range(4)]
        self.far = [
            cp(4, far_out.at[0], far_in.at[0], to_up),
            cp(5, far_out.at[1], far_in.at[1], to_dn),
        ]
        self.early = [
            cp(6, near_out.at[0, last], near_in.at[0, last], to_up),
            cp(7, near_out.at[1, first], near_in.at[1, first], to_dn),
        ]
        self.late = [
            cp(8, near_out.at[0, first], near_in.at[0, first], to_up),
            cp(9, near_out.at[1, last], near_in.at[1, last], to_dn),
        ]

    def both(self, j, rows):
        return self.mine(j, rows) + self.sib_in[j, rows, :].astype(F32)

    def send_far(self):
        self.sib[0].wait_recv()
        for k in range(2):

            def add(r, k=k):
                q = pl.ds(k * HALF + r.start, r.size)
                self.far_out[k, r, :] = self.both(0, q).astype(BF)

            rows_loop(HALF, 32, add)
            self.far[k].start()

    def send_early(self, k):
        self.sib[1 + k].wait_recv()

        def add(r):
            q = pl.ds((1 - k) * HALF + r.start, r.size)
            self.near_out[k, q, :] = self.both(1 + k, q).astype(BF)

        rows_loop(HALF, 32, add)
        self.early[k].start()

    def send_late(self):
        for k in range(2):
            self.far[k].wait_recv()

            def add(r, k=k):
                q = pl.ds(k * HALF + r.start, r.size)
                self.near_out[k, q, :] = (
                    self.both(1 + k, q) + self.far_in[k, r, :].astype(F32)
                ).astype(BF)

            rows_loop(HALF, 32, add)
            self.late[k].start()

    def wait(self):
        self.sib[3].wait_recv()
        for one in self.early + self.late:
            one.wait_recv()

    def total(self, rows):
        return (
            self.both(3, rows)
            + self.near_in[0, rows, :].astype(F32)
            + self.near_in[1, rows, :].astype(F32)
        )

    def finish(self):
        for one in self.sib + self.far + self.early + self.late:
            one.wait_send()


def ring_scatter(partial, scratch, between=None):
    part, sib_out = scratch[:2]
    c = lax.axis_index("core")
    scatter = RingScatter(
        lambda j, rows: part[j, rows, :], lambda j: sib_out.at[j], *scratch[2:]
    )

    def produce(j):
        def put(columns, value):
            part[j, :, columns] = jnp.where(c == 0, value[0], value[1])
            sib_out[j, :, columns] = jnp.where(c == 0, value[1], value[0]).astype(BF)

        partial(scatter.order[j], put)
        scatter.sib[j].start()

    produce(0)
    produce(1)
    scatter.send_far()
    scatter.send_early(0)
    produce(2)
    scatter.send_early(1)
    scatter.send_late()
    produce(3)
    if between is not None:
        between()
    scatter.wait()
    return scatter


AG_SCRATCH = [
    pltpu.VMEM((BLOCK, D), BF),
    pltpu.SemaphoreType.DMA,
    pltpu.SemaphoreType.DMA((N_AG,)),
    pltpu.SemaphoreType.DMA((N_AG,)),
]
FULL = jax.ShapeDtypeStruct((4, 2, BLOCK, D), BF)


def order_out(gathered, weight):
    for x in range(4):
        for zl in range(2):
            for a in range(2):
                row = x * 64 + zl * 32 + a * 16
                weight[row : row + 16, :] = gathered[x, a * 2 + zl]


OUT_ROWS = pltpu.VMEM((HD, D), BF)


def kernel_out_proj(attended, gathered, hidden, gains, middle, full, weight, *scratch):
    own, local_sem, *sems = scratch[:4]
    y, c, up, opp, dn = ring()
    meet(ring_peers(up, dn, c))
    order_out(gathered, weight)

    def partial(block, put):
        a = attended[block].reshape(2 * BLOCK, HD)
        for i in range(4):
            q = slice(i * 512, (i + 1) * 512)
            put(q, dot(a, weight[:, q], NN).reshape(2, BLOCK, 512))

    scatter = ring_scatter(partial, scratch[4:])

    def norm(r):
        row = hidden[r, :].astype(F32) + scatter.total(r)
        middle[r, :] = row
        normed, _ = layer_norm(row)
        own[r, :] = (normed * gains[2:3, :] + gains[3:4, :]).astype(BF)

    rows_loop(BLOCK, 16, norm)
    RingGather(own, full, local_sem, sems).run()
    scatter.finish()


def out_proj(attended, weight, hidden, gains, cid):
    return pl.pallas_call(
        kernel_out_proj,
        out_shape=(jax.ShapeDtypeStruct((BLOCK, D), F32), FULL),
        in_specs=[VM] * 4,
        out_specs=(VM, ANY),
        scratch_shapes=[OUT_ROWS] + AG_SCRATCH + RS_SCRATCH,
        compiler_params=params(cid),
        name="out_proj",
    )(attended, weight, hidden, gains)


NN = (((1,), (0,)), ((), ()))
NT = (((1,), (1,)), ((), ()))
TN = (((0,), (0,)), ((), ()))
TOKENS = 4 * BLOCK
KEYS = 2 * TOKENS
TILE = 2 * BLOCK


def dot(a, b, dims):
    return lax.dot_general(a, b, dims, preferred_element_type=F32)


def lane(n):
    return lax.broadcasted_iota(jnp.int32, (1, n), 1)


def turn_tables(base):
    entry = lax.rem(lane(BLOCK), HEAD_DIM)
    freq = jnp.exp(
        lax.rem(entry, ROT // 2).astype(F32) * (-2.0 / ROT * 9.210340371976184)
    )
    freq = jnp.where(entry < ROT, freq, 0.0)
    place = (base + lax.broadcasted_iota(jnp.int32, (BLOCK, 1), 0)).astype(F32)
    phase = place * freq
    return jnp.cos(phase), jnp.sin(phase)


def turn(v, cosine, sines, direction):
    entry = lax.rem(lane(BLOCK), HEAD_DIM)
    s = sines * direction
    ahead = pltpu.roll(v, BLOCK - ROT // 2, 1)
    behind = pltpu.roll(v, ROT // 2, 1)
    return v * cosine + jnp.where(entry < ROT // 2, -ahead, behind) * s


def key_bias(table, g, tile, blocks):
    token = lane(BLOCK)
    q_code, q_low = [], []
    for j in range(2):
        low = table[g, 1, 2 * tile + j] * 4096
        q_code.append(low + table[g, 0, 2 * tile + j] + token)
        q_low.append(low + jnp.zeros_like(token))
    q_code = jnp.concatenate(q_code, axis=1)
    q_low = jnp.concatenate(q_low, axis=1)
    column = lax.broadcasted_iota(jnp.int32, (BLOCK, 1), 0)
    rows = []
    for k in blocks:
        place = table[g, 0, k] + column
        code = jnp.where(place < table[g, 2, k], table[g, 1, k] * 4096 + place, 1 << 20)
        kept = jnp.logical_and(code <= q_code, code >= q_low)
        rows.append(jnp.where(kept, 0.0, NEG))
    return jnp.concatenate(rows, axis=0)


def head_mask(h):
    first = lane(BLOCK) < HEAD_DIM
    return jnp.where(first if h == 0 else jnp.logical_not(first), 1.0, 0.0).astype(BF)


def load(pairs, sems, first=0):
    copies = []
    for i, (src, dst) in enumerate(pairs):
        copies.append(pltpu.make_async_copy(src, dst, sems.at[first + i]))
        copies[-1].start()
    return copies


def kernel_attend(
    table,
    tokens_hbm,
    weight_hbm,
    shift,
    cotangent,
    out_in,
    queries,
    kv,
    lse,
    attended,
    grad_out,
    grad_all,
    out_full,
    out_rows,
    tokens,
    weight,
    cosines,
    sines,
    tops,
    totals,
    mixed,
    local,
    send,
    recv,
    *sems,
):
    partner = {"zh": 1 - lax.axis_index("zh")}
    weight_in, *token_in = load(
        [(weight_hbm, weight)] + [(tokens_hbm.at[y], tokens.at[y]) for y in range(4)], local
    )
    y0, c, up, opp, dn = ring()
    base, limit = table[c, 0, y0], table[c, 2, y0]

    def mask(r):
        place = base + r.start + lax.broadcasted_iota(jnp.int32, (16, 1), 0)
        row = jnp.where(place < limit, cotangent[r, :].astype(F32), 0.0)
        grad_out[r, :] = permute_rows(row).astype(BF)

    rows_loop(BLOCK, 16, mask)
    out_rows[...] = permute_rows(out_in[...].astype(F32)).astype(BF)
    meet(list(ring_peers(up, dn, c)) + plane_peers())
    gather = RingGather(grad_out, grad_all, sems[0], sems[1:3])
    gather.start()
    plane = PlaneGather(out_rows, out_full, *sems[3:])
    plane.start()

    for y in range(4):
        for g in range(2):
            at = slice(y * BLOCK, (y + 1) * BLOCK)
            cosine, sine = turn_tables(table[g, 0, y])
            cosines[g, at, :] = cosine
            sines[g, at, :] = sine
    weight_in.wait()
    for y in range(4):
        token_in[y].wait()
        at = slice(y * BLOCK, (y + 1) * BLOCK)
        new = dot(tokens[y].reshape(TILE, D), weight[:, HD:], NN) + shift[:, HD:]
        for g in range(2):
            rows = slice(g * BLOCK, (g + 1) * BLOCK)
            for pair in range(2):
                q = slice(pair * BLOCK, (pair + 1) * BLOCK)
                turned = turn(new[rows, q], cosines[g, at, :], sines[g, at, :], 1.0)
                kv[0, g, at, q] = turned.astype(BF)
            kv[1, g, at, :] = new[rows, HD:].astype(BF)

    own, other = pl.ds(0, TOKENS), pl.ds(TOKENS, TOKENS)
    trade = [
        remote((send, recv), g, kv.at[:, g, own, :], kv.at[:, g, other, :], partner)
        for g in range(2)
    ]
    for one in trade:
        one.start()
    gather.forward()
    for y in range(4):
        at = slice(y * BLOCK, (y + 1) * BLOCK)
        new = dot(tokens[y].reshape(TILE, D), weight[:, :HD], NN) + shift[:, :HD]
        for g in range(2):
            rows = slice(g * BLOCK, (g + 1) * BLOCK)
            for pair in range(2):
                q = slice(pair * BLOCK, (pair + 1) * BLOCK)
                turned = turn(new[rows, q], cosines[g, at, :], sines[g, at, :], 1.0)
                queries[g, at, q] = turned.astype(BF) * jnp.asarray(SCALE, BF)

    plane.middle()
    first_head = lax.broadcasted_iota(jnp.int32, (BLOCK, 1), 0) < HEAD_DIM

    def work(part, g):
        rows = slice(part * TOKENS, (part + 1) * TOKENS)

        @pl.loop(0, 2)
        def _(tile):
            at = pl.ds(pl.multiple_of(tile * TILE, TILE), TILE)
            bias = key_bias(table, g, tile, range(4 * part, 4 * part + 4))
            for pair in range(2):
                q = slice(pair * BLOCK, (pair + 1) * BLOCK)
                k_all = kv[0, g, rows, q]
                v_all = kv[1, g, rows, q]
                out = jnp.zeros((BLOCK, TILE), F32)
                keep, share = [], []
                for h in range(2):
                    row = slice(2 * pair + h, 2 * pair + h + 1)
                    s = dot(k_all, queries[g, at, q] * head_mask(h), NT) + bias
                    top = jnp.max(s, axis=0, keepdims=True)
                    if part == 1:
                        top = jnp.maximum(top, tops[g, row, at])
                    p = jnp.exp(s - top)
                    total = jnp.sum(p, axis=0, keepdims=True)
                    out = out + dot(v_all * head_mask(h), p.astype(BF), TN)
                    if part == 0:
                        tops[g, row, at] = top
                        totals[g, row, at] = total
                    else:
                        keep.append(jnp.exp(tops[g, row, at] - top))
                        total = total + totals[g, row, at] * keep[h]
                        lse[g, row, at] = top + jnp.log(total)
                        share.append(1.0 / total)
                if part == 0:
                    mixed[g, q, at] = out
                else:
                    out = out + mixed[g, q, at] * jnp.where(first_head, keep[0], keep[1])
                    out = (out * jnp.where(first_head, share[0], share[1])).T.astype(BF)
                    for j in range(2):
                        attended[2 * tile + j, g, :, q] = out[j * BLOCK : (j + 1) * BLOCK]

    for g in range(2):
        work(0, g)
    gather.share()
    for g in range(2):
        trade[g].wait_recv()
        if g == 1:
            gather.share_far()
        work(1, g)
    for one in trade:
        one.wait_send()
    gather.finish()
    plane.finish()


SM = pl.BlockSpec(memory_space=pltpu.SMEM)


def attend(table, tokens, weight, shift, cotangent, out_in, cid):
    return pl.pallas_call(
        kernel_attend,
        out_shape=(
            jax.ShapeDtypeStruct((2, TOKENS, HD), BF),
            jax.ShapeDtypeStruct((2, 2, KEYS, HD), BF),
            jax.ShapeDtypeStruct((2, 8, TOKENS), F32),
            jax.ShapeDtypeStruct((4, 2, BLOCK, HD), BF),
            jax.ShapeDtypeStruct((BLOCK, D), BF),
            FULL,
            jax.ShapeDtypeStruct((4, 4, 16, D), BF),
        ),
        in_specs=[SM, ANY, ANY, VM, VM, VM],
        out_specs=(VM, VM, VM, VM, VM, ANY, ANY),
        scratch_shapes=[
            pltpu.VMEM((16, D), BF),
            pltpu.VMEM((4, 2, BLOCK, D), BF),
            pltpu.VMEM((D, 3 * HD), BF),
            pltpu.VMEM((2, TOKENS, BLOCK), F32),
            pltpu.VMEM((2, TOKENS, BLOCK), F32),
            pltpu.VMEM((2, 8, TOKENS), F32),
            pltpu.VMEM((2, 8, TOKENS), F32),
            pltpu.VMEM((2, HD, TOKENS), F32),
            pltpu.SemaphoreType.DMA((5,)),
            pltpu.SemaphoreType.DMA((2,)),
            pltpu.SemaphoreType.DMA((2,)),
        ]
        + AG_SCRATCH[1:]
        + PG_SEMS,
        compiler_params=params(cid),
        name="attend",
    )(table, tokens, weight, shift, cotangent, out_in)


def kernel_attend_back(
    table,
    branch_own,
    gathered,
    attended,
    queries,
    kv,
    lse,
    mlp_out,
    middle_hbm,
    joined_grad,
    out_part,
    hidden_out,
    branch,
    middle,
    own_out,
    probs,
    local,
    weight,
    grads,
    dq,
    mean,
    dkv,
    kv_out,
    kv_in,
    send,
    recv,
    local_sem,
    gather_send,
    gather_recv,
    *scratch,
):
    partner = {"zh": 1 - lax.axis_index("zh")}
    y0, c, up, opp, dn = ring()
    order = (opp, up, dn, y0)
    out_in = load([(mlp_out.at[order[j], c], own_out.at[j]) for j in range(4)], local)
    (middle_in,) = load([(middle_hbm, middle)], local, 4)
    meet(list(ring_peers(up, dn, c)) + [partner])
    gather = RingGather(branch_own, branch, local_sem, (gather_send, gather_recv))
    gather.start()
    sems = (send, recv)
    scatter = RingScatter(
        lambda j, rows: own_out[j, rows, :].astype(F32),
        lambda j: mlp_out.at[order[j], 1 - c],
        *scratch,
    )
    for one in scatter.sib:
        one.start()
    order_out(gathered, weight)

    def recompute(g):
        @pl.loop(0, 2)
        def _(tile):
            at = pl.ds(pl.multiple_of(tile * TILE, TILE), TILE)
            bias = key_bias(table, g, tile, range(8))
            for pair in range(2):
                q = slice(pair * BLOCK, (pair + 1) * BLOCK)
                for h in range(2):
                    row = slice(2 * pair + h, 2 * pair + h + 1)
                    s = dot(kv[0, g, :, q], queries[g, at, q] * head_mask(h), NT) + bias
                    probs[g, tile, 2 * pair + h] = jnp.exp(s - lse[g, row, at])

    recompute(0)
    gather.forward()
    recompute(1)
    gather.share()
    gather.share_far()
    gather.finish()

    @pl.loop(0, 4)
    def _(y):
        at = pl.ds(pl.multiple_of(y * BLOCK, BLOCK), BLOCK)
        new = dot(branch[y].reshape(TILE, D), weight[...], NT)
        for g in range(2):
            grads[g, at, :] = new[g * BLOCK : (g + 1) * BLOCK].astype(BF)

    for one in out_in:
        one.wait()
    scatter.send_far()
    scatter.send_early(0)
    scatter.send_early(1)
    trade = [remote(sems, g, kv_out.at[g], kv_in.at[g], partner) for g in range(2)]
    dq[...] = jnp.zeros_like(dq)
    dkv[...] = jnp.zeros_like(dkv)
    heads = jnp.concatenate([head_mask(0), head_mask(1)] * 4, axis=0).astype(F32)

    def back(part, g):
        rows = slice(part * TOKENS, (part + 1) * TOKENS)

        @pl.loop(0, 2)
        def _(tile):
            at = pl.ds(pl.multiple_of(tile * TILE, TILE), TILE)
            for pair in range(2):
                q = slice(pair * BLOCK, (pair + 1) * BLOCK)
                both = slice(2 * pair, 2 * pair + 2)
                if part == 1:
                    mixed = attended[pl.ds(2 * tile, 2), g, :, q].reshape(TILE, BLOCK).astype(F32)
                    mixed = mixed * grads[g, at, q].astype(F32)
                    mean[g, both, at] = lax.dot_general(
                        heads, mixed, NT, precision=lax.Precision.HIGHEST
                    )[0:2]
                k_all = kv[0, g, rows, q]
                v_all = kv[1, g, rows, q]
                new_q = jnp.zeros((BLOCK, TILE), F32)
                new_k = jnp.zeros((TOKENS, BLOCK), F32)
                new_v = jnp.zeros((TOKENS, BLOCK), F32)
                for h in range(2):
                    row = slice(2 * pair + h, 2 * pair + h + 1)
                    q_head = queries[g, at, q] * head_mask(h)
                    g_head = grads[g, at, q] * head_mask(h)
                    p = probs[g, tile, 2 * pair + h, rows, :]
                    p_grad = dot(v_all, g_head, NT)
                    s_grad = (p * (p_grad - mean[g, row, at])).astype(BF)
                    new_v = new_v + dot(p.astype(BF), g_head, NN)
                    new_k = new_k + dot(s_grad, q_head, NN)
                    new_q = new_q + dot(k_all * head_mask(h), s_grad, TN)
                dq[g, q, at] += new_q
                dkv[0, g, rows, q] += new_k
                dkv[1, g, rows, q] += new_v

    for g in range(2):
        back(1, g)
        for i in range(2):
            kv_out[g, i] = dkv[i, g, pl.ds(TOKENS, TOKENS), :].astype(BF)
        trade[g].start()
    scatter.send_late()
    for g in range(2):
        back(0, g)

    @pl.loop(0, 8)
    def _(i):
        q = pl.ds(pl.multiple_of(i * TILE, TILE), TILE)
        new = dot(attended[...].reshape(8 * BLOCK, HD), branch[:, :, :, q].reshape(8 * BLOCK, TILE), TN)
        for x in range(4):
            for zl in range(2):
                for a in range(2):
                    row = x * 64 + zl * 32 + a * 16
                    out_part[x * 4 + a * 2 + zl, :, q] = new[row : row + 16].astype(BF)

    scatter.wait()
    middle_in.wait()

    def add(r):
        hidden_out[r, :] = restore_rows(middle[r, :] + scatter.total(r)).astype(BF)

    rows_loop(BLOCK, 16, add)
    for g in range(2):
        trade[g].wait_recv()

        @pl.loop(0, 4)
        def _(y, g=g):
            at = pl.ds(pl.multiple_of(y * BLOCK, BLOCK), BLOCK)
            cosine, sine = turn_tables(table[g, 0, y])
            for pair in range(2):
                q = slice(pair * BLOCK, (pair + 1) * BLOCK)
                new = dq[g, q, at].T * SCALE
                joined_grad[y, g, :, q] = turn(new, cosine, sine, -1.0).astype(BF)
                new = dkv[0, g, at, q] + kv_in[g, 0, at, q].astype(F32)
                joined_grad[y, g, :, HD + pair * BLOCK : HD + (pair + 1) * BLOCK] = turn(
                    new, cosine, sine, -1.0
                ).astype(BF)
            joined_grad[y, g, :, 2 * HD :] = (
                dkv[1, g, at, :] + kv_in[g, 1, at, :].astype(F32)
            ).astype(BF)

    for one in trade:
        one.wait_send()
    scatter.finish()


def attend_back(table, branch, weight, attended, queries, kv, lse, mlp_out, middle, cid):
    return pl.pallas_call(
        kernel_attend_back,
        out_shape=(
            jax.ShapeDtypeStruct((4, 2, BLOCK, 3 * HD), BF),
            jax.ShapeDtypeStruct((16, 16, D), BF),
            jax.ShapeDtypeStruct((BLOCK, D), BF),
        ),
        in_specs=[SM] + [VM] * 6 + [ANY, ANY],
        out_specs=(VM, VM, VM),
        scratch_shapes=[
            pltpu.VMEM((4, 2, BLOCK, D), BF),
            pltpu.VMEM((BLOCK, D), F32),
            pltpu.VMEM((4, BLOCK, D), BF),
            pltpu.VMEM((2, 2, 4, KEYS, TILE), F32),
            pltpu.SemaphoreType.DMA((5,)),
            OUT_ROWS,
            pltpu.VMEM((2, TOKENS, HD), BF),
            pltpu.VMEM((2, HD, TOKENS), F32),
            pltpu.VMEM((2, 8, TOKENS), F32),
            pltpu.VMEM((2, 2, KEYS, HD), F32),
            pltpu.VMEM((2, 2, TOKENS, HD), BF),
            pltpu.VMEM((2, 2, TOKENS, HD), BF),
            pltpu.SemaphoreType.DMA((2,)),
            pltpu.SemaphoreType.DMA((2,)),
        ]
        + AG_SCRATCH[1:]
        + RS_SCRATCH[2:],
        compiler_params=params(cid),
        name="attend_back",
    )(table, branch, weight, attended, queries, kv, lse, mlp_out, middle)


def kernel_mlp(
    two_hbm,
    grad_hbm,
    w_hbm,
    middle,
    grad_out,
    gains,
    middle_grad,
    sums,
    own,
    out_hbm,
    part_hbm,
    two,
    grad_all,
    w,
    out_part,
    mlp_part,
    inner,
    both_grads,
    local,
    leave,
    *scratch,
):
    y, c, up, opp, dn = ring()
    order = (opp, up, dn, y)
    w_in = load([(w_hbm.at[:, k], w.at[k]) for k in range(3)], local)
    block_in = load(
        [(src.at[b], dst.at[b]) for b in order for src, dst in ((two_hbm, two), (grad_hbm, grad_all))],
        local,
        3,
    )
    meet(ring_peers(up, dn, c))
    held = jnp.logical_or(lane(FP) >= BLOCK, y < 2)
    gate_lanes, up_lanes = pl.ds(0, FP), pl.ds(FP, FP)
    waits = [w_in + block_in[0:2], block_in[2:4], block_in[4:6], block_in[6:8]]
    outs = []

    def partial(block, put):
        for one in waits[len(outs)]:
            one.wait()
        a = two[block].reshape(TILE, D)
        gate = dot(a, w[0].reshape(D, FP), NN)
        up_proj = dot(a, w[1].reshape(D, FP), NN)
        grad = dot(grad_all[block].reshape(TILE, D), w[2].reshape(D, FP), NN)
        sig = 1.0 / (1.0 + jnp.exp(-gate))
        active = gate * sig
        low = (active * up_proj).astype(BF)
        low_gate = (grad * up_proj * sig * (1.0 + gate * (1.0 - sig))).astype(BF)
        low_up = (grad * active).astype(BF)
        zero = jnp.zeros((), BF)
        inner[block] = jnp.where(held, low, zero).reshape(2, BLOCK, FP)
        both_grads[block, :, :, gate_lanes] = jnp.where(held, low_gate, zero).reshape(2, BLOCK, FP)
        both_grads[block, :, :, up_lanes] = jnp.where(held, low_up, zero).reshape(2, BLOCK, FP)

        low_gate = both_grads[block, :, :, gate_lanes].reshape(TILE, FP)
        low_up = both_grads[block, :, :, up_lanes].reshape(TILE, FP)
        for i in range(4):
            q, wide = slice(i * 512, (i + 1) * 512), slice(i * 4, (i + 1) * 4)
            new = dot(low_gate, w[0, wide].reshape(512, FP), NT)
            new = new + dot(low_up, w[1, wide].reshape(512, FP), NT)
            put(q, new.reshape(2, BLOCK, 512))
        low = inner[block].reshape(TILE, FP)
        for i in range(4):
            q, wide = slice(i * 512, (i + 1) * 512), slice(i * 4, (i + 1) * 4)
            new = dot(low, w[2, wide].reshape(512, FP), NT)
            out_part[block, :, :, q] = new.astype(BF).reshape(2, BLOCK, 512)

        outs.extend(load([(out_part.at[block], out_hbm.at[block])], leave, len(outs)))

    done = []

    def weight_grads(count=1):
        begin = len(done)

        @pl.loop(begin, begin + count)
        def _(i):
            q = pl.ds(pl.multiple_of(i * TILE, TILE), TILE)
            a = two[:, :, :, q].reshape(TP * BLOCK, TILE)
            b = grad_all[:, :, :, q].reshape(TP * BLOCK, TILE)
            new = dot(a, both_grads[...].reshape(TP * BLOCK, 2 * FP), TN).astype(BF)
            at = pl.ds(2 * i, 2)
            mlp_part[at, 0] = new[:, :FP].reshape(2, BLOCK, FP)
            mlp_part[at, 1] = new[:, FP:].reshape(2, BLOCK, FP)
            new = dot(b, inner[...].reshape(TP * BLOCK, FP), TN).astype(BF)
            mlp_part[at, 2] = new.reshape(2, BLOCK, FP)

        for i in range(begin, begin + count):
            done.extend(
                load([(mlp_part.at[pl.ds(2 * i, 2)], part_hbm.at[pl.ds(2 * i, 2)])], leave, 4 + i)
            )

    scatter = ring_scatter(partial, scratch, lambda: weight_grads(8))
    sums[...] = jnp.zeros_like(sums)

    def back(r):
        row = scatter.total(r)
        normed, inv = layer_norm(middle[r, :])
        grad = grad_out[r, :].astype(F32) + norm_back(row, normed, inv, gains[2:3, :])
        middle_grad[r, :] = grad
        own[r, :] = grad.astype(BF)
        sums[0:1, :] += jnp.sum(row * normed, axis=0, keepdims=True)
        sums[1:2, :] += jnp.sum(row, axis=0, keepdims=True)

    rows_loop(BLOCK, 16, back)
    scatter.finish()
    for one in outs + done:
        one.wait()


def mlp(two, grad_all, w, middle, grad_out, gains, cid):
    block = (4, 2, BLOCK, D)
    return pl.pallas_call(
        kernel_mlp,
        out_shape=(
            jax.ShapeDtypeStruct((BLOCK, D), F32),
            jax.ShapeDtypeStruct((8, D), F32),
            jax.ShapeDtypeStruct((BLOCK, D), BF),
            FULL,
            jax.ShapeDtypeStruct((16, 3, BLOCK, FP), BF),
        ),
        in_specs=[ANY] * 3 + [VM] * 3,
        out_specs=(VM, VM, VM, ANY, ANY),
        scratch_shapes=[
            pltpu.VMEM(block, BF),
            pltpu.VMEM(block, BF),
            pltpu.VMEM((3, 16, BLOCK, FP), BF),
            pltpu.VMEM(block, BF),
            pltpu.VMEM((16, 3, BLOCK, FP), BF),
            pltpu.VMEM((4, 2, BLOCK, FP), BF),
            pltpu.VMEM((4, 2, BLOCK, 2 * FP), BF),
            pltpu.SemaphoreType.DMA((11,)),
            pltpu.SemaphoreType.DMA((12,)),
        ]
        + RS_SCRATCH,
        compiler_params=params(cid),
        name="mlp",
    )(two, grad_all, w, middle, grad_out, gains)


class PlaneScatter:
    COPIES = 12

    def __init__(self, part, a_in, b_in, a_mid, b_mid, a_last, b_last, send, recv):
        self.refs = part, a_in, b_in, a_mid, b_mid, a_last, b_last
        sems = send, recv
        half = part.shape[-1] // 2
        self.lanes = pl.ds(0, half), pl.ds(half, half)
        self.x = lax.axis_index("x")
        self.z = lax.axis_index("zh") * 2 + lax.axis_index("zl")
        self.one, self.two = [], []
        for d in range(1, 4):
            x = lax.rem(self.x + d, 4)
            z = lax.rem(self.z + d, 4)
            to_x = {"x": x}
            to_z = {"zh": z // 2, "zl": lax.rem(z, 2)}
            a, b = self.lanes
            k = d - 1
            self.one.append(remote(sems, k, part.at[:, z, :, a], a_in.at[k], to_z))
            self.one.append(remote(sems, 3 + k, part.at[x, :, :, b], b_in.at[k], to_x))
            self.two.append(remote(sems, 6 + k, a_mid.at[x], a_last.at[k], to_x))
            self.two.append(remote(sems, 9 + k, b_mid.at[z], b_last.at[k], to_z))

    def start(self):
        for copy in self.one:
            copy.start()

    def middle(self):
        part, a_in, b_in, a_mid, b_mid, _, _ = self.refs
        for copy in self.one:
            copy.wait_recv()
        a, b = self.lanes

        @pl.loop(0, 4)
        def _(i):
            a_mid[i] = (
                part[i, self.z, :, a].astype(F32) + jnp.sum(a_in[:, i].astype(F32), axis=0)
            ).astype(BF)
            b_mid[i] = (
                part[self.x, i, :, b].astype(F32) + jnp.sum(b_in[:, i].astype(F32), axis=0)
            ).astype(BF)

        for copy in self.two:
            copy.start()

    def finish(self, out):
        _, _, _, a_mid, b_mid, a_last, b_last = self.refs
        for copy in self.two:
            copy.wait_recv()
        a, b = self.lanes
        out[:, a] = (
            a_mid[self.x].astype(F32) + jnp.sum(a_last[...].astype(F32), axis=0)
        ).astype(BF)
        out[:, b] = (
            b_mid[self.z].astype(F32) + jnp.sum(b_last[...].astype(F32), axis=0)
        ).astype(BF)
        for copy in self.one + self.two:
            copy.wait_send()


def plane_scratch(rows, lanes):
    half = lanes // 2
    return [
        pltpu.VMEM((3, 4, rows, half), BF),
        pltpu.VMEM((3, 4, rows, half), BF),
        pltpu.VMEM((4, rows, half), BF),
        pltpu.VMEM((4, rows, half), BF),
        pltpu.VMEM((3, rows, half), BF),
        pltpu.VMEM((3, rows, half), BF),
        pltpu.SemaphoreType.DMA((PlaneScatter.COPIES,)),
        pltpu.SemaphoreType.DMA((PlaneScatter.COPIES,)),
    ]


def plane_peers():
    peers = []
    for d in range(1, 4):
        z = lax.rem(lax.axis_index("zh") * 2 + lax.axis_index("zl") + d, 4)
        peers.append({"x": lax.rem(lax.axis_index("x") + d, 4)})
        peers.append({"zh": z // 2, "zl": lax.rem(z, 2)})
    return peers


def kernel_qkv_back(
    joined_grad,
    weight_hbm,
    hidden,
    middle_hbm,
    gains,
    tokens_hbm,
    out_part,
    input_grad,
    sums,
    shift_sum,
    qkv_sum,
    out_sum,
    tokens,
    weight,
    middle_grad,
    local,
    part,
    *scratch,
):
    token_in = load([(tokens_hbm.at[y], tokens.at[y]) for y in range(4)], local)
    weight_in, middle_in = load([(weight_hbm, weight), (middle_hbm, middle_grad)], local, 4)
    y, c, up, opp, dn = ring()
    meet(list(ring_peers(up, dn, c)) + plane_peers())
    out_scatter = PlaneScatter(out_part, *scratch[:8])
    qkv_scatter = PlaneScatter(part, *scratch[8:16])
    out_scatter.start()
    flat = joined_grad[...].reshape(TP * BLOCK, 3 * HD)
    for one in token_in:
        one.wait()

    for i in range(4):
        q = slice(i * 512, (i + 1) * 512)
        new = dot(tokens[:, :, :, q].reshape(TP * BLOCK, 512), flat, TN).astype(BF)
        part[i] = new.reshape(4, BLOCK, 3 * HD)

    qkv_scatter.start()
    weight_in.wait()
    middle_in.wait()

    def partial(block, put):
        a = joined_grad[block].reshape(2 * BLOCK, 3 * HD)
        for i in range(4):
            q = slice(i * 512, (i + 1) * 512)
            put(q, dot(a, weight[q, :], NT).reshape(2, BLOCK, 512))

    def between():
        out_scatter.middle()
        shift_sum[...] = jnp.broadcast_to(
            jnp.sum(flat.astype(F32), axis=0, keepdims=True), shift_sum.shape
        )
        qkv_scatter.middle()

    scatter = ring_scatter(partial, scratch[16:], between)
    sums[...] = jnp.zeros_like(sums)

    def back(r):
        row = scatter.total(r)
        normed, inv = layer_norm(hidden[r, :].astype(F32))
        input_grad[r, :] = restore_rows(
            middle_grad[r, :] + norm_back(row, normed, inv, gains[0:1, :])
        )
        sums[0:1, :] += jnp.sum(row * normed, axis=0, keepdims=True)
        sums[1:2, :] += jnp.sum(row, axis=0, keepdims=True)

    rows_loop(BLOCK, 16, back)
    scatter.finish()
    out_scatter.finish(out_sum)
    qkv_scatter.finish(qkv_sum)


def qkv_back(joined_grad, weight, hidden, middle_grad, gains, tokens, out_part, cid):
    return pl.pallas_call(
        kernel_qkv_back,
        out_shape=(
            jax.ShapeDtypeStruct((BLOCK, D), F32),
            jax.ShapeDtypeStruct((8, D), F32),
            jax.ShapeDtypeStruct((8, 3 * HD), F32),
            jax.ShapeDtypeStruct((BLOCK, 3 * HD), BF),
            jax.ShapeDtypeStruct((16, D), BF),
        ),
        in_specs=[VM, ANY, VM, ANY, VM, ANY, VM],
        out_specs=(VM,) * 5,
        scratch_shapes=[
            pltpu.VMEM((4, 2, BLOCK, D), BF),
            pltpu.VMEM((D, 3 * HD), BF),
            pltpu.VMEM((BLOCK, D), F32),
            pltpu.SemaphoreType.DMA((6,)),
            pltpu.VMEM((4, 4, BLOCK, 3 * HD), BF),
        ]
        + plane_scratch(16, D)
        + plane_scratch(BLOCK, 3 * HD)
        + RS_SCRATCH,
        compiler_params=params(cid),
        name="qkv_back",
    )(joined_grad, weight, hidden, middle_grad, gains, tokens, out_part.reshape(4, 4, 16, D))


TP_STEPS = [(dy, dc) for dy in range(4) for dc in range(2) if (dy, dc) != (0, 0)]
XZ_STEPS = [(dx, dz) for dx in range(4) for dz in range(4) if (dx, dz) != (0, 0)]


def tp_peer(step):
    y = lax.rem(lax.axis_index("y") + step[0], 4)
    c = lax.rem(lax.axis_index("core") + step[1], 2)
    return {"y": y, "core": c}, y * 2 + c


def xz_peer(step):
    x = lax.rem(lax.axis_index("x") + step[0], 4)
    z = lax.rem(lax.axis_index("zh") * 2 + lax.axis_index("zl") + step[1], 4)
    return {"x": x, "zh": z // 2, "zl": lax.rem(z, 2)}, x * 4 + z


def meet_all(split):
    peers = [tp_peer(s)[0] for s in TP_STEPS] + [xz_peer(s)[0] for s in XZ_STEPS]
    barrier = pltpu.get_barrier_semaphore()
    for peer in peers:
        pl.semaphore_signal(
            barrier, inc=1, device_id=peer, device_id_type=pl.DeviceIdType.MESH
        )

    @pl.when(split)
    def _():
        pl.semaphore_signal(
            barrier, inc=1, device_id=swap_peer(), device_id_type=pl.DeviceIdType.MESH
        )

    pl.semaphore_wait(barrier, len(peers) + split.astype(jnp.int32))


def swap_peer():
    return {"zh": lax.axis_index("core"), "core": lax.axis_index("zh")}


def swap_start(split, src, dst, local_sem, sems, i):
    @pl.when(split)
    def _():
        remote(sems, i, src, dst, swap_peer()).start()

    @pl.when(jnp.logical_not(split))
    def _():
        pltpu.make_async_copy(src, dst, local_sem).start()


def swap_wait(split, src, dst, local_sem, sems, i):
    @pl.when(split)
    def _():
        remote(sems, i, src, dst, swap_peer()).wait()

    @pl.when(jnp.logical_not(split))
    def _():
        pltpu.make_async_copy(src, dst, local_sem).wait()


N_TP = len(TP_STEPS)
N_XZ = len(XZ_STEPS)


class PlaneGather:
    COPIES = 12

    def __init__(self, src, full, local_sem, send, recv):
        sems = send, recv
        half = src.shape[-1] // 2
        a, b = pl.ds(0, half), pl.ds(half, half)
        rest = (slice(None),) * (len(src.shape) - 1)
        x = lax.axis_index("x")
        z = lax.axis_index("zh") * 2 + lax.axis_index("zl")
        self.one, self.two = [], []
        every = slice(None)
        for d in range(1, 4):
            k = d - 1
            z_to = lax.rem(z + d, 4)
            to_x = {"x": lax.rem(x + d, 4)}
            to_z = {"zh": z_to // 2, "zl": lax.rem(z_to, 2)}
            self.one.append(remote(sems, k, src.at[rest + (a,)], full.at[(x, z) + rest + (a,)], to_x))
            self.one.append(remote(sems, 3 + k, src.at[rest + (b,)], full.at[(x, z) + rest + (b,)], to_z))
            row = full.at[(every, z) + rest + (a,)]
            self.two.append(remote(sems, 6 + k, row, row, to_z))
            row = full.at[(x, every) + rest + (b,)]
            self.two.append(remote(sems, 9 + k, row, row, to_x))
        self.here = pltpu.make_async_copy(src, full.at[x, z], local_sem)

    def start(self):
        for copy in self.one:
            copy.start()
        self.here.start()

    def middle(self):
        self.here.wait()
        for copy in self.one:
            copy.wait_recv()
        for copy in self.two:
            copy.start()

    def finish(self):
        for copy in self.two:
            copy.wait_recv()
        for copy in self.one + self.two:
            copy.wait_send()


PG_SEMS = [
    pltpu.SemaphoreType.DMA,
    pltpu.SemaphoreType.DMA((PlaneGather.COPIES,)),
    pltpu.SemaphoreType.DMA((PlaneGather.COPIES,)),
]


def first_lane(rank):
    return jnp.where(rank < 4, 6 * rank, 5 * rank + 3) * BLOCK


def head_lane(part, rank):
    return part * D + (lax.rem(rank, 2) * 4 + rank // 2) * HD


def lanes_at(start, n):
    return pl.ds(pl.multiple_of(start, BLOCK), n)


def spread_gains(small_all, gains, shift, rank):
    rows = small_all[...].reshape(BLOCK, BLOCK)
    source = lax.broadcasted_iota(jnp.int32, (BLOCK, 1), 0)
    f = lane(D)
    mine = (f // 16) == source
    for i in range(4):
        pick = (source == 16 * i + lax.rem(f, 16)).astype(F32)
        value = jnp.dot(rows, pick, preferred_element_type=F32)
        gains[i : i + 1, :] = jnp.sum(jnp.where(mine, value, 0.0), axis=0, keepdims=True)
    core = lax.rem(source, 2)
    y = lax.rem(source // 2, 4)
    zl = lax.rem(source // 8, 2)
    zh = lax.rem(source // 16, 2)
    x = source // 32
    owner = (zh * 4 + y) * 16 + x * 4 + zl * 2 + core
    for i in range(3):
        j = head_lane(i, rank) + lane(HD)
        pick = (source == 64 + lax.rem(j, 48)).astype(F32)
        value = jnp.dot(rows, pick, preferred_element_type=F32)
        value = jnp.sum(jnp.where(j // 48 == owner, value, 0.0), axis=0, keepdims=True)
        shift[:, i * HD : (i + 1) * HD] = value


def kernel_front(
    small,
    hidden_in,
    w_qkv,
    w_gate,
    w_up,
    w_down,
    w_out,
    small_all,
    gains,
    shift,
    qkv_full,
    mlp_rows,
    out_rows,
    hidden,
    full,
    own,
    qkv_rows,
    local,
    send,
    recv,
    *sems,
):
    me = lax.axis_index("y") * 2 + lax.axis_index("core")
    xz = lax.axis_index("x") * 4 + lax.axis_index("zh") * 2 + lax.axis_index("zl")
    split = lax.axis_index("zh") != lax.axis_index("core")
    meet_all(split)
    cp = functools.partial(remote, (send, recv))
    tiny, qkv, mlp = [], [], []
    for k, step in enumerate(TP_STEPS):
        peer, there = tp_peer(step)
        tiny.append(cp(k, small, small_all.at[xz, me], peer))
        for i in range(3):
            src = w_qkv.at[:, lanes_at(head_lane(i, there), HD)]
            dst = qkv_rows.at[me, :, pl.ds(i * HD, HD)]
            qkv.append(cp((1 + i) * N_TP + k, src, dst, peer))
        for i, w in enumerate((w_gate, w_up, w_down)):
            src = w.at[:, lanes_at(first_lane(there), FP)]
            mlp.append(cp((4 + i) * N_TP + k, src, mlp_rows.at[i, me], peer))
    keep = [pltpu.make_async_copy(small, small_all.at[xz, me], local.at[0])]
    for i, w in enumerate((w_gate, w_up, w_down)):
        src = w_qkv.at[:, lanes_at(head_lane(i, me), HD)]
        dst = qkv_rows.at[me, :, pl.ds(i * HD, HD)]
        keep.append(pltpu.make_async_copy(src, dst, local.at[1 + i]))
        src = w.at[:, lanes_at(first_lane(me), FP)]
        keep.append(pltpu.make_async_copy(src, mlp_rows.at[i, me], local.at[4 + i]))
    for one in tiny + qkv + keep:
        one.start()
    last = 7 * N_TP + N_XZ
    for one in tiny:
        one.wait()
    keep[0].wait()
    wide = []
    for k, step in enumerate(XZ_STEPS):
        peer, _ = xz_peer(step)
        wide.append(cp(7 * N_TP + k, small_all.at[xz], small_all.at[xz], peer))
    for one in wide:
        one.start()
    for one in qkv + keep[1:]:
        one.wait()
    plane = PlaneGather(qkv_rows, qkv_full, *sems[:3])
    plane.start()
    for one in mlp:
        one.start()
    swap_start(split, w_out, out_rows, local.at[7], (send, recv), last)
    for one in wide:
        one.wait()
    gains[...] = jnp.zeros_like(gains)
    spread_gains(small_all, gains, shift, me)

    def norm(r):
        row = permute_rows(hidden_in[r, :].astype(F32))
        hidden[r, :] = row.astype(BF)
        normed, _ = layer_norm(row)
        own[r, :] = (normed * gains[0:1, :] + gains[1:2, :]).astype(BF)

    rows_loop(BLOCK, 16, norm)
    gather = RingGather(own, full, sems[3], sems[4:])
    gather.start()
    plane.middle()
    gather.forward()
    gather.share()
    gather.share_far()
    for one in mlp:
        one.wait()
    swap_wait(split, w_out, out_rows, local.at[7], (send, recv), last)
    gather.finish()
    plane.finish()


def front(small, hidden, w_qkv, w_gate, w_up, w_down, w_out, cid):
    n = 7 * N_TP + N_XZ + 1
    return pl.pallas_call(
        kernel_front,
        out_shape=(
            jax.ShapeDtypeStruct((16, TP, 1, BLOCK), F32),
            jax.ShapeDtypeStruct((8, D), F32),
            jax.ShapeDtypeStruct((1, 3 * HD), F32),
            jax.ShapeDtypeStruct((4, 4, TP, 16, 3 * HD), BF),
            jax.ShapeDtypeStruct((3, TP, 16, FP), BF),
            jax.ShapeDtypeStruct((16, D), BF),
            jax.ShapeDtypeStruct((BLOCK, D), BF),
            FULL,
        ),
        in_specs=[ANY, VM] + [ANY] * 5,
        out_specs=(VM, VM, VM, ANY, ANY, ANY, VM, ANY),
        scratch_shapes=[
            pltpu.VMEM((BLOCK, D), BF),
            pltpu.VMEM((TP, 16, 3 * HD), BF),
            pltpu.SemaphoreType.DMA((8,)),
            pltpu.SemaphoreType.DMA((n,)),
            pltpu.SemaphoreType.DMA((n,)),
        ]
        + PG_SEMS
        + AG_SCRATCH[1:],
        compiler_params=params(cid),
        name="front",
    )(small, hidden, w_qkv, w_gate, w_up, w_down, w_out)


def kernel_collect(
    one_sums,
    two_sums,
    shift,
    qkv,
    mlp,
    out,
    small,
    qkv_grad,
    gate_grad,
    up_grad,
    down_grad,
    out_grad,
    terms,
    terms_in,
    own,
    small_all,
    qkv_all,
    mlp_all,
    out_all,
    local,
    *sems,
):
    me = lax.axis_index("y") * 2 + lax.axis_index("core")
    xz = lax.axis_index("x") * 4 + lax.axis_index("zh") * 2 + lax.axis_index("zl")
    split = lax.axis_index("zh") != lax.axis_index("core")
    for p in range(16):
        q = slice(p * BLOCK, (p + 1) * BLOCK)
        terms[p, 0:2, :] = one_sums[0:2, q]
        terms[p, 2:4, :] = two_sums[0:2, q]
        for i in range(6):
            terms[p, 8 + i : 9 + i, :] = shift[0:1, i * BLOCK : (i + 1) * BLOCK]
        for i in (4, 5, 6, 7, 14, 15):
            terms[p, i : i + 1, :] = jnp.zeros((1, BLOCK), F32)
    meet_all(split)
    cp = functools.partial(remote, sems)
    big, extra, wide = [], [], []
    near, tile = pl.ds(BLOCK, FP - BLOCK), pl.ds(0, BLOCK)
    base = N_XZ + N_TP
    for k, step in enumerate(TP_STEPS):
        peer, there = tp_peer(step)
        dst = mlp_all.at[:, :, lanes_at(first_lane(me) + BLOCK, FP - BLOCK)]
        big.append(cp(base + k, mlp.at[:, there, :, near], dst, peer))
        dst = mlp_all.at[:, :, lanes_at(first_lane(me), BLOCK)]
        extra.append(cp(base + N_TP + k, mlp.at[:, there, :, tile], dst, peer))
        big.append(cp(base + 2 * N_TP + k, qkv.at[there], qkv_all.at[me], peer))
    for k, step in enumerate(XZ_STEPS):
        peer, there = xz_peer(step)
        wide.append(cp(k, terms.at[there], terms_in.at[xz], peer))
    dst = mlp_all.at[:, :, lanes_at(first_lane(me) + BLOCK, FP - BLOCK)]
    keep = [
        pltpu.make_async_copy(mlp.at[:, me, :, near], dst, local.at[0]),
        pltpu.make_async_copy(qkv.at[me], qkv_all.at[me], local.at[1]),
    ]
    dst = mlp_all.at[:, :, lanes_at(first_lane(me), BLOCK)]
    keep_tile = pltpu.make_async_copy(mlp.at[:, me, :, tile], dst, local.at[2])
    first_four = me < 4
    for one in wide + big + keep:
        one.start()

    @pl.when(first_four)
    def _():
        keep_tile.start()
        for one in extra:
            one.start()

    last = base + 3 * N_TP
    swap_start(split, out, out_all, local.at[3], sems, last)
    for one in wide:
        one.wait()
    terms_in[xz] = terms[xz]
    own[...] = jnp.sum(terms_in[...], axis=0)
    tiny = []
    for k, step in enumerate(TP_STEPS):
        peer, _ = tp_peer(step)
        tiny.append(cp(N_XZ + k, own, small_all.at[me], peer))
    for one in tiny:
        one.start()
    for one in big + keep:
        one.wait()
    for k, step in enumerate(TP_STEPS):
        source = lax.rem(lax.axis_index("y") + 4 - step[0], 4) * 2 + lax.rem(
            lax.axis_index("core") + 2 - step[1], 2
        )

        @pl.when(source < 4)
        def _(k=k):
            extra[k].wait_recv()

    @pl.when(first_four)
    def _():
        keep_tile.wait()
        for one in extra:
            one.wait_send()

    for t in range(TP):
        for i in range(3):
            first = i * D + (t % 2 * 4 + t // 2) * HD
            qkv_grad[:, first : first + HD] = qkv_all[t, :, i * HD : (i + 1) * HD].astype(F32)
    gate_grad[...] = mlp_all[0].astype(F32)
    up_grad[...] = mlp_all[1].astype(F32)
    down_grad[...] = mlp_all[2].astype(F32)
    swap_wait(split, out, out_all, local.at[3], sems, last)
    out_grad[...] = restore_rows(out_all[...].astype(F32))
    for one in tiny:
        one.wait()
    small_all[me] = own[...]
    small[...] = small_all[...]


def collect(one_sums, two_sums, shift, qkv, mlp, out, cid):
    n = N_XZ + 4 * N_TP + 1
    wide = jax.ShapeDtypeStruct((16, FF), F32)
    return pl.pallas_call(
        kernel_collect,
        out_shape=(
            jax.ShapeDtypeStruct((TP, 16, BLOCK), F32),
            jax.ShapeDtypeStruct((16, 3 * D), F32),
            wide,
            wide,
            wide,
            jax.ShapeDtypeStruct((16, D), F32),
        ),
        in_specs=[VM] * 3 + [ANY] * 3,
        out_specs=(VM,) * 6,
        scratch_shapes=[
            pltpu.VMEM((16, 16, BLOCK), F32),
            pltpu.VMEM((16, 16, BLOCK), F32),
            pltpu.VMEM((16, BLOCK), F32),
            pltpu.VMEM((TP, 16, BLOCK), F32),
            pltpu.VMEM((TP, 16, 3 * HD), BF),
            pltpu.VMEM((3, 16, FF), BF),
            pltpu.VMEM((16, D), BF),
            pltpu.SemaphoreType.DMA((4,)),
            pltpu.SemaphoreType.DMA((n,)),
            pltpu.SemaphoreType.DMA((n,)),
        ],
        compiler_params=params(cid),
        name="collect",
    )(one_sums, two_sums, shift, qkv, mlp, out)


def body(
    hidden_in,
    cotangent,
    seq_lengths,
    slot_block,
    ln1_gain,
    ln1_bias,
    w_qkv,
    qkv_bias,
    w_out,
    ln2_gain,
    ln2_bias,
    w_gate,
    w_up,
    w_down,
):
    f32 = F32
    zh = lax.axis_index("zh")
    y = lax.axis_index("y")
    core = lax.axis_index("core")
    xz = lax.axis_index("x") * 4 + zh * 2 + lax.axis_index("zl")

    small, first = jnp.zeros(BLOCK, f32), 0
    pieces = (ln1_gain, ln1_bias, ln2_gain, ln2_bias, qkv_bias, seq_lengths[0], slot_block[0])
    for piece in pieces:
        n = piece.shape[0]
        small = small + jnp.pad(piece.astype(f32), (first, BLOCK - first - n))
        first += n
    small_all, gains, shift, qkv_full, mlp_rows, out_rows, hidden, one_all = front(
        small.reshape(1, BLOCK), hidden_in[0], w_qkv, w_gate, w_up, w_down, w_out, 0
    )
    qkv_full = qkv_full.reshape(D, 3 * HD)
    mlp_full = lax.all_gather(mlp_rows.reshape(3, BLOCK, FP), XZ, axis=0, tiled=False)
    small_all = small_all.reshape(BLOCK, BLOCK)

    plan = lax.dynamic_slice_in_dim(small_all, xz * TP + y * 2, 2, 0)[:, 112:122].astype(jnp.int32)
    blocks = plan[:, 2:].reshape(2, 2, 4)
    own_blocks = lax.dynamic_index_in_dim(blocks, zh, axis=1, keepdims=False)
    other_blocks = lax.dynamic_index_in_dim(blocks, 1 - zh, axis=1, keepdims=False)
    start = jnp.concatenate([own_blocks, other_blocks], axis=1) * BLOCK
    first_pad = (plan[:, 0:1] + BLOCK - 1) // BLOCK * BLOCK
    second = (start >= first_pad).astype(jnp.int32)
    limit = jnp.where(second == 1, plan[:, 1:2], plan[:, 0:1])
    table = jnp.stack([start - second * first_pad, second, limit], axis=1)
    queries, kv, lse, attended, grad_out, grad_all, out_full = attend(
        table, one_all, qkv_full, shift, cotangent[0], out_rows, 6
    )
    middle, two_all = out_proj(attended, out_full, hidden, gains, 2)
    middle_grad, two_sums, branch, mlp_out, mlp_part = mlp(
        two_all, grad_all, mlp_full, middle, grad_out, gains, 3
    )
    mlp_sum = lax.psum_scatter(
        mlp_part.reshape(16 * 3 * BLOCK, FP), XZ, scatter_dimension=0, tiled=True
    )
    joined_grad, out_part, hidden_out = attend_back(
        table, branch, out_full, attended, queries, kv, lse, mlp_out, middle, 7
    )
    input_grad, one_sums, shift_sum, qkv_sum, out_sum = qkv_back(
        joined_grad, qkv_full, hidden, middle_grad, gains, one_all, out_part, 4
    )

    small_sum, qkv_grad, gate_sum, up_sum, down_sum, out_grad = collect(
        one_sums,
        two_sums,
        shift_sum,
        qkv_sum.reshape(TP, 16, FP),
        mlp_sum.reshape(3, TP, 16, FP),
        out_sum,
        5,
    )
    vectors = jnp.sum(small_sum[:, :4], axis=0)
    vectors = lax.dynamic_slice_in_dim(vectors, (y * 2 + core) * 16, 16, 1)
    shift_grad = small_sum[:, 8:14].reshape(4, 2, 3, HD).transpose(2, 1, 0, 3).reshape(128, 48)
    row = (zh * 4 + y) * 16 + lax.axis_index("x") * 4 + lax.axis_index("zl") * 2 + core
    shift_grad = lax.dynamic_index_in_dim(shift_grad, row, 0, False)
    return (
        hidden_out[None],
        input_grad[None],
        vectors[0],
        vectors[1],
        qkv_grad,
        shift_grad,
        out_grad,
        vectors[2],
        vectors[3],
        gate_sum,
        up_sum,
        down_sum,
    )


def solution(mesh):
    inner = Mesh(mesh.devices.reshape(2, 4, 4, 2, 2), ROWS)
    rows = P(ROWS)
    tokens = P(GRP, SLOT, None)
    placed = (
        tokens,
        tokens,
        P(GRP, None),
        P(GRP, None),
        rows,
        rows,
        P(ROWS, None),
        rows,
        P(ROWS, None),
        rows,
        rows,
        P(ROWS, None),
        P(ROWS, None),
        P(ROWS, None),
    )
    return jax.shard_map(
        body,
        mesh=inner,
        in_specs=placed,
        out_specs=(
            tokens,
            tokens,
            rows,
            rows,
            P(ROWS, None),
            rows,
            P(ROWS, None),
            rows,
            rows,
            P(ROWS, None),
            P(ROWS, None),
            P(ROWS, None),
        ),
        check_vma=False,
    )
```

```python
import functools

import jax
import jax.numpy as jnp
from jax import lax
from jax.experimental import pallas as pl
from jax.experimental.pallas import tpu as pltpu
from jax.sharding import Mesh
from jax.sharding import PartitionSpec as P

D = 2048
HEADS = 32
HEAD_DIM = 64
ROT = 16
FF = 5632
BLOCK = 128
TP = 8
HD = D // TP
FC = FF // TP

EPS = 1e-05
NEG = -1e30
SCALE = HEAD_DIM ** (-0.5)
TPA = ("y", "core")
XZ = ("x", "zh", "zl")
ROWS = ("zh", "y", "x", "zl", "core")
GRP = ("x", "zl", "core")
SLOT = ("zh", "y")


def permute_rows(row):
    group = lane(BLOCK) // 32
    tiles = []
    for x in range(4):
        for zh in range(2):
            for zl in range(2):
                out = None
                for y in range(4):
                    first = zh * 1024 + y * 256 + x * 64 + zl * 32
                    tile = first // BLOCK * BLOCK
                    shift = (32 * y - first % BLOCK) % BLOCK
                    value = row[:, tile : tile + BLOCK]
                    value = pltpu.roll(value, shift, 1) if shift else value
                    out = value if out is None else jnp.where(group == y, value, out)
                tiles.append(out)
    return jnp.concatenate(tiles, axis=1)


def restore_rows(row):
    group = lane(BLOCK) // 32
    tiles = []
    for t in range(D // BLOCK):
        out = None
        for j in range(4):
            first = t * BLOCK + 32 * j
            zh, y, x, zl = first // 1024, first // 256 % 4, first // 64 % 4, first // 32 % 2
            tile = (x * 4 + zh * 2 + zl) * BLOCK
            shift = (32 * j - 32 * y) % BLOCK
            value = row[:, tile : tile + BLOCK]
            value = pltpu.roll(value, shift, 1) if shift else value
            out = value if out is None else jnp.where(group == j, value, out)
        tiles.append(out)
    return jnp.concatenate(tiles, axis=1)


def layer_norm(values):
    average = jnp.mean(values, axis=-1, keepdims=True)
    centred = values - average
    inv_scale = lax.rsqrt(jnp.mean(centred * centred, axis=-1, keepdims=True) + EPS)
    return centred * inv_scale, inv_scale


def norm_back(grad_in, normed, inv_scale, gain):
    scaled = grad_in * gain
    return inv_scale * (
        scaled
        - jnp.mean(scaled, axis=-1, keepdims=True)
        - normed * jnp.mean(scaled * normed, axis=-1, keepdims=True)
    )


FP = 768
HALF = BLOCK // 2
ANY = pl.BlockSpec(memory_space=pl.ANY)
VM = pl.BlockSpec(memory_space=pltpu.VMEM)
BF = jnp.bfloat16
F32 = jnp.float32


def params(cid):
    return pltpu.CompilerParams(
        collective_id=cid, has_side_effects=True, vmem_limit_bytes=56 * 1024 * 1024
    )


def meet(peers):
    barrier = pltpu.get_barrier_semaphore()
    for peer in peers:
        pl.semaphore_signal(
            barrier, inc=1, device_id=peer, device_id_type=pl.DeviceIdType.MESH
        )
    pl.semaphore_wait(barrier, len(peers))


def remote(sems, i, src, dst, peer):
    return pltpu.make_async_remote_copy(
        src_ref=src,
        dst_ref=dst,
        send_sem=sems[0].at[i],
        recv_sem=sems[1].at[i],
        device_id=peer,
        device_id_type=pl.DeviceIdType.MESH,
    )


def ring():
    y = lax.axis_index("y")
    c = lax.axis_index("core")
    up = lax.rem(y + 1, 4)
    opp = lax.rem(y + 2, 4)
    dn = lax.rem(y + 3, 4)
    return y, c, up, opp, dn


def ring_peers(up, dn, c):
    return {"y": up}, {"y": dn}, {"core": 1 - c}


N_AG = 11
N_RS = 10


class RingGather:
    def __init__(self, own, full, local_sem, sems):
        y, c, up, opp, dn = ring()
        to_up, to_dn, to_sib = ring_peers(up, dn, c)
        first, last = pl.ds(0, HALF), pl.ds(HALF, HALF)
        cp = functools.partial(remote, sems)

        def pass_on(i, block, peer, *rows):
            ref = full.at[(block, c) + rows]
            return cp(i, ref, ref, peer)

        self.up1 = cp(0, own.at[first], full.at[y, c, first], to_up)
        self.dn1 = cp(1, own.at[last], full.at[y, c, last], to_dn)
        self.up2 = cp(2, own.at[last], full.at[y, c, last], to_up)
        self.dn2 = cp(3, own.at[first], full.at[y, c, first], to_dn)
        self.here = pltpu.make_async_copy(own, full.at[y, c], local_sem)
        self.far1 = pass_on(5, dn, to_up, first)
        self.far2 = pass_on(6, up, to_dn, last)
        self.sib = [
            cp(4, own, full.at[y, c], to_sib),
            pass_on(7, dn, to_sib),
            pass_on(8, up, to_sib),
            pass_on(9, opp, to_sib, first),
            pass_on(10, opp, to_sib, last),
        ]

    def start(self):
        for one in (self.up1, self.dn1, self.up2, self.dn2, self.sib[0], self.here):
            one.start()

    def forward(self):
        self.up1.wait_recv()
        self.far1.start()
        self.dn1.wait_recv()
        self.far2.start()

    def share(self):
        self.up2.wait_recv()
        self.sib[1].start()
        self.dn2.wait_recv()
        self.sib[2].start()

    def share_far(self):
        self.far1.wait_recv()
        self.sib[3].start()
        self.far2.wait_recv()
        self.sib[4].start()

    def sends(self):
        return [self.up1, self.dn1, self.up2, self.dn2, self.far1, self.far2] + self.sib

    def finish(self):
        for one in self.sib:
            one.wait_recv()
        self.here.wait()
        for one in self.sends():
            one.wait_send()

    def run(self, work=None):
        for step in (self.start, self.forward, self.share, self.share_far):
            step()
            if work is not None:
                work()
        self.finish()


def rows_loop(count, step, body):
    @pl.loop(0, count // step)
    def _(i):
        body(pl.ds(pl.multiple_of(i * step, step), step))


RS_SCRATCH = [
    pltpu.VMEM((4, BLOCK, D), F32),
    pltpu.VMEM((4, BLOCK, D), BF),
    pltpu.VMEM((4, BLOCK, D), BF),
    pltpu.VMEM((2, HALF, D), BF),
    pltpu.VMEM((2, HALF, D), BF),
    pltpu.VMEM((2, BLOCK, D), BF),
    pltpu.VMEM((2, BLOCK, D), BF),
    pltpu.SemaphoreType.DMA((N_RS,)),
    pltpu.SemaphoreType.DMA((N_RS,)),
]


class RingScatter:
    def __init__(self, mine, sib_out, sib_in, far_out, far_in, near_out, near_in, *sems):
        y, c, up, opp, dn = ring()
        to_up, to_dn, to_sib = ring_peers(up, dn, c)
        first, last = pl.ds(0, HALF), pl.ds(HALF, HALF)
        cp = functools.partial(remote, sems)
        self.order = (opp, up, dn, y)
        self.mine, self.sib_in = mine, sib_in
        self.far_out, self.far_in = far_out, far_in
        self.near_out, self.near_in = near_out, near_in
        self.sib = [cp(j, sib_out(j), sib_in.at[j], to_sib) for j in range(4)]
        self.far = [
            cp(4, far_out.at[0], far_in.at[0], to_up),
            cp(5, far_out.at[1], far_in.at[1], to_dn),
        ]
        self.early = [
            cp(6, near_out.at[0, last], near_in.at[0, last], to_up),
            cp(7, near_out.at[1, first], near_in.at[1, first], to_dn),
        ]
        self.late = [
            cp(8, near_out.at[0, first], near_in.at[0, first], to_up),
            cp(9, near_out.at[1, last], near_in.at[1, last], to_dn),
        ]

    def both(self, j, rows):
        return self.mine(j, rows) + self.sib_in[j, rows, :].astype(F32)

    def send_far(self):
        self.sib[0].wait_recv()
        for k in range(2):

            def add(r, k=k):
                q = pl.ds(k * HALF + r.start, r.size)
                self.far_out[k, r, :] = self.both(0, q).astype(BF)

            rows_loop(HALF, 32, add)
            self.far[k].start()

    def send_early(self, k):
        self.sib[1 + k].wait_recv()

        def add(r):
            q = pl.ds((1 - k) * HALF + r.start, r.size)
            self.near_out[k, q, :] = self.both(1 + k, q).astype(BF)

        rows_loop(HALF, 32, add)
        self.early[k].start()

    def send_late(self):
        for k in range(2):
            self.far[k].wait_recv()

            def add(r, k=k):
                q = pl.ds(k * HALF + r.start, r.size)
                self.near_out[k, q, :] = (
                    self.both(1 + k, q) + self.far_in[k, r, :].astype(F32)
                ).astype(BF)

            rows_loop(HALF, 32, add)
            self.late[k].start()

    def wait(self):
        self.sib[3].wait_recv()
        for one in self.early + self.late:
            one.wait_recv()

    def total(self, rows):
        return (
            self.both(3, rows)
            + self.near_in[0, rows, :].astype(F32)
            + self.near_in[1, rows, :].astype(F32)
        )

    def finish(self):
        for one in self.sib + self.far + self.early + self.late:
            one.wait_send()


def ring_scatter(partial, scratch, between=None):
    part, sib_out = scratch[:2]
    c = lax.axis_index("core")
    scatter = RingScatter(
        lambda j, rows: part[j, rows, :], lambda j: sib_out.at[j], *scratch[2:]
    )

    def produce(j):
        def put(columns, value):
            part[j, :, columns] = jnp.where(c == 0, value[0], value[1])
            sib_out[j, :, columns] = jnp.where(c == 0, value[1], value[0]).astype(BF)

        partial(scatter.order[j], put)
        scatter.sib[j].start()

    produce(0)
    produce(1)
    scatter.send_far()
    scatter.send_early(0)
    produce(2)
    scatter.send_early(1)
    scatter.send_late()
    produce(3)
    if between is not None:
        between()
    scatter.wait()
    return scatter


AG_SCRATCH = [
    pltpu.VMEM((BLOCK, D), BF),
    pltpu.SemaphoreType.DMA,
    pltpu.SemaphoreType.DMA((N_AG,)),
    pltpu.SemaphoreType.DMA((N_AG,)),
]
FULL = jax.ShapeDtypeStruct((4, 2, BLOCK, D), BF)


def order_out(gathered, weight):
    for x in range(4):
        for zl in range(2):
            for a in range(2):
                row = x * 64 + zl * 32 + a * 16
                weight[row : row + 16, :] = gathered[x, a * 2 + zl]


OUT_ROWS = pltpu.VMEM((HD, D), BF)


NN = (((1,), (0,)), ((), ()))
NT = (((1,), (1,)), ((), ()))
TN = (((0,), (0,)), ((), ()))
TOKENS = 4 * BLOCK
KEYS = 2 * TOKENS
TILE = 2 * BLOCK


def dot(a, b, dims):
    return lax.dot_general(a, b, dims, preferred_element_type=F32)


def lane(n):
    return lax.broadcasted_iota(jnp.int32, (1, n), 1)


def turn_tables(base):
    entry = lax.rem(lane(BLOCK), HEAD_DIM)
    freq = jnp.exp(
        lax.rem(entry, ROT // 2).astype(F32) * (-2.0 / ROT * 9.210340371976184)
    )
    freq = jnp.where(entry < ROT, freq, 0.0)
    place = (base + lax.broadcasted_iota(jnp.int32, (BLOCK, 1), 0)).astype(F32)
    phase = place * freq
    return jnp.cos(phase), jnp.sin(phase)


def turn(v, cosine, sines, direction):
    entry = lax.rem(lane(BLOCK), HEAD_DIM)
    s = sines * direction
    ahead = pltpu.roll(v, BLOCK - ROT // 2, 1)
    behind = pltpu.roll(v, ROT // 2, 1)
    return v * cosine + jnp.where(entry < ROT // 2, -ahead, behind) * s


def key_bias(table, g, tile, blocks, q_part=0):
    token = lane(BLOCK)
    q_code, q_low = [], []
    for j in range(2):
        block = 4 * q_part + 2 * tile + j
        low = table[g, 1, block] * 4096
        q_code.append(low + table[g, 0, block] + token)
        q_low.append(low + jnp.zeros_like(token))
    q_code = jnp.concatenate(q_code, axis=1)
    q_low = jnp.concatenate(q_low, axis=1)
    column = lax.broadcasted_iota(jnp.int32, (BLOCK, 1), 0)
    rows = []
    for k in blocks:
        place = table[g, 0, k] + column
        code = jnp.where(place < table[g, 2, k], table[g, 1, k] * 4096 + place, 1 << 20)
        kept = jnp.logical_and(code <= q_code, code >= q_low)
        rows.append(jnp.where(kept, 0.0, NEG))
    return jnp.concatenate(rows, axis=0)


def head_mask(h):
    first = lane(BLOCK) < HEAD_DIM
    return jnp.where(first if h == 0 else jnp.logical_not(first), 1.0, 0.0).astype(BF)


def load(pairs, sems, first=0):
    copies = []
    for i, (src, dst) in enumerate(pairs):
        copies.append(pltpu.make_async_copy(src, dst, sems.at[first + i]))
        copies[-1].start()
    return copies


def kernel_attend(
    table,
    tokens_hbm,
    weight_hbm,
    shift,
    cotangent,
    out_in,
    hidden,
    gains,
    queries,
    kv,
    lse,
    attended,
    grad_out,
    out_full,
    middle,
    grad_all,
    two_all,
    out_rows,
    out_weight,
    own_two,
    tokens,
    weight,
    cosines,
    sines,
    tops,
    totals,
    mixed,
    local,
    send,
    recv,
    *sems,
):
    partner = {"zh": 1 - lax.axis_index("zh")}
    weight_in, *token_in = load(
        [(weight_hbm, weight)] + [(tokens_hbm.at[y], tokens.at[y]) for y in range(4)], local
    )
    y0, c, up, opp, dn = ring()
    out_rows[...] = permute_rows(out_in[...].astype(F32)).astype(BF)
    meet(list(ring_peers(up, dn, c)) + plane_peers())
    gather = RingGather(grad_out, grad_all, sems[0], sems[1:3])
    plane = PlaneGather(out_rows, out_full, *sems[3:6], 0)
    two_gather = RingGather(own_two, two_all, sems[6], sems[7:9])
    part, sib_out = sems[9:11]
    scatter = RingScatter(
        lambda j, rows: part[j, rows, :], lambda j: sib_out.at[j], *sems[11:]
    )
    plane.start()
    lse[...] = jnp.zeros_like(lse)
    weight_in.wait()
    for y in range(4):
        at = slice(y * BLOCK, (y + 1) * BLOCK)
        for g in range(2):
            cosine, sine = turn_tables(table[g, 0, y])
            cosines[g, at, :] = cosine
            sines[g, at, :] = sine
        token_in[y].wait()
        new = dot(tokens[y].reshape(TILE, D), weight[:, HD:], NN) + shift[:, HD:]
        for g in range(2):
            rows = slice(g * BLOCK, (g + 1) * BLOCK)
            for pair in range(2):
                q = slice(pair * BLOCK, (pair + 1) * BLOCK)
                turned = turn(new[rows, q], cosines[g, at, :], sines[g, at, :], 1.0)
                kv[0, g, at, q] = turned.astype(BF)
            kv[1, g, at, :] = new[rows, HD:].astype(BF)

    own, other = pl.ds(0, TOKENS), pl.ds(TOKENS, TOKENS)
    trade = [
        remote((send, recv), g, kv.at[:, g, own, :], kv.at[:, g, other, :], partner)
        for g in range(2)
    ]
    for one in trade:
        one.start()
    plane.middle()
    base, limit = table[c, 0, y0], table[c, 2, y0]

    def mask(r):
        place = base + r.start + lax.broadcasted_iota(jnp.int32, (16, 1), 0)
        row = jnp.where(place < limit, cotangent[r, :].astype(F32), 0.0)
        grad_out[r, :] = permute_rows(row).astype(BF)

    rows_loop(BLOCK, 16, mask)
    gather.start()
    for y in range(4):
        at = slice(y * BLOCK, (y + 1) * BLOCK)
        new = dot(tokens[y].reshape(TILE, D), weight[:, :HD], NN) + shift[:, :HD]
        for g in range(2):
            rows = slice(g * BLOCK, (g + 1) * BLOCK)
            for pair in range(2):
                q = slice(pair * BLOCK, (pair + 1) * BLOCK)
                turned = turn(new[rows, q], cosines[g, at, :], sines[g, at, :], 1.0)
                queries[g, at, q] = turned.astype(BF) * jnp.asarray(SCALE, BF)

    first_head = lax.broadcasted_iota(jnp.int32, (BLOCK, 1), 0) < HEAD_DIM

    def work(part, g):
        rows = slice(part * TOKENS, (part + 1) * TOKENS)

        @pl.loop(0, 2)
        def _(tile):
            at = pl.ds(pl.multiple_of(tile * TILE, TILE), TILE)
            bias = key_bias(table, g, tile, range(4 * part, 4 * part + 4))
            for pair in range(2):
                q = slice(pair * BLOCK, (pair + 1) * BLOCK)
                k_all = kv[0, g, rows, q]
                v_all = kv[1, g, rows, q]
                out = jnp.zeros((BLOCK, TILE), F32)
                keep, share = [], []
                for h in range(2):
                    row = slice(2 * pair + h, 2 * pair + h + 1)
                    s = dot(k_all, queries[g, at, q] * head_mask(h), NT) + bias
                    top = jnp.max(s, axis=0, keepdims=True)
                    if part == 1:
                        top = jnp.maximum(top, tops[g, row, at])
                    p = jnp.exp(s - top)
                    total = jnp.sum(p, axis=0, keepdims=True)
                    out = out + dot(v_all * head_mask(h), p.astype(BF), TN)
                    if part == 0:
                        tops[g, row, at] = top
                        totals[g, row, at] = total
                    else:
                        keep.append(jnp.exp(tops[g, row, at] - top))
                        total = total + totals[g, row, at] * keep[h]
                        lse[g, row, at] = top + jnp.log(total)
                        share.append(1.0 / total)
                if part == 0:
                    mixed[g, q, at] = out
                else:
                    out = out + mixed[g, q, at] * jnp.where(first_head, keep[0], keep[1])
                    out = (out * jnp.where(first_head, share[0], share[1])).T.astype(BF)
                    for j in range(2):
                        attended[2 * tile + j, g, :, q] = out[j * BLOCK : (j + 1) * BLOCK]

    def project(g):
        for j in range(4):
            a = attended[scatter.order[j], g]
            for i in range(4):
                q = slice(i * 512, (i + 1) * 512)
                value = dot(a, out_weight[:, q], NN)

                @pl.when(c == g)
                def _(j=j, q=q, value=value):
                    part[j, :, q] = value

                @pl.when(c != g)
                def _(j=j, q=q, value=value):
                    sib_out[j, :, q] = value.astype(BF)

            @pl.when(c != g)
            def _(j=j):
                scatter.sib[j].start()

    def norm(r):
        row = hidden[r, :].astype(F32) + scatter.total(r)
        middle[r, :] = row
        normed, _ = layer_norm(row)
        own_two[r, :] = (normed * gains[2:3, :] + gains[3:4, :]).astype(BF)

    def exchange():
        scatter.send_far()
        scatter.send_early(0)
        scatter.send_early(1)

    def settle():
        scatter.send_late()
        scatter.wait()
        rows_loop(BLOCK, 16, norm)
        two_gather.start()

    def pass_on():
        two_gather.forward()
        two_gather.share()
        two_gather.share_far()

    work(0, 0)
    gather.forward()
    work(0, 1)
    gather.share()
    plane.finish()
    order_out(out_full, out_weight)
    trade[0].wait_recv()
    work(1, 0)
    project(0)
    gather.share_far()

    @pl.when(c == 0)
    def _():
        exchange()

    trade[1].wait_recv()
    work(1, 1)
    project(1)

    @pl.when(c == 1)
    def _():
        exchange()

    settle()
    pass_on()

    for one in trade:
        one.wait_send()
    gather.finish()
    two_gather.finish()
    scatter.finish()


SM = pl.BlockSpec(memory_space=pltpu.SMEM)


def attend(table, tokens, weight, shift, cotangent, out_in, hidden, gains, cid):
    return pl.pallas_call(
        kernel_attend,
        out_shape=(
            jax.ShapeDtypeStruct((2, TOKENS, HD), BF),
            jax.ShapeDtypeStruct((2, 2, KEYS, HD), BF),
            jax.ShapeDtypeStruct((2, 8, TOKENS), F32),
            jax.ShapeDtypeStruct((4, 2, BLOCK, HD), BF),
            jax.ShapeDtypeStruct((BLOCK, D), BF),
            jax.ShapeDtypeStruct((4, 4, 16, D), BF),
            jax.ShapeDtypeStruct((BLOCK, D), F32),
            FULL,
            FULL,
        ),
        in_specs=[SM, ANY, ANY] + [VM] * 5,
        out_specs=(VM,) * 7 + (ANY, ANY),
        scratch_shapes=[
            pltpu.VMEM((16, D), BF),
            OUT_ROWS,
            pltpu.VMEM((BLOCK, D), BF),
            pltpu.VMEM((4, 2, BLOCK, D), BF),
            pltpu.VMEM((D, 3 * HD), BF),
            pltpu.VMEM((2, TOKENS, BLOCK), F32),
            pltpu.VMEM((2, TOKENS, BLOCK), F32),
            pltpu.VMEM((2, 8, TOKENS), F32),
            pltpu.VMEM((2, 8, TOKENS), F32),
            pltpu.VMEM((2, HD, TOKENS), F32),
            pltpu.SemaphoreType.DMA((5,)),
            pltpu.SemaphoreType.DMA((2,)),
            pltpu.SemaphoreType.DMA((2,)),
        ]
        + AG_SCRATCH[1:]
        + PG_SEMS
        + AG_SCRATCH[1:]
        + RS_SCRATCH,
        compiler_params=params(cid),
        name="attend",
    )(table, tokens, weight, shift, cotangent, out_in, hidden, gains)


def kernel_attend_back(
    table,
    branch_own,
    gathered,
    attended,
    queries,
    kv,
    lse,
    other_queries,
    other_lse,
    mlp_out,
    middle_hbm,
    joined_grad,
    out_part,
    hidden_out,
    branch,
    middle,
    own_out,
    probs,
    other_probs,
    local,
    weight,
    grads,
    other_grads,
    dq,
    mean,
    other_mean,
    dkv,
    send,
    recv,
    local_sem,
    gather_send,
    gather_recv,
    *scratch,
):
    partner = {"zh": 1 - lax.axis_index("zh")}
    y0, c, up, opp, dn = ring()
    order = (opp, up, dn, y0)
    out_in = load([(mlp_out.at[order[j], c], own_out.at[j]) for j in range(4)], local)
    (middle_in,) = load([(middle_hbm, middle)], local, 4)
    meet(list(ring_peers(up, dn, c)) + [partner])
    gather = RingGather(branch_own, branch, local_sem, (gather_send, gather_recv))
    gather.start()
    scatter = RingScatter(
        lambda j, rows: own_out[j, rows, :].astype(F32),
        lambda j: mlp_out.at[order[j], 1 - c],
        *scratch,
    )
    for one in scatter.sib:
        one.start()
    order_out(gathered, weight)
    trade = [
        remote((send, recv), 0, grads, other_grads, partner),
        remote((send, recv), 1, mean, other_mean, partner),
    ]

    def recompute(part, g):
        q_src, lse_src = (queries, lse) if part == 0 else (other_queries, other_lse)
        dst = probs if part == 0 else other_probs
        blocks = range(8) if part == 0 else range(4)
        rows = slice(0, len(blocks) * BLOCK)

        @pl.loop(0, 2)
        def _(tile):
            at = pl.ds(pl.multiple_of(tile * TILE, TILE), TILE)
            bias = key_bias(table, g, tile, blocks, part)
            for pair in range(2):
                q = slice(pair * BLOCK, (pair + 1) * BLOCK)
                for h in range(2):
                    row = slice(2 * pair + h, 2 * pair + h + 1)
                    s = dot(kv[0, g, rows, q], q_src[g, at, q] * head_mask(h), NT) + bias
                    dst[g, tile, 2 * pair + h] = jnp.exp(s - lse_src[g, row, at])

    recompute(0, 0)
    gather.forward()
    recompute(0, 1)
    gather.share()
    gather.share_far()
    recompute(1, 0)
    recompute(1, 1)
    gather.finish()

    dq[...] = jnp.zeros_like(dq)
    dkv[...] = jnp.zeros_like(dkv)
    mean[...] = jnp.zeros_like(mean)
    heads = jnp.concatenate([head_mask(0), head_mask(1)] * 4, axis=0).astype(F32)
    for y in range(4):
        at = slice(y * BLOCK, (y + 1) * BLOCK)
        new = dot(branch[y].reshape(TILE, D), weight[...], NT)
        for g in range(2):
            rows = slice(g * BLOCK, (g + 1) * BLOCK)
            grads[g, at, :] = new[rows].astype(BF)
            for pair in range(2):
                q = slice(pair * BLOCK, (pair + 1) * BLOCK)
                both = slice(2 * pair, 2 * pair + 2)
                mixed = attended[y, g, :, q].astype(F32) * new[rows, q].astype(BF).astype(F32)
                mean[g, both, at] = lax.dot_general(
                    heads, mixed, NT, precision=lax.Precision.HIGHEST
                )[0:2]
    for one in trade:
        one.start()
    for one in out_in:
        one.wait()
    scatter.send_far()
    scatter.send_early(0)
    scatter.send_early(1)

    def back(part, g):
        q_src, g_src = (queries, grads) if part == 0 else (other_queries, other_grads)
        mean_src, p_src = (mean, probs) if part == 0 else (other_mean, other_probs)
        rows = slice(0, KEYS if part == 0 else TOKENS)

        @pl.loop(0, 2)
        def _(tile):
            at = pl.ds(pl.multiple_of(tile * TILE, TILE), TILE)
            for pair in range(2):
                q = slice(pair * BLOCK, (pair + 1) * BLOCK)
                k_all = kv[0, g, rows, q]
                v_all = kv[1, g, rows, q]
                new_q = jnp.zeros((BLOCK, TILE), F32)
                new_k = jnp.zeros((TOKENS, BLOCK), F32)
                new_v = jnp.zeros((TOKENS, BLOCK), F32)
                for h in range(2):
                    row = slice(2 * pair + h, 2 * pair + h + 1)
                    q_head = q_src[g, at, q] * head_mask(h)
                    g_head = g_src[g, at, q] * head_mask(h)
                    p = p_src[g, tile, 2 * pair + h]
                    p_grad = dot(v_all, g_head, NT)
                    s_grad = (p * (p_grad - mean_src[g, row, at])).astype(BF)
                    new_v = new_v + dot(p[:TOKENS].astype(BF), g_head, NN)
                    new_k = new_k + dot(s_grad[:TOKENS], q_head, NN)
                    if part == 0:
                        new_q = new_q + dot(k_all * head_mask(h), s_grad, TN)
                if part == 0:
                    dq[g, q, at] += new_q
                dkv[0, g, :, q] += new_k
                dkv[1, g, :, q] += new_v

    back(0, 0)
    scatter.send_late()
    back(0, 1)

    @pl.loop(0, 8)
    def _(i):
        q = pl.ds(pl.multiple_of(i * TILE, TILE), TILE)
        new = dot(attended[...].reshape(8 * BLOCK, HD), branch[:, :, :, q].reshape(8 * BLOCK, TILE), TN)
        for x in range(4):
            for zl in range(2):
                for a in range(2):
                    row = x * 64 + zl * 32 + a * 16
                    out_part[x * 4 + a * 2 + zl, :, q] = new[row : row + 16].astype(BF)

    for one in trade:
        one.wait_recv()
    back(1, 0)
    back(1, 1)
    scatter.wait()
    middle_in.wait()

    def add(r):
        hidden_out[r, :] = restore_rows(middle[r, :] + scatter.total(r)).astype(BF)

    rows_loop(BLOCK, 16, add)
    for g in range(2):

        @pl.loop(0, 4)
        def _(y, g=g):
            at = pl.ds(pl.multiple_of(y * BLOCK, BLOCK), BLOCK)
            cosine, sine = turn_tables(table[g, 0, y])
            for pair in range(2):
                q = slice(pair * BLOCK, (pair + 1) * BLOCK)
                new = dq[g, q, at].T * SCALE
                joined_grad[y, g, :, q] = turn(new, cosine, sine, -1.0).astype(BF)
                joined_grad[y, g, :, HD + pair * BLOCK : HD + (pair + 1) * BLOCK] = turn(
                    dkv[0, g, at, q], cosine, sine, -1.0
                ).astype(BF)
            joined_grad[y, g, :, 2 * HD :] = dkv[1, g, at, :].astype(BF)

    for one in trade:
        one.wait_send()
    scatter.finish()


def attend_back(
    table,
    branch,
    gathered,
    attended,
    queries,
    kv,
    lse,
    other_queries,
    other_lse,
    mlp_out,
    middle,
    cid,
):
    return pl.pallas_call(
        kernel_attend_back,
        out_shape=(
            jax.ShapeDtypeStruct((4, 2, BLOCK, 3 * HD), BF),
            jax.ShapeDtypeStruct((16, 16, D), BF),
            jax.ShapeDtypeStruct((BLOCK, D), BF),
        ),
        in_specs=[SM] + [VM] * 8 + [ANY, ANY],
        out_specs=(VM, VM, VM),
        scratch_shapes=[
            pltpu.VMEM((4, 2, BLOCK, D), BF),
            pltpu.VMEM((BLOCK, D), F32),
            pltpu.VMEM((4, BLOCK, D), BF),
            pltpu.VMEM((2, 2, 4, KEYS, TILE), F32),
            pltpu.VMEM((2, 2, 4, TOKENS, TILE), F32),
            pltpu.SemaphoreType.DMA((5,)),
            OUT_ROWS,
            pltpu.VMEM((2, TOKENS, HD), BF),
            pltpu.VMEM((2, TOKENS, HD), BF),
            pltpu.VMEM((2, HD, TOKENS), F32),
            pltpu.VMEM((2, 8, TOKENS), F32),
            pltpu.VMEM((2, 8, TOKENS), F32),
            pltpu.VMEM((2, 2, TOKENS, HD), F32),
            pltpu.SemaphoreType.DMA((2,)),
            pltpu.SemaphoreType.DMA((2,)),
        ]
        + AG_SCRATCH[1:]
        + RS_SCRATCH[2:],
        compiler_params=params(cid),
        name="attend_back",
    )(
        table,
        branch,
        gathered,
        attended,
        queries,
        kv,
        lse,
        other_queries,
        other_lse,
        mlp_out,
        middle,
    )


def kernel_mlp(
    two_hbm,
    grad_hbm,
    w_hbm,
    middle,
    grad_out,
    gains,
    queries,
    lse,
    middle_grad,
    sums,
    own,
    other_queries,
    other_lse,
    out_hbm,
    part_hbm,
    two,
    grad_all,
    w,
    out_part,
    mlp_part,
    inner,
    both_grads,
    local,
    leave,
    send,
    recv,
    *scratch,
):
    y, c, up, opp, dn = ring()
    partner = {"zh": 1 - lax.axis_index("zh")}
    order = (opp, up, dn, y)
    w_in = load([(w_hbm.at[:, k], w.at[k]) for k in range(3)], local)
    block_in = load(
        [(src.at[b], dst.at[b]) for b in order for src, dst in ((two_hbm, two), (grad_hbm, grad_all))],
        local,
        3,
    )
    meet(list(ring_peers(up, dn, c)) + [partner])
    trade = [
        remote((send, recv), 0, queries, other_queries, partner),
        remote((send, recv), 1, lse, other_lse, partner),
    ]
    for one in trade:
        one.start()
    held = jnp.logical_or(lane(FP) >= BLOCK, y < 2)
    gate_lanes, up_lanes = pl.ds(0, FP), pl.ds(FP, FP)
    waits = [w_in + block_in[0:2], block_in[2:4], block_in[4:6], block_in[6:8]]
    outs = []

    def partial(block, put):
        for one in waits[len(outs)]:
            one.wait()
        a = two[block].reshape(TILE, D)
        gate = dot(a, w[0].reshape(D, FP), NN)
        up_proj = dot(a, w[1].reshape(D, FP), NN)
        grad = dot(grad_all[block].reshape(TILE, D), w[2].reshape(D, FP), NN)
        sig = 1.0 / (1.0 + jnp.exp(-gate))
        active = gate * sig
        low = (active * up_proj).astype(BF)
        low_gate = (grad * up_proj * sig * (1.0 + gate * (1.0 - sig))).astype(BF)
        low_up = (grad * active).astype(BF)
        zero = jnp.zeros((), BF)
        inner[block] = jnp.where(held, low, zero).reshape(2, BLOCK, FP)
        both_grads[block, :, :, gate_lanes] = jnp.where(held, low_gate, zero).reshape(2, BLOCK, FP)
        both_grads[block, :, :, up_lanes] = jnp.where(held, low_up, zero).reshape(2, BLOCK, FP)

        low_gate = both_grads[block, :, :, gate_lanes].reshape(TILE, FP)
        low_up = both_grads[block, :, :, up_lanes].reshape(TILE, FP)
        for i in range(4):
            q, wide = slice(i * 512, (i + 1) * 512), slice(i * 4, (i + 1) * 4)
            new = dot(low_gate, w[0, wide].reshape(512, FP), NT)
            new = new + dot(low_up, w[1, wide].reshape(512, FP), NT)
            put(q, new.reshape(2, BLOCK, 512))
        low = inner[block].reshape(TILE, FP)
        for i in range(4):
            q, wide = slice(i * 512, (i + 1) * 512), slice(i * 4, (i + 1) * 4)
            new = dot(low, w[2, wide].reshape(512, FP), NT)
            out_part[block, :, :, q] = new.astype(BF).reshape(2, BLOCK, 512)

        outs.extend(load([(out_part.at[block], out_hbm.at[block])], leave, len(outs)))

    done = []

    def weight_grads(count=1):
        begin = len(done)

        @pl.loop(begin, begin + count)
        def _(i):
            q = pl.ds(pl.multiple_of(i * TILE, TILE), TILE)
            a = two[:, :, :, q].reshape(TP * BLOCK, TILE)
            b = grad_all[:, :, :, q].reshape(TP * BLOCK, TILE)
            new = dot(a, both_grads[...].reshape(TP * BLOCK, 2 * FP), TN).astype(BF)
            at = pl.ds(2 * i, 2)
            mlp_part[at, 0] = new[:, :FP].reshape(2, BLOCK, FP)
            mlp_part[at, 1] = new[:, FP:].reshape(2, BLOCK, FP)
            new = dot(b, inner[...].reshape(TP * BLOCK, FP), TN).astype(BF)
            mlp_part[at, 2] = new.reshape(2, BLOCK, FP)

        for i in range(begin, begin + count):
            done.extend(
                load([(mlp_part.at[pl.ds(2 * i, 2)], part_hbm.at[pl.ds(2 * i, 2)])], leave, 4 + i)
            )

    scatter = ring_scatter(partial, scratch, lambda: weight_grads(8))
    sums[...] = jnp.zeros_like(sums)

    def back(r):
        row = scatter.total(r)
        normed, inv = layer_norm(middle[r, :])
        grad = grad_out[r, :].astype(F32) + norm_back(row, normed, inv, gains[2:3, :])
        middle_grad[r, :] = grad
        own[r, :] = grad.astype(BF)
        sums[0:1, :] += jnp.sum(row * normed, axis=0, keepdims=True)
        sums[1:2, :] += jnp.sum(row, axis=0, keepdims=True)

    rows_loop(BLOCK, 16, back)
    scatter.finish()
    for one in outs + done + trade:
        one.wait()


def mlp(two, grad_all, w, middle, grad_out, gains, queries, lse, cid):
    block = (4, 2, BLOCK, D)
    return pl.pallas_call(
        kernel_mlp,
        out_shape=(
            jax.ShapeDtypeStruct((BLOCK, D), F32),
            jax.ShapeDtypeStruct((8, D), F32),
            jax.ShapeDtypeStruct((BLOCK, D), BF),
            jax.ShapeDtypeStruct((2, TOKENS, HD), BF),
            jax.ShapeDtypeStruct((2, 8, TOKENS), F32),
            FULL,
            jax.ShapeDtypeStruct((16, 3, BLOCK, FP), BF),
        ),
        in_specs=[ANY] * 3 + [VM] * 5,
        out_specs=(VM,) * 5 + (ANY, ANY),
        scratch_shapes=[
            pltpu.VMEM(block, BF),
            pltpu.VMEM(block, BF),
            pltpu.VMEM((3, 16, BLOCK, FP), BF),
            pltpu.VMEM(block, BF),
            pltpu.VMEM((16, 3, BLOCK, FP), BF),
            pltpu.VMEM((4, 2, BLOCK, FP), BF),
            pltpu.VMEM((4, 2, BLOCK, 2 * FP), BF),
            pltpu.SemaphoreType.DMA((11,)),
            pltpu.SemaphoreType.DMA((12,)),
            pltpu.SemaphoreType.DMA((2,)),
            pltpu.SemaphoreType.DMA((2,)),
        ]
        + RS_SCRATCH,
        compiler_params=params(cid),
        name="mlp",
    )(two, grad_all, w, middle, grad_out, gains, queries, lse)


class PlaneScatter:
    COPIES = 12

    def __init__(self, part, a_in, b_in, a_mid, b_mid, a_last, b_last, send, recv):
        self.refs = part, a_in, b_in, a_mid, b_mid, a_last, b_last
        sems = send, recv
        half = part.shape[-1] // 2
        self.lanes = pl.ds(0, half), pl.ds(half, half)
        self.x = lax.axis_index("x")
        self.z = lax.axis_index("zh") * 2 + lax.axis_index("zl")
        self.one, self.two = [], []
        for d in range(1, 4):
            x = lax.rem(self.x + d, 4)
            z = lax.rem(self.z + d, 4)
            to_x = {"x": x}
            to_z = {"zh": z // 2, "zl": lax.rem(z, 2)}
            a, b = self.lanes
            k = d - 1
            self.one.append(remote(sems, k, part.at[:, z, :, a], a_in.at[k], to_z))
            self.one.append(remote(sems, 3 + k, part.at[x, :, :, b], b_in.at[k], to_x))
            self.two.append(remote(sems, 6 + k, a_mid.at[x], a_last.at[k], to_x))
            self.two.append(remote(sems, 9 + k, b_mid.at[z], b_last.at[k], to_z))

    def start(self):
        for copy in self.one:
            copy.start()

    def middle(self):
        part, a_in, b_in, a_mid, b_mid, _, _ = self.refs
        for copy in self.one:
            copy.wait_recv()
        a, b = self.lanes

        @pl.loop(0, 4)
        def _(i):
            a_mid[i] = (
                part[i, self.z, :, a].astype(F32) + jnp.sum(a_in[:, i].astype(F32), axis=0)
            ).astype(BF)
            b_mid[i] = (
                part[self.x, i, :, b].astype(F32) + jnp.sum(b_in[:, i].astype(F32), axis=0)
            ).astype(BF)

        for copy in self.two:
            copy.start()

    def finish(self, out):
        _, _, _, a_mid, b_mid, a_last, b_last = self.refs
        for copy in self.two:
            copy.wait_recv()
        a, b = self.lanes
        out[:, a] = (
            a_mid[self.x].astype(F32) + jnp.sum(a_last[...].astype(F32), axis=0)
        ).astype(BF)
        out[:, b] = (
            b_mid[self.z].astype(F32) + jnp.sum(b_last[...].astype(F32), axis=0)
        ).astype(BF)
        for copy in self.one + self.two:
            copy.wait_send()


def plane_scratch(rows, lanes):
    half = lanes // 2
    return [
        pltpu.VMEM((3, 4, rows, half), BF),
        pltpu.VMEM((3, 4, rows, half), BF),
        pltpu.VMEM((4, rows, half), BF),
        pltpu.VMEM((4, rows, half), BF),
        pltpu.VMEM((3, rows, half), BF),
        pltpu.VMEM((3, rows, half), BF),
        pltpu.SemaphoreType.DMA((PlaneScatter.COPIES,)),
        pltpu.SemaphoreType.DMA((PlaneScatter.COPIES,)),
    ]


def plane_peers():
    peers = []
    for d in range(1, 4):
        z = lax.rem(lax.axis_index("zh") * 2 + lax.axis_index("zl") + d, 4)
        peers.append({"x": lax.rem(lax.axis_index("x") + d, 4)})
        peers.append({"zh": z // 2, "zl": lax.rem(z, 2)})
    return peers


def kernel_qkv_back(
    joined_grad,
    weight_hbm,
    hidden,
    middle_hbm,
    gains,
    tokens_hbm,
    out_part,
    input_grad,
    sums,
    shift_sum,
    qkv_sum,
    out_sum,
    tokens,
    weight,
    middle_grad,
    local,
    part,
    *scratch,
):
    token_in = load([(tokens_hbm.at[y], tokens.at[y]) for y in range(4)], local)
    weight_in, middle_in = load([(weight_hbm, weight), (middle_hbm, middle_grad)], local, 4)
    y, c, up, opp, dn = ring()
    meet(list(ring_peers(up, dn, c)) + plane_peers())
    out_scatter = PlaneScatter(out_part, *scratch[:8])
    qkv_scatter = PlaneScatter(part, *scratch[8:16])
    out_scatter.start()
    flat = joined_grad[...].reshape(TP * BLOCK, 3 * HD)
    for one in token_in:
        one.wait()

    for i in range(4):
        q = slice(i * 512, (i + 1) * 512)
        new = dot(tokens[:, :, :, q].reshape(TP * BLOCK, 512), flat, TN).astype(BF)
        part[i] = new.reshape(4, BLOCK, 3 * HD)

    qkv_scatter.start()
    weight_in.wait()
    middle_in.wait()

    def partial(block, put):
        a = joined_grad[block].reshape(2 * BLOCK, 3 * HD)
        for i in range(4):
            q = slice(i * 512, (i + 1) * 512)
            put(q, dot(a, weight[q, :], NT).reshape(2, BLOCK, 512))

    def between():
        out_scatter.middle()
        shift_sum[...] = jnp.broadcast_to(
            jnp.sum(flat.astype(F32), axis=0, keepdims=True), shift_sum.shape
        )
        qkv_scatter.middle()

    scatter = ring_scatter(partial, scratch[16:], between)
    sums[...] = jnp.zeros_like(sums)

    def back(r):
        row = scatter.total(r)
        normed, inv = layer_norm(hidden[r, :].astype(F32))
        input_grad[r, :] = restore_rows(
            middle_grad[r, :] + norm_back(row, normed, inv, gains[0:1, :])
        )
        sums[0:1, :] += jnp.sum(row * normed, axis=0, keepdims=True)
        sums[1:2, :] += jnp.sum(row, axis=0, keepdims=True)

    rows_loop(BLOCK, 16, back)
    scatter.finish()
    out_scatter.finish(out_sum)
    qkv_scatter.finish(qkv_sum)


def qkv_back(joined_grad, weight, hidden, middle_grad, gains, tokens, out_part, cid):
    return pl.pallas_call(
        kernel_qkv_back,
        out_shape=(
            jax.ShapeDtypeStruct((BLOCK, D), F32),
            jax.ShapeDtypeStruct((8, D), F32),
            jax.ShapeDtypeStruct((8, 3 * HD), F32),
            jax.ShapeDtypeStruct((BLOCK, 3 * HD), BF),
            jax.ShapeDtypeStruct((16, D), BF),
        ),
        in_specs=[VM, ANY, VM, ANY, VM, ANY, VM],
        out_specs=(VM,) * 5,
        scratch_shapes=[
            pltpu.VMEM((4, 2, BLOCK, D), BF),
            pltpu.VMEM((D, 3 * HD), BF),
            pltpu.VMEM((BLOCK, D), F32),
            pltpu.SemaphoreType.DMA((6,)),
            pltpu.VMEM((4, 4, BLOCK, 3 * HD), BF),
        ]
        + plane_scratch(16, D)
        + plane_scratch(BLOCK, 3 * HD)
        + RS_SCRATCH,
        compiler_params=params(cid),
        name="qkv_back",
    )(joined_grad, weight, hidden, middle_grad, gains, tokens, out_part.reshape(4, 4, 16, D))


TP_STEPS = [(dy, dc) for dy in range(4) for dc in range(2) if (dy, dc) != (0, 0)]
XZ_STEPS = [(dx, dz) for dx in range(4) for dz in range(4) if (dx, dz) != (0, 0)]


def tp_peer(step):
    y = lax.rem(lax.axis_index("y") + step[0], 4)
    c = lax.rem(lax.axis_index("core") + step[1], 2)
    return {"y": y, "core": c}, y * 2 + c


def xz_peer(step):
    x = lax.rem(lax.axis_index("x") + step[0], 4)
    z = lax.rem(lax.axis_index("zh") * 2 + lax.axis_index("zl") + step[1], 4)
    return {"x": x, "zh": z // 2, "zl": lax.rem(z, 2)}, x * 4 + z


def meet_all(split):
    peers = [tp_peer(s)[0] for s in TP_STEPS] + [xz_peer(s)[0] for s in XZ_STEPS]
    barrier = pltpu.get_barrier_semaphore()
    for peer in peers:
        pl.semaphore_signal(
            barrier, inc=1, device_id=peer, device_id_type=pl.DeviceIdType.MESH
        )

    @pl.when(split)
    def _():
        pl.semaphore_signal(
            barrier, inc=1, device_id=swap_peer(), device_id_type=pl.DeviceIdType.MESH
        )

    pl.semaphore_wait(barrier, len(peers) + split.astype(jnp.int32))


def swap_peer():
    return {"zh": lax.axis_index("core"), "core": lax.axis_index("zh")}


def swap_start(split, src, dst, local_sem, sems, i):
    @pl.when(split)
    def _():
        remote(sems, i, src, dst, swap_peer()).start()

    @pl.when(jnp.logical_not(split))
    def _():
        pltpu.make_async_copy(src, dst, local_sem).start()


def swap_wait(split, src, dst, local_sem, sems, i):
    @pl.when(split)
    def _():
        remote(sems, i, src, dst, swap_peer()).wait()

    @pl.when(jnp.logical_not(split))
    def _():
        pltpu.make_async_copy(src, dst, local_sem).wait()


N_TP = len(TP_STEPS)
N_XZ = len(XZ_STEPS)


class PlaneGather:
    COPIES = 12

    def __init__(self, src, full, local_sem, send, recv, x_first):
        sems = send, recv
        a, b = pl.ds(0, x_first), pl.ds(x_first, src.shape[-1] - x_first)
        rest = (slice(None),) * (len(src.shape) - 1)
        x = lax.axis_index("x")
        z = lax.axis_index("zh") * 2 + lax.axis_index("zl")
        self.one, self.two = [], []
        every = slice(None)
        for d in range(1, 4):
            k = d - 1
            z_to = lax.rem(z + d, 4)
            to_x = {"x": lax.rem(x + d, 4)}
            to_z = {"zh": z_to // 2, "zl": lax.rem(z_to, 2)}
            if x_first:
                at = rest + (a,)
                self.one.append(remote(sems, k, src.at[at], full.at[(x, z) + at], to_x))
                row = full.at[(every, z) + at]
                self.two.append(remote(sems, 6 + k, row, row, to_z))
            at = rest + (b,)
            self.one.append(remote(sems, 3 + k, src.at[at], full.at[(x, z) + at], to_z))
            row = full.at[(x, every) + at]
            self.two.append(remote(sems, 9 + k, row, row, to_x))
        self.here = pltpu.make_async_copy(src, full.at[x, z], local_sem)

    def start(self):
        for copy in self.one:
            copy.start()
        self.here.start()

    def middle(self):
        self.here.wait()
        for copy in self.one:
            copy.wait_recv()
        for copy in self.two:
            copy.start()

    def finish(self):
        for copy in self.two:
            copy.wait_recv()
        for copy in self.one + self.two:
            copy.wait_send()


PG_SEMS = [
    pltpu.SemaphoreType.DMA,
    pltpu.SemaphoreType.DMA((PlaneGather.COPIES,)),
    pltpu.SemaphoreType.DMA((PlaneGather.COPIES,)),
]


def first_lane(rank):
    return jnp.where(rank < 4, 6 * rank, 5 * rank + 3) * BLOCK


def head_lane(part, rank):
    return part * D + (lax.rem(rank, 2) * 4 + rank // 2) * HD


def lanes_at(start, n):
    return pl.ds(pl.multiple_of(start, BLOCK), n)


def spread_gains(small_all, gains, shift, rank):
    rows = small_all[...].reshape(BLOCK, BLOCK)
    source = lax.broadcasted_iota(jnp.int32, (BLOCK, 1), 0)
    f = lane(D)
    mine = (f // 16) == source
    for i in range(4):
        pick = (source == 16 * i + lax.rem(f, 16)).astype(F32)
        value = jnp.dot(rows, pick, preferred_element_type=F32)
        gains[i : i + 1, :] = jnp.sum(jnp.where(mine, value, 0.0), axis=0, keepdims=True)
    core = lax.rem(source, 2)
    y = lax.rem(source // 2, 4)
    zl = lax.rem(source // 8, 2)
    zh = lax.rem(source // 16, 2)
    x = source // 32
    owner = (zh * 4 + y) * 16 + x * 4 + zl * 2 + core
    for i in range(3):
        j = head_lane(i, rank) + lane(HD)
        pick = (source == 64 + lax.rem(j, 48)).astype(F32)
        value = jnp.dot(rows, pick, preferred_element_type=F32)
        value = jnp.sum(jnp.where(j // 48 == owner, value, 0.0), axis=0, keepdims=True)
        shift[:, i * HD : (i + 1) * HD] = value


def kernel_front(
    small,
    hidden_in,
    w_qkv,
    w_gate,
    w_up,
    w_down,
    w_out,
    small_all,
    gains,
    shift,
    qkv_full,
    mlp_rows,
    out_rows,
    hidden,
    full,
    own,
    qkv_rows,
    local,
    send,
    recv,
    *sems,
):
    me = lax.axis_index("y") * 2 + lax.axis_index("core")
    xz = lax.axis_index("x") * 4 + lax.axis_index("zh") * 2 + lax.axis_index("zl")
    split = lax.axis_index("zh") != lax.axis_index("core")
    meet_all(split)
    cp = functools.partial(remote, (send, recv))
    tiny, qkv, mlp = [], [], []
    for k, step in enumerate(TP_STEPS):
        peer, there = tp_peer(step)
        tiny.append(cp(k, small, small_all.at[xz, me], peer))
        for i in range(3):
            src = w_qkv.at[:, lanes_at(head_lane(i, there), HD)]
            dst = qkv_rows.at[me, :, pl.ds(i * HD, HD)]
            qkv.append(cp((1 + i) * N_TP + k, src, dst, peer))
        for i, w in enumerate((w_gate, w_up, w_down)):
            src = w.at[:, lanes_at(first_lane(there), FP)]
            mlp.append(cp((4 + i) * N_TP + k, src, mlp_rows.at[i, me], peer))
    keep = [pltpu.make_async_copy(small, small_all.at[xz, me], local.at[0])]
    for i, w in enumerate((w_gate, w_up, w_down)):
        src = w_qkv.at[:, lanes_at(head_lane(i, me), HD)]
        dst = qkv_rows.at[me, :, pl.ds(i * HD, HD)]
        keep.append(pltpu.make_async_copy(src, dst, local.at[1 + i]))
        src = w.at[:, lanes_at(first_lane(me), FP)]
        keep.append(pltpu.make_async_copy(src, mlp_rows.at[i, me], local.at[4 + i]))
    for one in tiny + qkv + keep:
        one.start()
    last = 7 * N_TP + N_XZ
    for one in tiny:
        one.wait()
    keep[0].wait()
    wide = []
    for k, step in enumerate(XZ_STEPS):
        peer, _ = xz_peer(step)
        wide.append(cp(7 * N_TP + k, small_all.at[xz], small_all.at[xz], peer))
    for one in wide:
        one.start()
    for one in qkv + keep[1:]:
        one.wait()
    plane = PlaneGather(qkv_rows, qkv_full, *sems[:3], 3 * HD // 2)
    plane.start()
    for one in mlp:
        one.start()
    swap_start(split, w_out, out_rows, local.at[7], (send, recv), last)
    for one in wide:
        one.wait()
    gains[...] = jnp.zeros_like(gains)
    spread_gains(small_all, gains, shift, me)

    def norm(r):
        row = permute_rows(hidden_in[r, :].astype(F32))
        hidden[r, :] = row.astype(BF)
        normed, _ = layer_norm(row)
        own[r, :] = (normed * gains[0:1, :] + gains[1:2, :]).astype(BF)

    rows_loop(BLOCK, 16, norm)
    gather = RingGather(own, full, sems[3], sems[4:])
    gather.start()
    plane.middle()
    gather.forward()
    gather.share()
    gather.share_far()
    for one in mlp:
        one.wait()
    swap_wait(split, w_out, out_rows, local.at[7], (send, recv), last)
    gather.finish()
    plane.finish()


def front(small, hidden, w_qkv, w_gate, w_up, w_down, w_out, cid):
    n = 7 * N_TP + N_XZ + 1
    return pl.pallas_call(
        kernel_front,
        out_shape=(
            jax.ShapeDtypeStruct((16, TP, 1, BLOCK), F32),
            jax.ShapeDtypeStruct((8, D), F32),
            jax.ShapeDtypeStruct((1, 3 * HD), F32),
            jax.ShapeDtypeStruct((4, 4, TP, 16, 3 * HD), BF),
            jax.ShapeDtypeStruct((3, TP, 16, FP), BF),
            jax.ShapeDtypeStruct((16, D), BF),
            jax.ShapeDtypeStruct((BLOCK, D), BF),
            FULL,
        ),
        in_specs=[ANY, VM] + [ANY] * 5,
        out_specs=(VM, VM, VM, ANY, ANY, ANY, VM, ANY),
        scratch_shapes=[
            pltpu.VMEM((BLOCK, D), BF),
            pltpu.VMEM((TP, 16, 3 * HD), BF),
            pltpu.SemaphoreType.DMA((8,)),
            pltpu.SemaphoreType.DMA((n,)),
            pltpu.SemaphoreType.DMA((n,)),
        ]
        + PG_SEMS
        + AG_SCRATCH[1:],
        compiler_params=params(cid),
        name="front",
    )(small, hidden, w_qkv, w_gate, w_up, w_down, w_out)


def kernel_collect(
    one_sums,
    two_sums,
    shift,
    qkv,
    mlp,
    out,
    small,
    qkv_grad,
    gate_grad,
    up_grad,
    down_grad,
    out_grad,
    terms,
    terms_in,
    own,
    small_all,
    qkv_all,
    mlp_all,
    out_all,
    local,
    *sems,
):
    me = lax.axis_index("y") * 2 + lax.axis_index("core")
    xz = lax.axis_index("x") * 4 + lax.axis_index("zh") * 2 + lax.axis_index("zl")
    split = lax.axis_index("zh") != lax.axis_index("core")
    for p in range(16):
        q = slice(p * BLOCK, (p + 1) * BLOCK)
        terms[p, 0:2, :] = one_sums[0:2, q]
        terms[p, 2:4, :] = two_sums[0:2, q]
        for i in range(6):
            terms[p, 8 + i : 9 + i, :] = shift[0:1, i * BLOCK : (i + 1) * BLOCK]
        for i in (4, 5, 6, 7, 14, 15):
            terms[p, i : i + 1, :] = jnp.zeros((1, BLOCK), F32)
    meet_all(split)
    cp = functools.partial(remote, sems)
    big, extra, wide = [], [], []
    near, tile = pl.ds(BLOCK, FP - BLOCK), pl.ds(0, BLOCK)
    base = N_XZ + N_TP
    for k, step in enumerate(TP_STEPS):
        peer, there = tp_peer(step)
        dst = mlp_all.at[:, :, lanes_at(first_lane(me) + BLOCK, FP - BLOCK)]
        big.append(cp(base + k, mlp.at[:, there, :, near], dst, peer))
        dst = mlp_all.at[:, :, lanes_at(first_lane(me), BLOCK)]
        extra.append(cp(base + N_TP + k, mlp.at[:, there, :, tile], dst, peer))
        big.append(cp(base + 2 * N_TP + k, qkv.at[there], qkv_all.at[me], peer))
    for k, step in enumerate(XZ_STEPS):
        peer, there = xz_peer(step)
        wide.append(cp(k, terms.at[there], terms_in.at[xz], peer))
    dst = mlp_all.at[:, :, lanes_at(first_lane(me) + BLOCK, FP - BLOCK)]
    keep = [
        pltpu.make_async_copy(mlp.at[:, me, :, near], dst, local.at[0]),
        pltpu.make_async_copy(qkv.at[me], qkv_all.at[me], local.at[1]),
    ]
    dst = mlp_all.at[:, :, lanes_at(first_lane(me), BLOCK)]
    keep_tile = pltpu.make_async_copy(mlp.at[:, me, :, tile], dst, local.at[2])
    first_four = me < 4
    for one in wide + big + keep:
        one.start()

    @pl.when(first_four)
    def _():
        keep_tile.start()
        for one in extra:
            one.start()

    last = base + 3 * N_TP
    swap_start(split, out, out_all, local.at[3], sems, last)
    for one in wide:
        one.wait()
    terms_in[xz] = terms[xz]
    own[...] = jnp.sum(terms_in[...], axis=0)
    tiny = []
    for k, step in enumerate(TP_STEPS):
        peer, _ = tp_peer(step)
        tiny.append(cp(N_XZ + k, own, small_all.at[me], peer))
    for one in tiny:
        one.start()
    for one in big + keep:
        one.wait()
    for k, step in enumerate(TP_STEPS):
        source = lax.rem(lax.axis_index("y") + 4 - step[0], 4) * 2 + lax.rem(
            lax.axis_index("core") + 2 - step[1], 2
        )

        @pl.when(source < 4)
        def _(k=k):
            extra[k].wait_recv()

    @pl.when(first_four)
    def _():
        keep_tile.wait()
        for one in extra:
            one.wait_send()

    for t in range(TP):
        for i in range(3):
            first = i * D + (t % 2 * 4 + t // 2) * HD
            qkv_grad[:, first : first + HD] = qkv_all[t, :, i * HD : (i + 1) * HD].astype(F32)
    gate_grad[...] = mlp_all[0].astype(F32)
    up_grad[...] = mlp_all[1].astype(F32)
    down_grad[...] = mlp_all[2].astype(F32)
    swap_wait(split, out, out_all, local.at[3], sems, last)
    out_grad[...] = restore_rows(out_all[...].astype(F32))
    for one in tiny:
        one.wait()
    small_all[me] = own[...]
    small[...] = small_all[...]


def collect(one_sums, two_sums, shift, qkv, mlp, out, cid):
    n = N_XZ + 4 * N_TP + 1
    wide = jax.ShapeDtypeStruct((16, FF), F32)
    return pl.pallas_call(
        kernel_collect,
        out_shape=(
            jax.ShapeDtypeStruct((TP, 16, BLOCK), F32),
            jax.ShapeDtypeStruct((16, 3 * D), F32),
            wide,
            wide,
            wide,
            jax.ShapeDtypeStruct((16, D), F32),
        ),
        in_specs=[VM] * 3 + [ANY] * 3,
        out_specs=(VM,) * 6,
        scratch_shapes=[
            pltpu.VMEM((16, 16, BLOCK), F32),
            pltpu.VMEM((16, 16, BLOCK), F32),
            pltpu.VMEM((16, BLOCK), F32),
            pltpu.VMEM((TP, 16, BLOCK), F32),
            pltpu.VMEM((TP, 16, 3 * HD), BF),
            pltpu.VMEM((3, 16, FF), BF),
            pltpu.VMEM((16, D), BF),
            pltpu.SemaphoreType.DMA((4,)),
            pltpu.SemaphoreType.DMA((n,)),
            pltpu.SemaphoreType.DMA((n,)),
        ],
        compiler_params=params(cid),
        name="collect",
    )(one_sums, two_sums, shift, qkv, mlp, out)


def body(
    hidden_in,
    cotangent,
    seq_lengths,
    slot_block,
    ln1_gain,
    ln1_bias,
    w_qkv,
    qkv_bias,
    w_out,
    ln2_gain,
    ln2_bias,
    w_gate,
    w_up,
    w_down,
):
    f32 = F32
    zh = lax.axis_index("zh")
    y = lax.axis_index("y")
    core = lax.axis_index("core")
    xz = lax.axis_index("x") * 4 + zh * 2 + lax.axis_index("zl")

    small, first = jnp.zeros(BLOCK, f32), 0
    pieces = (ln1_gain, ln1_bias, ln2_gain, ln2_bias, qkv_bias, seq_lengths[0], slot_block[0])
    for piece in pieces:
        n = piece.shape[0]
        small = small + jnp.pad(piece.astype(f32), (first, BLOCK - first - n))
        first += n
    small_all, gains, shift, qkv_full, mlp_rows, out_rows, hidden, one_all = front(
        small.reshape(1, BLOCK), hidden_in[0], w_qkv, w_gate, w_up, w_down, w_out, 0
    )
    qkv_full = qkv_full.reshape(D, 3 * HD)
    mlp_full = lax.all_gather(mlp_rows.reshape(3, BLOCK, FP), XZ, axis=0, tiled=False)
    small_all = small_all.reshape(BLOCK, BLOCK)

    plan = lax.dynamic_slice_in_dim(small_all, xz * TP + y * 2, 2, 0)[:, 112:122].astype(jnp.int32)
    blocks = plan[:, 2:].reshape(2, 2, 4)
    own_blocks = lax.dynamic_index_in_dim(blocks, zh, axis=1, keepdims=False)
    other_blocks = lax.dynamic_index_in_dim(blocks, 1 - zh, axis=1, keepdims=False)
    start = jnp.concatenate([own_blocks, other_blocks], axis=1) * BLOCK
    first_pad = (plan[:, 0:1] + BLOCK - 1) // BLOCK * BLOCK
    second = (start >= first_pad).astype(jnp.int32)
    limit = jnp.where(second == 1, plan[:, 1:2], plan[:, 0:1])
    table = jnp.stack([start - second * first_pad, second, limit], axis=1)
    queries, kv, lse, attended, grad_out, out_full, middle, grad_all, two_all = attend(
        table, one_all, qkv_full, shift, cotangent[0], out_rows, hidden, gains, 6
    )
    middle_grad, two_sums, branch, other_queries, other_lse, mlp_out, mlp_part = mlp(
        two_all, grad_all, mlp_full, middle, grad_out, gains, queries, lse, 3
    )
    mlp_sum = lax.psum_scatter(
        mlp_part.reshape(16 * 3 * BLOCK, FP), XZ, scatter_dimension=0, tiled=True
    )
    joined_grad, out_part, hidden_out = attend_back(
        table,
        branch,
        out_full,
        attended,
        queries,
        kv,
        lse,
        other_queries,
        other_lse,
        mlp_out,
        middle,
        7,
    )
    input_grad, one_sums, shift_sum, qkv_sum, out_sum = qkv_back(
        joined_grad, qkv_full, hidden, middle_grad, gains, one_all, out_part, 4
    )

    small_sum, qkv_grad, gate_sum, up_sum, down_sum, out_grad = collect(
        one_sums,
        two_sums,
        shift_sum,
        qkv_sum.reshape(TP, 16, FP),
        mlp_sum.reshape(3, TP, 16, FP),
        out_sum,
        5,
    )
    vectors = jnp.sum(small_sum[:, :4], axis=0)
    vectors = lax.dynamic_slice_in_dim(vectors, (y * 2 + core) * 16, 16, 1)
    shift_grad = small_sum[:, 8:14].reshape(4, 2, 3, HD).transpose(2, 1, 0, 3).reshape(128, 48)
    row = (zh * 4 + y) * 16 + lax.axis_index("x") * 4 + lax.axis_index("zl") * 2 + core
    shift_grad = lax.dynamic_index_in_dim(shift_grad, row, 0, False)
    return (
        hidden_out[None],
        input_grad[None],
        vectors[0],
        vectors[1],
        qkv_grad,
        shift_grad,
        out_grad,
        vectors[2],
        vectors[3],
        gate_sum,
        up_sum,
        down_sum,
    )


def solution(mesh):
    inner = Mesh(mesh.devices.reshape(2, 4, 4, 2, 2), ROWS)
    rows = P(ROWS)
    tokens = P(GRP, SLOT, None)
    placed = (
        tokens,
        tokens,
        P(GRP, None),
        P(GRP, None),
        rows,
        rows,
        P(ROWS, None),
        rows,
        P(ROWS, None),
        rows,
        rows,
        P(ROWS, None),
        P(ROWS, None),
        P(ROWS, None),
    )
    return jax.shard_map(
        body,
        mesh=inner,
        in_specs=placed,
        out_specs=(
            tokens,
            tokens,
            rows,
            rows,
            P(ROWS, None),
            rows,
            P(ROWS, None),
            rows,
            rows,
            P(ROWS, None),
            P(ROWS, None),
            P(ROWS, None),
        ),
        check_vma=False,
    )
```

```python
import functools

import jax
import jax.numpy as jnp
from jax import lax
from jax.experimental import pallas as pl
from jax.experimental.pallas import tpu as pltpu
from jax.sharding import Mesh
from jax.sharding import PartitionSpec as P

D = 2048
HEADS = 32
HEAD_DIM = 64
ROT = 16
FF = 5632
BLOCK = 128
TP = 8
HD = D // TP
FC = FF // TP

EPS = 1e-05
NEG = -1e30
SCALE = HEAD_DIM ** (-0.5)
TPA = ("y", "core")
ZX = ("zh", "zl", "x")
ROWS = ("zh", "y", "x", "zl", "core")
GRP = ("x", "zl", "core")
SLOT = ("zh", "y")


def permute_rows(row):
    group = lane(BLOCK) // 32
    tiles = []
    for x in range(4):
        for zh in range(2):
            for zl in range(2):
                out = None
                for y in range(4):
                    first = zh * 1024 + y * 256 + x * 64 + zl * 32
                    tile = first // BLOCK * BLOCK
                    shift = (32 * y - first % BLOCK) % BLOCK
                    value = row[:, tile : tile + BLOCK]
                    value = pltpu.roll(value, shift, 1) if shift else value
                    out = value if out is None else jnp.where(group == y, value, out)
                tiles.append(out)
    return jnp.concatenate(tiles, axis=1)


def restore_rows(row):
    group = lane(BLOCK) // 32
    tiles = []
    for t in range(D // BLOCK):
        out = None
        for j in range(4):
            first = t * BLOCK + 32 * j
            zh, y, x, zl = first // 1024, first // 256 % 4, first // 64 % 4, first // 32 % 2
            tile = (x * 4 + zh * 2 + zl) * BLOCK
            shift = (32 * j - 32 * y) % BLOCK
            value = row[:, tile : tile + BLOCK]
            value = pltpu.roll(value, shift, 1) if shift else value
            out = value if out is None else jnp.where(group == j, value, out)
        tiles.append(out)
    return jnp.concatenate(tiles, axis=1)


def layer_norm(values):
    average = jnp.mean(values, axis=-1, keepdims=True)
    centred = values - average
    inv_scale = lax.rsqrt(jnp.mean(centred * centred, axis=-1, keepdims=True) + EPS)
    return centred * inv_scale, inv_scale


def norm_back(grad_in, normed, inv_scale, gain):
    scaled = grad_in * gain
    return inv_scale * (
        scaled
        - jnp.mean(scaled, axis=-1, keepdims=True)
        - normed * jnp.mean(scaled * normed, axis=-1, keepdims=True)
    )


FP = 768
HALF = BLOCK // 2
ANY = pl.BlockSpec(memory_space=pl.ANY)
VM = pl.BlockSpec(memory_space=pltpu.VMEM)
BF = jnp.bfloat16
F32 = jnp.float32


def params(cid):
    return pltpu.CompilerParams(
        collective_id=cid, has_side_effects=True, vmem_limit_bytes=56 * 1024 * 1024
    )


def meet(peers):
    barrier = pltpu.get_barrier_semaphore()
    for peer in peers:
        pl.semaphore_signal(
            barrier, inc=1, device_id=peer, device_id_type=pl.DeviceIdType.MESH
        )
    pl.semaphore_wait(barrier, len(peers))


def remote(sems, i, src, dst, peer):
    return pltpu.make_async_remote_copy(
        src_ref=src,
        dst_ref=dst,
        send_sem=sems[0].at[i],
        recv_sem=sems[1].at[i],
        device_id=peer,
        device_id_type=pl.DeviceIdType.MESH,
    )


def ring():
    y = lax.axis_index("y")
    c = lax.axis_index("core")
    up = lax.rem(y + 1, 4)
    opp = lax.rem(y + 2, 4)
    dn = lax.rem(y + 3, 4)
    return y, c, up, opp, dn


def ring_peers(up, dn, c):
    return {"y": up}, {"y": dn}, {"core": 1 - c}


N_AG = 11
N_RS = 10


class RingGather:
    def __init__(self, own, full, local_sem, sems):
        y, c, up, opp, dn = ring()
        to_up, to_dn, to_sib = ring_peers(up, dn, c)
        first, last = pl.ds(0, HALF), pl.ds(HALF, HALF)
        cp = functools.partial(remote, sems)

        def pass_on(i, block, peer, *rows):
            ref = full.at[(block, c) + rows]
            return cp(i, ref, ref, peer)

        self.up1 = cp(0, own.at[first], full.at[y, c, first], to_up)
        self.dn1 = cp(1, own.at[last], full.at[y, c, last], to_dn)
        self.up2 = cp(2, own.at[last], full.at[y, c, last], to_up)
        self.dn2 = cp(3, own.at[first], full.at[y, c, first], to_dn)
        self.here = pltpu.make_async_copy(own, full.at[y, c], local_sem)
        self.far1 = pass_on(5, dn, to_up, first)
        self.far2 = pass_on(6, up, to_dn, last)
        self.sib = [
            cp(4, own, full.at[y, c], to_sib),
            pass_on(7, dn, to_sib),
            pass_on(8, up, to_sib),
            pass_on(9, opp, to_sib, first),
            pass_on(10, opp, to_sib, last),
        ]

    def start(self):
        for one in (self.up1, self.dn1, self.up2, self.dn2, self.sib[0], self.here):
            one.start()

    def forward(self):
        self.up1.wait_recv()
        self.far1.start()
        self.dn1.wait_recv()
        self.far2.start()

    def share(self):
        self.up2.wait_recv()
        self.sib[1].start()
        self.dn2.wait_recv()
        self.sib[2].start()

    def share_far(self):
        self.far1.wait_recv()
        self.sib[3].start()
        self.far2.wait_recv()
        self.sib[4].start()

    def sends(self):
        return [self.up1, self.dn1, self.up2, self.dn2, self.far1, self.far2] + self.sib

    def finish(self):
        for one in self.sib:
            one.wait_recv()
        self.here.wait()
        for one in self.sends():
            one.wait_send()

    def run(self, work=None):
        for step in (self.start, self.forward, self.share, self.share_far):
            step()
            if work is not None:
                work()
        self.finish()


def rows_loop(count, step, body):
    @pl.loop(0, count // step)
    def _(i):
        body(pl.ds(pl.multiple_of(i * step, step), step))


RS_SCRATCH = [
    pltpu.VMEM((4, BLOCK, D), F32),
    pltpu.VMEM((4, BLOCK, D), BF),
    pltpu.VMEM((4, BLOCK, D), BF),
    pltpu.VMEM((2, HALF, D), BF),
    pltpu.VMEM((2, HALF, D), BF),
    pltpu.VMEM((2, BLOCK, D), BF),
    pltpu.VMEM((2, BLOCK, D), BF),
    pltpu.SemaphoreType.DMA((N_RS,)),
    pltpu.SemaphoreType.DMA((N_RS,)),
]


class RingScatter:
    def __init__(self, mine, sib_out, sib_in, far_out, far_in, near_out, near_in, *sems):
        y, c, up, opp, dn = ring()
        to_up, to_dn, to_sib = ring_peers(up, dn, c)
        first, last = pl.ds(0, HALF), pl.ds(HALF, HALF)
        cp = functools.partial(remote, sems)
        self.order = (opp, up, dn, y)
        self.mine, self.sib_in = mine, sib_in
        self.far_out, self.far_in = far_out, far_in
        self.near_out, self.near_in = near_out, near_in
        self.sib = [cp(j, sib_out(j), sib_in.at[j], to_sib) for j in range(4)]
        self.far = [
            cp(4, far_out.at[0], far_in.at[0], to_up),
            cp(5, far_out.at[1], far_in.at[1], to_dn),
        ]
        self.early = [
            cp(6, near_out.at[0, last], near_in.at[0, last], to_up),
            cp(7, near_out.at[1, first], near_in.at[1, first], to_dn),
        ]
        self.late = [
            cp(8, near_out.at[0, first], near_in.at[0, first], to_up),
            cp(9, near_out.at[1, last], near_in.at[1, last], to_dn),
        ]

    def both(self, j, rows):
        return self.mine(j, rows) + self.sib_in[j, rows, :].astype(F32)

    def send_far(self):
        self.sib[0].wait_recv()
        for k in range(2):

            def add(r, k=k):
                q = pl.ds(k * HALF + r.start, r.size)
                self.far_out[k, r, :] = self.both(0, q).astype(BF)

            rows_loop(HALF, 32, add)
            self.far[k].start()

    def send_early(self, k):
        self.sib[1 + k].wait_recv()

        def add(r):
            q = pl.ds((1 - k) * HALF + r.start, r.size)
            self.near_out[k, q, :] = self.both(1 + k, q).astype(BF)

        rows_loop(HALF, 32, add)
        self.early[k].start()

    def send_late(self):
        for k in range(2):
            self.far[k].wait_recv()

            def add(r, k=k):
                q = pl.ds(k * HALF + r.start, r.size)
                self.near_out[k, q, :] = (
                    self.both(1 + k, q) + self.far_in[k, r, :].astype(F32)
                ).astype(BF)

            rows_loop(HALF, 32, add)
            self.late[k].start()

    def wait(self):
        self.sib[3].wait_recv()
        for one in self.early + self.late:
            one.wait_recv()

    def total(self, rows):
        return (
            self.both(3, rows)
            + self.near_in[0, rows, :].astype(F32)
            + self.near_in[1, rows, :].astype(F32)
        )

    def finish(self):
        for one in self.sib + self.far + self.early + self.late:
            one.wait_send()


def ring_scatter(partial, scratch, between=None):
    part, sib_out = scratch[:2]
    c = lax.axis_index("core")
    scatter = RingScatter(
        lambda j, rows: part[j, rows, :], lambda j: sib_out.at[j], *scratch[2:]
    )

    def produce(j):
        def put(columns, value):
            part[j, :, columns] = jnp.where(c == 0, value[0], value[1])
            sib_out[j, :, columns] = jnp.where(c == 0, value[1], value[0]).astype(BF)

        partial(scatter.order[j], put)
        scatter.sib[j].start()

    produce(0)
    produce(1)
    scatter.send_far()
    scatter.send_early(0)
    produce(2)
    scatter.send_early(1)
    scatter.send_late()
    produce(3)
    if between is not None:
        between()
    scatter.wait()
    return scatter


AG_SCRATCH = [
    pltpu.VMEM((BLOCK, D), BF),
    pltpu.SemaphoreType.DMA,
    pltpu.SemaphoreType.DMA((N_AG,)),
    pltpu.SemaphoreType.DMA((N_AG,)),
]
FULL = jax.ShapeDtypeStruct((4, 2, BLOCK, D), BF)


def order_out(gathered, weight):
    for x in range(4):
        for zl in range(2):
            for a in range(2):
                row = x * 64 + zl * 32 + a * 16
                weight[row : row + 16, :] = gathered[x, a * 2 + zl]


OUT_ROWS = pltpu.VMEM((HD, D), BF)


NN = (((1,), (0,)), ((), ()))
NT = (((1,), (1,)), ((), ()))
TN = (((0,), (0,)), ((), ()))
TOKENS = 4 * BLOCK
KEYS = 2 * TOKENS
TILE = 2 * BLOCK


def dot(a, b, dims):
    return lax.dot_general(a, b, dims, preferred_element_type=F32)


def lane(n):
    return lax.broadcasted_iota(jnp.int32, (1, n), 1)


def turn_tables(base):
    entry = lax.rem(lane(BLOCK), HEAD_DIM)
    freq = jnp.exp(
        lax.rem(entry, ROT // 2).astype(F32) * (-2.0 / ROT * 9.210340371976184)
    )
    freq = jnp.where(entry < ROT, freq, 0.0)
    place = (base + lax.broadcasted_iota(jnp.int32, (BLOCK, 1), 0)).astype(F32)
    phase = place * freq
    return jnp.cos(phase), jnp.sin(phase)


def turn(v, cosine, sines, direction):
    entry = lax.rem(lane(BLOCK), HEAD_DIM)
    s = sines * direction
    ahead = pltpu.roll(v, BLOCK - ROT // 2, 1)
    behind = pltpu.roll(v, ROT // 2, 1)
    return v * cosine + jnp.where(entry < ROT // 2, -ahead, behind) * s


def key_bias(table, g, tile, blocks, q_part=0):
    token = lane(BLOCK)
    q_code, q_low = [], []
    for j in range(2):
        block = 4 * q_part + 2 * tile + j
        low = table[g, 1, block] * 4096
        q_code.append(low + table[g, 0, block] + token)
        q_low.append(low + jnp.zeros_like(token))
    q_code = jnp.concatenate(q_code, axis=1)
    q_low = jnp.concatenate(q_low, axis=1)
    column = lax.broadcasted_iota(jnp.int32, (BLOCK, 1), 0)
    rows = []
    for k in blocks:
        place = table[g, 0, k] + column
        code = jnp.where(place < table[g, 2, k], table[g, 1, k] * 4096 + place, 1 << 20)
        kept = jnp.logical_and(code <= q_code, code >= q_low)
        rows.append(jnp.where(kept, 0.0, NEG))
    return jnp.concatenate(rows, axis=0)


def head_mask(h):
    first = lane(BLOCK) < HEAD_DIM
    return jnp.where(first if h == 0 else jnp.logical_not(first), 1.0, 0.0).astype(BF)


def load(pairs, sems, first=0):
    copies = []
    for i, (src, dst) in enumerate(pairs):
        copies.append(pltpu.make_async_copy(src, dst, sems.at[first + i]))
        copies[-1].start()
    return copies


def kernel_attend(
    table,
    tokens_hbm,
    weight_hbm,
    shift,
    cotangent,
    out_in,
    hidden,
    gains,
    queries,
    kv,
    lse,
    attended,
    grad_out,
    out_full,
    middle,
    grad_all,
    two_all,
    out_rows,
    out_weight,
    own_two,
    tokens,
    weight,
    cosines,
    sines,
    tops,
    totals,
    mixed,
    local,
    send,
    recv,
    *sems,
):
    partner = {"zh": 1 - lax.axis_index("zh")}
    weight_in, *token_in = load(
        [(weight_hbm, weight)] + [(tokens_hbm.at[y], tokens.at[y]) for y in range(4)], local
    )
    y0, c, up, opp, dn = ring()
    out_rows[...] = permute_rows(out_in[...].astype(F32)).astype(BF)
    meet(list(ring_peers(up, dn, c)) + plane_peers())
    gather = RingGather(grad_out, grad_all, sems[0], sems[1:3])
    plane = PlaneGather(out_rows, out_full, *sems[3:6], 0)
    two_gather = RingGather(own_two, two_all, sems[6], sems[7:9])
    part, sib_out = sems[9:11]
    scatter = RingScatter(
        lambda j, rows: part[j, rows, :], lambda j: sib_out.at[j], *sems[11:]
    )
    plane.start()
    lse[...] = jnp.zeros_like(lse)
    weight_in.wait()
    for y in range(4):
        at = slice(y * BLOCK, (y + 1) * BLOCK)
        for g in range(2):
            cosine, sine = turn_tables(table[g, 0, y])
            cosines[g, at, :] = cosine
            sines[g, at, :] = sine
        token_in[y].wait()
        new = dot(tokens[y].reshape(TILE, D), weight[:, HD:], NN) + shift[:, HD:]
        for g in range(2):
            rows = slice(g * BLOCK, (g + 1) * BLOCK)
            for pair in range(2):
                q = slice(pair * BLOCK, (pair + 1) * BLOCK)
                turned = turn(new[rows, q], cosines[g, at, :], sines[g, at, :], 1.0)
                kv[0, g, at, q] = turned.astype(BF)
            kv[1, g, at, :] = new[rows, HD:].astype(BF)

    own, other = pl.ds(0, TOKENS), pl.ds(TOKENS, TOKENS)
    trade = [
        remote((send, recv), g, kv.at[:, g, own, :], kv.at[:, g, other, :], partner)
        for g in range(2)
    ]
    for one in trade:
        one.start()
    plane.middle()
    base, limit = table[c, 0, y0], table[c, 2, y0]

    def mask(r):
        place = base + r.start + lax.broadcasted_iota(jnp.int32, (16, 1), 0)
        row = jnp.where(place < limit, cotangent[r, :].astype(F32), 0.0)
        grad_out[r, :] = permute_rows(row).astype(BF)

    rows_loop(BLOCK, 16, mask)
    gather.start()
    for y in range(4):
        at = slice(y * BLOCK, (y + 1) * BLOCK)
        new = dot(tokens[y].reshape(TILE, D), weight[:, :HD], NN) + shift[:, :HD]
        for g in range(2):
            rows = slice(g * BLOCK, (g + 1) * BLOCK)
            for pair in range(2):
                q = slice(pair * BLOCK, (pair + 1) * BLOCK)
                turned = turn(new[rows, q], cosines[g, at, :], sines[g, at, :], 1.0)
                queries[g, at, q] = turned.astype(BF) * jnp.asarray(SCALE, BF)

    first_head = lax.broadcasted_iota(jnp.int32, (BLOCK, 1), 0) < HEAD_DIM

    def work(part, g):
        rows = slice(part * TOKENS, (part + 1) * TOKENS)

        @pl.loop(0, 2)
        def _(tile):
            at = pl.ds(pl.multiple_of(tile * TILE, TILE), TILE)
            bias = key_bias(table, g, tile, range(4 * part, 4 * part + 4))
            for pair in range(2):
                q = slice(pair * BLOCK, (pair + 1) * BLOCK)
                k_all = kv[0, g, rows, q]
                v_all = kv[1, g, rows, q]
                out = jnp.zeros((BLOCK, TILE), F32)
                keep, share = [], []
                for h in range(2):
                    row = slice(2 * pair + h, 2 * pair + h + 1)
                    s = dot(k_all, queries[g, at, q] * head_mask(h), NT) + bias
                    top = jnp.max(s, axis=0, keepdims=True)
                    if part == 1:
                        top = jnp.maximum(top, tops[g, row, at])
                    p = jnp.exp(s - top)
                    total = jnp.sum(p, axis=0, keepdims=True)
                    out = out + dot(v_all * head_mask(h), p.astype(BF), TN)
                    if part == 0:
                        tops[g, row, at] = top
                        totals[g, row, at] = total
                    else:
                        keep.append(jnp.exp(tops[g, row, at] - top))
                        total = total + totals[g, row, at] * keep[h]
                        lse[g, row, at] = top + jnp.log(total)
                        share.append(1.0 / total)
                if part == 0:
                    mixed[g, q, at] = out
                else:
                    out = out + mixed[g, q, at] * jnp.where(first_head, keep[0], keep[1])
                    out = (out * jnp.where(first_head, share[0], share[1])).T.astype(BF)
                    for j in range(2):
                        attended[2 * tile + j, g, :, q] = out[j * BLOCK : (j + 1) * BLOCK]

    def project(g):
        for j in range(4):
            a = attended[scatter.order[j], g]
            for i in range(4):
                q = slice(i * 512, (i + 1) * 512)
                value = dot(a, out_weight[:, q], NN)

                @pl.when(c == g)
                def _(j=j, q=q, value=value):
                    part[j, :, q] = value

                @pl.when(c != g)
                def _(j=j, q=q, value=value):
                    sib_out[j, :, q] = value.astype(BF)

            @pl.when(c != g)
            def _(j=j):
                scatter.sib[j].start()

    def norm(r):
        row = hidden[r, :].astype(F32) + scatter.total(r)
        middle[r, :] = row
        normed, _ = layer_norm(row)
        own_two[r, :] = (normed * gains[2:3, :] + gains[3:4, :]).astype(BF)

    def exchange():
        scatter.send_far()
        scatter.send_early(0)
        scatter.send_early(1)

    def settle():
        scatter.send_late()
        scatter.wait()
        rows_loop(BLOCK, 16, norm)
        two_gather.start()

    def pass_on():
        two_gather.forward()
        two_gather.share()
        two_gather.share_far()

    work(0, 0)
    plane.forward()
    gather.forward()
    work(0, 1)
    gather.share()
    plane.finish()
    order_out(out_full, out_weight)
    trade[0].wait_recv()
    work(1, 0)
    project(0)
    gather.share_far()

    @pl.when(c == 0)
    def _():
        exchange()

    trade[1].wait_recv()
    work(1, 1)
    project(1)

    @pl.when(c == 1)
    def _():
        exchange()

    settle()
    pass_on()

    for one in trade:
        one.wait_send()
    gather.finish()
    two_gather.finish()
    scatter.finish()


SM = pl.BlockSpec(memory_space=pltpu.SMEM)


def attend(table, tokens, weight, shift, cotangent, out_in, hidden, gains, cid):
    return pl.pallas_call(
        kernel_attend,
        out_shape=(
            jax.ShapeDtypeStruct((2, TOKENS, HD), BF),
            jax.ShapeDtypeStruct((2, 2, KEYS, HD), BF),
            jax.ShapeDtypeStruct((2, 8, TOKENS), F32),
            jax.ShapeDtypeStruct((4, 2, BLOCK, HD), BF),
            jax.ShapeDtypeStruct((BLOCK, D), BF),
            jax.ShapeDtypeStruct((4, 4, 16, D), BF),
            jax.ShapeDtypeStruct((BLOCK, D), F32),
            FULL,
            FULL,
        ),
        in_specs=[SM, ANY, ANY] + [VM] * 5,
        out_specs=(VM,) * 7 + (ANY, ANY),
        scratch_shapes=[
            pltpu.VMEM((16, D), BF),
            OUT_ROWS,
            pltpu.VMEM((BLOCK, D), BF),
            pltpu.VMEM((4, 2, BLOCK, D), BF),
            pltpu.VMEM((D, 3 * HD), BF),
            pltpu.VMEM((2, TOKENS, BLOCK), F32),
            pltpu.VMEM((2, TOKENS, BLOCK), F32),
            pltpu.VMEM((2, 8, TOKENS), F32),
            pltpu.VMEM((2, 8, TOKENS), F32),
            pltpu.VMEM((2, HD, TOKENS), F32),
            pltpu.SemaphoreType.DMA((5,)),
            pltpu.SemaphoreType.DMA((2,)),
            pltpu.SemaphoreType.DMA((2,)),
        ]
        + AG_SCRATCH[1:]
        + PG_SEMS
        + AG_SCRATCH[1:]
        + RS_SCRATCH,
        compiler_params=params(cid),
        name="attend",
    )(table, tokens, weight, shift, cotangent, out_in, hidden, gains)


def kernel_attend_back(
    table,
    branch_own,
    gathered,
    attended,
    queries,
    kv,
    lse,
    other_queries,
    other_lse,
    mlp_out,
    middle_hbm,
    joined_grad,
    out_part,
    hidden_out,
    branch,
    middle,
    own_out,
    probs,
    other_probs,
    local,
    weight,
    grads,
    other_grads,
    dq,
    mean,
    other_mean,
    dkv,
    send,
    recv,
    local_sem,
    gather_send,
    gather_recv,
    *scratch,
):
    partner = {"zh": 1 - lax.axis_index("zh")}
    y0, c, up, opp, dn = ring()
    order = (opp, up, dn, y0)
    out_in = load([(mlp_out.at[order[j], c], own_out.at[j]) for j in range(4)], local)
    (middle_in,) = load([(middle_hbm, middle)], local, 4)
    meet(list(ring_peers(up, dn, c)) + [partner])
    gather = RingGather(branch_own, branch, local_sem, (gather_send, gather_recv))
    gather.start()
    scatter = RingScatter(
        lambda j, rows: own_out[j, rows, :].astype(F32),
        lambda j: mlp_out.at[order[j], 1 - c],
        *scratch,
    )
    for one in scatter.sib:
        one.start()
    order_out(gathered, weight)
    trade = [
        remote((send, recv), 0, grads, other_grads, partner),
        remote((send, recv), 1, mean, other_mean, partner),
    ]

    def recompute(part, g):
        q_src, lse_src = (queries, lse) if part == 0 else (other_queries, other_lse)
        dst = probs if part == 0 else other_probs
        blocks = range(8) if part == 0 else range(4)
        rows = slice(0, len(blocks) * BLOCK)

        @pl.loop(0, 2)
        def _(tile):
            at = pl.ds(pl.multiple_of(tile * TILE, TILE), TILE)
            bias = key_bias(table, g, tile, blocks, part)
            for pair in range(2):
                q = slice(pair * BLOCK, (pair + 1) * BLOCK)
                for h in range(2):
                    row = slice(2 * pair + h, 2 * pair + h + 1)
                    s = dot(kv[0, g, rows, q], q_src[g, at, q] * head_mask(h), NT) + bias
                    dst[g, tile, 2 * pair + h] = jnp.exp(s - lse_src[g, row, at])

    recompute(0, 0)
    gather.forward()
    recompute(0, 1)
    gather.share()
    gather.share_far()
    recompute(1, 0)
    recompute(1, 1)
    gather.finish()

    dq[...] = jnp.zeros_like(dq)
    dkv[...] = jnp.zeros_like(dkv)
    mean[...] = jnp.zeros_like(mean)
    heads = jnp.concatenate([head_mask(0), head_mask(1)] * 8, axis=0)
    for y in range(4):
        at = slice(y * BLOCK, (y + 1) * BLOCK)
        new = dot(branch[y].reshape(TILE, D), weight[...], NT)
        for g in range(2):
            rows = slice(g * BLOCK, (g + 1) * BLOCK)
            grads[g, at, :] = new[rows].astype(BF)
    for g in range(2):
        for pair in range(2):
            q = slice(pair * BLOCK, (pair + 1) * BLOCK)
            mixed = attended[:, g, :, q].reshape(TOKENS, BLOCK).astype(F32)
            mixed = mixed * grads[g, :, q].astype(F32)
            high = mixed.astype(BF)
            low = (mixed - high.astype(F32)).astype(BF)
            both = dot(heads, high, NT) + dot(heads, low, NT)
            mean[g, 2 * pair : 2 * pair + 2, :] = both[0:2]
    for one in trade:
        one.start()
    for one in out_in:
        one.wait()
    scatter.send_far()
    scatter.send_early(0)
    scatter.send_early(1)

    def back(part, g):
        q_src, g_src = (queries, grads) if part == 0 else (other_queries, other_grads)
        mean_src, p_src = (mean, probs) if part == 0 else (other_mean, other_probs)
        rows = slice(0, KEYS if part == 0 else TOKENS)

        @pl.loop(0, 2)
        def _(tile):
            at = pl.ds(pl.multiple_of(tile * TILE, TILE), TILE)
            for pair in range(2):
                q = slice(pair * BLOCK, (pair + 1) * BLOCK)
                k_all = kv[0, g, rows, q]
                v_all = kv[1, g, rows, q]
                new_q = jnp.zeros((BLOCK, TILE), F32)
                new_k = jnp.zeros((TOKENS, BLOCK), F32)
                new_v = jnp.zeros((TOKENS, BLOCK), F32)
                for h in range(2):
                    row = slice(2 * pair + h, 2 * pair + h + 1)
                    q_head = q_src[g, at, q] * head_mask(h)
                    g_head = g_src[g, at, q] * head_mask(h)
                    p = p_src[g, tile, 2 * pair + h]
                    p_grad = dot(v_all, g_head, NT)
                    s_grad = (p * (p_grad - mean_src[g, row, at])).astype(BF)
                    new_v = new_v + dot(p[:TOKENS].astype(BF), g_head, NN)
                    new_k = new_k + dot(s_grad[:TOKENS], q_head, NN)
                    if part == 0:
                        new_q = new_q + dot(k_all * head_mask(h), s_grad, TN)
                if part == 0:
                    dq[g, q, at] += new_q
                dkv[0, g, :, q] += new_k
                dkv[1, g, :, q] += new_v

    back(0, 0)
    scatter.send_late()
    back(0, 1)

    for i in range(2):
        q = slice(i * 1024, (i + 1) * 1024)
        new = dot(attended[...].reshape(8 * BLOCK, HD), branch[:, :, :, q].reshape(8 * BLOCK, 1024), TN)
        for x in range(4):
            for zl in range(2):
                for a in range(2):
                    row = x * 64 + zl * 32 + a * 16
                    out_part[x * 4 + a * 2 + zl, :, q] = new[row : row + 16].astype(BF)

    for one in trade:
        one.wait_recv()
    back(1, 0)
    back(1, 1)
    scatter.wait()
    middle_in.wait()

    def add(r):
        hidden_out[r, :] = restore_rows(middle[r, :] + scatter.total(r)).astype(BF)

    rows_loop(BLOCK, 16, add)
    for g in range(2):

        @pl.loop(0, 4)
        def _(y, g=g):
            at = pl.ds(pl.multiple_of(y * BLOCK, BLOCK), BLOCK)
            cosine, sine = turn_tables(table[g, 0, y])
            for pair in range(2):
                q = slice(pair * BLOCK, (pair + 1) * BLOCK)
                new = dq[g, q, at].T * SCALE
                joined_grad[y, g, :, q] = turn(new, cosine, sine, -1.0).astype(BF)
                joined_grad[y, g, :, HD + pair * BLOCK : HD + (pair + 1) * BLOCK] = turn(
                    dkv[0, g, at, q], cosine, sine, -1.0
                ).astype(BF)
            joined_grad[y, g, :, 2 * HD :] = dkv[1, g, at, :].astype(BF)

    for one in trade:
        one.wait_send()
    scatter.finish()


def attend_back(
    table,
    branch,
    gathered,
    attended,
    queries,
    kv,
    lse,
    other_queries,
    other_lse,
    mlp_out,
    middle,
    cid,
):
    return pl.pallas_call(
        kernel_attend_back,
        out_shape=(
            jax.ShapeDtypeStruct((4, 2, BLOCK, 3 * HD), BF),
            jax.ShapeDtypeStruct((16, 16, D), BF),
            jax.ShapeDtypeStruct((BLOCK, D), BF),
        ),
        in_specs=[SM] + [VM] * 8 + [ANY, ANY],
        out_specs=(VM, VM, VM),
        scratch_shapes=[
            pltpu.VMEM((4, 2, BLOCK, D), BF),
            pltpu.VMEM((BLOCK, D), F32),
            pltpu.VMEM((4, BLOCK, D), BF),
            pltpu.VMEM((2, 2, 4, KEYS, TILE), F32),
            pltpu.VMEM((2, 2, 4, TOKENS, TILE), F32),
            pltpu.SemaphoreType.DMA((5,)),
            OUT_ROWS,
            pltpu.VMEM((2, TOKENS, HD), BF),
            pltpu.VMEM((2, TOKENS, HD), BF),
            pltpu.VMEM((2, HD, TOKENS), F32),
            pltpu.VMEM((2, 8, TOKENS), F32),
            pltpu.VMEM((2, 8, TOKENS), F32),
            pltpu.VMEM((2, 2, TOKENS, HD), F32),
            pltpu.SemaphoreType.DMA((2,)),
            pltpu.SemaphoreType.DMA((2,)),
        ]
        + AG_SCRATCH[1:]
        + RS_SCRATCH[2:],
        compiler_params=params(cid),
        name="attend_back",
    )(
        table,
        branch,
        gathered,
        attended,
        queries,
        kv,
        lse,
        other_queries,
        other_lse,
        mlp_out,
        middle,
    )


def kernel_mlp(
    two_hbm,
    grad_hbm,
    w_hbm,
    middle,
    grad_out,
    gains,
    queries,
    lse,
    middle_grad,
    sums,
    own,
    other_queries,
    other_lse,
    out_hbm,
    part_hbm,
    two,
    grad_all,
    w,
    out_part,
    mlp_part,
    inner,
    both_grads,
    local,
    leave,
    send,
    recv,
    *scratch,
):
    y, c, up, opp, dn = ring()
    partner = {"zh": 1 - lax.axis_index("zh")}
    order = (opp, up, dn, y)
    first = order[0]
    loads = load([(two_hbm.at[first], two.at[first])], local)
    weights_in = [
        load([(w_hbm.at[z, :, k], w.at[k, :, z]) for z in range(4)], local, 8 + 4 * k)
        for k in range(3)
    ]
    loads += load([(grad_hbm.at[first], grad_all.at[first])], local, 1)
    for i, b in enumerate(order[1:]):
        pairs = [(two_hbm.at[b], two.at[b]), (grad_hbm.at[b], grad_all.at[b])]
        loads += load(pairs, local, 2 + 2 * i)
    meet(list(ring_peers(up, dn, c)) + [partner])
    trade = [
        remote((send, recv), 0, queries, other_queries, partner),
        remote((send, recv), 1, lse, other_lse, partner),
    ]
    for one in trade:
        one.start()
    held = jnp.logical_or(lane(FP) >= BLOCK, y < 2)
    gate_lanes, up_lanes = pl.ds(0, FP), pl.ds(FP, FP)
    outs = []

    def arrive(k):
        loads.pop(0).wait()
        if not outs:
            for one in weights_in[k]:
                one.wait()

    def partial(block, put):
        arrive(0)
        a = two[block].reshape(TILE, D)
        gate = dot(a, w[0].reshape(D, FP), NN)
        if not outs:
            for one in weights_in[1]:
                one.wait()
        up_proj = dot(a, w[1].reshape(D, FP), NN)
        arrive(2)
        grad = dot(grad_all[block].reshape(TILE, D), w[2].reshape(D, FP), NN)
        sig = 1.0 / (1.0 + jnp.exp(-gate))
        active = gate * sig
        low = (active * up_proj).astype(BF)
        low_gate = (grad * up_proj * sig * (1.0 + gate * (1.0 - sig))).astype(BF)
        low_up = (grad * active).astype(BF)
        zero = jnp.zeros((), BF)
        inner[block] = jnp.where(held, low, zero).reshape(2, BLOCK, FP)
        both_grads[block, :, :, gate_lanes] = jnp.where(held, low_gate, zero).reshape(2, BLOCK, FP)
        both_grads[block, :, :, up_lanes] = jnp.where(held, low_up, zero).reshape(2, BLOCK, FP)

        low_gate = both_grads[block, :, :, gate_lanes].reshape(TILE, FP)
        low_up = both_grads[block, :, :, up_lanes].reshape(TILE, FP)
        for i in range(4):
            q = slice(i * 512, (i + 1) * 512)
            new = dot(low_gate, w[0, i].reshape(512, FP), NT)
            new = new + dot(low_up, w[1, i].reshape(512, FP), NT)
            put(q, new.reshape(2, BLOCK, 512))
        low = inner[block].reshape(TILE, FP)
        for i in range(4):
            q = slice(i * 512, (i + 1) * 512)
            new = dot(low, w[2, i].reshape(512, FP), NT)
            out_part[block, :, :, q] = new.astype(BF).reshape(2, BLOCK, 512)

        outs.extend(load([(out_part.at[block], out_hbm.at[block])], leave, len(outs)))

    done = []

    def weight_grads(count=1):
        begin = len(done)

        @pl.loop(begin, begin + count)
        def _(i):
            q = pl.ds(pl.multiple_of(i * TILE, TILE), TILE)
            a = two[:, :, :, q].reshape(TP * BLOCK, TILE)
            b = grad_all[:, :, :, q].reshape(TP * BLOCK, TILE)
            new = dot(a, both_grads[...].reshape(TP * BLOCK, 2 * FP), TN).astype(BF)
            at = pl.ds(2 * i, 2)
            mlp_part[at, 0] = new[:, :FP].reshape(2, BLOCK, FP)
            mlp_part[at, 1] = new[:, FP:].reshape(2, BLOCK, FP)
            new = dot(b, inner[...].reshape(TP * BLOCK, FP), TN).astype(BF)
            mlp_part[at, 2] = new.reshape(2, BLOCK, FP)

        for i in range(begin, begin + count):
            done.extend(
                load(
                    [(mlp_part.at[pl.ds(2 * i, 2)], part_hbm.at[pl.ds(i % 2 * 2, 2), i // 2])],
                    leave,
                    4 + i,
                )
            )

    scatter = ring_scatter(partial, scratch, lambda: weight_grads(8))
    sums[...] = jnp.zeros_like(sums)

    def back(r):
        row = scatter.total(r)
        normed, inv = layer_norm(middle[r, :])
        grad = grad_out[r, :].astype(F32) + norm_back(row, normed, inv, gains[2:3, :])
        middle_grad[r, :] = grad
        own[r, :] = grad.astype(BF)
        sums[0:1, :] += jnp.sum(row * normed, axis=0, keepdims=True)
        sums[1:2, :] += jnp.sum(row, axis=0, keepdims=True)

    rows_loop(BLOCK, 16, back)
    scatter.finish()
    for one in outs + done + trade:
        one.wait()


def mlp(two, grad_all, w, middle, grad_out, gains, queries, lse, cid):
    block = (4, 2, BLOCK, D)
    return pl.pallas_call(
        kernel_mlp,
        out_shape=(
            jax.ShapeDtypeStruct((BLOCK, D), F32),
            jax.ShapeDtypeStruct((8, D), F32),
            jax.ShapeDtypeStruct((BLOCK, D), BF),
            jax.ShapeDtypeStruct((2, TOKENS, HD), BF),
            jax.ShapeDtypeStruct((2, 8, TOKENS), F32),
            FULL,
            jax.ShapeDtypeStruct((4, 4, 3, BLOCK, FP), BF),
        ),
        in_specs=[ANY] * 3 + [VM] * 5,
        out_specs=(VM,) * 5 + (ANY, ANY),
        scratch_shapes=[
            pltpu.VMEM(block, BF),
            pltpu.VMEM(block, BF),
            pltpu.VMEM((3, 4, 4, BLOCK, FP), BF),
            pltpu.VMEM(block, BF),
            pltpu.VMEM((16, 3, BLOCK, FP), BF),
            pltpu.VMEM((4, 2, BLOCK, FP), BF),
            pltpu.VMEM((4, 2, BLOCK, 2 * FP), BF),
            pltpu.SemaphoreType.DMA((20,)),
            pltpu.SemaphoreType.DMA((12,)),
            pltpu.SemaphoreType.DMA((2,)),
            pltpu.SemaphoreType.DMA((2,)),
        ]
        + RS_SCRATCH,
        compiler_params=params(cid),
        name="mlp",
    )(two, grad_all, w, middle, grad_out, gains, queries, lse)


class PlaneScatter:
    COPIES = 12

    def __init__(self, part, a_in, b_in, a_mid, b_mid, a_last, b_last, send, recv):
        self.refs = part, a_in, b_in, a_mid, b_mid, a_last, b_last
        sems = send, recv
        half = part.shape[-1] // 2
        self.lanes = pl.ds(0, half), pl.ds(half, half)
        self.x = lax.axis_index("x")
        self.z = lax.axis_index("zh") * 2 + lax.axis_index("zl")
        self.one, self.two = [], []
        for d in range(1, 4):
            x = lax.rem(self.x + d, 4)
            z = lax.rem(self.z + d, 4)
            to_x = {"x": x}
            to_z = {"zh": z // 2, "zl": lax.rem(z, 2)}
            a, b = self.lanes
            k = d - 1
            self.one.append(remote(sems, k, part.at[:, z, :, a], a_in.at[k], to_z))
            self.one.append(remote(sems, 3 + k, part.at[x, :, :, b], b_in.at[k], to_x))
            self.two.append(remote(sems, 6 + k, a_mid.at[x], a_last.at[k], to_x))
            self.two.append(remote(sems, 9 + k, b_mid.at[z], b_last.at[k], to_z))

    def start(self):
        for copy in self.one:
            copy.start()

    def middle(self):
        part, a_in, b_in, a_mid, b_mid, _, _ = self.refs
        for copy in self.one:
            copy.wait_recv()
        a, b = self.lanes

        @pl.loop(0, 4)
        def _(i):
            a_mid[i] = (
                part[i, self.z, :, a].astype(F32) + jnp.sum(a_in[:, i].astype(F32), axis=0)
            ).astype(BF)
            b_mid[i] = (
                part[self.x, i, :, b].astype(F32) + jnp.sum(b_in[:, i].astype(F32), axis=0)
            ).astype(BF)

        for copy in self.two:
            copy.start()

    def finish(self, out):
        _, _, _, a_mid, b_mid, a_last, b_last = self.refs
        for copy in self.two:
            copy.wait_recv()
        a, b = self.lanes
        out[:, a] = (
            a_mid[self.x].astype(F32) + jnp.sum(a_last[...].astype(F32), axis=0)
        ).astype(BF)
        out[:, b] = (
            b_mid[self.z].astype(F32) + jnp.sum(b_last[...].astype(F32), axis=0)
        ).astype(BF)
        for copy in self.one + self.two:
            copy.wait_send()


def plane_scratch(rows, lanes):
    half = lanes // 2
    return [
        pltpu.VMEM((3, 4, rows, half), BF),
        pltpu.VMEM((3, 4, rows, half), BF),
        pltpu.VMEM((4, rows, half), BF),
        pltpu.VMEM((4, rows, half), BF),
        pltpu.VMEM((3, rows, half), BF),
        pltpu.VMEM((3, rows, half), BF),
        pltpu.SemaphoreType.DMA((PlaneScatter.COPIES,)),
        pltpu.SemaphoreType.DMA((PlaneScatter.COPIES,)),
    ]


def plane_peers():
    peers = []
    for d in range(1, 4):
        z = lax.rem(lax.axis_index("zh") * 2 + lax.axis_index("zl") + d, 4)
        peers.append({"x": lax.rem(lax.axis_index("x") + d, 4)})
        peers.append({"zh": z // 2, "zl": lax.rem(z, 2)})
    return peers


def kernel_qkv_back(
    joined_grad,
    weight_hbm,
    hidden,
    middle_hbm,
    gains,
    tokens_hbm,
    out_part,
    input_grad,
    sums,
    shift_sum,
    qkv_sum,
    out_sum,
    tokens,
    weight,
    middle_grad,
    local,
    part,
    *scratch,
):
    token_in = load([(tokens_hbm.at[y], tokens.at[y]) for y in range(4)], local)
    weight_in, middle_in = load([(weight_hbm, weight), (middle_hbm, middle_grad)], local, 4)
    y, c, up, opp, dn = ring()
    meet(list(ring_peers(up, dn, c)) + plane_peers())
    out_scatter = PlaneScatter(out_part, *scratch[:8])
    qkv_scatter = PlaneScatter(part, *scratch[8:16])
    out_scatter.start()
    flat = joined_grad[...].reshape(TP * BLOCK, 3 * HD)
    def weight_grads():
        for one in token_in:
            one.wait()
        for i in range(4):
            q = slice(i * 512, (i + 1) * 512)
            new = dot(tokens[:, :, :, q].reshape(TP * BLOCK, 512), flat, TN).astype(BF)
            part[i] = new.reshape(4, BLOCK, 3 * HD)
        qkv_scatter.start()
        weight_in.wait()
        middle_in.wait()

    def partial(block, put):
        a = joined_grad[block].reshape(2 * BLOCK, 3 * HD)
        for i in range(4):
            q = slice(i * 512, (i + 1) * 512)
            put(q, dot(a, weight[q, :], NT).reshape(2, BLOCK, 512))

    def between():
        out_scatter.middle()
        shift_sum[...] = jnp.broadcast_to(
            jnp.sum(flat.astype(F32), axis=0, keepdims=True), shift_sum.shape
        )
        qkv_scatter.middle()

    weight_grads()
    scatter = ring_scatter(partial, scratch[16:], between)
    sums[...] = jnp.zeros_like(sums)

    def back(r):
        row = scatter.total(r)
        normed, inv = layer_norm(hidden[r, :].astype(F32))
        input_grad[r, :] = restore_rows(
            middle_grad[r, :] + norm_back(row, normed, inv, gains[0:1, :])
        )
        sums[0:1, :] += jnp.sum(row * normed, axis=0, keepdims=True)
        sums[1:2, :] += jnp.sum(row, axis=0, keepdims=True)

    rows_loop(BLOCK, 16, back)
    scatter.finish()
    out_scatter.finish(out_sum)
    qkv_scatter.finish(qkv_sum)


def qkv_back(joined_grad, weight, hidden, middle_grad, gains, tokens, out_part, cid):
    return pl.pallas_call(
        kernel_qkv_back,
        out_shape=(
            jax.ShapeDtypeStruct((BLOCK, D), F32),
            jax.ShapeDtypeStruct((8, D), F32),
            jax.ShapeDtypeStruct((8, 3 * HD), F32),
            jax.ShapeDtypeStruct((BLOCK, 3 * HD), BF),
            jax.ShapeDtypeStruct((16, D), BF),
        ),
        in_specs=[VM, ANY, VM, ANY, VM, ANY, VM],
        out_specs=(VM,) * 5,
        scratch_shapes=[
            pltpu.VMEM((4, 2, BLOCK, D), BF),
            pltpu.VMEM((D, 3 * HD), BF),
            pltpu.VMEM((BLOCK, D), F32),
            pltpu.SemaphoreType.DMA((6,)),
            pltpu.VMEM((4, 4, BLOCK, 3 * HD), BF),
        ]
        + plane_scratch(16, D)
        + plane_scratch(BLOCK, 3 * HD)
        + RS_SCRATCH,
        compiler_params=params(cid),
        name="qkv_back",
    )(joined_grad, weight, hidden, middle_grad, gains, tokens, out_part.reshape(4, 4, 16, D))


TP_STEPS = [(dy, dc) for dy in range(4) for dc in range(2) if (dy, dc) != (0, 0)]
XZ_STEPS = [(dx, dz) for dx in range(4) for dz in range(4) if (dx, dz) != (0, 0)]


def tp_peer(step):
    y = lax.rem(lax.axis_index("y") + step[0], 4)
    c = lax.rem(lax.axis_index("core") + step[1], 2)
    return {"y": y, "core": c}, y * 2 + c


def xz_peer(step):
    x = lax.rem(lax.axis_index("x") + step[0], 4)
    z = lax.rem(lax.axis_index("zh") * 2 + lax.axis_index("zl") + step[1], 4)
    return {"x": x, "zh": z // 2, "zl": lax.rem(z, 2)}, x * 4 + z


def meet_all(split):
    peers = [tp_peer(s)[0] for s in TP_STEPS] + [xz_peer(s)[0] for s in XZ_STEPS]
    barrier = pltpu.get_barrier_semaphore()
    for peer in peers:
        pl.semaphore_signal(
            barrier, inc=1, device_id=peer, device_id_type=pl.DeviceIdType.MESH
        )

    @pl.when(split)
    def _():
        pl.semaphore_signal(
            barrier, inc=1, device_id=swap_peer(), device_id_type=pl.DeviceIdType.MESH
        )

    pl.semaphore_wait(barrier, len(peers) + split.astype(jnp.int32))


def swap_peer():
    return {"zh": lax.axis_index("core"), "core": lax.axis_index("zh")}


def swap_start(split, src, dst, local_sem, sems, i):
    @pl.when(split)
    def _():
        remote(sems, i, src, dst, swap_peer()).start()

    @pl.when(jnp.logical_not(split))
    def _():
        pltpu.make_async_copy(src, dst, local_sem).start()


def swap_wait(split, src, dst, local_sem, sems, i):
    @pl.when(split)
    def _():
        remote(sems, i, src, dst, swap_peer()).wait()

    @pl.when(jnp.logical_not(split))
    def _():
        pltpu.make_async_copy(src, dst, local_sem).wait()


N_TP = len(TP_STEPS)
N_XZ = len(XZ_STEPS)


class PlaneGather:
    COPIES = 14

    def __init__(self, src, full, local_sem, send, recv, x_first):
        sems = send, recv
        a, b = pl.ds(0, x_first), pl.ds(x_first, src.shape[-1] - x_first)
        rest = (slice(None),) * (len(src.shape) - 1)
        x = lax.axis_index("x")
        z = lax.axis_index("zh") * 2 + lax.axis_index("zl")
        self.one, self.two, self.three = [], [], []
        every, low, high = slice(None), pl.ds(0, 2), pl.ds(2, 2)

        def x_at(d):
            return lax.rem(x + d, 4)

        def z_at(d):
            return lax.rem(z + d, 4)

        def to_x(d):
            return {"x": x_at(d)}

        def to_z(d):
            return {"zh": z_at(d) // 2, "zl": lax.rem(z_at(d), 2)}

        def pass_on(i, at, peer):
            return remote(sems, i, full.at[at], full.at[at], peer)

        if x_first:
            at = rest + (a,)
            for d in range(1, 4):
                self.one.append(remote(sems, d - 1, src.at[at], full.at[(x, z) + at], to_x(d)))
            self.two.append(pass_on(6, (every, z) + at, to_z(1)))
            self.two.append(pass_on(7, (every, z) + at, to_z(3)))
            self.three.append(pass_on(8, (low, z_at(3)) + at, to_z(1)))
            self.three.append(pass_on(9, (high, z_at(1)) + at, to_z(3)))
        at = rest + (b,)
        for d in range(1, 4):
            self.one.append(remote(sems, 2 + d, src.at[at], full.at[(x, z) + at], to_z(d)))
        self.two.append(pass_on(10, (x, every) + at, to_x(1)))
        self.two.append(pass_on(11, (x, every) + at, to_x(3)))
        self.three.append(pass_on(12, (x_at(3), low) + at, to_x(1)))
        self.three.append(pass_on(13, (x_at(1), high) + at, to_x(3)))
        self.here = pltpu.make_async_copy(src, full.at[x, z], local_sem)

    def start(self):
        for copy in self.one:
            copy.start()
        self.here.start()

    def middle(self):
        self.here.wait()
        for copy in self.one:
            copy.wait_recv()
        for copy in self.two:
            copy.start()

    def forward(self):
        for copy, later in zip(self.two, self.three):
            copy.wait_recv()
            later.start()

    def finish(self):
        for copy in self.three:
            copy.wait_recv()
        for copy in self.one + self.two + self.three:
            copy.wait_send()


PG_SEMS = [
    pltpu.SemaphoreType.DMA,
    pltpu.SemaphoreType.DMA((PlaneGather.COPIES,)),
    pltpu.SemaphoreType.DMA((PlaneGather.COPIES,)),
]


def first_lane(rank):
    return jnp.where(rank < 4, 6 * rank, 5 * rank + 3) * BLOCK


def head_lane(part, rank):
    return part * D + (lax.rem(rank, 2) * 4 + rank // 2) * HD


def lanes_at(start, n):
    return pl.ds(pl.multiple_of(start, BLOCK), n)


def spread_gains(small_all, gains, entries):
    rows = small_all[...].reshape(BLOCK, BLOCK)
    source = lax.broadcasted_iota(jnp.int32, (BLOCK, 1), 0)
    f = lane(D)
    mine = (f // 16) == source
    for i in entries:
        pick = (source == 16 * i + lax.rem(f, 16)).astype(F32)
        value = jnp.dot(rows, pick, preferred_element_type=F32)
        gains[i : i + 1, :] = jnp.sum(jnp.where(mine, value, 0.0), axis=0, keepdims=True)


def spread_shift(small_all, shift, rank):
    rows = small_all[...].reshape(BLOCK, BLOCK)
    source = lax.broadcasted_iota(jnp.int32, (BLOCK, 1), 0)
    core = lax.rem(source, 2)
    y = lax.rem(source // 2, 4)
    zl = lax.rem(source // 8, 2)
    zh = lax.rem(source // 16, 2)
    x = source // 32
    owner = (zh * 4 + y) * 16 + x * 4 + zl * 2 + core
    for i in range(3):
        j = head_lane(i, rank) + lane(HD)
        pick = (source == 64 + lax.rem(j, 48)).astype(F32)
        value = jnp.dot(rows, pick, preferred_element_type=F32)
        value = jnp.sum(jnp.where(j // 48 == owner, value, 0.0), axis=0, keepdims=True)
        shift[:, i * HD : (i + 1) * HD] = value


def kernel_front(
    small,
    hidden_in,
    w_qkv,
    w_gate,
    w_up,
    w_down,
    w_out,
    small_all,
    gains,
    shift,
    qkv_full,
    mlp_rows,
    out_rows,
    hidden,
    full,
    own,
    normed,
    qkv_rows,
    local,
    send,
    recv,
    *sems,
):
    me = lax.axis_index("y") * 2 + lax.axis_index("core")
    xz = lax.axis_index("x") * 4 + lax.axis_index("zh") * 2 + lax.axis_index("zl")
    split = lax.axis_index("zh") != lax.axis_index("core")
    meet_all(split)
    cp = functools.partial(remote, (send, recv))
    tiny, qkv, mlp = [], [], []
    for k, step in enumerate(TP_STEPS):
        peer, there = tp_peer(step)
        tiny.append(cp(k, small, small_all.at[xz, me], peer))
        for i in range(3):
            src = w_qkv.at[:, lanes_at(head_lane(i, there), HD)]
            dst = qkv_rows.at[me, :, pl.ds(i * HD, HD)]
            qkv.append(cp((1 + i) * N_TP + k, src, dst, peer))
        for i, w in enumerate((w_gate, w_up, w_down)):
            src = w.at[:, lanes_at(first_lane(there), FP)]
            mlp.append(cp((4 + i) * N_TP + k, src, mlp_rows.at[i, me], peer))
    keep = [pltpu.make_async_copy(small, small_all.at[xz, me], local.at[0])]
    for i, w in enumerate((w_gate, w_up, w_down)):
        src = w_qkv.at[:, lanes_at(head_lane(i, me), HD)]
        dst = qkv_rows.at[me, :, pl.ds(i * HD, HD)]
        keep.append(pltpu.make_async_copy(src, dst, local.at[1 + i]))
        src = w.at[:, lanes_at(first_lane(me), FP)]
        keep.append(pltpu.make_async_copy(src, mlp_rows.at[i, me], local.at[4 + i]))
    for one in tiny + qkv + mlp + keep:
        one.start()
    last = 7 * N_TP + N_XZ
    for one in tiny:
        one.wait()
    keep[0].wait()
    wide = []
    for k, step in enumerate(XZ_STEPS):
        peer, _ = xz_peer(step)
        wide.append(cp(7 * N_TP + k, small_all.at[xz], small_all.at[xz], peer))
    for one in wide:
        one.start()
    for one in qkv + keep[1:]:
        one.wait()
    plane = PlaneGather(qkv_rows, qkv_full, *sems[:3], 3 * HD // 2)
    plane.start()
    swap_start(split, w_out, out_rows, local.at[7], (send, recv), last)

    def norm(r):
        row = permute_rows(hidden_in[r, :].astype(F32))
        hidden[r, :] = row.astype(BF)
        normed[r, :], _ = layer_norm(row)

    rows_loop(BLOCK, 16, norm)
    gains[...] = jnp.zeros_like(gains)
    for one in wide:
        one.wait()
    spread_gains(small_all, gains, (0, 1))

    def scale(r):
        own[r, :] = (normed[r, :] * gains[0:1, :] + gains[1:2, :]).astype(BF)

    rows_loop(BLOCK, 16, scale)
    gather = RingGather(own, full, sems[3], sems[4:])
    gather.start()
    plane.middle()
    gather.forward()
    spread_gains(small_all, gains, (2, 3))
    spread_shift(small_all, shift, me)
    gather.share()
    plane.forward()
    gather.share_far()
    for one in mlp:
        one.wait()
    swap_wait(split, w_out, out_rows, local.at[7], (send, recv), last)
    gather.finish()
    plane.finish()


def front(small, hidden, w_qkv, w_gate, w_up, w_down, w_out, cid):
    n = 7 * N_TP + N_XZ + 1
    return pl.pallas_call(
        kernel_front,
        out_shape=(
            jax.ShapeDtypeStruct((16, TP, 1, BLOCK), F32),
            jax.ShapeDtypeStruct((8, D), F32),
            jax.ShapeDtypeStruct((1, 3 * HD), F32),
            jax.ShapeDtypeStruct((4, 4, TP, 16, 3 * HD), BF),
            jax.ShapeDtypeStruct((3, TP, 16, FP), BF),
            jax.ShapeDtypeStruct((16, D), BF),
            jax.ShapeDtypeStruct((BLOCK, D), BF),
            FULL,
        ),
        in_specs=[ANY, VM] + [ANY] * 5,
        out_specs=(VM, VM, VM, ANY, ANY, ANY, VM, ANY),
        scratch_shapes=[
            pltpu.VMEM((BLOCK, D), BF),
            pltpu.VMEM((BLOCK, D), F32),
            pltpu.VMEM((TP, 16, 3 * HD), BF),
            pltpu.SemaphoreType.DMA((8,)),
            pltpu.SemaphoreType.DMA((n,)),
            pltpu.SemaphoreType.DMA((n,)),
        ]
        + PG_SEMS
        + AG_SCRATCH[1:],
        compiler_params=params(cid),
        name="front",
    )(small, hidden, w_qkv, w_gate, w_up, w_down, w_out)


def kernel_collect(
    one_sums,
    two_sums,
    shift,
    qkv,
    mlp,
    out,
    small_all,
    qkv_all,
    mlp_all,
    out_all,
    terms,
    terms_in,
    own,
    local,
    *sems,
):
    me = lax.axis_index("y") * 2 + lax.axis_index("core")
    xz = lax.axis_index("x") * 4 + lax.axis_index("zh") * 2 + lax.axis_index("zl")
    split = lax.axis_index("zh") != lax.axis_index("core")
    for p in range(16):
        q = slice(p * BLOCK, (p + 1) * BLOCK)
        terms[p, 0:2, :] = one_sums[0:2, q]
        terms[p, 2:4, :] = two_sums[0:2, q]
        for i in range(6):
            terms[p, 8 + i : 9 + i, :] = shift[0:1, i * BLOCK : (i + 1) * BLOCK]
        for i in (4, 5, 6, 7, 14, 15):
            terms[p, i : i + 1, :] = jnp.zeros((1, BLOCK), F32)
    meet_all(split)
    cp = functools.partial(remote, sems)
    big, extra, wide = [], [], []
    near, tile = pl.ds(BLOCK, FP - BLOCK), pl.ds(0, BLOCK)
    base = N_XZ + N_TP
    for k, step in enumerate(TP_STEPS):
        peer, there = tp_peer(step)
        dst = mlp_all.at[:, :, lanes_at(first_lane(me) + BLOCK, FP - BLOCK)]
        big.append(cp(base + k, mlp.at[:, there, :, near], dst, peer))
        dst = mlp_all.at[:, :, lanes_at(first_lane(me), BLOCK)]
        extra.append(cp(base + N_TP + k, mlp.at[:, there, :, tile], dst, peer))
        big.append(cp(base + 2 * N_TP + k, qkv.at[there], qkv_all.at[me], peer))
    for k, step in enumerate(XZ_STEPS):
        peer, there = xz_peer(step)
        wide.append(cp(k, terms.at[there], terms_in.at[xz], peer))
    dst = mlp_all.at[:, :, lanes_at(first_lane(me) + BLOCK, FP - BLOCK)]
    keep = [
        pltpu.make_async_copy(mlp.at[:, me, :, near], dst, local.at[0]),
        pltpu.make_async_copy(qkv.at[me], qkv_all.at[me], local.at[1]),
    ]
    dst = mlp_all.at[:, :, lanes_at(first_lane(me), BLOCK)]
    keep_tile = pltpu.make_async_copy(mlp.at[:, me, :, tile], dst, local.at[2])
    first_four = me < 4
    for one in big[0::2]:
        one.start()

    @pl.when(first_four)
    def _():
        keep_tile.start()
        for one in extra:
            one.start()

    for one in wide + big[1::2] + keep:
        one.start()

    last = base + 3 * N_TP
    swap_start(split, out, out_all, local.at[3], sems, last)
    for one in wide:
        one.wait()
    terms_in[xz] = terms[xz]
    own[...] = jnp.sum(terms_in[...], axis=0)
    tiny = []
    for k, step in enumerate(TP_STEPS):
        peer, _ = tp_peer(step)
        tiny.append(cp(N_XZ + k, own, small_all.at[me], peer))
    for one in tiny:
        one.start()
    for one in big + keep:
        one.wait()
    for k, step in enumerate(TP_STEPS):
        source = lax.rem(lax.axis_index("y") + 4 - step[0], 4) * 2 + lax.rem(
            lax.axis_index("core") + 2 - step[1], 2
        )

        @pl.when(source < 4)
        def _(k=k):
            extra[k].wait_recv()

    @pl.when(first_four)
    def _():
        keep_tile.wait()
        for one in extra:
            one.wait_send()

    swap_wait(split, out, out_all, local.at[3], sems, last)
    for one in tiny:
        one.wait()
    small_all[me] = own[...]


def collect(one_sums, two_sums, shift, qkv, mlp, out, cid):
    n = N_XZ + 4 * N_TP + 1
    return pl.pallas_call(
        kernel_collect,
        out_shape=(
            jax.ShapeDtypeStruct((TP, 16, BLOCK), F32),
            jax.ShapeDtypeStruct((TP, 16, 3 * HD), BF),
            jax.ShapeDtypeStruct((3, 16, FF), BF),
            jax.ShapeDtypeStruct((16, D), BF),
        ),
        in_specs=[VM] * 3 + [ANY] * 3,
        out_specs=(VM, ANY, ANY, ANY),
        scratch_shapes=[
            pltpu.VMEM((16, 16, BLOCK), F32),
            pltpu.VMEM((16, 16, BLOCK), F32),
            pltpu.VMEM((16, BLOCK), F32),
            pltpu.SemaphoreType.DMA((4,)),
            pltpu.SemaphoreType.DMA((n,)),
            pltpu.SemaphoreType.DMA((n,)),
        ],
        compiler_params=params(cid),
        name="collect",
    )(one_sums, two_sums, shift, qkv, mlp, out)


def kernel_finish(
    qkv_hbm,
    mlp_hbm,
    out_hbm,
    hidden_hbm,
    grad_hbm,
    qkv_grad,
    gate,
    up,
    down,
    out,
    hidden_out,
    input_grad,
    qkv_all,
    mlp_all,
    out_all,
    local,
):
    pairs = [(qkv_hbm, qkv_all), (mlp_hbm, mlp_all), (out_hbm, out_all)]
    pairs += [(hidden_hbm, hidden_out), (grad_hbm, input_grad)]
    for one in load(pairs, local):
        one.wait()
    for t in range(TP):
        for i in range(3):
            first = i * D + (t % 2 * 4 + t // 2) * HD
            qkv_grad[:, first : first + HD] = qkv_all[t, :, i * HD : (i + 1) * HD].astype(F32)
    gate[...] = mlp_all[0].astype(F32)
    up[...] = mlp_all[1].astype(F32)
    down[...] = mlp_all[2].astype(F32)
    out[...] = restore_rows(out_all[...].astype(F32))


def finish(qkv_all, mlp_all, out_all, hidden, grad):
    wide = jax.ShapeDtypeStruct((16, FF), F32)
    return pl.pallas_call(
        kernel_finish,
        out_shape=(
            jax.ShapeDtypeStruct((16, 3 * D), F32),
            wide,
            wide,
            wide,
            jax.ShapeDtypeStruct((16, D), F32),
            jax.ShapeDtypeStruct((BLOCK, D), BF),
            jax.ShapeDtypeStruct((BLOCK, D), F32),
        ),
        in_specs=[ANY] * 5,
        out_specs=(VM,) * 7,
        scratch_shapes=[
            pltpu.VMEM((TP, 16, 3 * HD), BF),
            pltpu.VMEM((3, 16, FF), BF),
            pltpu.VMEM((16, D), BF),
            pltpu.SemaphoreType.DMA((5,)),
        ],
        compiler_params=pltpu.CompilerParams(vmem_limit_bytes=60 * 1024 * 1024),
        name="finish",
    )(qkv_all, mlp_all, out_all, hidden, grad)


def body(
    hidden_in,
    cotangent,
    seq_lengths,
    slot_block,
    ln1_gain,
    ln1_bias,
    w_qkv,
    qkv_bias,
    w_out,
    ln2_gain,
    ln2_bias,
    w_gate,
    w_up,
    w_down,
):
    f32 = F32
    zh = lax.axis_index("zh")
    y = lax.axis_index("y")
    core = lax.axis_index("core")
    xz = lax.axis_index("x") * 4 + zh * 2 + lax.axis_index("zl")

    small, first = jnp.zeros(BLOCK, f32), 0
    pieces = (ln1_gain, ln1_bias, ln2_gain, ln2_bias, qkv_bias, seq_lengths[0], slot_block[0])
    for piece in pieces:
        n = piece.shape[0]
        small = small + jnp.pad(piece.astype(f32), (first, BLOCK - first - n))
        first += n
    small_all, gains, shift, qkv_full, mlp_rows, out_rows, hidden, one_all = front(
        small.reshape(1, BLOCK), hidden_in[0], w_qkv, w_gate, w_up, w_down, w_out, 0
    )
    qkv_full = qkv_full.reshape(D, 3 * HD)
    mlp_full = lax.all_gather(mlp_rows.reshape(3, BLOCK, FP), ZX, axis=0, tiled=False)
    small_all = small_all.reshape(BLOCK, BLOCK)

    plan = lax.dynamic_slice_in_dim(small_all, xz * TP + y * 2, 2, 0)[:, 112:122].astype(jnp.int32)
    blocks = plan[:, 2:].reshape(2, 2, 4)
    own_blocks = lax.dynamic_index_in_dim(blocks, zh, axis=1, keepdims=False)
    other_blocks = lax.dynamic_index_in_dim(blocks, 1 - zh, axis=1, keepdims=False)
    start = jnp.concatenate([own_blocks, other_blocks], axis=1) * BLOCK
    first_pad = (plan[:, 0:1] + BLOCK - 1) // BLOCK * BLOCK
    second = (start >= first_pad).astype(jnp.int32)
    limit = jnp.where(second == 1, plan[:, 1:2], plan[:, 0:1])
    table = jnp.stack([start - second * first_pad, second, limit], axis=1)
    queries, kv, lse, attended, grad_out, out_full, middle, grad_all, two_all = attend(
        table, one_all, qkv_full, shift, cotangent[0], out_rows, hidden, gains, 6
    )
    middle_grad, two_sums, branch, other_queries, other_lse, mlp_out, mlp_part = mlp(
        two_all, grad_all, mlp_full.reshape(4, 4, 3, BLOCK, FP), middle, grad_out, gains, queries, lse, 3
    )
    mlp_sum = lax.psum_scatter(
        mlp_part.reshape(16 * 3 * BLOCK, FP), ZX, scatter_dimension=0, tiled=True
    )
    joined_grad, out_part, hidden_out = attend_back(
        table,
        branch,
        out_full,
        attended,
        queries,
        kv,
        lse,
        other_queries,
        other_lse,
        mlp_out,
        middle,
        7,
    )
    input_grad, one_sums, shift_sum, qkv_sum, out_sum = qkv_back(
        joined_grad, qkv_full, hidden, middle_grad, gains, one_all, out_part, 4
    )

    small_sum, qkv_all, mlp_all, out_all = collect(
        one_sums,
        two_sums,
        shift_sum,
        qkv_sum.reshape(TP, 16, FP),
        mlp_sum.reshape(3, TP, 16, FP),
        out_sum,
        5,
    )
    qkv_grad, gate_sum, up_sum, down_sum, out_grad, hidden_out, input_grad = finish(
        qkv_all, mlp_all, out_all, hidden_out, input_grad
    )
    vectors = jnp.sum(small_sum[:, :4], axis=0)
    vectors = lax.dynamic_slice_in_dim(vectors, (y * 2 + core) * 16, 16, 1)
    shift_grad = small_sum[:, 8:14].reshape(4, 2, 3, HD).transpose(2, 1, 0, 3).reshape(128, 48)
    row = (zh * 4 + y) * 16 + lax.axis_index("x") * 4 + lax.axis_index("zl") * 2 + core
    shift_grad = lax.dynamic_index_in_dim(shift_grad, row, 0, False)
    return (
        hidden_out[None],
        input_grad[None],
        vectors[0],
        vectors[1],
        qkv_grad,
        shift_grad,
        out_grad,
        vectors[2],
        vectors[3],
        gate_sum,
        up_sum,
        down_sum,
    )


def solution(mesh):
    inner = Mesh(mesh.devices.reshape(2, 4, 4, 2, 2), ROWS)
    rows = P(ROWS)
    tokens = P(GRP, SLOT, None)
    placed = (
        tokens,
        tokens,
        P(GRP, None),
        P(GRP, None),
        rows,
        rows,
        P(ROWS, None),
        rows,
        P(ROWS, None),
        rows,
        rows,
        P(ROWS, None),
        P(ROWS, None),
        P(ROWS, None),
    )
    return jax.shard_map(
        body,
        mesh=inner,
        in_specs=placed,
        out_specs=(
            tokens,
            tokens,
            rows,
            rows,
            P(ROWS, None),
            rows,
            P(ROWS, None),
            rows,
            rows,
            P(ROWS, None),
            P(ROWS, None),
            P(ROWS, None),
        ),
        check_vma=False,
    )
```

```python
import functools

import jax
import jax.numpy as jnp
from jax import lax
from jax.experimental import pallas as pl
from jax.experimental.pallas import tpu as pltpu
from jax.sharding import Mesh
from jax.sharding import PartitionSpec as P

D = 2048
HEADS = 32
HEAD_DIM = 64
ROT = 16
FF = 5632
BLOCK = 128
TP = 8
HD = D // TP
FC = FF // TP

EPS = 1e-05
NEG = -1e30
SCALE = HEAD_DIM ** (-0.5)
TPA = ("y", "core")
ZX = ("zh", "zl", "x")
ROWS = ("zh", "y", "x", "zl", "core")
GRP = ("x", "zl", "core")
SLOT = ("zh", "y")


def permute_rows(row):
    group = lane(BLOCK) // 32
    tiles = []
    for x in range(4):
        for zh in range(2):
            for zl in range(2):
                out = None
                for y in range(4):
                    first = zh * 1024 + y * 256 + x * 64 + zl * 32
                    tile = first // BLOCK * BLOCK
                    shift = (32 * y - first % BLOCK) % BLOCK
                    value = row[:, tile : tile + BLOCK]
                    value = pltpu.roll(value, shift, 1) if shift else value
                    out = value if out is None else jnp.where(group == y, value, out)
                tiles.append(out)
    return jnp.concatenate(tiles, axis=1)


def restore_rows(row):
    group = lane(BLOCK) // 32
    tiles = []
    for t in range(D // BLOCK):
        out = None
        for j in range(4):
            first = t * BLOCK + 32 * j
            zh, y, x, zl = first // 1024, first // 256 % 4, first // 64 % 4, first // 32 % 2
            tile = (x * 4 + zh * 2 + zl) * BLOCK
            shift = (32 * j - 32 * y) % BLOCK
            value = row[:, tile : tile + BLOCK]
            value = pltpu.roll(value, shift, 1) if shift else value
            out = value if out is None else jnp.where(group == j, value, out)
        tiles.append(out)
    return jnp.concatenate(tiles, axis=1)


def layer_norm(values):
    average = jnp.mean(values, axis=-1, keepdims=True)
    centred = values - average
    inv_scale = lax.rsqrt(jnp.mean(centred * centred, axis=-1, keepdims=True) + EPS)
    return centred * inv_scale, inv_scale


def norm_back(grad_in, normed, inv_scale, gain):
    scaled = grad_in * gain
    return inv_scale * (
        scaled
        - jnp.mean(scaled, axis=-1, keepdims=True)
        - normed * jnp.mean(scaled * normed, axis=-1, keepdims=True)
    )


FP = 768
HALF = BLOCK // 2
ANY = pl.BlockSpec(memory_space=pl.ANY)
VM = pl.BlockSpec(memory_space=pltpu.VMEM)
BF = jnp.bfloat16
F32 = jnp.float32


def params(cid):
    return pltpu.CompilerParams(
        collective_id=cid, has_side_effects=True, vmem_limit_bytes=56 * 1024 * 1024
    )


def meet(peers):
    barrier = pltpu.get_barrier_semaphore()
    for peer in peers:
        pl.semaphore_signal(
            barrier, inc=1, device_id=peer, device_id_type=pl.DeviceIdType.MESH
        )
    pl.semaphore_wait(barrier, len(peers))


def remote(sems, i, src, dst, peer):
    return pltpu.make_async_remote_copy(
        src_ref=src,
        dst_ref=dst,
        send_sem=sems[0].at[i],
        recv_sem=sems[1].at[i],
        device_id=peer,
        device_id_type=pl.DeviceIdType.MESH,
    )


def ring():
    y = lax.axis_index("y")
    c = lax.axis_index("core")
    up = lax.rem(y + 1, 4)
    opp = lax.rem(y + 2, 4)
    dn = lax.rem(y + 3, 4)
    return y, c, up, opp, dn


def ring_peers(up, dn, c):
    return {"y": up}, {"y": dn}, {"core": 1 - c}


N_AG = 11
N_RS = 10


class RingGather:
    def __init__(self, own, full, local_sem, sems):
        y, c, up, opp, dn = ring()
        to_up, to_dn, to_sib = ring_peers(up, dn, c)
        first, last = pl.ds(0, HALF), pl.ds(HALF, HALF)
        cp = functools.partial(remote, sems)

        def pass_on(i, block, peer, *rows):
            ref = full.at[(block, c) + rows]
            return cp(i, ref, ref, peer)

        self.up1 = cp(0, own.at[first], full.at[y, c, first], to_up)
        self.dn1 = cp(1, own.at[last], full.at[y, c, last], to_dn)
        self.up2 = cp(2, own.at[last], full.at[y, c, last], to_up)
        self.dn2 = cp(3, own.at[first], full.at[y, c, first], to_dn)
        self.here = pltpu.make_async_copy(own, full.at[y, c], local_sem)
        self.far1 = pass_on(5, dn, to_up, first)
        self.far2 = pass_on(6, up, to_dn, last)
        self.sib = [
            cp(4, own, full.at[y, c], to_sib),
            pass_on(7, dn, to_sib),
            pass_on(8, up, to_sib),
            pass_on(9, opp, to_sib, first),
            pass_on(10, opp, to_sib, last),
        ]

    def start(self):
        for one in (self.up1, self.dn1, self.up2, self.dn2, self.sib[0], self.here):
            one.start()

    def forward(self):
        self.up1.wait_recv()
        self.far1.start()
        self.dn1.wait_recv()
        self.far2.start()

    def share(self):
        self.up2.wait_recv()
        self.sib[1].start()
        self.dn2.wait_recv()
        self.sib[2].start()

    def share_far(self):
        self.far1.wait_recv()
        self.sib[3].start()
        self.far2.wait_recv()
        self.sib[4].start()

    def sends(self):
        return [self.up1, self.dn1, self.up2, self.dn2, self.far1, self.far2] + self.sib

    def finish(self):
        for one in self.sib:
            one.wait_recv()
        self.here.wait()
        for one in self.sends():
            one.wait_send()

    def run(self, work=None):
        for step in (self.start, self.forward, self.share, self.share_far):
            step()
            if work is not None:
                work()
        self.finish()


def rows_loop(count, step, body):
    @pl.loop(0, count // step)
    def _(i):
        body(pl.ds(pl.multiple_of(i * step, step), step))


RS_SCRATCH = [
    pltpu.VMEM((4, BLOCK, D), F32),
    pltpu.VMEM((4, BLOCK, D), BF),
    pltpu.VMEM((4, BLOCK, D), BF),
    pltpu.VMEM((2, HALF, D), BF),
    pltpu.VMEM((2, HALF, D), BF),
    pltpu.VMEM((2, BLOCK, D), BF),
    pltpu.VMEM((2, BLOCK, D), BF),
    pltpu.SemaphoreType.DMA((N_RS,)),
    pltpu.SemaphoreType.DMA((N_RS,)),
]


class RingScatter:
    def __init__(self, mine, sib_out, sib_in, far_out, far_in, near_out, near_in, *sems):
        y, c, up, opp, dn = ring()
        to_up, to_dn, to_sib = ring_peers(up, dn, c)
        first, last = pl.ds(0, HALF), pl.ds(HALF, HALF)
        cp = functools.partial(remote, sems)
        self.order = (opp, up, dn, y)
        self.mine, self.sib_in = mine, sib_in
        self.far_out, self.far_in = far_out, far_in
        self.near_out, self.near_in = near_out, near_in
        self.sib = [cp(j, sib_out(j), sib_in.at[j], to_sib) for j in range(4)]
        self.far = [
            cp(4, far_out.at[0], far_in.at[0], to_up),
            cp(5, far_out.at[1], far_in.at[1], to_dn),
        ]
        self.early = [
            cp(6, near_out.at[0, last], near_in.at[0, last], to_up),
            cp(7, near_out.at[1, first], near_in.at[1, first], to_dn),
        ]
        self.late = [
            cp(8, near_out.at[0, first], near_in.at[0, first], to_up),
            cp(9, near_out.at[1, last], near_in.at[1, last], to_dn),
        ]

    def both(self, j, rows):
        return self.mine(j, rows) + self.sib_in[j, rows, :].astype(F32)

    def send_far(self):
        self.sib[0].wait_recv()
        for k in range(2):

            def add(r, k=k):
                q = pl.ds(k * HALF + r.start, r.size)
                self.far_out[k, r, :] = self.both(0, q).astype(BF)

            rows_loop(HALF, 32, add)
            self.far[k].start()

    def send_early(self, k):
        self.sib[1 + k].wait_recv()

        def add(r):
            q = pl.ds((1 - k) * HALF + r.start, r.size)
            self.near_out[k, q, :] = self.both(1 + k, q).astype(BF)

        rows_loop(HALF, 32, add)
        self.early[k].start()

    def send_late(self):
        for k in range(2):
            self.far[k].wait_recv()

            def add(r, k=k):
                q = pl.ds(k * HALF + r.start, r.size)
                self.near_out[k, q, :] = (
                    self.both(1 + k, q) + self.far_in[k, r, :].astype(F32)
                ).astype(BF)

            rows_loop(HALF, 32, add)
            self.late[k].start()

    def wait(self):
        self.sib[3].wait_recv()
        for one in self.early + self.late:
            one.wait_recv()

    def total(self, rows):
        return (
            self.both(3, rows)
            + self.near_in[0, rows, :].astype(F32)
            + self.near_in[1, rows, :].astype(F32)
        )

    def finish(self):
        for one in self.sib + self.far + self.early + self.late:
            one.wait_send()


def ring_scatter(partial, scratch, between=None):
    part, sib_out = scratch[:2]
    c = lax.axis_index("core")
    scatter = RingScatter(
        lambda j, rows: part[j, rows, :], lambda j: sib_out.at[j], *scratch[2:]
    )

    def produce(j):
        def put(columns, value):
            part[j, :, columns] = jnp.where(c == 0, value[0], value[1])
            sib_out[j, :, columns] = jnp.where(c == 0, value[1], value[0]).astype(BF)

        partial(scatter.order[j], put)
        scatter.sib[j].start()

    produce(0)
    produce(1)
    scatter.send_far()
    scatter.send_early(0)
    produce(2)
    scatter.send_early(1)
    scatter.send_late()
    produce(3)
    if between is not None:
        between()
    scatter.wait()
    return scatter


AG_SCRATCH = [
    pltpu.VMEM((BLOCK, D), BF),
    pltpu.SemaphoreType.DMA,
    pltpu.SemaphoreType.DMA((N_AG,)),
    pltpu.SemaphoreType.DMA((N_AG,)),
]
FULL = jax.ShapeDtypeStruct((4, 2, BLOCK, D), BF)


def order_out(gathered, weight):
    for x in range(4):
        for zl in range(2):
            for a in range(2):
                row = x * 64 + zl * 32 + a * 16
                weight[row : row + 16, :] = gathered[x, a * 2 + zl]


OUT_ROWS = pltpu.VMEM((HD, D), BF)


NN = (((1,), (0,)), ((), ()))
NT = (((1,), (1,)), ((), ()))
TN = (((0,), (0,)), ((), ()))
TOKENS = 4 * BLOCK
KEYS = 2 * TOKENS
TILE = 2 * BLOCK


def dot(a, b, dims):
    return lax.dot_general(a, b, dims, preferred_element_type=F32)


def lane(n):
    return lax.broadcasted_iota(jnp.int32, (1, n), 1)


def turn_tables(base):
    entry = lax.rem(lane(BLOCK), HEAD_DIM)
    freq = jnp.exp(
        lax.rem(entry, ROT // 2).astype(F32) * (-2.0 / ROT * 9.210340371976184)
    )
    freq = jnp.where(entry < ROT, freq, 0.0)
    place = (base + lax.broadcasted_iota(jnp.int32, (BLOCK, 1), 0)).astype(F32)
    phase = place * freq
    return jnp.cos(phase), jnp.sin(phase)


def turn(v, cosine, sines, direction):
    entry = lax.rem(lane(BLOCK), HEAD_DIM)
    s = sines * direction
    ahead = pltpu.roll(v, BLOCK - ROT // 2, 1)
    behind = pltpu.roll(v, ROT // 2, 1)
    return v * cosine + jnp.where(entry < ROT // 2, -ahead, behind) * s


def key_bias(table, g, tile, blocks, q_part=0):
    token = lane(BLOCK)
    q_code, q_low = [], []
    for j in range(2):
        block = 4 * q_part + 2 * tile + j
        low = table[g, 1, block] * 4096
        q_code.append(low + table[g, 0, block] + token)
        q_low.append(low + jnp.zeros_like(token))
    q_code = jnp.concatenate(q_code, axis=1)
    q_low = jnp.concatenate(q_low, axis=1)
    column = lax.broadcasted_iota(jnp.int32, (BLOCK, 1), 0)
    rows = []
    for k in blocks:
        place = table[g, 0, k] + column
        code = jnp.where(place < table[g, 2, k], table[g, 1, k] * 4096 + place, 1 << 20)
        kept = jnp.logical_and(code <= q_code, code >= q_low)
        rows.append(jnp.where(kept, 0.0, NEG))
    return jnp.concatenate(rows, axis=0)


def head_mask(h):
    first = lane(BLOCK) < HEAD_DIM
    return jnp.where(first if h == 0 else jnp.logical_not(first), 1.0, 0.0).astype(BF)


def load(pairs, sems, first=0):
    copies = []
    for i, (src, dst) in enumerate(pairs):
        copies.append(pltpu.make_async_copy(src, dst, sems.at[first + i]))
        copies[-1].start()
    return copies


def kernel_attend(
    table,
    tokens_hbm,
    weight_hbm,
    shift,
    cotangent,
    out_in,
    hidden,
    gains,
    queries,
    kv,
    lse,
    attended,
    grad_out,
    out_full,
    middle,
    grad_all,
    two_all,
    out_rows,
    out_weight,
    own_two,
    tokens,
    weight,
    cosines,
    sines,
    tops,
    totals,
    mixed,
    local,
    send,
    recv,
    *sems,
):
    partner = {"zh": 1 - lax.axis_index("zh")}
    weight_in, *token_in = load(
        [(weight_hbm, weight)] + [(tokens_hbm.at[y], tokens.at[y]) for y in range(4)], local
    )
    y0, c, up, opp, dn = ring()
    out_rows[...] = permute_rows(out_in[...].astype(F32)).astype(BF)
    meet(list(ring_peers(up, dn, c)) + plane_peers())
    gather = RingGather(grad_out, grad_all, sems[0], sems[1:3])
    plane = PlaneGather(out_rows, out_full, *sems[3:6], 0)
    two_gather = RingGather(own_two, two_all, sems[6], sems[7:9])
    part, sib_out = sems[9:11]
    scatter = RingScatter(
        lambda j, rows: part[j, rows, :], lambda j: sib_out.at[j], *sems[11:]
    )
    plane.start()
    lse[...] = jnp.zeros_like(lse)
    weight_in.wait()
    for y in range(4):
        at = slice(y * BLOCK, (y + 1) * BLOCK)
        for g in range(2):
            cosine, sine = turn_tables(table[g, 0, y])
            cosines[g, at, :] = cosine
            sines[g, at, :] = sine
        token_in[y].wait()
        new = dot(tokens[y].reshape(TILE, D), weight[:, HD:], NN) + shift[:, HD:]
        for g in range(2):
            rows = slice(g * BLOCK, (g + 1) * BLOCK)
            for pair in range(2):
                q = slice(pair * BLOCK, (pair + 1) * BLOCK)
                turned = turn(new[rows, q], cosines[g, at, :], sines[g, at, :], 1.0)
                kv[0, g, at, q] = turned.astype(BF)
            kv[1, g, at, :] = new[rows, HD:].astype(BF)

    own, other = pl.ds(0, TOKENS), pl.ds(TOKENS, TOKENS)
    trade = [
        remote((send, recv), g, kv.at[:, g, own, :], kv.at[:, g, other, :], partner)
        for g in range(2)
    ]
    for one in trade:
        one.start()
    plane.middle()
    base, limit = table[c, 0, y0], table[c, 2, y0]

    def mask(r):
        place = base + r.start + lax.broadcasted_iota(jnp.int32, (16, 1), 0)
        row = jnp.where(place < limit, cotangent[r, :].astype(F32), 0.0)
        grad_out[r, :] = permute_rows(row).astype(BF)

    rows_loop(BLOCK, 16, mask)
    gather.start()
    for y in range(4):
        at = slice(y * BLOCK, (y + 1) * BLOCK)
        new = dot(tokens[y].reshape(TILE, D), weight[:, :HD], NN) + shift[:, :HD]
        for g in range(2):
            rows = slice(g * BLOCK, (g + 1) * BLOCK)
            for pair in range(2):
                q = slice(pair * BLOCK, (pair + 1) * BLOCK)
                turned = turn(new[rows, q], cosines[g, at, :], sines[g, at, :], 1.0)
                queries[g, at, q] = turned.astype(BF) * jnp.asarray(SCALE, BF)

    first_head = lax.broadcasted_iota(jnp.int32, (BLOCK, 1), 0) < HEAD_DIM

    def work(part, g):
        rows = slice(part * TOKENS, (part + 1) * TOKENS)

        @pl.loop(0, 2)
        def _(tile):
            at = pl.ds(pl.multiple_of(tile * TILE, TILE), TILE)
            bias = key_bias(table, g, tile, range(4 * part, 4 * part + 4))
            for pair in range(2):
                q = slice(pair * BLOCK, (pair + 1) * BLOCK)
                k_all = kv[0, g, rows, q]
                v_all = kv[1, g, rows, q]
                out = jnp.zeros((BLOCK, TILE), F32)
                keep, share = [], []
                for h in range(2):
                    row = slice(2 * pair + h, 2 * pair + h + 1)
                    s = dot(k_all, queries[g, at, q] * head_mask(h), NT) + bias
                    top = jnp.max(s, axis=0, keepdims=True)
                    if part == 1:
                        top = jnp.maximum(top, tops[g, row, at])
                    p = jnp.exp(s - top)
                    total = jnp.sum(p, axis=0, keepdims=True)
                    out = out + dot(v_all * head_mask(h), p.astype(BF), TN)
                    if part == 0:
                        tops[g, row, at] = top
                        totals[g, row, at] = total
                    else:
                        keep.append(jnp.exp(tops[g, row, at] - top))
                        total = total + totals[g, row, at] * keep[h]
                        lse[g, row, at] = top + jnp.log(total)
                        share.append(1.0 / total)
                if part == 0:
                    mixed[g, q, at] = out
                else:
                    out = out + mixed[g, q, at] * jnp.where(first_head, keep[0], keep[1])
                    out = (out * jnp.where(first_head, share[0], share[1])).T.astype(BF)
                    for j in range(2):
                        attended[2 * tile + j, g, :, q] = out[j * BLOCK : (j + 1) * BLOCK]

    def project(g):
        for j in range(4):
            a = attended[scatter.order[j], g]
            for i in range(4):
                q = slice(i * 512, (i + 1) * 512)
                value = dot(a, out_weight[:, q], NN)

                @pl.when(c == g)
                def _(j=j, q=q, value=value):
                    part[j, :, q] = value

                @pl.when(c != g)
                def _(j=j, q=q, value=value):
                    sib_out[j, :, q] = value.astype(BF)

            @pl.when(c != g)
            def _(j=j):
                scatter.sib[j].start()

    def norm(r):
        row = hidden[r, :].astype(F32) + scatter.total(r)
        middle[r, :] = row
        normed, _ = layer_norm(row)
        own_two[r, :] = (normed * gains[2:3, :] + gains[3:4, :]).astype(BF)

    def exchange():
        scatter.send_far()
        scatter.send_early(0)
        scatter.send_early(1)

    def settle():
        scatter.send_late()
        scatter.wait()
        rows_loop(BLOCK, 16, norm)
        two_gather.start()

    def pass_on():
        two_gather.forward()
        two_gather.share()
        two_gather.share_far()

    work(0, 0)
    plane.forward()
    gather.forward()
    work(0, 1)
    gather.share()
    plane.finish()
    order_out(out_full, out_weight)
    trade[0].wait_recv()
    work(1, 0)
    project(0)
    gather.share_far()

    @pl.when(c == 0)
    def _():
        exchange()

    trade[1].wait_recv()
    work(1, 1)
    project(1)

    @pl.when(c == 1)
    def _():
        exchange()

    settle()
    pass_on()

    for one in trade:
        one.wait_send()
    gather.finish()
    two_gather.finish()
    scatter.finish()


SM = pl.BlockSpec(memory_space=pltpu.SMEM)


def attend(table, tokens, weight, shift, cotangent, out_in, hidden, gains, cid):
    return pl.pallas_call(
        kernel_attend,
        out_shape=(
            jax.ShapeDtypeStruct((2, TOKENS, HD), BF),
            jax.ShapeDtypeStruct((2, 2, KEYS, HD), BF),
            jax.ShapeDtypeStruct((2, 8, TOKENS), F32),
            jax.ShapeDtypeStruct((4, 2, BLOCK, HD), BF),
            jax.ShapeDtypeStruct((BLOCK, D), BF),
            jax.ShapeDtypeStruct((4, 4, 16, D), BF),
            jax.ShapeDtypeStruct((BLOCK, D), F32),
            FULL,
            FULL,
        ),
        in_specs=[SM, ANY, ANY] + [VM] * 5,
        out_specs=(VM,) * 7 + (ANY, ANY),
        scratch_shapes=[
            pltpu.VMEM((16, D), BF),
            OUT_ROWS,
            pltpu.VMEM((BLOCK, D), BF),
            pltpu.VMEM((4, 2, BLOCK, D), BF),
            pltpu.VMEM((D, 3 * HD), BF),
            pltpu.VMEM((2, TOKENS, BLOCK), F32),
            pltpu.VMEM((2, TOKENS, BLOCK), F32),
            pltpu.VMEM((2, 8, TOKENS), F32),
            pltpu.VMEM((2, 8, TOKENS), F32),
            pltpu.VMEM((2, HD, TOKENS), F32),
            pltpu.SemaphoreType.DMA((5,)),
            pltpu.SemaphoreType.DMA((2,)),
            pltpu.SemaphoreType.DMA((2,)),
        ]
        + AG_SCRATCH[1:]
        + PG_SEMS
        + AG_SCRATCH[1:]
        + RS_SCRATCH,
        compiler_params=params(cid),
        name="attend",
    )(table, tokens, weight, shift, cotangent, out_in, hidden, gains)


def kernel_attend_back(
    table,
    branch_own,
    gathered,
    attended,
    queries,
    kv,
    lse,
    other_queries,
    other_lse,
    mlp_out,
    middle_hbm,
    joined_grad,
    out_part,
    hidden_out,
    branch,
    middle,
    own_out,
    probs,
    other_probs,
    local,
    weight,
    grads,
    other_grads,
    dq,
    mean,
    other_mean,
    dkv,
    send,
    recv,
    local_sem,
    gather_send,
    gather_recv,
    *scratch,
):
    partner = {"zh": 1 - lax.axis_index("zh")}
    y0, c, up, opp, dn = ring()
    order = (opp, up, dn, y0)
    out_in = load([(mlp_out.at[order[j], c], own_out.at[j]) for j in range(4)], local)
    (middle_in,) = load([(middle_hbm, middle)], local, 4)
    meet(list(ring_peers(up, dn, c)) + [partner])
    gather = RingGather(branch_own, branch, local_sem, (gather_send, gather_recv))
    gather.start()
    scatter = RingScatter(
        lambda j, rows: own_out[j, rows, :].astype(F32),
        lambda j: mlp_out.at[order[j], 1 - c],
        *scratch,
    )
    for one in scatter.sib:
        one.start()
    order_out(gathered, weight)
    trade = [
        remote((send, recv), 0, mean, other_mean, partner),
        remote((send, recv), 1, grads.at[0], other_grads.at[0], partner),
        remote((send, recv), 2, grads.at[1], other_grads.at[1], partner),
    ]

    def recompute(part, g):
        q_src, lse_src = (queries, lse) if part == 0 else (other_queries, other_lse)
        dst = probs if part == 0 else other_probs
        blocks = range(8) if part == 0 else range(4)
        rows = slice(0, len(blocks) * BLOCK)

        @pl.loop(0, 2)
        def _(tile):
            at = pl.ds(pl.multiple_of(tile * TILE, TILE), TILE)
            bias = key_bias(table, g, tile, blocks, part)
            for pair in range(2):
                q = slice(pair * BLOCK, (pair + 1) * BLOCK)
                for h in range(2):
                    row = slice(2 * pair + h, 2 * pair + h + 1)
                    s = dot(kv[0, g, rows, q], q_src[g, at, q] * head_mask(h), NT) + bias
                    dst[g, tile, 2 * pair + h] = jnp.exp(s - lse_src[g, row, at])

    recompute(0, 0)
    gather.forward()
    recompute(0, 1)
    gather.share()
    gather.share_far()
    recompute(1, 0)
    recompute(1, 1)
    gather.finish()

    dq[...] = jnp.zeros_like(dq)
    dkv[...] = jnp.zeros_like(dkv)
    mean[...] = jnp.zeros_like(mean)
    heads = jnp.concatenate([head_mask(0), head_mask(1)] * 8, axis=0)
    for y in range(4):
        at = slice(y * BLOCK, (y + 1) * BLOCK)
        new = dot(branch[y].reshape(TILE, D), weight[...], NT)
        for g in range(2):
            rows = slice(g * BLOCK, (g + 1) * BLOCK)
            grads[g, at, :] = new[rows].astype(BF)
    for g in range(2):
        for pair in range(2):
            q = slice(pair * BLOCK, (pair + 1) * BLOCK)
            mixed = attended[:, g, :, q].reshape(TOKENS, BLOCK).astype(F32)
            mixed = mixed * grads[g, :, q].astype(F32)
            high = mixed.astype(BF)
            low = (mixed - high.astype(F32)).astype(BF)
            both = dot(heads, high, NT) + dot(heads, low, NT)
            mean[g, 2 * pair : 2 * pair + 2, :] = both[0:2]
    for one in trade:
        one.start()
    for one in out_in:
        one.wait()
    scatter.send_far()
    scatter.send_early(0)
    scatter.send_early(1)

    def back(part, g):
        q_src, g_src = (queries, grads) if part == 0 else (other_queries, other_grads)
        mean_src, p_src = (mean, probs) if part == 0 else (other_mean, other_probs)
        rows = slice(0, KEYS if part == 0 else TOKENS)

        @pl.loop(0, 2)
        def _(tile):
            at = pl.ds(pl.multiple_of(tile * TILE, TILE), TILE)
            for pair in range(2):
                q = slice(pair * BLOCK, (pair + 1) * BLOCK)
                k_all = kv[0, g, rows, q]
                v_all = kv[1, g, rows, q]
                new_q = jnp.zeros((BLOCK, TILE), F32)
                new_k = jnp.zeros((TOKENS, BLOCK), F32)
                new_v = jnp.zeros((TOKENS, BLOCK), F32)
                for h in range(2):
                    row = slice(2 * pair + h, 2 * pair + h + 1)
                    q_head = q_src[g, at, q] * head_mask(h)
                    g_head = g_src[g, at, q] * head_mask(h)
                    p = p_src[g, tile, 2 * pair + h]
                    p_grad = dot(v_all, g_head, NT)
                    s_grad = (p * (p_grad - mean_src[g, row, at])).astype(BF)
                    new_v = new_v + dot(p[:TOKENS].astype(BF), g_head, NN)
                    new_k = new_k + dot(s_grad[:TOKENS], q_head, NN)
                    if part == 0:
                        new_q = new_q + dot(k_all * head_mask(h), s_grad, TN)
                if part == 0:
                    dq[g, q, at] += new_q
                dkv[0, g, :, q] += new_k
                dkv[1, g, :, q] += new_v

    back(0, 0)
    scatter.send_late()
    back(0, 1)

    for i in range(2):
        q = slice(i * 1024, (i + 1) * 1024)
        new = dot(attended[...].reshape(8 * BLOCK, HD), branch[:, :, :, q].reshape(8 * BLOCK, 1024), TN)
        for x in range(4):
            for zl in range(2):
                for a in range(2):
                    row = x * 64 + zl * 32 + a * 16
                    out_part[x * 4 + a * 2 + zl, :, q] = new[row : row + 16].astype(BF)

    scatter.wait()
    middle_in.wait()

    def add(r):
        hidden_out[r, :] = restore_rows(middle[r, :] + scatter.total(r)).astype(BF)

    rows_loop(BLOCK, 16, add)

    def turn_back(g, queries_part):
        @pl.loop(0, 4)
        def _(y):
            at = pl.ds(pl.multiple_of(y * BLOCK, BLOCK), BLOCK)
            cosine, sine = turn_tables(table[g, 0, y])
            for pair in range(2):
                q = slice(pair * BLOCK, (pair + 1) * BLOCK)
                if queries_part:
                    new = dq[g, q, at].T * SCALE
                    joined_grad[y, g, :, q] = turn(new, cosine, sine, -1.0).astype(BF)
                else:
                    joined_grad[y, g, :, HD + pair * BLOCK : HD + (pair + 1) * BLOCK] = turn(
                        dkv[0, g, at, q], cosine, sine, -1.0
                    ).astype(BF)
            if not queries_part:
                joined_grad[y, g, :, 2 * HD :] = dkv[1, g, at, :].astype(BF)

    for g in range(2):
        turn_back(g, True)
    trade[0].wait_recv()
    for g in range(2):
        trade[1 + g].wait_recv()
        back(1, g)
        turn_back(g, False)

    for one in trade:
        one.wait_send()
    scatter.finish()


def attend_back(
    table,
    branch,
    gathered,
    attended,
    queries,
    kv,
    lse,
    other_queries,
    other_lse,
    mlp_out,
    middle,
    cid,
):
    return pl.pallas_call(
        kernel_attend_back,
        out_shape=(
            jax.ShapeDtypeStruct((4, 2, BLOCK, 3 * HD), BF),
            jax.ShapeDtypeStruct((16, 16, D), BF),
            jax.ShapeDtypeStruct((BLOCK, D), BF),
        ),
        in_specs=[SM] + [VM] * 8 + [ANY, ANY],
        out_specs=(VM, VM, VM),
        scratch_shapes=[
            pltpu.VMEM((4, 2, BLOCK, D), BF),
            pltpu.VMEM((BLOCK, D), F32),
            pltpu.VMEM((4, BLOCK, D), BF),
            pltpu.VMEM((2, 2, 4, KEYS, TILE), F32),
            pltpu.VMEM((2, 2, 4, TOKENS, TILE), F32),
            pltpu.SemaphoreType.DMA((5,)),
            OUT_ROWS,
            pltpu.VMEM((2, TOKENS, HD), BF),
            pltpu.VMEM((2, TOKENS, HD), BF),
            pltpu.VMEM((2, HD, TOKENS), F32),
            pltpu.VMEM((2, 8, TOKENS), F32),
            pltpu.VMEM((2, 8, TOKENS), F32),
            pltpu.VMEM((2, 2, TOKENS, HD), F32),
            pltpu.SemaphoreType.DMA((3,)),
            pltpu.SemaphoreType.DMA((3,)),
        ]
        + AG_SCRATCH[1:]
        + RS_SCRATCH[2:],
        compiler_params=params(cid),
        name="attend_back",
    )(
        table,
        branch,
        gathered,
        attended,
        queries,
        kv,
        lse,
        other_queries,
        other_lse,
        mlp_out,
        middle,
    )


def kernel_mlp(
    two_hbm,
    grad_hbm,
    w_hbm,
    middle,
    grad_out,
    gains,
    queries,
    lse,
    middle_grad,
    sums,
    own,
    other_queries,
    other_lse,
    out_hbm,
    part_hbm,
    two,
    grad_all,
    w,
    out_part,
    mlp_part,
    inner,
    both_grads,
    local,
    leave,
    send,
    recv,
    *scratch,
):
    y, c, up, opp, dn = ring()
    partner = {"zh": 1 - lax.axis_index("zh")}
    order = (opp, up, dn, y)
    first = order[0]
    loads = load([(two_hbm.at[first], two.at[first])], local)
    weights_in = [
        load([(w_hbm.at[z, :, k], w.at[k, :, z]) for z in range(4)], local, 8 + 4 * k)
        for k in range(3)
    ]
    loads += load([(grad_hbm.at[first], grad_all.at[first])], local, 1)
    for i, b in enumerate(order[1:]):
        pairs = [(two_hbm.at[b], two.at[b]), (grad_hbm.at[b], grad_all.at[b])]
        loads += load(pairs, local, 2 + 2 * i)
    meet(list(ring_peers(up, dn, c)) + [partner])
    trade = [
        remote((send, recv), 0, queries, other_queries, partner),
        remote((send, recv), 1, lse, other_lse, partner),
    ]
    for one in trade:
        one.start()
    held = jnp.logical_or(lane(FP) >= BLOCK, y < 2)
    gate_lanes, up_lanes = pl.ds(0, FP), pl.ds(FP, FP)
    outs = []

    def arrive(k):
        loads.pop(0).wait()
        if not outs:
            for one in weights_in[k]:
                one.wait()

    def partial(block, put):
        arrive(0)
        a = two[block].reshape(TILE, D)
        gate = dot(a, w[0].reshape(D, FP), NN)
        if not outs:
            for one in weights_in[1]:
                one.wait()
        up_proj = dot(a, w[1].reshape(D, FP), NN)
        arrive(2)
        grad = dot(grad_all[block].reshape(TILE, D), w[2].reshape(D, FP), NN)
        sig = 1.0 / (1.0 + jnp.exp(-gate))
        active = gate * sig
        low = (active * up_proj).astype(BF)
        low_gate = (grad * up_proj * sig * (1.0 + gate * (1.0 - sig))).astype(BF)
        low_up = (grad * active).astype(BF)
        zero = jnp.zeros((), BF)
        inner[block] = jnp.where(held, low, zero).reshape(2, BLOCK, FP)
        both_grads[block, :, :, gate_lanes] = jnp.where(held, low_gate, zero).reshape(2, BLOCK, FP)
        both_grads[block, :, :, up_lanes] = jnp.where(held, low_up, zero).reshape(2, BLOCK, FP)

        low_gate = both_grads[block, :, :, gate_lanes].reshape(TILE, FP)
        low_up = both_grads[block, :, :, up_lanes].reshape(TILE, FP)
        for i in range(4):
            q = slice(i * 512, (i + 1) * 512)
            new = dot(low_gate, w[0, i].reshape(512, FP), NT)
            new = new + dot(low_up, w[1, i].reshape(512, FP), NT)
            put(q, new.reshape(2, BLOCK, 512))
        low = inner[block].reshape(TILE, FP)
        for i in range(4):
            q = slice(i * 512, (i + 1) * 512)
            new = dot(low, w[2, i].reshape(512, FP), NT)
            out_part[block, :, :, q] = new.astype(BF).reshape(2, BLOCK, 512)

        outs.extend(load([(out_part.at[block], out_hbm.at[block])], leave, len(outs)))

    done = []

    def weight_grads(count=1):
        begin = len(done)

        @pl.loop(begin, begin + count)
        def _(i):
            q = pl.ds(pl.multiple_of(i * TILE, TILE), TILE)
            a = two[:, :, :, q].reshape(TP * BLOCK, TILE)
            b = grad_all[:, :, :, q].reshape(TP * BLOCK, TILE)
            new = dot(a, both_grads[...].reshape(TP * BLOCK, 2 * FP), TN).astype(BF)
            at = pl.ds(2 * i, 2)
            mlp_part[at, 0] = new[:, :FP].reshape(2, BLOCK, FP)
            mlp_part[at, 1] = new[:, FP:].reshape(2, BLOCK, FP)
            new = dot(b, inner[...].reshape(TP * BLOCK, FP), TN).astype(BF)
            mlp_part[at, 2] = new.reshape(2, BLOCK, FP)

        for i in range(begin, begin + count):
            done.extend(
                load(
                    [(mlp_part.at[pl.ds(2 * i, 2)], part_hbm.at[pl.ds(i % 2 * 2, 2), i // 2])],
                    leave,
                    4 + i,
                )
            )

    scatter = ring_scatter(partial, scratch, lambda: weight_grads(8))
    sums[...] = jnp.zeros_like(sums)

    def back(r):
        row = scatter.total(r)
        normed, inv = layer_norm(middle[r, :])
        grad = grad_out[r, :].astype(F32) + norm_back(row, normed, inv, gains[2:3, :])
        middle_grad[r, :] = grad
        own[r, :] = grad.astype(BF)
        sums[0:1, :] += jnp.sum(row * normed, axis=0, keepdims=True)
        sums[1:2, :] += jnp.sum(row, axis=0, keepdims=True)

    rows_loop(BLOCK, 16, back)
    scatter.finish()
    for one in outs + done + trade:
        one.wait()


def mlp(two, grad_all, w, middle, grad_out, gains, queries, lse, cid):
    block = (4, 2, BLOCK, D)
    return pl.pallas_call(
        kernel_mlp,
        out_shape=(
            jax.ShapeDtypeStruct((BLOCK, D), F32),
            jax.ShapeDtypeStruct((8, D), F32),
            jax.ShapeDtypeStruct((BLOCK, D), BF),
            jax.ShapeDtypeStruct((2, TOKENS, HD), BF),
            jax.ShapeDtypeStruct((2, 8, TOKENS), F32),
            FULL,
            jax.ShapeDtypeStruct((4, 4, 3, BLOCK, FP), BF),
        ),
        in_specs=[ANY] * 3 + [VM] * 5,
        out_specs=(VM,) * 5 + (ANY, ANY),
        scratch_shapes=[
            pltpu.VMEM(block, BF),
            pltpu.VMEM(block, BF),
            pltpu.VMEM((3, 4, 4, BLOCK, FP), BF),
            pltpu.VMEM(block, BF),
            pltpu.VMEM((16, 3, BLOCK, FP), BF),
            pltpu.VMEM((4, 2, BLOCK, FP), BF),
            pltpu.VMEM((4, 2, BLOCK, 2 * FP), BF),
            pltpu.SemaphoreType.DMA((20,)),
            pltpu.SemaphoreType.DMA((12,)),
            pltpu.SemaphoreType.DMA((2,)),
            pltpu.SemaphoreType.DMA((2,)),
        ]
        + RS_SCRATCH,
        compiler_params=params(cid),
        name="mlp",
    )(two, grad_all, w, middle, grad_out, gains, queries, lse)


class PlaneScatter:
    COPIES = 18

    def __init__(self, part, *scratch):
        near, far, relay, mid, last = (scratch[2 * i : 2 * i + 2] for i in range(5))
        sems = scratch[10:12]
        self.part, self.near, self.far, self.passed, self.mid, self.last = (
            part,
            near,
            far,
            relay,
            mid,
            last,
        )
        half = part.shape[-1] // 2
        self.lanes = pl.ds(0, half), pl.ds(half, half)
        x = lax.axis_index("x")
        z = lax.axis_index("zh") * 2 + lax.axis_index("zl")
        self.place = z, x
        low, high = pl.ds(0, 2), pl.ds(2, 2)
        self.low, self.high = low, high

        def to_x(d):
            return {"x": lax.rem(x + d, 4)}

        def to_z(d):
            there = lax.rem(z + d, 4)
            return {"zh": there // 2, "zl": lax.rem(there, 2)}

        self.first, self.late, self.two = [], [], []
        for k in range(2):
            first_to, second_to = (to_z, to_x) if k == 0 else (to_x, to_z)
            base = 9 * k
            up, dn = first_to(1), first_to(3)
            pieces = (
                (self.piece(k, low, 2), far[k].at[0], up),
                (self.piece(k, high, 2), far[k].at[1], dn),
                (self.piece(k, high, 1), near[k].at[0, high], up),
                (self.piece(k, low, 3), near[k].at[1, low], dn),
            )
            for i, (src, dst, peer) in enumerate(pieces):
                self.first.append(remote(sems, base + i, src, dst, peer))
            self.late.append(remote(sems, base + 4, relay[k].at[0], near[k].at[0, low], up))
            self.late.append(remote(sems, base + 5, relay[k].at[1], near[k].at[1, high], dn))
            for d in range(1, 4):
                there = lax.rem(self.place[1 - k] + d, 4)
                copy = remote(sems, base + 5 + d, mid[k].at[there], last[k].at[d - 1], second_to(d))
                self.two.append(copy)

    def piece(self, k, rest, d):
        there = lax.rem(self.place[k] + d, 4)
        at = (rest, there) if k == 0 else (there, rest)
        return self.part.at[at + (slice(None), self.lanes[k])]

    def start(self):
        for copy in self.first:
            copy.start()

    def relay(self):
        for k in range(2):
            for i, (rest, d) in enumerate(((self.low, 1), (self.high, 3))):
                self.first[4 * k + i].wait_recv()
                self.passed[k][i] = (
                    self.piece(k, rest, d)[...].astype(F32) + self.far[k][i].astype(F32)
                ).astype(BF)
                self.late[2 * k + i].start()

    def middle(self):
        for k in range(2):
            for copy in self.first[4 * k + 2 : 4 * k + 4] + self.late[2 * k : 2 * k + 2]:
                copy.wait_recv()

            @pl.loop(0, 4)
            def _(i, k=k):
                at = (i, self.place[0]) if k == 0 else (self.place[1], i)
                own = self.part[at + (slice(None), self.lanes[k])].astype(F32)
                near = self.near[k][0, i].astype(F32) + self.near[k][1, i].astype(F32)
                self.mid[k][i] = (own + near).astype(BF)

            for copy in self.two[3 * k : 3 * k + 3]:
                copy.start()

    def finish(self, out):
        for copy in self.two:
            copy.wait_recv()
        for k in range(2):
            out[:, self.lanes[k]] = (
                self.mid[k][self.place[1 - k]].astype(F32)
                + jnp.sum(self.last[k][...].astype(F32), axis=0)
            ).astype(BF)
        for copy in self.first + self.late + self.two:
            copy.wait_send()


def plane_scratch(rows, lanes):
    half = lanes // 2
    shapes = [(2, 4, rows, half), (2, 2, rows, half), (2, 2, rows, half), (4, rows, half)]
    shapes += [(3, rows, half)]
    return [pltpu.VMEM(shape, BF) for shape in shapes for _ in range(2)] + [
        pltpu.SemaphoreType.DMA((PlaneScatter.COPIES,)),
        pltpu.SemaphoreType.DMA((PlaneScatter.COPIES,)),
    ]


def plane_peers():
    peers = []
    for d in range(1, 4):
        z = lax.rem(lax.axis_index("zh") * 2 + lax.axis_index("zl") + d, 4)
        peers.append({"x": lax.rem(lax.axis_index("x") + d, 4)})
        peers.append({"zh": z // 2, "zl": lax.rem(z, 2)})
    return peers


def kernel_qkv_back(
    joined_grad,
    weight_hbm,
    hidden,
    middle_hbm,
    gains,
    tokens_hbm,
    out_part,
    input_grad,
    sums,
    shift_sum,
    qkv_sum,
    out_sum,
    tokens,
    weight,
    middle_grad,
    local,
    part,
    *scratch,
):
    token_in = load([(tokens_hbm.at[y], tokens.at[y]) for y in range(4)], local)
    weight_in, middle_in = load([(weight_hbm, weight), (middle_hbm, middle_grad)], local, 4)
    y, c, up, opp, dn = ring()
    meet(list(ring_peers(up, dn, c)) + plane_peers())
    out_scatter = PlaneScatter(out_part, *scratch[:12])
    qkv_scatter = PlaneScatter(part, *scratch[12:24])
    out_scatter.start()
    flat = joined_grad[...].reshape(TP * BLOCK, 3 * HD)
    def weight_grads():
        for one in token_in:
            one.wait()
        for i in range(4):
            q = slice(i * 512, (i + 1) * 512)
            new = dot(tokens[:, :, :, q].reshape(TP * BLOCK, 512), flat, TN).astype(BF)
            part[i] = new.reshape(4, BLOCK, 3 * HD)
        qkv_scatter.start()
        weight_in.wait()
        middle_in.wait()

    def partial(block, put):
        a = joined_grad[block].reshape(2 * BLOCK, 3 * HD)
        for i in range(4):
            q = slice(i * 512, (i + 1) * 512)
            put(q, dot(a, weight[q, :], NT).reshape(2, BLOCK, 512))

    weight_grads()
    out_scatter.relay()
    scatter = ring_scatter(partial, scratch[24:], qkv_scatter.relay)
    sums[...] = jnp.zeros_like(sums)

    def back(r):
        row = scatter.total(r)
        normed, inv = layer_norm(hidden[r, :].astype(F32))
        input_grad[r, :] = restore_rows(
            middle_grad[r, :] + norm_back(row, normed, inv, gains[0:1, :])
        )
        sums[0:1, :] += jnp.sum(row * normed, axis=0, keepdims=True)
        sums[1:2, :] += jnp.sum(row, axis=0, keepdims=True)

    rows_loop(BLOCK, 16, back)
    out_scatter.middle()
    qkv_scatter.middle()
    shift_sum[...] = jnp.broadcast_to(
        jnp.sum(flat.astype(F32), axis=0, keepdims=True), shift_sum.shape
    )
    scatter.finish()
    out_scatter.finish(out_sum)
    qkv_scatter.finish(qkv_sum)


def qkv_back(joined_grad, weight, hidden, middle_grad, gains, tokens, out_part, cid):
    return pl.pallas_call(
        kernel_qkv_back,
        out_shape=(
            jax.ShapeDtypeStruct((BLOCK, D), F32),
            jax.ShapeDtypeStruct((8, D), F32),
            jax.ShapeDtypeStruct((8, 3 * HD), F32),
            jax.ShapeDtypeStruct((BLOCK, 3 * HD), BF),
            jax.ShapeDtypeStruct((16, D), BF),
        ),
        in_specs=[VM, ANY, VM, ANY, VM, ANY, VM],
        out_specs=(VM,) * 5,
        scratch_shapes=[
            pltpu.VMEM((4, 2, BLOCK, D), BF),
            pltpu.VMEM((D, 3 * HD), BF),
            pltpu.VMEM((BLOCK, D), F32),
            pltpu.SemaphoreType.DMA((6,)),
            pltpu.VMEM((4, 4, BLOCK, 3 * HD), BF),
        ]
        + plane_scratch(16, D)
        + plane_scratch(BLOCK, 3 * HD)
        + RS_SCRATCH,
        compiler_params=params(cid),
        name="qkv_back",
    )(joined_grad, weight, hidden, middle_grad, gains, tokens, out_part.reshape(4, 4, 16, D))


TP_STEPS = [(dy, dc) for dy in range(4) for dc in range(2) if (dy, dc) != (0, 0)]
XZ_STEPS = [(dx, dz) for dx in range(4) for dz in range(4) if (dx, dz) != (0, 0)]


def tp_peer(step):
    y = lax.rem(lax.axis_index("y") + step[0], 4)
    c = lax.rem(lax.axis_index("core") + step[1], 2)
    return {"y": y, "core": c}, y * 2 + c


def xz_peer(step):
    x = lax.rem(lax.axis_index("x") + step[0], 4)
    z = lax.rem(lax.axis_index("zh") * 2 + lax.axis_index("zl") + step[1], 4)
    return {"x": x, "zh": z // 2, "zl": lax.rem(z, 2)}, x * 4 + z


def meet_all(split):
    peers = [tp_peer(s)[0] for s in TP_STEPS] + [xz_peer(s)[0] for s in XZ_STEPS]
    barrier = pltpu.get_barrier_semaphore()
    for peer in peers:
        pl.semaphore_signal(
            barrier, inc=1, device_id=peer, device_id_type=pl.DeviceIdType.MESH
        )

    @pl.when(split)
    def _():
        pl.semaphore_signal(
            barrier, inc=1, device_id=swap_peer(), device_id_type=pl.DeviceIdType.MESH
        )

    pl.semaphore_wait(barrier, len(peers) + split.astype(jnp.int32))


def swap_peer():
    return {"zh": lax.axis_index("core"), "core": lax.axis_index("zh")}


def swap_start(split, src, dst, local_sem, sems, i):
    @pl.when(split)
    def _():
        remote(sems, i, src, dst, swap_peer()).start()

    @pl.when(jnp.logical_not(split))
    def _():
        pltpu.make_async_copy(src, dst, local_sem).start()


def swap_wait(split, src, dst, local_sem, sems, i):
    @pl.when(split)
    def _():
        remote(sems, i, src, dst, swap_peer()).wait()

    @pl.when(jnp.logical_not(split))
    def _():
        pltpu.make_async_copy(src, dst, local_sem).wait()


N_TP = len(TP_STEPS)
N_XZ = len(XZ_STEPS)


class PlaneGather:
    COPIES = 14

    def __init__(self, src, full, local_sem, send, recv, x_first):
        sems = send, recv
        a, b = pl.ds(0, x_first), pl.ds(x_first, src.shape[-1] - x_first)
        rest = (slice(None),) * (len(src.shape) - 1)
        x = lax.axis_index("x")
        z = lax.axis_index("zh") * 2 + lax.axis_index("zl")
        self.one, self.two, self.three = [], [], []
        every, low, high = slice(None), pl.ds(0, 2), pl.ds(2, 2)

        def x_at(d):
            return lax.rem(x + d, 4)

        def z_at(d):
            return lax.rem(z + d, 4)

        def to_x(d):
            return {"x": x_at(d)}

        def to_z(d):
            return {"zh": z_at(d) // 2, "zl": lax.rem(z_at(d), 2)}

        def pass_on(i, at, peer):
            return remote(sems, i, full.at[at], full.at[at], peer)

        if x_first:
            at = rest + (a,)
            for d in range(1, 4):
                self.one.append(remote(sems, d - 1, src.at[at], full.at[(x, z) + at], to_x(d)))
            self.two.append(pass_on(6, (every, z) + at, to_z(1)))
            self.two.append(pass_on(7, (every, z) + at, to_z(3)))
            self.three.append(pass_on(8, (low, z_at(3)) + at, to_z(1)))
            self.three.append(pass_on(9, (high, z_at(1)) + at, to_z(3)))
        at = rest + (b,)
        for d in range(1, 4):
            self.one.append(remote(sems, 2 + d, src.at[at], full.at[(x, z) + at], to_z(d)))
        self.two.append(pass_on(10, (x, every) + at, to_x(1)))
        self.two.append(pass_on(11, (x, every) + at, to_x(3)))
        self.three.append(pass_on(12, (x_at(3), low) + at, to_x(1)))
        self.three.append(pass_on(13, (x_at(1), high) + at, to_x(3)))
        self.here = pltpu.make_async_copy(src, full.at[x, z], local_sem)

    def start(self):
        for copy in self.one:
            copy.start()
        self.here.start()

    def middle(self):
        self.here.wait()
        for copy in self.one:
            copy.wait_recv()
        for copy in self.two:
            copy.start()

    def forward(self):
        for copy, later in zip(self.two, self.three):
            copy.wait_recv()
            later.start()

    def finish(self):
        for copy in self.three:
            copy.wait_recv()
        for copy in self.one + self.two + self.three:
            copy.wait_send()


PG_SEMS = [
    pltpu.SemaphoreType.DMA,
    pltpu.SemaphoreType.DMA((PlaneGather.COPIES,)),
    pltpu.SemaphoreType.DMA((PlaneGather.COPIES,)),
]


def first_lane(rank):
    return jnp.where(rank < 4, 6 * rank, 5 * rank + 3) * BLOCK


def head_lane(part, rank):
    return part * D + (lax.rem(rank, 2) * 4 + rank // 2) * HD


def lanes_at(start, n):
    return pl.ds(pl.multiple_of(start, BLOCK), n)


def spread_gains(small_all, gains, entries):
    rows = small_all[...].reshape(BLOCK, BLOCK)
    source = lax.broadcasted_iota(jnp.int32, (BLOCK, 1), 0)
    f = lane(D)
    mine = (f // 16) == source
    for i in entries:
        pick = (source == 16 * i + lax.rem(f, 16)).astype(F32)
        value = jnp.dot(rows, pick, preferred_element_type=F32)
        gains[i : i + 1, :] = jnp.sum(jnp.where(mine, value, 0.0), axis=0, keepdims=True)


def spread_shift(small_all, shift, rank):
    rows = small_all[...].reshape(BLOCK, BLOCK)
    source = lax.broadcasted_iota(jnp.int32, (BLOCK, 1), 0)
    core = lax.rem(source, 2)
    y = lax.rem(source // 2, 4)
    zl = lax.rem(source // 8, 2)
    zh = lax.rem(source // 16, 2)
    x = source // 32
    owner = (zh * 4 + y) * 16 + x * 4 + zl * 2 + core
    for i in range(3):
        j = head_lane(i, rank) + lane(HD)
        pick = (source == 64 + lax.rem(j, 48)).astype(F32)
        value = jnp.dot(rows, pick, preferred_element_type=F32)
        value = jnp.sum(jnp.where(j // 48 == owner, value, 0.0), axis=0, keepdims=True)
        shift[:, i * HD : (i + 1) * HD] = value


def kernel_front(
    small,
    hidden_in,
    w_qkv,
    w_gate,
    w_up,
    w_down,
    w_out,
    small_all,
    gains,
    shift,
    qkv_full,
    mlp_rows,
    out_rows,
    hidden,
    full,
    own,
    normed,
    qkv_rows,
    local,
    send,
    recv,
    *sems,
):
    me = lax.axis_index("y") * 2 + lax.axis_index("core")
    xz = lax.axis_index("x") * 4 + lax.axis_index("zh") * 2 + lax.axis_index("zl")
    split = lax.axis_index("zh") != lax.axis_index("core")
    meet_all(split)
    cp = functools.partial(remote, (send, recv))
    tiny, qkv, mlp = [], [], []
    for k, step in enumerate(TP_STEPS):
        peer, there = tp_peer(step)
        tiny.append(cp(k, small, small_all.at[xz, me], peer))
        for i in range(3):
            src = w_qkv.at[:, lanes_at(head_lane(i, there), HD)]
            dst = qkv_rows.at[me, :, pl.ds(i * HD, HD)]
            qkv.append(cp((1 + i) * N_TP + k, src, dst, peer))
        for i, w in enumerate((w_gate, w_up, w_down)):
            src = w.at[:, lanes_at(first_lane(there), FP)]
            mlp.append(cp((4 + i) * N_TP + k, src, mlp_rows.at[i, me], peer))
    keep = [pltpu.make_async_copy(small, small_all.at[xz, me], local.at[0])]
    for i, w in enumerate((w_gate, w_up, w_down)):
        src = w_qkv.at[:, lanes_at(head_lane(i, me), HD)]
        dst = qkv_rows.at[me, :, pl.ds(i * HD, HD)]
        keep.append(pltpu.make_async_copy(src, dst, local.at[1 + i]))
        src = w.at[:, lanes_at(first_lane(me), FP)]
        keep.append(pltpu.make_async_copy(src, mlp_rows.at[i, me], local.at[4 + i]))
    for one in tiny + qkv + mlp + keep:
        one.start()
    last = 7 * N_TP + N_XZ
    for one in tiny:
        one.wait()
    keep[0].wait()
    wide = []
    for k, step in enumerate(XZ_STEPS):
        peer, _ = xz_peer(step)
        wide.append(cp(7 * N_TP + k, small_all.at[xz], small_all.at[xz], peer))
    for one in wide:
        one.start()
    for one in qkv + keep[1:]:
        one.wait()
    plane = PlaneGather(qkv_rows, qkv_full, *sems[:3], 3 * HD // 2)
    plane.start()
    swap_start(split, w_out, out_rows, local.at[7], (send, recv), last)

    def norm(r):
        row = permute_rows(hidden_in[r, :].astype(F32))
        hidden[r, :] = row.astype(BF)
        normed[r, :], _ = layer_norm(row)

    rows_loop(BLOCK, 16, norm)
    gains[...] = jnp.zeros_like(gains)
    for one in wide:
        one.wait()
    spread_gains(small_all, gains, (0, 1))

    def scale(r):
        own[r, :] = (normed[r, :] * gains[0:1, :] + gains[1:2, :]).astype(BF)

    rows_loop(BLOCK, 16, scale)
    gather = RingGather(own, full, sems[3], sems[4:])
    gather.start()
    plane.middle()
    gather.forward()
    spread_gains(small_all, gains, (2, 3))
    spread_shift(small_all, shift, me)
    gather.share()
    plane.forward()
    gather.share_far()
    for one in mlp:
        one.wait()
    swap_wait(split, w_out, out_rows, local.at[7], (send, recv), last)
    gather.finish()
    plane.finish()


def front(small, hidden, w_qkv, w_gate, w_up, w_down, w_out, cid):
    n = 7 * N_TP + N_XZ + 1
    return pl.pallas_call(
        kernel_front,
        out_shape=(
            jax.ShapeDtypeStruct((16, TP, 1, BLOCK), F32),
            jax.ShapeDtypeStruct((8, D), F32),
            jax.ShapeDtypeStruct((1, 3 * HD), F32),
            jax.ShapeDtypeStruct((4, 4, TP, 16, 3 * HD), BF),
            jax.ShapeDtypeStruct((3, TP, 16, FP), BF),
            jax.ShapeDtypeStruct((16, D), BF),
            jax.ShapeDtypeStruct((BLOCK, D), BF),
            FULL,
        ),
        in_specs=[ANY, VM] + [ANY] * 5,
        out_specs=(VM, VM, VM, ANY, ANY, ANY, VM, ANY),
        scratch_shapes=[
            pltpu.VMEM((BLOCK, D), BF),
            pltpu.VMEM((BLOCK, D), F32),
            pltpu.VMEM((TP, 16, 3 * HD), BF),
            pltpu.SemaphoreType.DMA((8,)),
            pltpu.SemaphoreType.DMA((n,)),
            pltpu.SemaphoreType.DMA((n,)),
        ]
        + PG_SEMS
        + AG_SCRATCH[1:],
        compiler_params=params(cid),
        name="front",
    )(small, hidden, w_qkv, w_gate, w_up, w_down, w_out)


def kernel_collect(
    one_sums,
    two_sums,
    shift,
    qkv,
    mlp,
    out,
    small_all,
    qkv_all,
    mlp_all,
    out_all,
    terms,
    terms_in,
    own,
    local,
    *sems,
):
    me = lax.axis_index("y") * 2 + lax.axis_index("core")
    xz = lax.axis_index("x") * 4 + lax.axis_index("zh") * 2 + lax.axis_index("zl")
    split = lax.axis_index("zh") != lax.axis_index("core")
    for p in range(16):
        q = slice(p * BLOCK, (p + 1) * BLOCK)
        terms[p, 0:2, :] = one_sums[0:2, q]
        terms[p, 2:4, :] = two_sums[0:2, q]
        for i in range(6):
            terms[p, 8 + i : 9 + i, :] = shift[0:1, i * BLOCK : (i + 1) * BLOCK]
        for i in (4, 5, 6, 7, 14, 15):
            terms[p, i : i + 1, :] = jnp.zeros((1, BLOCK), F32)
    meet_all(split)
    cp = functools.partial(remote, sems)
    big, extra, wide = [], [], []
    near, tile = pl.ds(BLOCK, FP - BLOCK), pl.ds(0, BLOCK)
    base = N_XZ + N_TP
    for k, step in enumerate(TP_STEPS):
        peer, there = tp_peer(step)
        dst = mlp_all.at[:, :, lanes_at(first_lane(me) + BLOCK, FP - BLOCK)]
        big.append(cp(base + k, mlp.at[:, there, :, near], dst, peer))
        dst = mlp_all.at[:, :, lanes_at(first_lane(me), BLOCK)]
        extra.append(cp(base + N_TP + k, mlp.at[:, there, :, tile], dst, peer))
        big.append(cp(base + 2 * N_TP + k, qkv.at[there], qkv_all.at[me], peer))
    for k, step in enumerate(XZ_STEPS):
        peer, there = xz_peer(step)
        wide.append(cp(k, terms.at[there], terms_in.at[xz], peer))
    dst = mlp_all.at[:, :, lanes_at(first_lane(me) + BLOCK, FP - BLOCK)]
    keep = [
        pltpu.make_async_copy(mlp.at[:, me, :, near], dst, local.at[0]),
        pltpu.make_async_copy(qkv.at[me], qkv_all.at[me], local.at[1]),
    ]
    dst = mlp_all.at[:, :, lanes_at(first_lane(me), BLOCK)]
    keep_tile = pltpu.make_async_copy(mlp.at[:, me, :, tile], dst, local.at[2])
    first_four = me < 4
    for one in big[0::2]:
        one.start()

    @pl.when(first_four)
    def _():
        keep_tile.start()
        for one in extra:
            one.start()

    for one in wide + big[1::2] + keep:
        one.start()

    last = base + 3 * N_TP
    swap_start(split, out, out_all, local.at[3], sems, last)
    for one in wide:
        one.wait()
    terms_in[xz] = terms[xz]
    own[...] = jnp.sum(terms_in[...], axis=0)
    tiny = []
    for k, step in enumerate(TP_STEPS):
        peer, _ = tp_peer(step)
        tiny.append(cp(N_XZ + k, own, small_all.at[me], peer))
    for one in tiny:
        one.start()
    for one in big + keep:
        one.wait()
    for k, step in enumerate(TP_STEPS):
        source = lax.rem(lax.axis_index("y") + 4 - step[0], 4) * 2 + lax.rem(
            lax.axis_index("core") + 2 - step[1], 2
        )

        @pl.when(source < 4)
        def _(k=k):
            extra[k].wait_recv()

    @pl.when(first_four)
    def _():
        keep_tile.wait()
        for one in extra:
            one.wait_send()

    swap_wait(split, out, out_all, local.at[3], sems, last)
    for one in tiny:
        one.wait()
    small_all[me] = own[...]


def collect(one_sums, two_sums, shift, qkv, mlp, out, cid):
    n = N_XZ + 4 * N_TP + 1
    return pl.pallas_call(
        kernel_collect,
        out_shape=(
            jax.ShapeDtypeStruct((TP, 16, BLOCK), F32),
            jax.ShapeDtypeStruct((TP, 16, 3 * HD), BF),
            jax.ShapeDtypeStruct((3, 16, FF), BF),
            jax.ShapeDtypeStruct((16, D), BF),
        ),
        in_specs=[VM] * 3 + [ANY] * 3,
        out_specs=(VM, ANY, ANY, ANY),
        scratch_shapes=[
            pltpu.VMEM((16, 16, BLOCK), F32),
            pltpu.VMEM((16, 16, BLOCK), F32),
            pltpu.VMEM((16, BLOCK), F32),
            pltpu.SemaphoreType.DMA((4,)),
            pltpu.SemaphoreType.DMA((n,)),
            pltpu.SemaphoreType.DMA((n,)),
        ],
        compiler_params=params(cid),
        name="collect",
    )(one_sums, two_sums, shift, qkv, mlp, out)


def kernel_finish(
    qkv_hbm,
    mlp_hbm,
    out_hbm,
    hidden_hbm,
    grad_hbm,
    qkv_grad,
    gate,
    up,
    down,
    out,
    hidden_out,
    input_grad,
    qkv_all,
    mlp_all,
    out_all,
    local,
):
    pairs = [(qkv_hbm, qkv_all), (mlp_hbm, mlp_all), (out_hbm, out_all)]
    pairs += [(hidden_hbm, hidden_out), (grad_hbm, input_grad)]
    for one in load(pairs, local):
        one.wait()
    for t in range(TP):
        for i in range(3):
            first = i * D + (t % 2 * 4 + t // 2) * HD
            qkv_grad[:, first : first + HD] = qkv_all[t, :, i * HD : (i + 1) * HD].astype(F32)
    gate[...] = mlp_all[0].astype(F32)
    up[...] = mlp_all[1].astype(F32)
    down[...] = mlp_all[2].astype(F32)
    out[...] = restore_rows(out_all[...].astype(F32))


def finish(qkv_all, mlp_all, out_all, hidden, grad):
    wide = jax.ShapeDtypeStruct((16, FF), F32)
    return pl.pallas_call(
        kernel_finish,
        out_shape=(
            jax.ShapeDtypeStruct((16, 3 * D), F32),
            wide,
            wide,
            wide,
            jax.ShapeDtypeStruct((16, D), F32),
            jax.ShapeDtypeStruct((BLOCK, D), BF),
            jax.ShapeDtypeStruct((BLOCK, D), F32),
        ),
        in_specs=[ANY] * 5,
        out_specs=(VM,) * 7,
        scratch_shapes=[
            pltpu.VMEM((TP, 16, 3 * HD), BF),
            pltpu.VMEM((3, 16, FF), BF),
            pltpu.VMEM((16, D), BF),
            pltpu.SemaphoreType.DMA((5,)),
        ],
        compiler_params=pltpu.CompilerParams(vmem_limit_bytes=60 * 1024 * 1024),
        name="finish",
    )(qkv_all, mlp_all, out_all, hidden, grad)


def body(
    hidden_in,
    cotangent,
    seq_lengths,
    slot_block,
    ln1_gain,
    ln1_bias,
    w_qkv,
    qkv_bias,
    w_out,
    ln2_gain,
    ln2_bias,
    w_gate,
    w_up,
    w_down,
):
    f32 = F32
    zh = lax.axis_index("zh")
    y = lax.axis_index("y")
    core = lax.axis_index("core")
    xz = lax.axis_index("x") * 4 + zh * 2 + lax.axis_index("zl")

    small, first = jnp.zeros(BLOCK, f32), 0
    pieces = (ln1_gain, ln1_bias, ln2_gain, ln2_bias, qkv_bias, seq_lengths[0], slot_block[0])
    for piece in pieces:
        n = piece.shape[0]
        small = small + jnp.pad(piece.astype(f32), (first, BLOCK - first - n))
        first += n
    small_all, gains, shift, qkv_full, mlp_rows, out_rows, hidden, one_all = front(
        small.reshape(1, BLOCK), hidden_in[0], w_qkv, w_gate, w_up, w_down, w_out, 0
    )
    qkv_full = qkv_full.reshape(D, 3 * HD)
    mlp_full = lax.all_gather(mlp_rows.reshape(3, BLOCK, FP), ZX, axis=0, tiled=False)
    small_all = small_all.reshape(BLOCK, BLOCK)

    plan = lax.dynamic_slice_in_dim(small_all, xz * TP + y * 2, 2, 0)[:, 112:122].astype(jnp.int32)
    blocks = plan[:, 2:].reshape(2, 2, 4)
    own_blocks = lax.dynamic_index_in_dim(blocks, zh, axis=1, keepdims=False)
    other_blocks = lax.dynamic_index_in_dim(blocks, 1 - zh, axis=1, keepdims=False)
    start = jnp.concatenate([own_blocks, other_blocks], axis=1) * BLOCK
    first_pad = (plan[:, 0:1] + BLOCK - 1) // BLOCK * BLOCK
    second = (start >= first_pad).astype(jnp.int32)
    limit = jnp.where(second == 1, plan[:, 1:2], plan[:, 0:1])
    table = jnp.stack([start - second * first_pad, second, limit], axis=1)
    queries, kv, lse, attended, grad_out, out_full, middle, grad_all, two_all = attend(
        table, one_all, qkv_full, shift, cotangent[0], out_rows, hidden, gains, 6
    )
    middle_grad, two_sums, branch, other_queries, other_lse, mlp_out, mlp_part = mlp(
        two_all, grad_all, mlp_full.reshape(4, 4, 3, BLOCK, FP), middle, grad_out, gains, queries, lse, 3
    )
    mlp_sum = lax.psum_scatter(
        mlp_part.reshape(16 * 3 * BLOCK, FP), ZX, scatter_dimension=0, tiled=True
    )
    joined_grad, out_part, hidden_out = attend_back(
        table,
        branch,
        out_full,
        attended,
        queries,
        kv,
        lse,
        other_queries,
        other_lse,
        mlp_out,
        middle,
        7,
    )
    input_grad, one_sums, shift_sum, qkv_sum, out_sum = qkv_back(
        joined_grad, qkv_full, hidden, middle_grad, gains, one_all, out_part, 4
    )

    small_sum, qkv_all, mlp_all, out_all = collect(
        one_sums,
        two_sums,
        shift_sum,
        qkv_sum.reshape(TP, 16, FP),
        mlp_sum.reshape(3, TP, 16, FP),
        out_sum,
        5,
    )
    qkv_grad, gate_sum, up_sum, down_sum, out_grad, hidden_out, input_grad = finish(
        qkv_all, mlp_all, out_all, hidden_out, input_grad
    )
    vectors = jnp.sum(small_sum[:, :4], axis=0)
    vectors = lax.dynamic_slice_in_dim(vectors, (y * 2 + core) * 16, 16, 1)
    shift_grad = small_sum[:, 8:14].reshape(4, 2, 3, HD).transpose(2, 1, 0, 3).reshape(128, 48)
    row = (zh * 4 + y) * 16 + lax.axis_index("x") * 4 + lax.axis_index("zl") * 2 + core
    shift_grad = lax.dynamic_index_in_dim(shift_grad, row, 0, False)
    return (
        hidden_out[None],
        input_grad[None],
        vectors[0],
        vectors[1],
        qkv_grad,
        shift_grad,
        out_grad,
        vectors[2],
        vectors[3],
        gate_sum,
        up_sum,
        down_sum,
    )


def solution(mesh):
    inner = Mesh(mesh.devices.reshape(2, 4, 4, 2, 2), ROWS)
    rows = P(ROWS)
    tokens = P(GRP, SLOT, None)
    placed = (
        tokens,
        tokens,
        P(GRP, None),
        P(GRP, None),
        rows,
        rows,
        P(ROWS, None),
        rows,
        P(ROWS, None),
        rows,
        rows,
        P(ROWS, None),
        P(ROWS, None),
        P(ROWS, None),
    )
    return jax.shard_map(
        body,
        mesh=inner,
        in_specs=placed,
        out_specs=(
            tokens,
            tokens,
            rows,
            rows,
            P(ROWS, None),
            rows,
            P(ROWS, None),
            rows,
            rows,
            P(ROWS, None),
            P(ROWS, None),
            P(ROWS, None),
        ),
        check_vma=False,
    )
```

```python
import functools

import jax
import jax.numpy as jnp
from jax import lax
from jax.experimental import pallas as pl
from jax.experimental.pallas import tpu as pltpu
from jax.sharding import Mesh
from jax.sharding import PartitionSpec as P

D = 2048
HEADS = 32
HEAD_DIM = 64
ROT = 16
FF = 5632
BLOCK = 128
TP = 8
HD = D // TP
FC = FF // TP

EPS = 1e-05
NEG = -1e30
SCALE = HEAD_DIM ** (-0.5)
TPA = ("y", "core")
ZX = ("zh", "zl", "x")
ROWS = ("zh", "y", "x", "zl", "core")
GRP = ("x", "zl", "core")
SLOT = ("zh", "y")


def permute_rows(row):
    group = lane(BLOCK) // 32
    tiles = []
    for x in range(4):
        for zh in range(2):
            for zl in range(2):
                out = None
                for y in range(4):
                    first = zh * 1024 + y * 256 + x * 64 + zl * 32
                    tile = first // BLOCK * BLOCK
                    shift = (32 * y - first % BLOCK) % BLOCK
                    value = row[:, tile : tile + BLOCK]
                    value = pltpu.roll(value, shift, 1) if shift else value
                    out = value if out is None else jnp.where(group == y, value, out)
                tiles.append(out)
    return jnp.concatenate(tiles, axis=1)


def restore_rows(row):
    group = lane(BLOCK) // 32
    tiles = []
    for t in range(D // BLOCK):
        out = None
        for j in range(4):
            first = t * BLOCK + 32 * j
            zh, y, x, zl = first // 1024, first // 256 % 4, first // 64 % 4, first // 32 % 2
            tile = (x * 4 + zh * 2 + zl) * BLOCK
            shift = (32 * j - 32 * y) % BLOCK
            value = row[:, tile : tile + BLOCK]
            value = pltpu.roll(value, shift, 1) if shift else value
            out = value if out is None else jnp.where(group == j, value, out)
        tiles.append(out)
    return jnp.concatenate(tiles, axis=1)


def layer_norm(values):
    average = jnp.mean(values, axis=-1, keepdims=True)
    centred = values - average
    inv_scale = lax.rsqrt(jnp.mean(centred * centred, axis=-1, keepdims=True) + EPS)
    return centred * inv_scale, inv_scale


def norm_back(grad_in, normed, inv_scale, gain):
    scaled = grad_in * gain
    return inv_scale * (
        scaled
        - jnp.mean(scaled, axis=-1, keepdims=True)
        - normed * jnp.mean(scaled * normed, axis=-1, keepdims=True)
    )


FP = 768
HALF = BLOCK // 2
ANY = pl.BlockSpec(memory_space=pl.ANY)
VM = pl.BlockSpec(memory_space=pltpu.VMEM)
BF = jnp.bfloat16
F32 = jnp.float32


def params(cid):
    return pltpu.CompilerParams(
        collective_id=cid, has_side_effects=True, vmem_limit_bytes=56 * 1024 * 1024
    )


def meet(peers):
    barrier = pltpu.get_barrier_semaphore()
    for peer in peers:
        pl.semaphore_signal(
            barrier, inc=1, device_id=peer, device_id_type=pl.DeviceIdType.MESH
        )
    pl.semaphore_wait(barrier, len(peers))


def remote(sems, i, src, dst, peer):
    return pltpu.make_async_remote_copy(
        src_ref=src,
        dst_ref=dst,
        send_sem=sems[0].at[i],
        recv_sem=sems[1].at[i],
        device_id=peer,
        device_id_type=pl.DeviceIdType.MESH,
    )


def ring():
    y = lax.axis_index("y")
    c = lax.axis_index("core")
    up = lax.rem(y + 1, 4)
    opp = lax.rem(y + 2, 4)
    dn = lax.rem(y + 3, 4)
    return y, c, up, opp, dn


def ring_peers(up, dn, c):
    return {"y": up}, {"y": dn}, {"core": 1 - c}


N_AG = 11
N_RS = 10


class RingGather:
    def __init__(self, own, full, local_sem, sems):
        y, c, up, opp, dn = ring()
        to_up, to_dn, to_sib = ring_peers(up, dn, c)
        first, last = pl.ds(0, HALF), pl.ds(HALF, HALF)
        cp = functools.partial(remote, sems)

        def pass_on(i, block, peer, *rows):
            ref = full.at[(block, c) + rows]
            return cp(i, ref, ref, peer)

        self.up1 = cp(0, own.at[first], full.at[y, c, first], to_up)
        self.dn1 = cp(1, own.at[last], full.at[y, c, last], to_dn)
        self.up2 = cp(2, own.at[last], full.at[y, c, last], to_up)
        self.dn2 = cp(3, own.at[first], full.at[y, c, first], to_dn)
        self.here = pltpu.make_async_copy(own, full.at[y, c], local_sem)
        self.far1 = pass_on(5, dn, to_up, first)
        self.far2 = pass_on(6, up, to_dn, last)
        self.sib = [
            cp(4, own, full.at[y, c], to_sib),
            pass_on(7, dn, to_sib),
            pass_on(8, up, to_sib),
            pass_on(9, opp, to_sib, first),
            pass_on(10, opp, to_sib, last),
        ]

    def start(self):
        for one in (self.up1, self.dn1, self.up2, self.dn2, self.sib[0], self.here):
            one.start()

    def forward(self):
        self.up1.wait_recv()
        self.far1.start()
        self.dn1.wait_recv()
        self.far2.start()

    def share(self):
        self.up2.wait_recv()
        self.sib[1].start()
        self.dn2.wait_recv()
        self.sib[2].start()

    def share_far(self):
        self.far1.wait_recv()
        self.sib[3].start()
        self.far2.wait_recv()
        self.sib[4].start()

    def sends(self):
        return [self.up1, self.dn1, self.up2, self.dn2, self.far1, self.far2] + self.sib

    def finish(self):
        for one in self.sib:
            one.wait_recv()
        self.here.wait()
        for one in self.sends():
            one.wait_send()

    def run(self, work=None):
        for step in (self.start, self.forward, self.share, self.share_far):
            step()
            if work is not None:
                work()
        self.finish()


def rows_loop(count, step, body):
    @pl.loop(0, count // step)
    def _(i):
        body(pl.ds(pl.multiple_of(i * step, step), step))


RS_SCRATCH = [
    pltpu.VMEM((4, BLOCK, D), F32),
    pltpu.VMEM((4, BLOCK, D), BF),
    pltpu.VMEM((4, BLOCK, D), BF),
    pltpu.VMEM((2, HALF, D), BF),
    pltpu.VMEM((2, HALF, D), BF),
    pltpu.VMEM((2, BLOCK, D), BF),
    pltpu.VMEM((2, BLOCK, D), BF),
    pltpu.SemaphoreType.DMA((N_RS,)),
    pltpu.SemaphoreType.DMA((N_RS,)),
]


class RingScatter:
    def __init__(self, mine, sib_out, sib_in, far_out, far_in, near_out, near_in, *sems):
        y, c, up, opp, dn = ring()
        to_up, to_dn, to_sib = ring_peers(up, dn, c)
        first, last = pl.ds(0, HALF), pl.ds(HALF, HALF)
        cp = functools.partial(remote, sems)
        self.order = (opp, up, dn, y)
        self.mine, self.sib_in = mine, sib_in
        self.far_out, self.far_in = far_out, far_in
        self.near_out, self.near_in = near_out, near_in
        self.sib = [cp(j, sib_out(j), sib_in.at[j], to_sib) for j in range(4)]
        self.far = [
            cp(4, far_out.at[0], far_in.at[0], to_up),
            cp(5, far_out.at[1], far_in.at[1], to_dn),
        ]
        self.early = [
            cp(6, near_out.at[0, last], near_in.at[0, last], to_up),
            cp(7, near_out.at[1, first], near_in.at[1, first], to_dn),
        ]
        self.late = [
            cp(8, near_out.at[0, first], near_in.at[0, first], to_up),
            cp(9, near_out.at[1, last], near_in.at[1, last], to_dn),
        ]

    def both(self, j, rows):
        return self.mine(j, rows) + self.sib_in[j, rows, :].astype(F32)

    def send_far(self):
        self.sib[0].wait_recv()
        for k in range(2):

            def add(r, k=k):
                q = pl.ds(k * HALF + r.start, r.size)
                self.far_out[k, r, :] = self.both(0, q).astype(BF)

            rows_loop(HALF, 32, add)
            self.far[k].start()

    def send_early(self, k):
        self.sib[1 + k].wait_recv()

        def add(r):
            q = pl.ds((1 - k) * HALF + r.start, r.size)
            self.near_out[k, q, :] = self.both(1 + k, q).astype(BF)

        rows_loop(HALF, 32, add)
        self.early[k].start()

    def send_late(self):
        for k in range(2):
            self.far[k].wait_recv()

            def add(r, k=k):
                q = pl.ds(k * HALF + r.start, r.size)
                self.near_out[k, q, :] = (
                    self.both(1 + k, q) + self.far_in[k, r, :].astype(F32)
                ).astype(BF)

            rows_loop(HALF, 32, add)
            self.late[k].start()

    def wait(self):
        self.sib[3].wait_recv()
        for one in self.early + self.late:
            one.wait_recv()

    def total(self, rows):
        return (
            self.both(3, rows)
            + self.near_in[0, rows, :].astype(F32)
            + self.near_in[1, rows, :].astype(F32)
        )

    def finish(self):
        for one in self.sib + self.far + self.early + self.late:
            one.wait_send()


def ring_scatter(partial, scratch, between=None, before_late=None):
    part, sib_out = scratch[:2]
    c = lax.axis_index("core")
    scatter = RingScatter(
        lambda j, rows: part[j, rows, :], lambda j: sib_out.at[j], *scratch[2:]
    )

    def produce(j):
        def put(columns, value):
            part[j, :, columns] = jnp.where(c == 0, value[0], value[1])
            sib_out[j, :, columns] = jnp.where(c == 0, value[1], value[0]).astype(BF)

        partial(scatter.order[j], put)
        scatter.sib[j].start()

    produce(0)
    produce(1)
    scatter.send_far()
    scatter.send_early(0)
    produce(2)
    scatter.send_early(1)
    if before_late is not None:
        before_late()
    scatter.send_late()
    produce(3)
    if between is not None:
        between()
    scatter.wait()
    return scatter


AG_SCRATCH = [
    pltpu.VMEM((BLOCK, D), BF),
    pltpu.SemaphoreType.DMA,
    pltpu.SemaphoreType.DMA((N_AG,)),
    pltpu.SemaphoreType.DMA((N_AG,)),
]
FULL = jax.ShapeDtypeStruct((4, 2, BLOCK, D), BF)


def order_out(gathered, weight):
    for x in range(4):
        for zl in range(2):
            for a in range(2):
                row = x * 64 + zl * 32 + a * 16
                weight[row : row + 16, :] = gathered[x, a * 2 + zl]


OUT_ROWS = pltpu.VMEM((HD, D), BF)


NN = (((1,), (0,)), ((), ()))
NT = (((1,), (1,)), ((), ()))
TN = (((0,), (0,)), ((), ()))
TOKENS = 4 * BLOCK
KEYS = 2 * TOKENS
TILE = 2 * BLOCK


def dot(a, b, dims):
    return lax.dot_general(a, b, dims, preferred_element_type=F32)


def lane(n):
    return lax.broadcasted_iota(jnp.int32, (1, n), 1)


def turn_tables(base):
    entry = lax.rem(lane(BLOCK), HEAD_DIM)
    freq = jnp.exp(
        lax.rem(entry, ROT // 2).astype(F32) * (-2.0 / ROT * 9.210340371976184)
    )
    freq = jnp.where(entry < ROT, freq, 0.0)
    place = (base + lax.broadcasted_iota(jnp.int32, (BLOCK, 1), 0)).astype(F32)
    phase = place * freq
    return jnp.cos(phase), jnp.sin(phase)


def turn(v, cosine, sines, direction):
    entry = lax.rem(lane(BLOCK), HEAD_DIM)
    s = sines * direction
    ahead = pltpu.roll(v, BLOCK - ROT // 2, 1)
    behind = pltpu.roll(v, ROT // 2, 1)
    return v * cosine + jnp.where(entry < ROT // 2, -ahead, behind) * s


def key_bias(table, g, tile, blocks, q_part=0):
    token = lane(BLOCK)
    q_code, q_low = [], []
    for j in range(2):
        block = 4 * q_part + 2 * tile + j
        low = table[g, 1, block] * 4096
        q_code.append(low + table[g, 0, block] + token)
        q_low.append(low + jnp.zeros_like(token))
    q_code = jnp.concatenate(q_code, axis=1)
    q_low = jnp.concatenate(q_low, axis=1)
    column = lax.broadcasted_iota(jnp.int32, (BLOCK, 1), 0)
    rows = []
    for k in blocks:
        place = table[g, 0, k] + column
        code = jnp.where(place < table[g, 2, k], table[g, 1, k] * 4096 + place, 1 << 20)
        kept = jnp.logical_and(code <= q_code, code >= q_low)
        rows.append(jnp.where(kept, 0.0, NEG))
    return jnp.concatenate(rows, axis=0)


def head_mask(h):
    first = lane(BLOCK) < HEAD_DIM
    return jnp.where(first if h == 0 else jnp.logical_not(first), 1.0, 0.0).astype(BF)


def load(pairs, sems, first=0):
    copies = []
    for i, (src, dst) in enumerate(pairs):
        copies.append(pltpu.make_async_copy(src, dst, sems.at[first + i]))
        copies[-1].start()
    return copies


def kernel_attend(
    table,
    tokens_hbm,
    weight_hbm,
    shift,
    cotangent,
    out_in,
    hidden,
    gains,
    queries,
    kv,
    lse,
    attended,
    grad_out,
    out_full,
    middle,
    grad_all,
    two_all,
    out_rows,
    out_weight,
    own_two,
    tokens,
    weight,
    cosines,
    sines,
    tops,
    totals,
    mixed,
    local,
    send,
    recv,
    *sems,
):
    partner = {"zh": 1 - lax.axis_index("zh")}
    weight_in, *token_in = load(
        [(weight_hbm, weight)] + [(tokens_hbm.at[y], tokens.at[y]) for y in range(4)], local
    )
    y0, c, up, opp, dn = ring()
    out_rows[...] = permute_rows(out_in[...].astype(F32)).astype(BF)
    meet(list(ring_peers(up, dn, c)) + plane_peers())
    gather = RingGather(grad_out, grad_all, sems[0], sems[1:3])
    plane = PlaneGather(out_rows, out_full, *sems[3:6], 0)
    two_gather = RingGather(own_two, two_all, sems[6], sems[7:9])
    part, sib_out = sems[9:11]
    scatter = RingScatter(
        lambda j, rows: part[j, rows, :], lambda j: sib_out.at[j], *sems[11:]
    )
    plane.start()
    lse[...] = jnp.zeros_like(lse)
    weight_in.wait()
    for y in range(4):
        at = slice(y * BLOCK, (y + 1) * BLOCK)
        for g in range(2):
            cosine, sine = turn_tables(table[g, 0, y])
            cosines[g, at, :] = cosine
            sines[g, at, :] = sine
        token_in[y].wait()
        new = dot(tokens[y].reshape(TILE, D), weight[:, HD:], NN) + shift[:, HD:]
        for g in range(2):
            rows = slice(g * BLOCK, (g + 1) * BLOCK)
            for pair in range(2):
                q = slice(pair * BLOCK, (pair + 1) * BLOCK)
                turned = turn(new[rows, q], cosines[g, at, :], sines[g, at, :], 1.0)
                kv[0, g, at, q] = turned.astype(BF)
            kv[1, g, at, :] = new[rows, HD:].astype(BF)

    own, other = pl.ds(0, TOKENS), pl.ds(TOKENS, TOKENS)
    trade = [
        remote((send, recv), g, kv.at[:, g, own, :], kv.at[:, g, other, :], partner)
        for g in range(2)
    ]
    for one in trade:
        one.start()
    plane.middle()
    base, limit = table[c, 0, y0], table[c, 2, y0]

    def mask(r):
        place = base + r.start + lax.broadcasted_iota(jnp.int32, (16, 1), 0)
        row = jnp.where(place < limit, cotangent[r, :].astype(F32), 0.0)
        grad_out[r, :] = permute_rows(row).astype(BF)

    rows_loop(BLOCK, 16, mask)
    gather.start()
    for y in range(4):
        at = slice(y * BLOCK, (y + 1) * BLOCK)
        new = dot(tokens[y].reshape(TILE, D), weight[:, :HD], NN) + shift[:, :HD]
        for g in range(2):
            rows = slice(g * BLOCK, (g + 1) * BLOCK)
            for pair in range(2):
                q = slice(pair * BLOCK, (pair + 1) * BLOCK)
                turned = turn(new[rows, q], cosines[g, at, :], sines[g, at, :], 1.0)
                queries[g, at, q] = turned.astype(BF) * jnp.asarray(SCALE, BF)

    first_head = lax.broadcasted_iota(jnp.int32, (BLOCK, 1), 0) < HEAD_DIM

    def work(part, g):
        rows = slice(part * TOKENS, (part + 1) * TOKENS)

        @pl.loop(0, 2)
        def _(tile):
            at = pl.ds(pl.multiple_of(tile * TILE, TILE), TILE)
            bias = key_bias(table, g, tile, range(4 * part, 4 * part + 4))
            for pair in range(2):
                q = slice(pair * BLOCK, (pair + 1) * BLOCK)
                k_all = kv[0, g, rows, q]
                v_all = kv[1, g, rows, q]
                out = jnp.zeros((BLOCK, TILE), F32)
                keep, share = [], []
                for h in range(2):
                    row = slice(2 * pair + h, 2 * pair + h + 1)
                    s = dot(k_all, queries[g, at, q] * head_mask(h), NT) + bias
                    top = jnp.max(s, axis=0, keepdims=True)
                    if part == 1:
                        top = jnp.maximum(top, tops[g, row, at])
                    p = jnp.exp(s - top)
                    total = jnp.sum(p, axis=0, keepdims=True)
                    out = out + dot(v_all * head_mask(h), p.astype(BF), TN)
                    if part == 0:
                        tops[g, row, at] = top
                        totals[g, row, at] = total
                    else:
                        keep.append(jnp.exp(tops[g, row, at] - top))
                        total = total + totals[g, row, at] * keep[h]
                        lse[g, row, at] = top + jnp.log(total)
                        share.append(1.0 / total)
                if part == 0:
                    mixed[g, q, at] = out
                else:
                    out = out + mixed[g, q, at] * jnp.where(first_head, keep[0], keep[1])
                    out = (out * jnp.where(first_head, share[0], share[1])).T.astype(BF)
                    for j in range(2):
                        attended[2 * tile + j, g, :, q] = out[j * BLOCK : (j + 1) * BLOCK]

    def project(g):
        for j in range(4):
            a = attended[scatter.order[j], g]
            for i in range(4):
                q = slice(i * 512, (i + 1) * 512)
                value = dot(a, out_weight[:, q], NN)

                @pl.when(c == g)
                def _(j=j, q=q, value=value):
                    part[j, :, q] = value

                @pl.when(c != g)
                def _(j=j, q=q, value=value):
                    sib_out[j, :, q] = value.astype(BF)

            @pl.when(c != g)
            def _(j=j):
                scatter.sib[j].start()

    def norm(r):
        row = hidden[r, :].astype(F32) + scatter.total(r)
        middle[r, :] = row
        normed, _ = layer_norm(row)
        own_two[r, :] = (normed * gains[2:3, :] + gains[3:4, :]).astype(BF)

    def exchange():
        scatter.send_far()
        scatter.send_early(0)
        scatter.send_early(1)

    def settle():
        scatter.send_late()
        scatter.wait()
        rows_loop(BLOCK, 16, norm)
        two_gather.start()

    def pass_on():
        two_gather.forward()
        two_gather.share()
        two_gather.share_far()

    work(0, 0)
    plane.forward()
    gather.forward()
    work(0, 1)
    gather.share()
    plane.finish()
    order_out(out_full, out_weight)
    trade[0].wait_recv()
    work(1, 0)
    project(0)
    gather.share_far()

    @pl.when(c == 0)
    def _():
        exchange()

    trade[1].wait_recv()
    work(1, 1)
    project(1)

    @pl.when(c == 1)
    def _():
        exchange()

    settle()
    pass_on()

    for one in trade:
        one.wait_send()
    gather.finish()
    two_gather.finish()
    scatter.finish()


SM = pl.BlockSpec(memory_space=pltpu.SMEM)


def attend(table, tokens, weight, shift, cotangent, out_in, hidden, gains, cid):
    return pl.pallas_call(
        kernel_attend,
        out_shape=(
            jax.ShapeDtypeStruct((2, TOKENS, HD), BF),
            jax.ShapeDtypeStruct((2, 2, KEYS, HD), BF),
            jax.ShapeDtypeStruct((2, 8, TOKENS), F32),
            jax.ShapeDtypeStruct((4, 2, BLOCK, HD), BF),
            jax.ShapeDtypeStruct((BLOCK, D), BF),
            jax.ShapeDtypeStruct((4, 4, 16, D), BF),
            jax.ShapeDtypeStruct((BLOCK, D), F32),
            FULL,
            FULL,
        ),
        in_specs=[SM, ANY, ANY] + [VM] * 5,
        out_specs=(VM,) * 7 + (ANY, ANY),
        scratch_shapes=[
            pltpu.VMEM((16, D), BF),
            OUT_ROWS,
            pltpu.VMEM((BLOCK, D), BF),
            pltpu.VMEM((4, 2, BLOCK, D), BF),
            pltpu.VMEM((D, 3 * HD), BF),
            pltpu.VMEM((2, TOKENS, BLOCK), F32),
            pltpu.VMEM((2, TOKENS, BLOCK), F32),
            pltpu.VMEM((2, 8, TOKENS), F32),
            pltpu.VMEM((2, 8, TOKENS), F32),
            pltpu.VMEM((2, HD, TOKENS), F32),
            pltpu.SemaphoreType.DMA((5,)),
            pltpu.SemaphoreType.DMA((2,)),
            pltpu.SemaphoreType.DMA((2,)),
        ]
        + AG_SCRATCH[1:]
        + PG_SEMS
        + AG_SCRATCH[1:]
        + RS_SCRATCH,
        compiler_params=params(cid),
        name="attend",
    )(table, tokens, weight, shift, cotangent, out_in, hidden, gains)


def kernel_attend_back(
    table,
    branch_own,
    gathered,
    attended,
    queries,
    kv,
    lse,
    other_queries,
    other_lse,
    mlp_out,
    middle_hbm,
    joined_grad,
    out_part,
    hidden_out,
    branch,
    middle,
    own_out,
    probs,
    other_probs,
    local,
    weight,
    grads,
    other_grads,
    dq,
    mean,
    other_mean,
    dkv,
    send,
    recv,
    local_sem,
    gather_send,
    gather_recv,
    *scratch,
):
    partner = {"zh": 1 - lax.axis_index("zh")}
    y0, c, up, opp, dn = ring()
    order = (opp, up, dn, y0)
    out_in = load([(mlp_out.at[order[j], c], own_out.at[j]) for j in range(4)], local)
    (middle_in,) = load([(middle_hbm, middle)], local, 4)
    meet(list(ring_peers(up, dn, c)) + [partner])
    gather = RingGather(branch_own, branch, local_sem, (gather_send, gather_recv))
    gather.start()
    scatter = RingScatter(
        lambda j, rows: own_out[j, rows, :].astype(F32),
        lambda j: mlp_out.at[order[j], 1 - c],
        *scratch,
    )
    for one in scatter.sib:
        one.start()
    order_out(gathered, weight)
    trade = [
        remote((send, recv), 0, mean, other_mean, partner),
        remote((send, recv), 1, grads.at[0], other_grads.at[0], partner),
        remote((send, recv), 2, grads.at[1], other_grads.at[1], partner),
    ]

    def recompute(part, g):
        q_src, lse_src = (queries, lse) if part == 0 else (other_queries, other_lse)
        dst = probs if part == 0 else other_probs
        blocks = range(8) if part == 0 else range(4)
        rows = slice(0, len(blocks) * BLOCK)

        @pl.loop(0, 2)
        def _(tile):
            at = pl.ds(pl.multiple_of(tile * TILE, TILE), TILE)
            bias = key_bias(table, g, tile, blocks, part)
            for pair in range(2):
                q = slice(pair * BLOCK, (pair + 1) * BLOCK)
                for h in range(2):
                    row = slice(2 * pair + h, 2 * pair + h + 1)
                    s = dot(kv[0, g, rows, q], q_src[g, at, q] * head_mask(h), NT) + bias
                    dst[g, tile, 2 * pair + h] = jnp.exp(s - lse_src[g, row, at])

    recompute(0, 0)
    gather.forward()
    recompute(0, 1)
    gather.share()
    gather.share_far()
    recompute(1, 0)
    recompute(1, 1)
    gather.finish()

    dq[...] = jnp.zeros_like(dq)
    dkv[...] = jnp.zeros_like(dkv)
    mean[...] = jnp.zeros_like(mean)
    heads = jnp.concatenate([head_mask(0), head_mask(1)] * 8, axis=0)
    for y in range(4):
        at = slice(y * BLOCK, (y + 1) * BLOCK)
        new = dot(branch[y].reshape(TILE, D), weight[...], NT)
        for g in range(2):
            rows = slice(g * BLOCK, (g + 1) * BLOCK)
            grads[g, at, :] = new[rows].astype(BF)
    for g in range(2):
        for pair in range(2):
            q = slice(pair * BLOCK, (pair + 1) * BLOCK)
            mixed = attended[:, g, :, q].reshape(TOKENS, BLOCK).astype(F32)
            mixed = mixed * grads[g, :, q].astype(F32)
            high = mixed.astype(BF)
            low = (mixed - high.astype(F32)).astype(BF)
            both = dot(heads, high, NT) + dot(heads, low, NT)
            mean[g, 2 * pair : 2 * pair + 2, :] = both[0:2]
    for one in trade:
        one.start()
    for one in out_in:
        one.wait()
    scatter.send_far()
    scatter.send_early(0)
    scatter.send_early(1)

    def back(part, g):
        q_src, g_src = (queries, grads) if part == 0 else (other_queries, other_grads)
        mean_src, p_src = (mean, probs) if part == 0 else (other_mean, other_probs)
        rows = slice(0, KEYS if part == 0 else TOKENS)

        @pl.loop(0, 2)
        def _(tile):
            at = pl.ds(pl.multiple_of(tile * TILE, TILE), TILE)
            for pair in range(2):
                q = slice(pair * BLOCK, (pair + 1) * BLOCK)
                k_all = kv[0, g, rows, q]
                v_all = kv[1, g, rows, q]
                new_q = jnp.zeros((BLOCK, TILE), F32)
                new_k = jnp.zeros((TOKENS, BLOCK), F32)
                new_v = jnp.zeros((TOKENS, BLOCK), F32)
                for h in range(2):
                    row = slice(2 * pair + h, 2 * pair + h + 1)
                    q_head = q_src[g, at, q] * head_mask(h)
                    g_head = g_src[g, at, q] * head_mask(h)
                    p = p_src[g, tile, 2 * pair + h]
                    p_grad = dot(v_all, g_head, NT)
                    s_grad = (p * (p_grad - mean_src[g, row, at])).astype(BF)
                    new_v = new_v + dot(p[:TOKENS].astype(BF), g_head, NN)
                    new_k = new_k + dot(s_grad[:TOKENS], q_head, NN)
                    if part == 0:
                        new_q = new_q + dot(k_all * head_mask(h), s_grad, TN)
                if part == 0:
                    dq[g, q, at] += new_q
                dkv[0, g, :, q] += new_k
                dkv[1, g, :, q] += new_v

    back(0, 0)
    scatter.send_late()
    back(0, 1)

    for i in range(2):
        q = slice(i * 1024, (i + 1) * 1024)
        new = dot(attended[...].reshape(8 * BLOCK, HD), branch[:, :, :, q].reshape(8 * BLOCK, 1024), TN)
        for x in range(4):
            for zl in range(2):
                for a in range(2):
                    row = x * 64 + zl * 32 + a * 16
                    out_part[x * 4 + a * 2 + zl, :, q] = new[row : row + 16].astype(BF)

    scatter.wait()
    middle_in.wait()

    def add(r):
        hidden_out[r, :] = restore_rows(middle[r, :] + scatter.total(r)).astype(BF)

    rows_loop(BLOCK, 16, add)

    def turn_back(g, queries_part):
        @pl.loop(0, 4)
        def _(y):
            at = pl.ds(pl.multiple_of(y * BLOCK, BLOCK), BLOCK)
            cosine, sine = turn_tables(table[g, 0, y])
            for pair in range(2):
                q = slice(pair * BLOCK, (pair + 1) * BLOCK)
                if queries_part:
                    new = dq[g, q, at].T * SCALE
                    joined_grad[y, g, :, q] = turn(new, cosine, sine, -1.0).astype(BF)
                else:
                    joined_grad[y, g, :, HD + pair * BLOCK : HD + (pair + 1) * BLOCK] = turn(
                        dkv[0, g, at, q], cosine, sine, -1.0
                    ).astype(BF)
            if not queries_part:
                joined_grad[y, g, :, 2 * HD :] = dkv[1, g, at, :].astype(BF)

    for g in range(2):
        turn_back(g, True)
    trade[0].wait_recv()
    for g in range(2):
        trade[1 + g].wait_recv()
        back(1, g)
        turn_back(g, False)

    for one in trade:
        one.wait_send()
    scatter.finish()


def attend_back(
    table,
    branch,
    gathered,
    attended,
    queries,
    kv,
    lse,
    other_queries,
    other_lse,
    mlp_out,
    middle,
    cid,
):
    return pl.pallas_call(
        kernel_attend_back,
        out_shape=(
            jax.ShapeDtypeStruct((4, 2, BLOCK, 3 * HD), BF),
            jax.ShapeDtypeStruct((16, 16, D), BF),
            jax.ShapeDtypeStruct((BLOCK, D), BF),
        ),
        in_specs=[SM] + [VM] * 8 + [ANY, ANY],
        out_specs=(VM, VM, VM),
        scratch_shapes=[
            pltpu.VMEM((4, 2, BLOCK, D), BF),
            pltpu.VMEM((BLOCK, D), F32),
            pltpu.VMEM((4, BLOCK, D), BF),
            pltpu.VMEM((2, 2, 4, KEYS, TILE), F32),
            pltpu.VMEM((2, 2, 4, TOKENS, TILE), F32),
            pltpu.SemaphoreType.DMA((5,)),
            OUT_ROWS,
            pltpu.VMEM((2, TOKENS, HD), BF),
            pltpu.VMEM((2, TOKENS, HD), BF),
            pltpu.VMEM((2, HD, TOKENS), F32),
            pltpu.VMEM((2, 8, TOKENS), F32),
            pltpu.VMEM((2, 8, TOKENS), F32),
            pltpu.VMEM((2, 2, TOKENS, HD), F32),
            pltpu.SemaphoreType.DMA((3,)),
            pltpu.SemaphoreType.DMA((3,)),
        ]
        + AG_SCRATCH[1:]
        + RS_SCRATCH[2:],
        compiler_params=params(cid),
        name="attend_back",
    )(
        table,
        branch,
        gathered,
        attended,
        queries,
        kv,
        lse,
        other_queries,
        other_lse,
        mlp_out,
        middle,
    )


def kernel_mlp(
    two_hbm,
    grad_hbm,
    w_hbm,
    middle,
    grad_out,
    gains,
    queries,
    lse,
    middle_grad,
    sums,
    own,
    other_queries,
    other_lse,
    out_hbm,
    part_hbm,
    two,
    grad_all,
    w,
    out_part,
    mlp_part,
    inner,
    both_grads,
    local,
    leave,
    send,
    recv,
    *scratch,
):
    y, c, up, opp, dn = ring()
    partner = {"zh": 1 - lax.axis_index("zh")}
    order = (opp, up, dn, y)
    first = order[0]
    loads = load([(two_hbm.at[first], two.at[first])], local)
    weights_in = [
        load([(w_hbm.at[z, :, k], w.at[k, :, z]) for z in range(4)], local, 8 + 4 * k)
        for k in range(3)
    ]
    loads += load([(grad_hbm.at[first], grad_all.at[first])], local, 1)
    for i, b in enumerate(order[1:]):
        pairs = [(two_hbm.at[b], two.at[b]), (grad_hbm.at[b], grad_all.at[b])]
        loads += load(pairs, local, 2 + 2 * i)
    meet(list(ring_peers(up, dn, c)) + [partner])
    trade = [
        remote((send, recv), 0, queries, other_queries, partner),
        remote((send, recv), 1, lse, other_lse, partner),
    ]
    for one in trade:
        one.start()
    held = jnp.logical_or(lane(FP) >= BLOCK, y < 2)
    gate_lanes, up_lanes = pl.ds(0, FP), pl.ds(FP, FP)
    outs = []

    def arrive(k):
        loads.pop(0).wait()
        if not outs:
            for one in weights_in[k]:
                one.wait()

    def partial(block, put):
        arrive(0)
        a = two[block].reshape(TILE, D)
        gate = dot(a, w[0].reshape(D, FP), NN)
        if not outs:
            for one in weights_in[1]:
                one.wait()
        up_proj = dot(a, w[1].reshape(D, FP), NN)
        arrive(2)
        grad = dot(grad_all[block].reshape(TILE, D), w[2].reshape(D, FP), NN)
        sig = 1.0 / (1.0 + jnp.exp(-gate))
        active = gate * sig
        low = (active * up_proj).astype(BF)
        low_gate = (grad * up_proj * sig * (1.0 + gate * (1.0 - sig))).astype(BF)
        low_up = (grad * active).astype(BF)
        zero = jnp.zeros((), BF)
        inner[block] = jnp.where(held, low, zero).reshape(2, BLOCK, FP)
        both_grads[block, :, :, gate_lanes] = jnp.where(held, low_gate, zero).reshape(2, BLOCK, FP)
        both_grads[block, :, :, up_lanes] = jnp.where(held, low_up, zero).reshape(2, BLOCK, FP)

        low_gate = both_grads[block, :, :, gate_lanes].reshape(TILE, FP)
        low_up = both_grads[block, :, :, up_lanes].reshape(TILE, FP)
        for i in range(4):
            q = slice(i * 512, (i + 1) * 512)
            new = dot(low_gate, w[0, i].reshape(512, FP), NT)
            new = new + dot(low_up, w[1, i].reshape(512, FP), NT)
            put(q, new.reshape(2, BLOCK, 512))
        low = inner[block].reshape(TILE, FP)
        for i in range(4):
            q = slice(i * 512, (i + 1) * 512)
            new = dot(low, w[2, i].reshape(512, FP), NT)
            out_part[block, :, :, q] = new.astype(BF).reshape(2, BLOCK, 512)

        outs.extend(load([(out_part.at[block], out_hbm.at[block])], leave, len(outs)))

    done = []

    def weight_grads(count=1):
        begin = len(done)

        @pl.loop(begin, begin + count)
        def _(i):
            q = pl.ds(pl.multiple_of(i * TILE, TILE), TILE)
            a = two[:, :, :, q].reshape(TP * BLOCK, TILE)
            b = grad_all[:, :, :, q].reshape(TP * BLOCK, TILE)
            new = dot(a, both_grads[...].reshape(TP * BLOCK, 2 * FP), TN).astype(BF)
            at = pl.ds(2 * i, 2)
            mlp_part[at, 0] = new[:, :FP].reshape(2, BLOCK, FP)
            mlp_part[at, 1] = new[:, FP:].reshape(2, BLOCK, FP)
            new = dot(b, inner[...].reshape(TP * BLOCK, FP), TN).astype(BF)
            mlp_part[at, 2] = new.reshape(2, BLOCK, FP)

        for i in range(begin, begin + count):
            done.extend(
                load(
                    [(mlp_part.at[pl.ds(2 * i, 2)], part_hbm.at[pl.ds(i % 2 * 2, 2), i // 2])],
                    leave,
                    4 + i,
                )
            )

    scatter = ring_scatter(partial, scratch, lambda: weight_grads(8))
    sums[...] = jnp.zeros_like(sums)

    def back(r):
        row = scatter.total(r)
        normed, inv = layer_norm(middle[r, :])
        grad = grad_out[r, :].astype(F32) + norm_back(row, normed, inv, gains[2:3, :])
        middle_grad[r, :] = grad
        own[r, :] = grad.astype(BF)
        sums[0:1, :] += jnp.sum(row * normed, axis=0, keepdims=True)
        sums[1:2, :] += jnp.sum(row, axis=0, keepdims=True)

    rows_loop(BLOCK, 16, back)
    scatter.finish()
    for one in outs + done + trade:
        one.wait()


def mlp(two, grad_all, w, middle, grad_out, gains, queries, lse, cid):
    block = (4, 2, BLOCK, D)
    return pl.pallas_call(
        kernel_mlp,
        out_shape=(
            jax.ShapeDtypeStruct((BLOCK, D), F32),
            jax.ShapeDtypeStruct((8, D), F32),
            jax.ShapeDtypeStruct((BLOCK, D), BF),
            jax.ShapeDtypeStruct((2, TOKENS, HD), BF),
            jax.ShapeDtypeStruct((2, 8, TOKENS), F32),
            FULL,
            jax.ShapeDtypeStruct((4, 4, 3, BLOCK, FP), BF),
        ),
        in_specs=[ANY] * 3 + [VM] * 5,
        out_specs=(VM,) * 5 + (ANY, ANY),
        scratch_shapes=[
            pltpu.VMEM(block, BF),
            pltpu.VMEM(block, BF),
            pltpu.VMEM((3, 4, 4, BLOCK, FP), BF),
            pltpu.VMEM(block, BF),
            pltpu.VMEM((16, 3, BLOCK, FP), BF),
            pltpu.VMEM((4, 2, BLOCK, FP), BF),
            pltpu.VMEM((4, 2, BLOCK, 2 * FP), BF),
            pltpu.SemaphoreType.DMA((20,)),
            pltpu.SemaphoreType.DMA((12,)),
            pltpu.SemaphoreType.DMA((2,)),
            pltpu.SemaphoreType.DMA((2,)),
        ]
        + RS_SCRATCH,
        compiler_params=params(cid),
        name="mlp",
    )(two, grad_all, w, middle, grad_out, gains, queries, lse)


class PlaneScatter:
    COPIES = 18

    def __init__(self, part, *scratch):
        near, far, relay, mid, last = (scratch[2 * i : 2 * i + 2] for i in range(5))
        sems = scratch[10:12]
        self.part, self.near, self.far, self.passed, self.mid, self.last = (
            part,
            near,
            far,
            relay,
            mid,
            last,
        )
        half = part.shape[-1] // 2
        self.lanes = pl.ds(0, half), pl.ds(half, half)
        x = lax.axis_index("x")
        z = lax.axis_index("zh") * 2 + lax.axis_index("zl")
        self.place = z, x
        low, high = pl.ds(0, 2), pl.ds(2, 2)
        self.low, self.high = low, high

        def to_x(d):
            return {"x": lax.rem(x + d, 4)}

        def to_z(d):
            there = lax.rem(z + d, 4)
            return {"zh": there // 2, "zl": lax.rem(there, 2)}

        self.first, self.late, self.two = [], [], []
        for k in range(2):
            first_to, second_to = (to_z, to_x) if k == 0 else (to_x, to_z)
            base = 9 * k
            up, dn = first_to(1), first_to(3)
            pieces = (
                (self.piece(k, low, 2), far[k].at[0], up),
                (self.piece(k, high, 2), far[k].at[1], dn),
                (self.piece(k, high, 1), near[k].at[0, high], up),
                (self.piece(k, low, 3), near[k].at[1, low], dn),
            )
            for i, (src, dst, peer) in enumerate(pieces):
                self.first.append(remote(sems, base + i, src, dst, peer))
            self.late.append(remote(sems, base + 4, relay[k].at[0], near[k].at[0, low], up))
            self.late.append(remote(sems, base + 5, relay[k].at[1], near[k].at[1, high], dn))
            for d in range(1, 4):
                there = lax.rem(self.place[1 - k] + d, 4)
                copy = remote(sems, base + 5 + d, mid[k].at[there], last[k].at[d - 1], second_to(d))
                self.two.append(copy)

    def piece(self, k, rest, d):
        there = lax.rem(self.place[k] + d, 4)
        at = (rest, there) if k == 0 else (there, rest)
        return self.part.at[at + (slice(None), self.lanes[k])]

    def start(self):
        for copy in self.first:
            copy.start()

    def relay(self):
        for k in range(2):
            for i, (rest, d) in enumerate(((self.low, 1), (self.high, 3))):
                self.first[4 * k + i].wait_recv()
                self.passed[k][i] = (
                    self.piece(k, rest, d)[...].astype(F32) + self.far[k][i].astype(F32)
                ).astype(BF)
                self.late[2 * k + i].start()

    def middle(self):
        for k in range(2):
            for copy in self.first[4 * k + 2 : 4 * k + 4] + self.late[2 * k : 2 * k + 2]:
                copy.wait_recv()

            @pl.loop(0, 4)
            def _(i, k=k):
                at = (i, self.place[0]) if k == 0 else (self.place[1], i)
                own = self.part[at + (slice(None), self.lanes[k])].astype(F32)
                near = self.near[k][0, i].astype(F32) + self.near[k][1, i].astype(F32)
                self.mid[k][i] = (own + near).astype(BF)

            for copy in self.two[3 * k : 3 * k + 3]:
                copy.start()

    def finish(self, out):
        for copy in self.two:
            copy.wait_recv()
        for k in range(2):
            out[:, self.lanes[k]] = (
                self.mid[k][self.place[1 - k]].astype(F32)
                + jnp.sum(self.last[k][...].astype(F32), axis=0)
            ).astype(BF)
        for copy in self.first + self.late + self.two:
            copy.wait_send()


def plane_scratch(rows, lanes):
    half = lanes // 2
    shapes = [(2, 4, rows, half), (2, 2, rows, half), (2, 2, rows, half), (4, rows, half)]
    shapes += [(3, rows, half)]
    return [pltpu.VMEM(shape, BF) for shape in shapes for _ in range(2)] + [
        pltpu.SemaphoreType.DMA((PlaneScatter.COPIES,)),
        pltpu.SemaphoreType.DMA((PlaneScatter.COPIES,)),
    ]


def plane_peers():
    peers = []
    for d in range(1, 4):
        z = lax.rem(lax.axis_index("zh") * 2 + lax.axis_index("zl") + d, 4)
        peers.append({"x": lax.rem(lax.axis_index("x") + d, 4)})
        peers.append({"zh": z // 2, "zl": lax.rem(z, 2)})
    return peers


def kernel_qkv_back(
    joined_grad,
    weight_hbm,
    hidden,
    middle_hbm,
    gains,
    tokens_hbm,
    out_part,
    input_grad,
    sums,
    shift_sum,
    qkv_sum,
    out_sum,
    tokens,
    weight,
    middle_grad,
    local,
    part,
    *scratch,
):
    token_in = load([(tokens_hbm.at[y], tokens.at[y]) for y in range(4)], local)
    weight_in, middle_in = load([(weight_hbm, weight), (middle_hbm, middle_grad)], local, 4)
    y, c, up, opp, dn = ring()
    meet(list(ring_peers(up, dn, c)) + plane_peers())
    out_scatter = PlaneScatter(out_part, *scratch[:12])
    qkv_scatter = PlaneScatter(part, *scratch[12:24])
    out_scatter.start()
    flat = joined_grad[...].reshape(TP * BLOCK, 3 * HD)
    def weight_grads():
        for one in token_in:
            one.wait()
        for i in range(4):
            q = slice(i * 512, (i + 1) * 512)
            new = dot(tokens[:, :, :, q].reshape(TP * BLOCK, 512), flat, TN).astype(BF)
            part[i] = new.reshape(4, BLOCK, 3 * HD)
        qkv_scatter.start()
        weight_in.wait()
        middle_in.wait()

    def partial(block, put):
        a = joined_grad[block].reshape(2 * BLOCK, 3 * HD)
        for i in range(4):
            q = slice(i * 512, (i + 1) * 512)
            put(q, dot(a, weight[q, :], NT).reshape(2, BLOCK, 512))

    weight_grads()
    out_scatter.relay()
    scatter = ring_scatter(partial, scratch[24:], out_scatter.middle, qkv_scatter.relay)
    sums[...] = jnp.zeros_like(sums)

    def back(r):
        row = scatter.total(r)
        normed, inv = layer_norm(hidden[r, :].astype(F32))
        input_grad[r, :] = restore_rows(
            middle_grad[r, :] + norm_back(row, normed, inv, gains[0:1, :])
        )
        sums[0:1, :] += jnp.sum(row * normed, axis=0, keepdims=True)
        sums[1:2, :] += jnp.sum(row, axis=0, keepdims=True)

    rows_loop(BLOCK, 16, back)
    qkv_scatter.middle()
    shift_sum[...] = jnp.broadcast_to(
        jnp.sum(flat.astype(F32), axis=0, keepdims=True), shift_sum.shape
    )
    scatter.finish()
    out_scatter.finish(out_sum)
    qkv_scatter.finish(qkv_sum)


def qkv_back(joined_grad, weight, hidden, middle_grad, gains, tokens, out_part, cid):
    return pl.pallas_call(
        kernel_qkv_back,
        out_shape=(
            jax.ShapeDtypeStruct((BLOCK, D), F32),
            jax.ShapeDtypeStruct((8, D), F32),
            jax.ShapeDtypeStruct((8, 3 * HD), F32),
            jax.ShapeDtypeStruct((BLOCK, 3 * HD), BF),
            jax.ShapeDtypeStruct((16, D), BF),
        ),
        in_specs=[VM, ANY, VM, ANY, VM, ANY, VM],
        out_specs=(VM,) * 5,
        scratch_shapes=[
            pltpu.VMEM((4, 2, BLOCK, D), BF),
            pltpu.VMEM((D, 3 * HD), BF),
            pltpu.VMEM((BLOCK, D), F32),
            pltpu.SemaphoreType.DMA((6,)),
            pltpu.VMEM((4, 4, BLOCK, 3 * HD), BF),
        ]
        + plane_scratch(16, D)
        + plane_scratch(BLOCK, 3 * HD)
        + RS_SCRATCH,
        compiler_params=params(cid),
        name="qkv_back",
    )(joined_grad, weight, hidden, middle_grad, gains, tokens, out_part.reshape(4, 4, 16, D))


TP_STEPS = [(dy, dc) for dy in range(4) for dc in range(2) if (dy, dc) != (0, 0)]
XZ_STEPS = [(dx, dz) for dx in range(4) for dz in range(4) if (dx, dz) != (0, 0)]


def tp_peer(step):
    y = lax.rem(lax.axis_index("y") + step[0], 4)
    c = lax.rem(lax.axis_index("core") + step[1], 2)
    return {"y": y, "core": c}, y * 2 + c


def xz_peer(step):
    x = lax.rem(lax.axis_index("x") + step[0], 4)
    z = lax.rem(lax.axis_index("zh") * 2 + lax.axis_index("zl") + step[1], 4)
    return {"x": x, "zh": z // 2, "zl": lax.rem(z, 2)}, x * 4 + z


def meet_all(split):
    peers = [tp_peer(s)[0] for s in TP_STEPS] + [xz_peer(s)[0] for s in XZ_STEPS]
    barrier = pltpu.get_barrier_semaphore()
    for peer in peers:
        pl.semaphore_signal(
            barrier, inc=1, device_id=peer, device_id_type=pl.DeviceIdType.MESH
        )

    @pl.when(split)
    def _():
        pl.semaphore_signal(
            barrier, inc=1, device_id=swap_peer(), device_id_type=pl.DeviceIdType.MESH
        )

    pl.semaphore_wait(barrier, len(peers) + split.astype(jnp.int32))


def swap_peer():
    return {"zh": lax.axis_index("core"), "core": lax.axis_index("zh")}


def swap_start(split, src, dst, local_sem, sems, i):
    @pl.when(split)
    def _():
        remote(sems, i, src, dst, swap_peer()).start()

    @pl.when(jnp.logical_not(split))
    def _():
        pltpu.make_async_copy(src, dst, local_sem).start()


def swap_wait(split, src, dst, local_sem, sems, i):
    @pl.when(split)
    def _():
        remote(sems, i, src, dst, swap_peer()).wait()

    @pl.when(jnp.logical_not(split))
    def _():
        pltpu.make_async_copy(src, dst, local_sem).wait()


N_TP = len(TP_STEPS)
N_XZ = len(XZ_STEPS)


class PlaneGather:
    COPIES = 14

    def __init__(self, src, full, local_sem, send, recv, x_first):
        sems = send, recv
        a, b = pl.ds(0, x_first), pl.ds(x_first, src.shape[-1] - x_first)
        rest = (slice(None),) * (len(src.shape) - 1)
        x = lax.axis_index("x")
        z = lax.axis_index("zh") * 2 + lax.axis_index("zl")
        self.one, self.two, self.three = [], [], []
        every, low, high = slice(None), pl.ds(0, 2), pl.ds(2, 2)

        def x_at(d):
            return lax.rem(x + d, 4)

        def z_at(d):
            return lax.rem(z + d, 4)

        def to_x(d):
            return {"x": x_at(d)}

        def to_z(d):
            return {"zh": z_at(d) // 2, "zl": lax.rem(z_at(d), 2)}

        def pass_on(i, at, peer):
            return remote(sems, i, full.at[at], full.at[at], peer)

        if x_first:
            at = rest + (a,)
            for d in range(1, 4):
                self.one.append(remote(sems, d - 1, src.at[at], full.at[(x, z) + at], to_x(d)))
            self.two.append(pass_on(6, (every, z) + at, to_z(1)))
            self.two.append(pass_on(7, (every, z) + at, to_z(3)))
            self.three.append(pass_on(8, (low, z_at(3)) + at, to_z(1)))
            self.three.append(pass_on(9, (high, z_at(1)) + at, to_z(3)))
        at = rest + (b,)
        for d in range(1, 4):
            self.one.append(remote(sems, 2 + d, src.at[at], full.at[(x, z) + at], to_z(d)))
        self.two.append(pass_on(10, (x, every) + at, to_x(1)))
        self.two.append(pass_on(11, (x, every) + at, to_x(3)))
        self.three.append(pass_on(12, (x_at(3), low) + at, to_x(1)))
        self.three.append(pass_on(13, (x_at(1), high) + at, to_x(3)))
        self.here = pltpu.make_async_copy(src, full.at[x, z], local_sem)

    def start(self):
        for copy in self.one:
            copy.start()
        self.here.start()

    def middle(self):
        self.here.wait()
        for copy in self.one:
            copy.wait_recv()
        for copy in self.two:
            copy.start()

    def forward(self):
        for copy, later in zip(self.two, self.three):
            copy.wait_recv()
            later.start()

    def finish(self):
        for copy in self.three:
            copy.wait_recv()
        for copy in self.one + self.two + self.three:
            copy.wait_send()


PG_SEMS = [
    pltpu.SemaphoreType.DMA,
    pltpu.SemaphoreType.DMA((PlaneGather.COPIES,)),
    pltpu.SemaphoreType.DMA((PlaneGather.COPIES,)),
]


def first_lane(rank):
    return jnp.where(rank < 4, 6 * rank, 5 * rank + 3) * BLOCK


def head_lane(part, rank):
    return part * D + (lax.rem(rank, 2) * 4 + rank // 2) * HD


def lanes_at(start, n):
    return pl.ds(pl.multiple_of(start, BLOCK), n)


def spread_gains(small_all, gains, entries):
    rows = small_all[...].reshape(BLOCK, BLOCK)
    source = lax.broadcasted_iota(jnp.int32, (BLOCK, 1), 0)
    f = lane(D)
    mine = (f // 16) == source
    for i in entries:
        pick = (source == 16 * i + lax.rem(f, 16)).astype(F32)
        value = jnp.dot(rows, pick, preferred_element_type=F32)
        gains[i : i + 1, :] = jnp.sum(jnp.where(mine, value, 0.0), axis=0, keepdims=True)


def spread_shift(small_all, shift, rank):
    rows = small_all[...].reshape(BLOCK, BLOCK)
    source = lax.broadcasted_iota(jnp.int32, (BLOCK, 1), 0)
    core = lax.rem(source, 2)
    y = lax.rem(source // 2, 4)
    zl = lax.rem(source // 8, 2)
    zh = lax.rem(source // 16, 2)
    x = source // 32
    owner = (zh * 4 + y) * 16 + x * 4 + zl * 2 + core
    for i in range(3):
        j = head_lane(i, rank) + lane(HD)
        pick = (source == 64 + lax.rem(j, 48)).astype(F32)
        value = jnp.dot(rows, pick, preferred_element_type=F32)
        value = jnp.sum(jnp.where(j // 48 == owner, value, 0.0), axis=0, keepdims=True)
        shift[:, i * HD : (i + 1) * HD] = value


def kernel_front(
    small,
    hidden_in,
    w_qkv,
    w_gate,
    w_up,
    w_down,
    w_out,
    small_all,
    gains,
    shift,
    qkv_full,
    mlp_rows,
    out_rows,
    hidden,
    full,
    own,
    normed,
    qkv_rows,
    local,
    send,
    recv,
    *sems,
):
    me = lax.axis_index("y") * 2 + lax.axis_index("core")
    xz = lax.axis_index("x") * 4 + lax.axis_index("zh") * 2 + lax.axis_index("zl")
    split = lax.axis_index("zh") != lax.axis_index("core")
    meet_all(split)
    cp = functools.partial(remote, (send, recv))
    tiny, qkv, mlp = [], [], []
    for k, step in enumerate(TP_STEPS):
        peer, there = tp_peer(step)
        tiny.append(cp(k, small, small_all.at[xz, me], peer))
        for i in range(3):
            src = w_qkv.at[:, lanes_at(head_lane(i, there), HD)]
            dst = qkv_rows.at[me, :, pl.ds(i * HD, HD)]
            qkv.append(cp((1 + i) * N_TP + k, src, dst, peer))
        for i, w in enumerate((w_gate, w_up, w_down)):
            src = w.at[:, lanes_at(first_lane(there), FP)]
            mlp.append(cp((4 + i) * N_TP + k, src, mlp_rows.at[i, me], peer))
    keep = [pltpu.make_async_copy(small, small_all.at[xz, me], local.at[0])]
    for i, w in enumerate((w_gate, w_up, w_down)):
        src = w_qkv.at[:, lanes_at(head_lane(i, me), HD)]
        dst = qkv_rows.at[me, :, pl.ds(i * HD, HD)]
        keep.append(pltpu.make_async_copy(src, dst, local.at[1 + i]))
        src = w.at[:, lanes_at(first_lane(me), FP)]
        keep.append(pltpu.make_async_copy(src, mlp_rows.at[i, me], local.at[4 + i]))
    for one in tiny + qkv + mlp + keep:
        one.start()
    last = 7 * N_TP + N_XZ
    for one in tiny:
        one.wait()
    keep[0].wait()
    wide = []
    for k, step in enumerate(XZ_STEPS):
        peer, _ = xz_peer(step)
        wide.append(cp(7 * N_TP + k, small_all.at[xz], small_all.at[xz], peer))
    for one in wide:
        one.start()
    for one in qkv + keep[1:]:
        one.wait()
    plane = PlaneGather(qkv_rows, qkv_full, *sems[:3], 3 * HD // 2)
    plane.start()
    swap_start(split, w_out, out_rows, local.at[7], (send, recv), last)

    def norm(r):
        row = permute_rows(hidden_in[r, :].astype(F32))
        hidden[r, :] = row.astype(BF)
        normed[r, :], _ = layer_norm(row)

    rows_loop(BLOCK, 16, norm)
    gains[...] = jnp.zeros_like(gains)
    for one in wide:
        one.wait()
    spread_gains(small_all, gains, (0, 1))

    def scale(r):
        own[r, :] = (normed[r, :] * gains[0:1, :] + gains[1:2, :]).astype(BF)

    rows_loop(BLOCK, 16, scale)
    gather = RingGather(own, full, sems[3], sems[4:])
    gather.start()
    plane.middle()
    gather.forward()
    spread_gains(small_all, gains, (2, 3))
    spread_shift(small_all, shift, me)
    gather.share()
    plane.forward()
    gather.share_far()
    for one in mlp:
        one.wait()
    swap_wait(split, w_out, out_rows, local.at[7], (send, recv), last)
    gather.finish()
    plane.finish()


def front(small, hidden, w_qkv, w_gate, w_up, w_down, w_out, cid):
    n = 7 * N_TP + N_XZ + 1
    return pl.pallas_call(
        kernel_front,
        out_shape=(
            jax.ShapeDtypeStruct((16, TP, 1, BLOCK), F32),
            jax.ShapeDtypeStruct((8, D), F32),
            jax.ShapeDtypeStruct((1, 3 * HD), F32),
            jax.ShapeDtypeStruct((4, 4, TP, 16, 3 * HD), BF),
            jax.ShapeDtypeStruct((3, TP, 16, FP), BF),
            jax.ShapeDtypeStruct((16, D), BF),
            jax.ShapeDtypeStruct((BLOCK, D), BF),
            FULL,
        ),
        in_specs=[ANY, VM] + [ANY] * 5,
        out_specs=(VM, VM, VM, ANY, ANY, ANY, VM, ANY),
        scratch_shapes=[
            pltpu.VMEM((BLOCK, D), BF),
            pltpu.VMEM((BLOCK, D), F32),
            pltpu.VMEM((TP, 16, 3 * HD), BF),
            pltpu.SemaphoreType.DMA((8,)),
            pltpu.SemaphoreType.DMA((n,)),
            pltpu.SemaphoreType.DMA((n,)),
        ]
        + PG_SEMS
        + AG_SCRATCH[1:],
        compiler_params=params(cid),
        name="front",
    )(small, hidden, w_qkv, w_gate, w_up, w_down, w_out)


def kernel_collect(
    one_sums,
    two_sums,
    shift,
    qkv,
    mlp,
    out,
    small_all,
    qkv_all,
    mlp_all,
    out_all,
    terms,
    terms_in,
    own,
    local,
    *sems,
):
    me = lax.axis_index("y") * 2 + lax.axis_index("core")
    xz = lax.axis_index("x") * 4 + lax.axis_index("zh") * 2 + lax.axis_index("zl")
    split = lax.axis_index("zh") != lax.axis_index("core")
    for p in range(16):
        q = slice(p * BLOCK, (p + 1) * BLOCK)
        terms[p, 0:2, :] = one_sums[0:2, q]
        terms[p, 2:4, :] = two_sums[0:2, q]
        for i in range(6):
            terms[p, 8 + i : 9 + i, :] = shift[0:1, i * BLOCK : (i + 1) * BLOCK]
        for i in (4, 5, 6, 7, 14, 15):
            terms[p, i : i + 1, :] = jnp.zeros((1, BLOCK), F32)
    meet_all(split)
    cp = functools.partial(remote, sems)
    big, extra, wide = [], [], []
    near, tile = pl.ds(BLOCK, FP - BLOCK), pl.ds(0, BLOCK)
    base = N_XZ + N_TP
    for k, step in enumerate(TP_STEPS):
        peer, there = tp_peer(step)
        dst = mlp_all.at[:, :, lanes_at(first_lane(me) + BLOCK, FP - BLOCK)]
        big.append(cp(base + k, mlp.at[:, there, :, near], dst, peer))
        dst = mlp_all.at[:, :, lanes_at(first_lane(me), BLOCK)]
        extra.append(cp(base + N_TP + k, mlp.at[:, there, :, tile], dst, peer))
        big.append(cp(base + 2 * N_TP + k, qkv.at[there], qkv_all.at[me], peer))
    for k, step in enumerate(XZ_STEPS):
        peer, there = xz_peer(step)
        wide.append(cp(k, terms.at[there], terms_in.at[xz], peer))
    dst = mlp_all.at[:, :, lanes_at(first_lane(me) + BLOCK, FP - BLOCK)]
    keep = [
        pltpu.make_async_copy(mlp.at[:, me, :, near], dst, local.at[0]),
        pltpu.make_async_copy(qkv.at[me], qkv_all.at[me], local.at[1]),
    ]
    dst = mlp_all.at[:, :, lanes_at(first_lane(me), BLOCK)]
    keep_tile = pltpu.make_async_copy(mlp.at[:, me, :, tile], dst, local.at[2])
    first_four = me < 4
    for one in big[0::2]:
        one.start()

    @pl.when(first_four)
    def _():
        keep_tile.start()
        for one in extra:
            one.start()

    for one in wide + big[1::2] + keep:
        one.start()

    last = base + 3 * N_TP
    swap_start(split, out, out_all, local.at[3], sems, last)
    for one in wide:
        one.wait()
    terms_in[xz] = terms[xz]
    own[...] = jnp.sum(terms_in[...], axis=0)
    tiny = []
    for k, step in enumerate(TP_STEPS):
        peer, _ = tp_peer(step)
        tiny.append(cp(N_XZ + k, own, small_all.at[me], peer))
    for one in tiny:
        one.start()
    for one in big + keep:
        one.wait()
    for k, step in enumerate(TP_STEPS):
        source = lax.rem(lax.axis_index("y") + 4 - step[0], 4) * 2 + lax.rem(
            lax.axis_index("core") + 2 - step[1], 2
        )

        @pl.when(source < 4)
        def _(k=k):
            extra[k].wait_recv()

    @pl.when(first_four)
    def _():
        keep_tile.wait()
        for one in extra:
            one.wait_send()

    swap_wait(split, out, out_all, local.at[3], sems, last)
    for one in tiny:
        one.wait()
    small_all[me] = own[...]


def collect(one_sums, two_sums, shift, qkv, mlp, out, cid):
    n = N_XZ + 4 * N_TP + 1
    return pl.pallas_call(
        kernel_collect,
        out_shape=(
            jax.ShapeDtypeStruct((TP, 16, BLOCK), F32),
            jax.ShapeDtypeStruct((TP, 16, 3 * HD), BF),
            jax.ShapeDtypeStruct((3, 16, FF), BF),
            jax.ShapeDtypeStruct((16, D), BF),
        ),
        in_specs=[VM] * 3 + [ANY] * 3,
        out_specs=(VM, ANY, ANY, ANY),
        scratch_shapes=[
            pltpu.VMEM((16, 16, BLOCK), F32),
            pltpu.VMEM((16, 16, BLOCK), F32),
            pltpu.VMEM((16, BLOCK), F32),
            pltpu.SemaphoreType.DMA((4,)),
            pltpu.SemaphoreType.DMA((n,)),
            pltpu.SemaphoreType.DMA((n,)),
        ],
        compiler_params=params(cid),
        name="collect",
    )(one_sums, two_sums, shift, qkv, mlp, out)


def kernel_finish(
    qkv_hbm,
    mlp_hbm,
    out_hbm,
    hidden_hbm,
    grad_hbm,
    qkv_grad,
    gate,
    up,
    down,
    out,
    hidden_out,
    input_grad,
    qkv_all,
    mlp_all,
    out_all,
    local,
):
    pairs = [(qkv_hbm, qkv_all), (mlp_hbm, mlp_all), (out_hbm, out_all)]
    pairs += [(hidden_hbm, hidden_out), (grad_hbm, input_grad)]
    for one in load(pairs, local):
        one.wait()
    for t in range(TP):
        for i in range(3):
            first = i * D + (t % 2 * 4 + t // 2) * HD
            qkv_grad[:, first : first + HD] = qkv_all[t, :, i * HD : (i + 1) * HD].astype(F32)
    gate[...] = mlp_all[0].astype(F32)
    up[...] = mlp_all[1].astype(F32)
    down[...] = mlp_all[2].astype(F32)
    out[...] = restore_rows(out_all[...].astype(F32))


def finish(qkv_all, mlp_all, out_all, hidden, grad):
    wide = jax.ShapeDtypeStruct((16, FF), F32)
    return pl.pallas_call(
        kernel_finish,
        out_shape=(
            jax.ShapeDtypeStruct((16, 3 * D), F32),
            wide,
            wide,
            wide,
            jax.ShapeDtypeStruct((16, D), F32),
            jax.ShapeDtypeStruct((BLOCK, D), BF),
            jax.ShapeDtypeStruct((BLOCK, D), F32),
        ),
        in_specs=[ANY] * 5,
        out_specs=(VM,) * 7,
        scratch_shapes=[
            pltpu.VMEM((TP, 16, 3 * HD), BF),
            pltpu.VMEM((3, 16, FF), BF),
            pltpu.VMEM((16, D), BF),
            pltpu.SemaphoreType.DMA((5,)),
        ],
        compiler_params=pltpu.CompilerParams(vmem_limit_bytes=60 * 1024 * 1024),
        name="finish",
    )(qkv_all, mlp_all, out_all, hidden, grad)


def body(
    hidden_in,
    cotangent,
    seq_lengths,
    slot_block,
    ln1_gain,
    ln1_bias,
    w_qkv,
    qkv_bias,
    w_out,
    ln2_gain,
    ln2_bias,
    w_gate,
    w_up,
    w_down,
):
    f32 = F32
    zh = lax.axis_index("zh")
    y = lax.axis_index("y")
    core = lax.axis_index("core")
    xz = lax.axis_index("x") * 4 + zh * 2 + lax.axis_index("zl")

    small, first = jnp.zeros(BLOCK, f32), 0
    pieces = (ln1_gain, ln1_bias, ln2_gain, ln2_bias, qkv_bias, seq_lengths[0], slot_block[0])
    for piece in pieces:
        n = piece.shape[0]
        small = small + jnp.pad(piece.astype(f32), (first, BLOCK - first - n))
        first += n
    small_all, gains, shift, qkv_full, mlp_rows, out_rows, hidden, one_all = front(
        small.reshape(1, BLOCK), hidden_in[0], w_qkv, w_gate, w_up, w_down, w_out, 0
    )
    qkv_full = qkv_full.reshape(D, 3 * HD)
    mlp_full = lax.all_gather(mlp_rows.reshape(3, BLOCK, FP), ZX, axis=0, tiled=False)
    small_all = small_all.reshape(BLOCK, BLOCK)

    plan = lax.dynamic_slice_in_dim(small_all, xz * TP + y * 2, 2, 0)[:, 112:122].astype(jnp.int32)
    blocks = plan[:, 2:].reshape(2, 2, 4)
    own_blocks = lax.dynamic_index_in_dim(blocks, zh, axis=1, keepdims=False)
    other_blocks = lax.dynamic_index_in_dim(blocks, 1 - zh, axis=1, keepdims=False)
    start = jnp.concatenate([own_blocks, other_blocks], axis=1) * BLOCK
    first_pad = (plan[:, 0:1] + BLOCK - 1) // BLOCK * BLOCK
    second = (start >= first_pad).astype(jnp.int32)
    limit = jnp.where(second == 1, plan[:, 1:2], plan[:, 0:1])
    table = jnp.stack([start - second * first_pad, second, limit], axis=1)
    queries, kv, lse, attended, grad_out, out_full, middle, grad_all, two_all = attend(
        table, one_all, qkv_full, shift, cotangent[0], out_rows, hidden, gains, 6
    )
    middle_grad, two_sums, branch, other_queries, other_lse, mlp_out, mlp_part = mlp(
        two_all, grad_all, mlp_full.reshape(4, 4, 3, BLOCK, FP), middle, grad_out, gains, queries, lse, 3
    )
    mlp_sum = lax.psum_scatter(
        mlp_part.reshape(16 * 3 * BLOCK, FP), ZX, scatter_dimension=0, tiled=True
    )
    joined_grad, out_part, hidden_out = attend_back(
        table,
        branch,
        out_full,
        attended,
        queries,
        kv,
        lse,
        other_queries,
        other_lse,
        mlp_out,
        middle,
        7,
    )
    input_grad, one_sums, shift_sum, qkv_sum, out_sum = qkv_back(
        joined_grad, qkv_full, hidden, middle_grad, gains, one_all, out_part, 4
    )

    small_sum, qkv_all, mlp_all, out_all = collect(
        one_sums,
        two_sums,
        shift_sum,
        qkv_sum.reshape(TP, 16, FP),
        mlp_sum.reshape(3, TP, 16, FP),
        out_sum,
        5,
    )
    qkv_grad, gate_sum, up_sum, down_sum, out_grad, hidden_out, input_grad = finish(
        qkv_all, mlp_all, out_all, hidden_out, input_grad
    )
    vectors = jnp.sum(small_sum[:, :4], axis=0)
    vectors = lax.dynamic_slice_in_dim(vectors, (y * 2 + core) * 16, 16, 1)
    shift_grad = small_sum[:, 8:14].reshape(4, 2, 3, HD).transpose(2, 1, 0, 3).reshape(128, 48)
    row = (zh * 4 + y) * 16 + lax.axis_index("x") * 4 + lax.axis_index("zl") * 2 + core
    shift_grad = lax.dynamic_index_in_dim(shift_grad, row, 0, False)
    return (
        hidden_out[None],
        input_grad[None],
        vectors[0],
        vectors[1],
        qkv_grad,
        shift_grad,
        out_grad,
        vectors[2],
        vectors[3],
        gate_sum,
        up_sum,
        down_sum,
    )


def solution(mesh):
    inner = Mesh(mesh.devices.reshape(2, 4, 4, 2, 2), ROWS)
    rows = P(ROWS)
    tokens = P(GRP, SLOT, None)
    placed = (
        tokens,
        tokens,
        P(GRP, None),
        P(GRP, None),
        rows,
        rows,
        P(ROWS, None),
        rows,
        P(ROWS, None),
        rows,
        rows,
        P(ROWS, None),
        P(ROWS, None),
        P(ROWS, None),
    )
    return jax.shard_map(
        body,
        mesh=inner,
        in_specs=placed,
        out_specs=(
            tokens,
            tokens,
            rows,
            rows,
            P(ROWS, None),
            rows,
            P(ROWS, None),
            rows,
            rows,
            P(ROWS, None),
            P(ROWS, None),
            P(ROWS, None),
        ),
        check_vma=False,
    )
```
